32 devices in a mesh: tmpl: 8 (over z, x), sta: 4 (over y, core).
Axes of the slice: x: 2, y: 2, z: 4, core: 2. Of those that a mesh axis runs over, the one named last changes fastest.
Arguments:
- waveforms: bfloat16 [2048, 3, 1664], P(('tmpl', 'sta')), may hold values from -70 to 70, as said below
- templates: bfloat16 [256, 20, 3, 1024], P(('tmpl', 'sta')), may hold values from -0.5 to 1.5
- stations: int32 [256, 20], P(('tmpl', 'sta')), may hold values from 0 to 2047, as said below
- moveouts: int32 [256, 20], P(('tmpl', 'sta')), may hold values from 0 to 384
Outputs:
- stacks: float32 [256, 256], P(('tmpl', 'sta'))
- strongest: float32 [256], replicated
The draws below stay inside these ranges and needn't reach their ends.
Inputs may be any that keep to these rules, and one draw needn't show every extreme that they name: Station s lies on device s // 64 in the order of tmpl+sta. Of the 160 entries of the templates on one device, at most 10 name stations of one device. `waveforms`: recorded traces of order one to tens.
All inputs are finite; a program needn't handle non-finite values.
Results may differ from the reference program's by a relative error of at most 0.0029.
Values may be sent and summed in bfloat16 or wider, within the bound.
No kernel may reach another device: no remote copies, remote signals or barrier semaphores. Data moves between devices by JAX's collectives and lax.ppermute only.
A program may use at most 64 MiB of HBM per device.

```python
import math
import jax
import jax.numpy as jnp
from jax import lax

L = 1024
SLOTS = 20
SHIFT_MAX = 384
LAGS = 256
TPL_DEV = 8
STN_DEV = 64
TEMPLATES = 256
RECEIVER_COUNT = 2048
SEG = 1280
SEISMOGRAM_LEN = 1664


def draw_waveforms(key, part):
    noise_key = jax.random.fold_in(key, 11)
    gain_key = jax.random.fold_in(key, 12)
    impulse_seed = jax.random.fold_in(key, 13)
    ambient_jitter = jax.random.truncated_normal(noise_key, -4.0, 4.0, (RECEIVER_COUNT, 3, SEISMOGRAM_LEN), jnp.float32)
    receiver_amplitudes = jnp.exp(jax.random.uniform(gain_key, (RECEIVER_COUNT, 3, 1), jnp.float32, -1.15, 1.15))
    impulse_arrivals = jnp.exp(jax.random.uniform(impulse_seed, (RECEIVER_COUNT, 1, SEISMOGRAM_LEN // 16, 1), jnp.float32, 0.0, 1.6))
    impulse_arrivals = jnp.broadcast_to(impulse_arrivals, (RECEIVER_COUNT, 1, SEISMOGRAM_LEN // 16, 16)).reshape(RECEIVER_COUNT, 1, SEISMOGRAM_LEN)
    return (ambient_jitter * receiver_amplitudes * impulse_arrivals).astype(jnp.bfloat16)


def draw_stations(key, part):
    order_key = jax.random.fold_in(key, 21)
    offset_key = jax.random.fold_in(key, 22)
    slot_key = jax.random.fold_in(key, 23)
    base_key = jax.random.fold_in(key, 24)
    owners = TEMPLATES // TPL_DEV
    pair_count = TPL_DEV * SLOTS
    quarter = owners // 4
    units = jnp.arange(pair_count, dtype=jnp.int32) * owners // pair_count
    ranks = jnp.where(units < 2 * quarter, units // 2, units - quarter)
    hot_order = jax.random.permutation(order_key, owners).astype(jnp.int32)
    offsets = jax.random.randint(offset_key, (owners, 1), 0, owners - 1)
    slot_keys = jax.random.split(slot_key, owners)
    arranged = jax.vmap(lambda one_key: jax.random.permutation(one_key, ranks))(slot_keys)
    slot_rank = jnp.where(arranged == 0, 0, 1 + (arranged - 1 + offsets) % (owners - 1))
    target = hot_order[slot_rank].reshape(TEMPLATES, SLOTS)
    matching = target[:, :, None] == target[:, None, :]
    earlier = jnp.arange(SLOTS)[None, :] < jnp.arange(SLOTS)[:, None]
    repeats = jnp.sum(jnp.logical_and(matching, earlier[None]).astype(jnp.int32), axis=2)
    base_row = jax.random.randint(base_key, (TEMPLATES, 1), 0, STN_DEV)
    local_row = (base_row + repeats) % STN_DEV
    return (target * STN_DEV + local_row).astype(jnp.int32)


def touch_ends(result, stream_key, low, top_value):
    spot = [jax.random.randint(jax.random.fold_in(stream_key, axis), (), 0, length) for axis, length in enumerate(result.shape)]
    longest = result.shape.index(max(result.shape))
    neighbour = spot[:longest] + [(spot[longest] + 1) % result.shape[longest]] + spot[longest + 1:]
    return result.at[tuple(spot)].set(low).at[tuple(neighbour)].set(top_value)


def block_scale(rng, extent, shards, low, high):
    loudness, own = 1.0, jax.random.fold_in(rng, 6)
    for dim, parts in shards:
        draws = jnp.exp(jax.random.uniform(jax.random.fold_in(own, dim), (parts,), jnp.float32, low / len(shards), high / len(shards)))
        loudness = loudness * jnp.repeat(draws, extent[dim] // parts).reshape([-1 if axis == dim else 1 for axis in range(len(extent))])
    return loudness


def setup_inputs(seed: int = 0) -> dict:
    streams_of = jax.random.split(jax.random.key(seed), 5)
    return {
        "waveforms": draw_waveforms(jax.random.fold_in(streams_of[4], 71), 0),
        "templates": jnp.clip(-0.5 + 2.0 * jax.random.uniform(streams_of[1], (TEMPLATES, SLOTS, 3, L), jnp.float32) ** block_scale(streams_of[1], (TEMPLATES, SLOTS, 3, L), ((0, 32),), -0.2, 0.2), -0.5, 1.5).astype(jnp.bfloat16),
        "stations": draw_stations(jax.random.fold_in(streams_of[4], 71), 0),
        "moveouts": touch_ends(jax.random.randint(streams_of[3], (TEMPLATES, SLOTS), 0, SHIFT_MAX + 1), jax.random.fold_in(streams_of[3], 1), 0, SHIFT_MAX).astype(jnp.int32),
    }


def normalize_panel(trace_panels):
    values = trace_panels.astype(jnp.float32)
    centred = values - lax.optimization_barrier(jnp.mean(values, axis=-1, keepdims=True))
    spread = jnp.sqrt(lax.optimization_barrier(jnp.mean(centred * centred, axis=-1, keepdims=True)) + 1e-05)
    return (centred / spread).astype(jnp.bfloat16)

def window_level(segment):
    values = segment.astype(jnp.float32)
    running = jnp.cumsum(values * values, axis=-1)
    running = jnp.concatenate([jnp.zeros(running.shape[:-1] + (1,), jnp.float32), running], axis=-1)
    energy = running[..., L:L + LAGS] - running[..., :LAGS]
    return jnp.sqrt(energy / L + 1e-05)

def correlate(shapes, segment):
    spectrum_data = jnp.fft.rfft(segment.astype(jnp.float32), n=SEG, axis=-1)
    spectrum_shape = jnp.fft.rfft(shapes.astype(jnp.float32), n=SEG, axis=-1)
    product = jnp.fft.irfft(spectrum_data * jnp.conj(spectrum_shape), n=SEG, axis=-1)
    return product[..., :LAGS]

def reference(waveforms, templates, stations, moveouts):
    factor = math.sqrt(L / (3.0 * SLOTS))

    def cut_one(one_row, one_start):
        return lax.dynamic_slice(waveforms, (one_row, jnp.int32(0), one_start), (1, 3, SEG))[0]

    def one_template(inputs):
        trace_panels, station_rows, shifts = inputs
        shapes = normalize_panel(trace_panels)
        segment = jax.vmap(cut_one)(station_rows.astype(jnp.int32), shifts.astype(jnp.int32))
        coefficients = correlate(shapes, segment) / (L * window_level(segment))
        return factor * lax.optimization_barrier(jnp.sum(coefficients, axis=(0, 1)))
    stacks = lax.map(one_template, (templates, stations, moveouts))
    return (stacks, lax.optimization_barrier(jnp.max(stacks, axis=0)))
```

```python
import functools
import math

import jax
import jax.numpy as jnp
import ml_dtypes
import numpy as np
from jax import lax
from jax.experimental import pallas as pl
from jax.experimental.pallas import tpu as pltpu
from jax.sharding import PartitionSpec as P

LAGS = 256
ROWS = 16
AXES = ("tmpl", "sta")
VMEM = 48 * 1024 * 1024


def spans(limit):
    return max(1, (limit - 1).bit_length())


def split_table(table):
    high = table.astype(ml_dtypes.bfloat16)
    low = (table - high.astype(np.float64)).astype(ml_dtypes.bfloat16)
    return high, low


def transform_tables(piece):
    size = 2 * piece
    angle = 2.0 * np.pi * (np.arange(piece) + 0.5) / size
    phase = np.arange(size)[:, None] * angle[None, :]
    forward = np.concatenate([np.cos(phase), -np.sin(phase)], axis=1)
    back = angle[:, None] * np.arange(piece)[None, :]
    inverse = np.concatenate([np.cos(back), -np.sin(back)], axis=0) * (2.0 / size)
    return split_table(forward) + split_table(inverse)


def band_table(length, lag_count):
    sample = np.arange(length + lag_count)[:, None]
    lag = np.arange(lag_count)[None, :]
    return ((sample >= lag) & (sample < lag + length)).astype(ml_dtypes.bfloat16)


def iota(shape, axis):
    return lax.broadcasted_iota(jnp.int32, shape, axis)


def dot(a, b):
    return jnp.dot(a, b, preferred_element_type=jnp.float32)


def exact_dot(a, b, dims):
    return lax.dot_general(
        a, b, (dims, ((), ())), precision=lax.Precision.HIGHEST, preferred_element_type=jnp.float32
    )


def pack_kernel(cfg, stations_ref, moveouts_ref, templates_ref, codes_ref, *rest):
    block_refs, shapes_ref = rest[:-1], rest[-1]
    tpl_count, slot_count = stations_ref.shape
    pairs = tpl_count * slot_count
    devices = cfg["devices"]

    first = iota((slot_count, pairs), 0) * tpl_count
    entry = iota((slot_count, pairs), 1)
    spread = jnp.where((entry >= first) & (entry < first + tpl_count), 1.0, 0.0)
    start = jnp.sum(spread * first.astype(jnp.float32), axis=0, keepdims=True)
    place = iota((1, pairs), 1).astype(jnp.float32) - start
    own = iota((tpl_count, pairs), 0).astype(jnp.float32) == place

    def as_row(ref):
        wide = exact_dot(ref[...].astype(jnp.float32), spread, ((1,), (0,)))
        return jnp.sum(jnp.where(own, wide, 0.0), axis=0, keepdims=True)

    station = as_row(stations_ref)
    shift = as_row(moveouts_ref)
    target = jnp.floor((station + 0.5) * (1.0 / cfg["station_dev"]))
    row = station - target * cfg["station_dev"]
    hit = iota((devices, pairs), 0).astype(jnp.float32) == target
    onehot = jnp.where(hit, 1.0, 0.0)
    earlier = jnp.where(iota((pairs, pairs), 0) < iota((pairs, pairs), 1), 1.0, 0.0)
    before = dot(onehot.astype(jnp.bfloat16), earlier.astype(jnp.bfloat16))
    rank = jnp.sum(onehot * before, axis=0, keepdims=True)
    code = ((place + 1.0) * cfg["row_span"] + row) * cfg["shift_span"] + shift
    lanes = codes_ref.shape[1]
    at_rank = jnp.where(iota((lanes, pairs), 0).astype(jnp.float32) == rank, 1.0, 0.0)
    codes = exact_dot(onehot * code, at_rank, ((1,), (1,)))
    codes_ref[...] = codes.astype(jnp.int32)

    length = templates_ref.shape[3]
    comps = templates_ref.shape[1]
    for c in range(comps):
        values = templates_ref[:, c].astype(jnp.float32).reshape(pairs, length)
        centred = values - jnp.mean(values, axis=-1, keepdims=True)
        spread_c = jnp.sqrt(jnp.mean(centred * centred, axis=-1, keepdims=True) + 1e-05)
        shapes_ref[c] = (centred * (1.0 / spread_c)).astype(jnp.bfloat16)

    per_block = cfg["per_block"]
    tile = 8 * ROWS
    for b, block_ref in enumerate(block_refs):
        local = rank - float(b * per_block)
        inside = (local >= 0.0) & (local < float(per_block))
        for top in range(0, devices * ROWS, tile):
            line = iota((tile, pairs), 0).astype(jnp.float32) + float(top)
            total = jnp.zeros((tile, length), jnp.float32)
            for c in range(comps):
                goal = jnp.where(inside, target * ROWS + local + float(c * per_block), -1.0)
                pick = jnp.where(line == goal, 1.0, 0.0).astype(jnp.bfloat16)
                total = total + dot(pick, shapes_ref[c])
            block_ref[pl.ds(top, tile), :] = total.astype(jnp.bfloat16)


def trace_kernel(cfg, codes_ref, waves_ref, high_ref, low_ref, band_ref, spectra_ref, scale_ref, sums_ref):
    block = pl.program_id(0)
    sources = codes_ref.shape[0]
    tile = sources * ROWS
    lanes = codes_ref.shape[1]
    comps, station_dev, samples = waves_ref.shape
    per_block = cfg["per_block"]
    seg_len, length = cfg["seg_len"], cfg["length"]
    piece = LAGS

    rep = jnp.broadcast_to(codes_ref[...].reshape(sources, 1, lanes), (sources, ROWS, lanes))
    rep = rep.reshape(tile, lanes).astype(jnp.float32)
    line = iota((tile, 1), 0) & (ROWS - 1)
    comp = jnp.zeros((tile, 1), jnp.int32)
    for c in range(1, comps + 1):
        comp = comp + jnp.where(line >= c * per_block, 1, 0)
    slot = line - comp * per_block + block * per_block
    chosen = (iota((tile, lanes), 1) == slot) & (comp < comps)
    code = jnp.sum(jnp.where(chosen, rep, 0.0), axis=1, keepdims=True).astype(jnp.int32)
    shift_bits, row_bits = cfg["shift_bits"], cfg["row_bits"]
    shift = code & (cfg["shift_span"] - 1)
    row = lax.shift_right_logical(code, shift_bits) & (cfg["row_span"] - 1)
    tpl = lax.shift_right_logical(code, shift_bits + row_bits)
    goal = jnp.where(tpl > 0, comp * station_dev + row, -1)

    pick = jnp.where(iota((tile, comps * station_dev), 1) == goal, 1.0, 0.0).astype(jnp.bfloat16)
    x = dot(pick, waves_ref[...].reshape(comps * station_dev, samples))

    for bit in range(shift_bits - 1, 6, -1):
        step = 1 << bit
        width = seg_len + step
        if x.shape[1] < width + step:
            x = jnp.concatenate([x, jnp.zeros((tile, width + step - x.shape[1]), jnp.float32)], axis=1)
        flag = (shift & step) != 0
        x = jnp.where(flag, x[:, step : step + width], x[:, :width])
    for bit in range(min(shift_bits, 7) - 1, -1, -1):
        step = 1 << bit
        flag = (shift & step) != 0
        x = jnp.where(flag, pltpu.roll(x, x.shape[1] - step, 1), x)
    segment = x[:, :seg_len]

    power = segment * segment
    power_high = power.astype(jnp.bfloat16)
    power_low = (power - power_high.astype(jnp.float32)).astype(jnp.bfloat16)
    energy = dot(power_high, band_ref[...]) + dot(power_low, band_ref[...])
    scale_ref[...] = 1.0 / (length * jnp.sqrt(energy * (1.0 / length) + 1e-05))

    narrow = segment.astype(jnp.bfloat16)
    for h in range(length // piece):
        part = narrow[:, h * piece : (h + 2) * piece]
        spectra_ref[:, h * 2 * piece : (h + 1) * 2 * piece] = dot(part, high_ref[...]) + dot(part, low_ref[...])

    tpl_count = cfg["tpl_count"]
    col = iota((tile, tile), 1)
    mine = lax.shift_right_logical(iota((tile, tile), 0), spans(ROWS)) * tpl_count + tpl - 1
    wanted = jnp.where((col == mine) & (tpl > 0), 1.0, 0.0)
    sums_ref[...] = wanted.T[: sources * tpl_count].astype(jnp.bfloat16)


def match_kernel(shapes_ref, spectra_ref, scale_ref, sums_ref, high_ref, low_ref, back_high_ref, back_low_ref, *rest):
    out_ref = rest[-1]
    piece = LAGS
    length = shapes_ref.shape[1]
    tile = shapes_ref.shape[0]
    real = jnp.zeros((tile, piece), jnp.float32)
    imag = jnp.zeros((tile, piece), jnp.float32)
    for h in range(length // piece):
        part = shapes_ref[:, h * piece : (h + 1) * piece]
        mine = dot(part, high_ref[...]) + dot(part, low_ref[...])
        mine_r, mine_i = mine[:, :piece], mine[:, piece:]
        trace_r = spectra_ref[:, h * 2 * piece : (2 * h + 1) * piece]
        trace_i = spectra_ref[:, (2 * h + 1) * piece : (h + 1) * 2 * piece]
        real = real + (trace_r * mine_r + trace_i * mine_i)
        imag = imag + (trace_i * mine_r - trace_r * mine_i)
    product = jnp.concatenate([real, imag], axis=1)
    product_high = product.astype(jnp.bfloat16)
    product_low = (product - product_high.astype(jnp.float32)).astype(jnp.bfloat16)
    lagged = (
        dot(product_high, back_high_ref[...])
        + dot(product_high, back_low_ref[...])
        + dot(product_low, back_high_ref[...])
    )
    left = lagged * scale_ref[...]
    total = jnp.zeros(out_ref.shape, jnp.float32) if len(rest) == 1 else rest[0][...]
    for _ in range(3):
        part = left.astype(jnp.bfloat16)
        left = left - part.astype(jnp.float32)
        total = total + dot(sums_ref[...], part)
    out_ref[...] = total


def stack_kernel(factor, parts_ref, stacks_ref, top_ref):
    stacks = jnp.sum(parts_ref[...], axis=0) * factor
    stacks_ref[...] = stacks
    top_ref[...] = jnp.max(stacks, axis=0, keepdims=True)


def params(**extra):
    return pltpu.CompilerParams(vmem_limit_bytes=VMEM, **extra)


def body(waveforms, templates, stations, moveouts):
    devices = lax.axis_size(AXES)
    tpl_count, slot_count = stations.shape
    comps, length = templates.shape[2:]
    station_dev, _, samples = waveforms.shape
    seg_len = length + LAGS
    pairs = tpl_count * slot_count
    capacity = (2 * pairs + devices - 1) // devices
    per_block = ROWS // comps
    blocks = -(-capacity // per_block)
    shift_bits = spans(samples - seg_len + 1)
    row_bits = spans(station_dev)
    cfg = dict(
        devices=devices,
        station_dev=station_dev,
        tpl_count=tpl_count,
        per_block=per_block,
        length=length,
        seg_len=seg_len,
        shift_bits=shift_bits,
        shift_span=1 << shift_bits,
        row_bits=row_bits,
        row_span=1 << row_bits,
    )
    high, low, back_high, back_low = (jnp.asarray(t) for t in transform_tables(LAGS))
    band = jnp.asarray(band_table(length, LAGS))
    lines = devices * ROWS
    sources = 8
    tile = sources * ROWS
    tiles = devices // sources
    lanes = 128

    whole = pl.BlockSpec(memory_space=pltpu.VMEM)
    codes, *blocks_out = pl.pallas_call(
        functools.partial(pack_kernel, cfg),
        out_shape=[jax.ShapeDtypeStruct((devices, lanes), jnp.int32)]
        + [jax.ShapeDtypeStruct((lines, length), jnp.bfloat16)] * blocks,
        in_specs=[whole] * 3,
        out_specs=[whole] * (1 + blocks),
        scratch_shapes=[pltpu.VMEM((comps, pairs, length), jnp.bfloat16)],
        compiler_params=params(),
        name="pack",
    )(stations, moveouts, templates.transpose(1, 2, 0, 3))

    def exchange(x):
        return lax.all_to_all(x, AXES, split_axis=0, concat_axis=0, tiled=True)

    codes_in = exchange(codes.reshape(devices, 1, lanes)).reshape(devices, lanes)
    shapes_in = [exchange(x.reshape(devices, ROWS, length)).reshape(lines, length) for x in blocks_out]

    pieces = length // LAGS
    spectra, scale, sums = pl.pallas_call(
        functools.partial(trace_kernel, cfg),
        grid=(blocks, tiles),
        out_shape=[
            jax.ShapeDtypeStruct((blocks, lines, pieces * 2 * LAGS), jnp.float32),
            jax.ShapeDtypeStruct((blocks, lines, LAGS), jnp.float32),
            jax.ShapeDtypeStruct((blocks, devices * tpl_count, tile), jnp.bfloat16),
        ],
        in_specs=[
            pl.BlockSpec((sources, lanes), lambda b, i: (i, 0)),
            pl.BlockSpec((comps, station_dev, samples), lambda b, i: (0, 0, 0)),
            pl.BlockSpec((2 * LAGS, 2 * LAGS), lambda b, i: (0, 0)),
            pl.BlockSpec((2 * LAGS, 2 * LAGS), lambda b, i: (0, 0)),
            pl.BlockSpec((seg_len, LAGS), lambda b, i: (0, 0)),
        ],
        out_specs=[
            pl.BlockSpec((None, tile, pieces * 2 * LAGS), lambda b, i: (b, i, 0)),
            pl.BlockSpec((None, tile, LAGS), lambda b, i: (b, i, 0)),
            pl.BlockSpec((None, sources * tpl_count, tile), lambda b, i: (b, i, 0)),
        ],
        compiler_params=params(),
        name="traces",
    )(codes_in, waveforms.transpose(1, 0, 2), high, low, band)

    partial = ()
    for b in range(blocks):
        partial = (
            pl.pallas_call(
                match_kernel,
                grid=(tiles,),
                out_shape=jax.ShapeDtypeStruct((devices * tpl_count, LAGS), jnp.float32),
                in_specs=[
                    pl.BlockSpec((tile, length), lambda i: (i, 0)),
                    pl.BlockSpec((None, tile, pieces * 2 * LAGS), lambda i, b=b: (b, i, 0)),
                    pl.BlockSpec((None, tile, LAGS), lambda i, b=b: (b, i, 0)),
                    pl.BlockSpec((None, sources * tpl_count, tile), lambda i, b=b: (b, i, 0)),
                    pl.BlockSpec((LAGS, 2 * LAGS), lambda i: (0, 0)),
                    pl.BlockSpec((LAGS, 2 * LAGS), lambda i: (0, 0)),
                    pl.BlockSpec((2 * LAGS, LAGS), lambda i: (0, 0)),
                    pl.BlockSpec((2 * LAGS, LAGS), lambda i: (0, 0)),
                ]
                + [pl.BlockSpec((sources * tpl_count, LAGS), lambda i: (i, 0))] * len(partial),
                out_specs=pl.BlockSpec((sources * tpl_count, LAGS), lambda i: (i, 0)),
                compiler_params=params(),
                name="match",
            )(shapes_in[b], spectra, scale, sums, high, low, back_high, back_low, *partial),
        )

    parts = exchange(partial[0].reshape(devices, tpl_count, LAGS))
    stacks, top = pl.pallas_call(
        functools.partial(stack_kernel, math.sqrt(length / (comps * slot_count))),
        out_shape=[
            jax.ShapeDtypeStruct((tpl_count, LAGS), jnp.float32),
            jax.ShapeDtypeStruct((1, LAGS), jnp.float32),
        ],
        in_specs=[whole],
        out_specs=[whole, whole],
        compiler_params=params(),
        name="stack",
    )(parts)
    tops = exchange(jnp.broadcast_to(top.reshape(1, 1, LAGS), (devices, 1, LAGS)))
    return stacks, jnp.max(tops, axis=(0, 1))


def solution(mesh):
    placed = (
        P(AXES, None, None),
        P(AXES, None, None, None),
        P(AXES, None),
        P(AXES, None),
    )
    return jax.shard_map(body, mesh=mesh, in_specs=placed, out_specs=(P(AXES, None), P()), check_vma=False)
```

```python
import functools
import math

import jax
import jax.numpy as jnp
import ml_dtypes
import numpy as np
from jax import lax
from jax.experimental import pallas as pl
from jax.experimental.pallas import tpu as pltpu
from jax.sharding import PartitionSpec as P

LAGS = 256
AXES = ("tmpl", "sta")
SOURCES = 8
MIB = 1024 * 1024


def bits_of(limit):
    return max(1, (limit - 1).bit_length())


def split_table(table):
    high = table.astype(ml_dtypes.bfloat16)
    low = (table - high.astype(np.float64)).astype(ml_dtypes.bfloat16)
    return np.concatenate([high, low], axis=0)


def transform_tables(piece):
    size = 2 * piece
    angle = 2.0 * np.pi * (np.arange(piece) + 0.5) / size
    phase = np.arange(size)[:, None] * angle[None, :]
    forward = np.concatenate([np.cos(phase), -np.sin(phase)], axis=1)
    back = angle[:, None] * np.arange(piece)[None, :]
    inverse = np.concatenate([np.cos(back), -np.sin(back)], axis=0) * (2.0 / size)
    return split_table(forward), split_table(inverse)


def band_table(length, lag_count):
    sample = np.arange(length + lag_count)[:, None]
    lag = np.arange(lag_count)[None, :]
    return ((sample >= lag) & (sample < lag + length)).astype(ml_dtypes.bfloat16)


def iota(shape, axis):
    return lax.broadcasted_iota(jnp.int32, shape, axis)


def dot(a, b):
    return jnp.dot(a, b, preferred_element_type=jnp.float32)


def exact_dot(a, b):
    return jnp.dot(a, b, precision=lax.Precision.HIGHEST, preferred_element_type=jnp.float32)


def entry_lanes(tpl_count, slot_count):
    pairs = tpl_count * slot_count
    first = iota((slot_count, pairs), 0) * tpl_count
    entry = iota((slot_count, pairs), 1)
    spread = jnp.where((entry >= first) & (entry < first + tpl_count), 1.0, 0.0)
    start = jnp.sum(spread * first.astype(jnp.float32), axis=0, keepdims=True)
    return spread, iota((1, pairs), 1).astype(jnp.float32) - start


def as_lanes(values, spread, place, tpl_count):
    owners = values.shape[0] // tpl_count
    pairs = spread.shape[1]
    wide = exact_dot(values.astype(jnp.float32), spread).reshape(owners, tpl_count, pairs)
    own = iota((1, tpl_count, pairs), 1).astype(jnp.float32) == place.reshape(1, 1, pairs)
    return jnp.sum(jnp.where(own, wide, 0.0), axis=1)


def count_before(hits):
    pairs = hits.shape[1]
    earlier = jnp.where(iota((pairs, pairs), 0) < iota((pairs, pairs), 1), 1.0, 0.0)
    return dot(hits.astype(jnp.bfloat16), earlier.astype(jnp.bfloat16))


def pack_kernel(cfg, stations_ref, templates_hbm, packed_hbm, raw_ref, shapes_ref, packed_ref, in_sem, out_sems):
    load = pltpu.make_async_copy(templates_hbm, raw_ref, in_sem)
    load.start()
    tpl_count, slot_count = stations_ref.shape
    pairs = tpl_count * slot_count
    spread, place = entry_lanes(tpl_count, slot_count)
    station = as_lanes(stations_ref[...], spread, place, tpl_count)
    target = jnp.floor((station + 0.5) * (1.0 / cfg["station_dev"]))
    hit = iota((cfg["devices"], pairs), 0).astype(jnp.float32) == target
    onehot = jnp.where(hit, 1.0, 0.0)
    rank = jnp.sum(onehot * count_before(onehot), axis=0, keepdims=True)
    capacity, rows = cfg["capacity"], cfg["rows"]
    goal = jnp.where(rank < float(capacity), target * rows + rank, -float(cfg["devices"] * rows))

    load.wait()
    comps, length = raw_ref.shape[1], raw_ref.shape[3]
    for c in range(comps):
        values = raw_ref[:, c].astype(jnp.float32).reshape(pairs, length)
        centred = values - jnp.mean(values, axis=-1, keepdims=True)
        spread_c = jnp.sqrt(jnp.mean(centred * centred, axis=-1, keepdims=True) + 1e-05)
        shapes_ref[c] = (centred * (1.0 / spread_c)).astype(jnp.bfloat16)

    tile = SOURCES * rows
    copies = []
    for step, top in enumerate(range(0, packed_ref.shape[0], tile)):
        line = iota((tile, pairs), 0).astype(jnp.float32) + float(top)
        total = jnp.zeros((tile, length), jnp.float32)
        for c in range(comps):
            pick = jnp.where(line == goal + float(c * capacity), 1.0, 0.0).astype(jnp.bfloat16)
            total = total + dot(pick, shapes_ref[c])
        part = pl.ds(top, tile)
        packed_ref[part, :] = total.astype(jnp.bfloat16)
        copies.append(pltpu.make_async_copy(packed_ref.at[part], packed_hbm.at[part], out_sems.at[step]))
        copies[-1].start()
    for copy in copies:
        copy.wait()


def trace_kernel(cfg, me_ref, lists_ref, waves_ref, forward_ref, band_ref, spectra_ref, scale_ref, sums_ref):
    comps, station_dev, samples = waves_ref.shape
    tpl_count, capacity, rows = cfg["tpl_count"], cfg["capacity"], cfg["rows"]
    seg_len, length, shift_bits = cfg["seg_len"], cfg["length"], cfg["shift_bits"]
    piece = LAGS
    tile = SOURCES * rows

    slot_count = lists_ref.shape[1]
    pairs = tpl_count * slot_count
    spread, place = entry_lanes(tpl_count, slot_count)
    lists = lists_ref[...]
    station = as_lanes(lax.shift_right_logical(lists, shift_bits), spread, place, tpl_count)
    moveout = as_lanes(lists & ((1 << shift_bits) - 1), spread, place, tpl_count)
    local = station - (me_ref[0] * station_dev).astype(jnp.float32)
    onehot = jnp.where((local >= 0.0) & (local < float(station_dev)), 1.0, 0.0)
    rank = jnp.where(onehot > 0.0, count_before(onehot), -1.0)

    def per_line(x):
        return jnp.broadcast_to(x.reshape(SOURCES, 1, pairs), (SOURCES, rows, pairs)).reshape(tile, pairs)

    line = iota((SOURCES, rows, 1), 1).reshape(tile, 1)
    owner = iota((SOURCES, rows, 1), 0).reshape(tile, 1)
    comp = jnp.zeros((tile, 1), jnp.int32)
    for c in range(1, comps + 1):
        comp = comp + jnp.where(line >= c * capacity, 1, 0)
    slot = (line - comp * capacity).astype(jnp.float32)
    chosen = jnp.where((per_line(rank) == slot) & (comp < comps), 1.0, 0.0)

    def pick_entry(x):
        return jnp.sum(chosen * x, axis=1, keepdims=True)

    used = pick_entry(1.0) > 0.0
    shift = pick_entry(per_line(moveout)).astype(jnp.int32)
    row = pick_entry(per_line(local)).astype(jnp.int32)
    tpl = pick_entry(place).astype(jnp.int32)

    goal = jnp.where(used, comp * station_dev + row, -1)
    pick = jnp.where(iota((tile, comps * station_dev), 1) == goal, 1.0, 0.0).astype(jnp.bfloat16)
    x = dot(pick, waves_ref[...].reshape(comps * station_dev, samples))

    for bit in range(shift_bits - 1, 6, -1):
        step = 1 << bit
        width = seg_len + step
        if x.shape[1] < width + step:
            x = jnp.concatenate([x, jnp.zeros((tile, width + step - x.shape[1]), jnp.float32)], axis=1)
        x = jnp.where((shift & step) != 0, x[:, step : step + width], x[:, :width])
    for bit in range(min(shift_bits, 7) - 1, -1, -1):
        step = 1 << bit
        x = jnp.where((shift & step) != 0, pltpu.roll(x, x.shape[1] - step, 1), x)
    segment = x[:, :seg_len]

    power = segment * segment
    power_high = power.astype(jnp.bfloat16)
    power_low = (power - power_high.astype(jnp.float32)).astype(jnp.bfloat16)
    energy = dot(power_high, band_ref[...]) + dot(power_low, band_ref[...])
    scale_ref[...] = 1.0 / (length * jnp.sqrt(energy * (1.0 / length) + 1e-05))

    narrow = segment.astype(jnp.bfloat16)
    for h in range(length // piece):
        part = narrow[:, h * piece : (h + 2) * piece]
        both = jnp.concatenate([part, part], axis=1)
        spectra_ref[:, h * 2 * piece : (h + 1) * 2 * piece] = dot(both, forward_ref[...])

    groups = SOURCES * tpl_count
    mine = jnp.where(used, owner * tpl_count + tpl, -1)
    sums_ref[...] = jnp.where(iota((tile, groups), 1) == mine, 1.0, 0.0).T.astype(jnp.bfloat16)


def match_kernel(cfg, shapes_ref, spectra_ref, scale_ref, sums_ref, forward_ref, inverse_ref, out_ref):
    piece = LAGS
    length = shapes_ref.shape[1]
    tile = SOURCES * cfg["rows"]
    groups = SOURCES * cfg["tpl_count"]
    forward = jnp.concatenate([forward_ref[:piece], forward_ref[2 * piece : 3 * piece]], axis=0)
    inverse = jnp.concatenate([inverse_ref[...], inverse_ref[: 2 * piece]], axis=0)

    def one_tile(step):
        lines = pl.ds(pl.multiple_of(step * tile, tile), tile)
        real = jnp.zeros((tile, piece), jnp.float32)
        imag = jnp.zeros((tile, piece), jnp.float32)
        for h in range(length // piece):
            part = shapes_ref[lines, h * piece : (h + 1) * piece]
            mine = dot(jnp.concatenate([part, part], axis=1), forward)
            mine_r, mine_i = mine[:, :piece], mine[:, piece:]
            trace_r = spectra_ref[lines, h * 2 * piece : (2 * h + 1) * piece]
            trace_i = spectra_ref[lines, (2 * h + 1) * piece : (h + 1) * 2 * piece]
            real = real + (trace_r * mine_r + trace_i * mine_i)
            imag = imag + (trace_i * mine_r - trace_r * mine_i)
        product = jnp.concatenate([real, imag], axis=1)
        high = product.astype(jnp.bfloat16)
        low = (product - high.astype(jnp.float32)).astype(jnp.bfloat16)
        left = dot(jnp.concatenate([high, high, low], axis=1), inverse) * scale_ref[lines, :]
        parts = []
        for _ in range(3):
            parts.append(left.astype(jnp.bfloat16))
            left = left - parts[-1].astype(jnp.float32)
        ends = pl.ds(pl.multiple_of(step * groups, groups), groups)
        picks = sums_ref[ends, :]
        total = dot(picks, parts[0]) + dot(picks, parts[1]) + dot(picks, parts[2])
        out_ref[ends, :] = total

    tiles = shapes_ref.shape[0] // tile
    if tiles <= 4:
        for step in range(tiles):
            one_tile(step)
    else:
        pl.loop(0, tiles)(one_tile)


def stack_kernel(factor, parts_ref, stacks_ref, top_ref):
    stacks = jnp.sum(parts_ref[...], axis=0) * factor
    stacks_ref[...] = stacks
    top_ref[...] = jnp.broadcast_to(jnp.max(stacks, axis=0, keepdims=True), top_ref.shape)


def body(waveforms, templates, stations, moveouts):
    devices = lax.axis_size(AXES)
    tpl_count, slot_count = stations.shape
    comps, length = templates.shape[2:]
    station_dev, _, samples = waveforms.shape
    seg_len = length + LAGS
    pairs = tpl_count * slot_count
    capacity = (2 * pairs + devices - 1) // devices
    rows = -(-comps * capacity // 16) * 16
    shift_bits = bits_of(samples - seg_len + 1)
    cfg = dict(
        devices=devices,
        station_dev=station_dev,
        tpl_count=tpl_count,
        capacity=capacity,
        rows=rows,
        length=length,
        seg_len=seg_len,
        shift_bits=shift_bits,
    )
    forward, inverse = (jnp.asarray(t) for t in transform_tables(LAGS))
    band = jnp.asarray(band_table(length, LAGS))
    lines = devices * rows
    tile = SOURCES * rows
    tiles = devices // SOURCES
    groups = SOURCES * tpl_count
    pieces = length // LAGS
    whole = pl.BlockSpec(memory_space=pltpu.VMEM)
    anywhere = pl.BlockSpec(memory_space=pl.ANY)

    lists = lax.all_gather(stations * (1 << shift_bits) + moveouts, AXES, axis=0, tiled=True)
    me = lax.axis_index(AXES).reshape(1)

    by_slot = templates.transpose(1, 2, 0, 3)
    packed = pl.pallas_call(
        functools.partial(pack_kernel, cfg),
        out_shape=jax.ShapeDtypeStruct((lines, length), jnp.bfloat16),
        in_specs=[whole, anywhere],
        out_specs=anywhere,
        scratch_shapes=[
            pltpu.VMEM(by_slot.shape, jnp.bfloat16),
            pltpu.VMEM((comps, pairs, length), jnp.bfloat16),
            pltpu.VMEM((lines, length), jnp.bfloat16),
            pltpu.SemaphoreType.DMA,
            pltpu.SemaphoreType.DMA((tiles,)),
        ],
        compiler_params=pltpu.CompilerParams(vmem_limit_bytes=56 * MIB),
        name="pack",
    )(stations, by_slot)

    def exchange(x):
        return lax.all_to_all(x, AXES, split_axis=0, concat_axis=0, tiled=True)

    arrived = exchange(packed.reshape(devices, rows, length)).reshape(lines, length)

    spectra, scale, sums = pl.pallas_call(
        functools.partial(trace_kernel, cfg),
        grid=(tiles,),
        out_shape=[
            jax.ShapeDtypeStruct((lines, pieces * 2 * LAGS), jnp.float32),
            jax.ShapeDtypeStruct((lines, LAGS), jnp.float32),
            jax.ShapeDtypeStruct((devices * tpl_count, tile), jnp.bfloat16),
        ],
        in_specs=[
            pl.BlockSpec(memory_space=pltpu.SMEM),
            pl.BlockSpec((groups, slot_count), lambda i: (i, 0)),
            pl.BlockSpec((comps, station_dev, samples), lambda i: (0, 0, 0)),
            pl.BlockSpec((4 * LAGS, 2 * LAGS), lambda i: (0, 0)),
            pl.BlockSpec((seg_len, LAGS), lambda i: (0, 0)),
        ],
        out_specs=[
            pl.BlockSpec((tile, pieces * 2 * LAGS), lambda i: (i, 0)),
            pl.BlockSpec((tile, LAGS), lambda i: (i, 0)),
            pl.BlockSpec((groups, tile), lambda i: (i, 0)),
        ],
        compiler_params=pltpu.CompilerParams(vmem_limit_bytes=28 * MIB),
        name="traces",
    )(me, lists, waveforms.transpose(1, 0, 2), forward, band)

    sent = pl.pallas_call(
        functools.partial(match_kernel, cfg),
        out_shape=jax.ShapeDtypeStruct((devices * tpl_count, LAGS), jnp.float32),
        in_specs=[whole] * 6,
        out_specs=whole,
        compiler_params=pltpu.CompilerParams(vmem_limit_bytes=40 * MIB),
        name="match",
    )(arrived, spectra, scale, sums, forward, inverse)

    parts = exchange(sent.reshape(devices, tpl_count, LAGS))
    stacks, top = pl.pallas_call(
        functools.partial(stack_kernel, math.sqrt(length / (comps * slot_count))),
        out_shape=[
            jax.ShapeDtypeStruct((tpl_count, LAGS), jnp.float32),
            jax.ShapeDtypeStruct((devices, 1, LAGS), jnp.float32),
        ],
        in_specs=[whole],
        out_specs=[whole, whole],
        name="stack",
    )(parts)
    return stacks, jnp.max(exchange(top), axis=(0, 1))


def solution(mesh):
    placed = (
        P(AXES, None, None),
        P(AXES, None, None, None),
        P(AXES, None),
        P(AXES, None),
    )
    return jax.shard_map(body, mesh=mesh, in_specs=placed, out_specs=(P(AXES, None), P()), check_vma=False)
```

```python
import functools
import math

import jax
import jax.numpy as jnp
import ml_dtypes
import numpy as np
from jax import lax
from jax.experimental import pallas as pl
from jax.experimental.pallas import tpu as pltpu
from jax.sharding import PartitionSpec as P

LAGS = 256
AXES = ("tmpl", "sta")
SOURCES = 8
ROWS = 16
DIGITS = 3
LANES = 128
MIB = 1024 * 1024


def bits_of(limit):
    return max(1, (limit - 1).bit_length())


def split_table(table):
    high = table.astype(ml_dtypes.bfloat16)
    low = (table - high.astype(np.float64)).astype(ml_dtypes.bfloat16)
    return np.concatenate([high, low], axis=0)


def transform_tables(piece):
    size = 2 * piece
    angle = 2.0 * np.pi * (np.arange(piece) + 0.5) / size
    phase = np.arange(size)[:, None] * angle[None, :]
    forward = np.concatenate([np.cos(phase), -np.sin(phase)], axis=1)
    back = angle[:, None] * np.arange(piece)[None, :]
    inverse = np.concatenate([np.cos(back), -np.sin(back)], axis=0) * (2.0 / size)
    return split_table(forward), split_table(inverse)


def band_table(length, lag_count):
    sample = np.arange(length + lag_count)[:, None]
    lag = np.arange(lag_count)[None, :]
    return ((sample >= lag) & (sample < lag + length)).astype(ml_dtypes.bfloat16)


def iota(shape, axis):
    return lax.broadcasted_iota(jnp.int32, shape, axis)


def dot(a, b):
    return jnp.dot(a, b, preferred_element_type=jnp.float32)


def exact_dot(a, b):
    return jnp.dot(a, b, precision=lax.Precision.HIGHEST, preferred_element_type=jnp.float32)


def entry_lanes(tpl_count, slot_count):
    pairs = tpl_count * slot_count
    first = iota((slot_count, pairs), 0) * tpl_count
    entry = iota((slot_count, pairs), 1)
    spread = jnp.where((entry >= first) & (entry < first + tpl_count), 1.0, 0.0)
    start = jnp.sum(spread * first.astype(jnp.float32), axis=0, keepdims=True)
    return spread, iota((1, pairs), 1).astype(jnp.float32) - start


def as_lanes(values, spread, place, tpl_count):
    owners = values.shape[0] // tpl_count
    pairs = spread.shape[1]
    wide = exact_dot(values.astype(jnp.float32), spread).reshape(owners, tpl_count, pairs)
    own = iota((1, tpl_count, pairs), 1).astype(jnp.float32) == place.reshape(1, 1, pairs)
    return jnp.sum(jnp.where(own, wide, 0.0), axis=1)


def count_before(hits):
    pairs = hits.shape[1]
    earlier = jnp.where(iota((pairs, pairs), 0) < iota((pairs, pairs), 1), 1.0, 0.0)
    return dot(hits.astype(jnp.bfloat16), earlier.astype(jnp.bfloat16))


def pack_kernel(cfg, first, count, rows, stations_ref, moveouts_ref, templates_hbm, packed_hbm, raw_ref, shapes_ref, packed_ref, in_sem, out_sems):
    load = pltpu.make_async_copy(templates_hbm, raw_ref, in_sem)
    load.start()
    tpl_count, slot_count = stations_ref.shape
    pairs = tpl_count * slot_count
    devices, station_dev = cfg["devices"], cfg["station_dev"]
    spread, place = entry_lanes(tpl_count, slot_count)
    station = as_lanes(stations_ref[...], spread, place, tpl_count)
    target = jnp.floor((station + 0.5) * (1.0 / station_dev))
    hit = iota((devices, pairs), 0).astype(jnp.float32) == target
    onehot = jnp.where(hit, 1.0, 0.0)
    rank = jnp.sum(onehot * count_before(onehot), axis=0, keepdims=True)
    slot = rank - float(first)
    inside = (slot >= 0.0) & (slot < float(count))
    goal = jnp.where(inside, target * rows + slot, -float(devices * rows))

    codes = None
    if first == 0:
        shift = as_lanes(moveouts_ref[...], spread, place, tpl_count)
        row = station - target * station_dev
        code = ((place + 1.0) * (1 << cfg["row_bits"]) + row) * (1 << cfg["shift_bits"]) + shift
        code = code.astype(jnp.int32)
        at_rank = jnp.where(iota((LANES, pairs), 0).astype(jnp.float32) == rank, 1.0, 0.0).astype(jnp.bfloat16)
        digits = []
        for d in range(DIGITS):
            digit = (lax.shift_right_logical(code, 8 * d) & 255).astype(jnp.float32)
            marked = (onehot * digit).astype(jnp.bfloat16)
            digits.append(
                lax.dot_general(marked, at_rank, (((1,), (1,)), ((), ())), preferred_element_type=jnp.float32)
            )
        codes = jnp.concatenate(digits, axis=1)

    load.wait()
    comps, length = raw_ref.shape[1], raw_ref.shape[3]
    for c in range(comps):
        values = raw_ref[:, c].astype(jnp.float32).reshape(pairs, length)
        centred = values - jnp.mean(values, axis=-1, keepdims=True)
        spread_c = jnp.sqrt(jnp.mean(centred * centred, axis=-1, keepdims=True) + 1e-05)
        shapes_ref[c] = (centred * (1.0 / spread_c)).astype(jnp.bfloat16)

    tile = SOURCES * rows
    copies = []
    for step in range(devices // SOURCES):
        top = step * tile
        line = iota((tile, pairs), 0).astype(jnp.float32) + float(top)
        total = jnp.zeros((tile, length), jnp.float32)
        for c in range(comps):
            pick = jnp.where(line == goal + float(c * count), 1.0, 0.0).astype(jnp.bfloat16)
            total = total + dot(pick, shapes_ref[c])
        if codes is not None:
            width = codes.shape[1]
            mine = codes[step * SOURCES : (step + 1) * SOURCES].reshape(SOURCES, 1, width)
            last = iota((SOURCES, rows, 1), 1) == rows - 1
            mine = jnp.where(last, mine, 0.0).reshape(tile, width)
            total = jnp.concatenate([total[:, :width] + mine, total[:, width:]], axis=1)
        part = pl.ds(top, tile)
        packed_ref[part, :] = total.astype(jnp.bfloat16)
        copies.append(pltpu.make_async_copy(packed_ref.at[part], packed_hbm.at[part], out_sems.at[step]))
        copies[-1].start()
    for copy in copies:
        copy.wait()


def read_codes(block):
    width = DIGITS * LANES
    rows = block.shape[0] // SOURCES
    values = block[:, :width].astype(jnp.float32).reshape(SOURCES, rows, width)
    last = iota((1, rows, 1), 1) == rows - 1
    digits = jnp.sum(jnp.where(last, values, 0.0), axis=1)
    return sum(digits[:, d * LANES : (d + 1) * LANES] * float(256**d) for d in range(DIGITS))


def cut_traces(cfg, codes, first, count, rows, waves_ref):
    comps, station_dev, samples = waves_ref.shape
    tpl_count, seg_len = cfg["tpl_count"], cfg["seg_len"]
    shift_bits, row_bits = cfg["shift_bits"], cfg["row_bits"]
    tile = SOURCES * rows
    line = iota((SOURCES, rows, 1), 1).reshape(tile, 1)
    owner = iota((SOURCES, rows, 1), 0).reshape(tile, 1)
    comp = jnp.zeros((tile, 1), jnp.int32)
    for c in range(1, comps + 1):
        comp = comp + jnp.where(line >= c * count, 1, 0)
    slot = line - comp * count + first
    repeated = jnp.broadcast_to(codes.reshape(SOURCES, 1, LANES), (SOURCES, rows, LANES)).reshape(tile, LANES)
    chosen = (iota((tile, LANES), 1) == slot) & (comp < comps)
    code = jnp.sum(jnp.where(chosen, repeated, 0.0), axis=1, keepdims=True).astype(jnp.int32)
    shift = code & ((1 << shift_bits) - 1)
    row = lax.shift_right_logical(code, shift_bits) & ((1 << row_bits) - 1)
    tpl = lax.shift_right_logical(code, shift_bits + row_bits) - 1

    goal = jnp.where(tpl >= 0, comp * station_dev + row, -1)
    pick = jnp.where(iota((tile, comps * station_dev), 1) == goal, 1.0, 0.0).astype(jnp.bfloat16)
    x = dot(pick, waves_ref[...].reshape(comps * station_dev, samples))

    for bit in range(shift_bits - 1, 6, -1):
        step = 1 << bit
        width = seg_len + step
        if x.shape[1] < width + step:
            x = jnp.concatenate([x, jnp.zeros((tile, width + step - x.shape[1]), jnp.float32)], axis=1)
        x = jnp.where((shift & step) != 0, x[:, step : step + width], x[:, :width])
    for bit in range(min(shift_bits, 7) - 1, -1, -1):
        step = 1 << bit
        x = jnp.where((shift & step) != 0, pltpu.roll(x, x.shape[1] - step, 1), x)

    mine = jnp.where(tpl >= 0, owner * tpl_count + tpl, -1)
    sums = jnp.where(iota((tile, SOURCES * tpl_count), 1) == mine, 1.0, 0.0).T.astype(jnp.bfloat16)
    return x[:, :seg_len], sums


def levels_scale(cfg, segment, band):
    length = cfg["length"]
    power = segment * segment
    high = power.astype(jnp.bfloat16)
    low = (power - high.astype(jnp.float32)).astype(jnp.bfloat16)
    energy = dot(high, band) + dot(low, band)
    return 1.0 / (length * jnp.sqrt(energy * (1.0 / length) + 1e-05))


def trace_spectrum(narrow, h, forward):
    part = narrow[:, h * LAGS : (h + 2) * LAGS]
    return dot(jnp.concatenate([part, part], axis=1), forward)


def match_lines(shapes, spectrum_of, scale, forward, inverse):
    real = imag = 0.0
    for h in range(shapes.shape[1] // LAGS):
        part = shapes[:, h * LAGS : (h + 1) * LAGS]
        mine = dot(jnp.concatenate([part, part], axis=1), forward)
        theirs = spectrum_of(h)
        mine_r, mine_i = mine[:, :LAGS], mine[:, LAGS:]
        theirs_r, theirs_i = theirs[:, :LAGS], theirs[:, LAGS:]
        real = real + (theirs_r * mine_r + theirs_i * mine_i)
        imag = imag + (theirs_i * mine_r - theirs_r * mine_i)
    product = jnp.concatenate([real, imag], axis=1)
    high = product.astype(jnp.bfloat16)
    low = (product - high.astype(jnp.float32)).astype(jnp.bfloat16)
    return dot(jnp.concatenate([high, high, low], axis=1), inverse) * scale


def sum_lines(sums, left):
    total = 0.0
    for _ in range(3):
        part = left.astype(jnp.bfloat16)
        left = left - part.astype(jnp.float32)
        total = total + dot(sums, part)
    return total


def short_tables(forward_ref, inverse_ref):
    forward = jnp.concatenate([forward_ref[:LAGS], forward_ref[2 * LAGS : 3 * LAGS]], axis=0)
    return forward, jnp.concatenate([inverse_ref[...], inverse_ref[: 2 * LAGS]], axis=0)


def hold_kernel(cfg, later, shapes_ref, waves_ref, forward_ref, inverse_ref, band_ref, sent_ref, *later_refs):
    codes = read_codes(shapes_ref[...])
    forward, inverse = short_tables(forward_ref, inverse_ref)
    band = band_ref[...]
    whole_forward = forward_ref[...]
    pieces = cfg["length"] // LAGS

    segment, sums = cut_traces(cfg, codes, 0, cfg["per_block"], ROWS, waves_ref)
    scale = levels_scale(cfg, segment, band)
    narrow = segment.astype(jnp.bfloat16)
    left = match_lines(
        shapes_ref[...], lambda h: trace_spectrum(narrow, h, whole_forward), scale, forward, inverse
    )
    sent_ref[...] = sum_lines(sums, left)

    if later:
        spectra_ref, scale_ref, sums_ref = later_refs
        segment, sums = cut_traces(cfg, codes, *later, waves_ref)
        scale_ref[...] = levels_scale(cfg, segment, band)
        narrow = segment.astype(jnp.bfloat16)
        for h in range(pieces):
            spectra_ref[:, h * 2 * LAGS : (h + 1) * 2 * LAGS] = trace_spectrum(narrow, h, whole_forward)
        sums_ref[...] = sums


def match_kernel(shapes_ref, spectra_ref, scale_ref, sums_ref, forward_ref, inverse_ref, before_ref, sent_ref):
    forward, inverse = short_tables(forward_ref, inverse_ref)
    left = match_lines(
        shapes_ref[...],
        lambda h: spectra_ref[:, h * 2 * LAGS : (h + 1) * 2 * LAGS],
        scale_ref[...],
        forward,
        inverse,
    )
    groups, tile = sums_ref.shape[0], sums_ref.shape[1]
    count = shapes_ref.shape[0] // tile
    groups = groups // count
    for q in range(count):
        ends = slice(q * groups, (q + 1) * groups)
        sent_ref[ends, :] = before_ref[ends, :] + sum_lines(sums_ref[ends, :], left[q * tile : (q + 1) * tile])


def stack_kernel(factor, parts_ref, stacks_ref, top_ref):
    stacks = jnp.sum(parts_ref[...], axis=0) * factor
    stacks_ref[...] = stacks
    top_ref[...] = jnp.broadcast_to(jnp.max(stacks, axis=0, keepdims=True), top_ref.shape)


def body(waveforms, templates, stations, moveouts):
    devices = lax.axis_size(AXES)
    tpl_count, slot_count = stations.shape
    comps, length = templates.shape[2:]
    station_dev, _, samples = waveforms.shape
    seg_len = length + LAGS
    pairs = tpl_count * slot_count
    capacity = (2 * pairs + devices - 1) // devices
    per_block = (ROWS - 1) // comps
    cfg = dict(
        devices=devices,
        station_dev=station_dev,
        tpl_count=tpl_count,
        per_block=per_block,
        length=length,
        seg_len=seg_len,
        shift_bits=bits_of(samples - seg_len + 1),
        row_bits=bits_of(station_dev),
    )
    forward, inverse = (jnp.asarray(t) for t in transform_tables(LAGS))
    band = jnp.asarray(band_table(length, LAGS))
    groups = SOURCES * tpl_count
    tiles = devices // SOURCES
    spectrum = length // LAGS * 2 * LAGS
    rest = max(0, capacity - per_block)
    rest_rows = -(-comps * rest // 16) * 16
    later = (per_block, rest, rest_rows) if rest else ()
    whole = pl.BlockSpec(memory_space=pltpu.VMEM)
    anywhere = pl.BlockSpec(memory_space=pl.ANY)
    params = pltpu.CompilerParams(vmem_limit_bytes=59 * MIB)
    by_slot = templates.transpose(1, 2, 0, 3)

    def exchange(x):
        return lax.all_to_all(x, AXES, split_axis=0, concat_axis=0, tiled=True)

    def pack_slots(first, count, rows):
        lines = devices * rows
        packed = pl.pallas_call(
            functools.partial(pack_kernel, cfg, first, count, rows),
            out_shape=jax.ShapeDtypeStruct((lines, length), jnp.bfloat16),
            in_specs=[whole, whole, anywhere],
            out_specs=anywhere,
            scratch_shapes=[
                pltpu.VMEM(by_slot.shape, jnp.bfloat16),
                pltpu.VMEM((comps, pairs, length), jnp.bfloat16),
                pltpu.VMEM((lines, length), jnp.bfloat16),
                pltpu.SemaphoreType.DMA,
                pltpu.SemaphoreType.DMA((tiles,)),
            ],
            compiler_params=params,
            cost_estimate=work(2 * lines * pairs * comps * length, 2 * (by_slot.size + lines * length)),
            name="pack",
        )(stations, moveouts, by_slot)
        return packed.reshape(devices, rows, length)

    def same(shape):
        return pl.BlockSpec(shape, lambda i: (0,) * len(shape))

    def tiled(*shape):
        return pl.BlockSpec(shape, lambda i: (i, 0))

    def work(flops, size):
        return pl.CostEstimate(flops=flops, bytes_accessed=size, transcendentals=0)

    first_rows = exchange(pack_slots(0, per_block, ROWS))
    if later:
        first_rows, later_rows = lax.optimization_barrier((first_rows, pack_slots(*later)))
        later_rows = exchange(later_rows).reshape(devices * rest_rows, length)
    first_rows = first_rows.reshape(devices * ROWS, length)
    tile = SOURCES * rest_rows
    sent, *kept = pl.pallas_call(
        functools.partial(hold_kernel, cfg, later),
        grid=(tiles,),
        out_shape=[jax.ShapeDtypeStruct((devices * tpl_count, LAGS), jnp.float32)]
        + [
            jax.ShapeDtypeStruct((devices * rest_rows, spectrum), jnp.float32),
            jax.ShapeDtypeStruct((devices * rest_rows, LAGS), jnp.float32),
            jax.ShapeDtypeStruct((devices * tpl_count, tile), jnp.bfloat16),
        ][: 3 if later else 0],
        in_specs=[
            tiled(SOURCES * ROWS, length),
            same((comps, station_dev, samples)),
            same(forward.shape),
            same(inverse.shape),
            same(band.shape),
        ],
        out_specs=[tiled(groups, LAGS)]
        + [tiled(tile, spectrum), tiled(tile, LAGS), tiled(groups, tile)][: 3 if later else 0],
        compiler_params=params,
        cost_estimate=work(
            2 * devices * (ROWS + rest_rows) * (length // LAGS * 8 * LAGS * LAGS + 2 * seg_len * LAGS),
            devices * (ROWS + rest_rows) * spectrum * 4,
        ),
        name="hold",
    )(first_rows, waveforms.transpose(1, 0, 2), forward, inverse, band)
    if later:
        step = 2 if tiles % 2 == 0 else 1
        sent = pl.pallas_call(
            match_kernel,
            grid=(tiles // step,),
            out_shape=jax.ShapeDtypeStruct(sent.shape, jnp.float32),
            in_specs=[
                tiled(step * tile, length),
                tiled(step * tile, spectrum),
                tiled(step * tile, LAGS),
                tiled(step * groups, tile),
                same(forward.shape),
                same(inverse.shape),
                tiled(step * groups, LAGS),
            ],
            out_specs=tiled(step * groups, LAGS),
            compiler_params=params,
            name="match",
        )(later_rows, *kept, forward, inverse, sent)

    parts = exchange(sent.reshape(devices, tpl_count, LAGS))
    stacks, top = pl.pallas_call(
        functools.partial(stack_kernel, math.sqrt(length / (comps * slot_count))),
        out_shape=[
            jax.ShapeDtypeStruct((tpl_count, LAGS), jnp.float32),
            jax.ShapeDtypeStruct((devices, 1, LAGS), jnp.float32),
        ],
        in_specs=[whole],
        out_specs=[whole, whole],
        compiler_params=pltpu.CompilerParams(vmem_limit_bytes=16 * MIB),
        name="stack",
    )(parts)
    return stacks, jnp.max(exchange(top), axis=(0, 1))


def solution(mesh):
    placed = (
        P(AXES, None, None),
        P(AXES, None, None, None),
        P(AXES, None),
        P(AXES, None),
    )
    return jax.shard_map(body, mesh=mesh, in_specs=placed, out_specs=(P(AXES, None), P()), check_vma=False)
```

```python
import functools
import math

import jax
import jax.numpy as jnp
import ml_dtypes
import numpy as np
from jax import lax
from jax.experimental import pallas as pl
from jax.experimental.pallas import tpu as pltpu
from jax.sharding import PartitionSpec as P

LAGS = 256
AXES = ("tmpl", "sta")
SOURCES = 16
ROWS = 16
DIGITS = 3
LANES = 128
MIB = 1024 * 1024


def bits_of(limit):
    return max(1, (limit - 1).bit_length())


def split_table(table):
    high = table.astype(ml_dtypes.bfloat16)
    low = (table - high.astype(np.float64)).astype(ml_dtypes.bfloat16)
    return np.concatenate([high, low], axis=0)


def transform_tables(piece):
    size = 2 * piece
    angle = 2.0 * np.pi * (np.arange(piece) + 0.5) / size
    phase = np.arange(size)[:, None] * angle[None, :]
    forward = np.concatenate([np.cos(phase), -np.sin(phase)], axis=1)
    short = split_table(forward[:piece])
    back = angle[:, None] * np.arange(piece)[None, :]
    inverse = np.concatenate([np.cos(back), -np.sin(back)], axis=0) * (2.0 / size)
    inverse = split_table(inverse)
    return split_table(forward), short, np.concatenate([inverse, inverse[:size]], axis=0)


def band_table(length, lag_count):
    sample = np.arange(length + lag_count)[:, None]
    lag = np.arange(lag_count)[None, :]
    return ((sample >= lag) & (sample < lag + length)).astype(ml_dtypes.bfloat16)


def iota(shape, axis):
    return lax.broadcasted_iota(jnp.int32, shape, axis)


def dot(a, b):
    return jnp.dot(a, b, preferred_element_type=jnp.float32)


def exact_dot(a, b):
    return jnp.dot(a, b, precision=lax.Precision.HIGHEST, preferred_element_type=jnp.float32)


def entry_lanes(tpl_count, slot_count):
    pairs = tpl_count * slot_count
    first = iota((slot_count, pairs), 0) * tpl_count
    entry = iota((slot_count, pairs), 1)
    spread = jnp.where((entry >= first) & (entry < first + tpl_count), 1.0, 0.0)
    start = jnp.sum(spread * first.astype(jnp.float32), axis=0, keepdims=True)
    return spread, iota((1, pairs), 1).astype(jnp.float32) - start


def as_lanes(values, spread, place, tpl_count):
    owners = values.shape[0] // tpl_count
    pairs = spread.shape[1]
    wide = exact_dot(values.astype(jnp.float32), spread).reshape(owners, tpl_count, pairs)
    own = iota((1, tpl_count, pairs), 1).astype(jnp.float32) == place.reshape(1, 1, pairs)
    return jnp.sum(jnp.where(own, wide, 0.0), axis=1)


def count_before(hits):
    pairs = hits.shape[1]
    earlier = jnp.where(iota((pairs, pairs), 0) < iota((pairs, pairs), 1), 1.0, 0.0)
    return dot(hits.astype(jnp.bfloat16), earlier.astype(jnp.bfloat16))


def pack_kernel(cfg, first, count, rows, stations_ref, moveouts_ref, templates_hbm, packed_hbm, raw_ref, shapes_ref, packed_ref, in_sem, out_sems):
    load = pltpu.make_async_copy(templates_hbm, raw_ref, in_sem)
    load.start()
    tpl_count, slot_count = stations_ref.shape
    pairs = tpl_count * slot_count
    devices, station_dev = cfg["devices"], cfg["station_dev"]
    spread, place = entry_lanes(tpl_count, slot_count)
    station = as_lanes(stations_ref[...], spread, place, tpl_count)
    target = jnp.floor((station + 0.5) * (1.0 / station_dev))
    hit = iota((devices, pairs), 0).astype(jnp.float32) == target
    onehot = jnp.where(hit, 1.0, 0.0)
    rank = jnp.sum(onehot * count_before(onehot), axis=0, keepdims=True)
    slot = rank - float(first)
    inside = (slot >= 0.0) & (slot < float(count))
    goal = jnp.where(inside, target * rows + slot, -float(devices * rows))

    codes = None
    if first == 0:
        shift = as_lanes(moveouts_ref[...], spread, place, tpl_count)
        row = station - target * station_dev
        code = ((place + 1.0) * (1 << cfg["row_bits"]) + row) * (1 << cfg["shift_bits"]) + shift
        code = code.astype(jnp.int32)
        at_rank = jnp.where(iota((LANES, pairs), 0).astype(jnp.float32) == rank, 1.0, 0.0).astype(jnp.bfloat16)
        digits = []
        for d in range(DIGITS):
            digit = (lax.shift_right_logical(code, 8 * d) & 255).astype(jnp.float32)
            marked = (onehot * digit).astype(jnp.bfloat16)
            digits.append(
                lax.dot_general(marked, at_rank, (((1,), (1,)), ((), ())), preferred_element_type=jnp.float32)
            )
        codes = jnp.concatenate(digits, axis=1)

    load.wait()
    comps, length = raw_ref.shape[1], raw_ref.shape[3]
    for c in range(comps):
        values = raw_ref[:, c].astype(jnp.float32).reshape(pairs, length)
        centred = values - jnp.mean(values, axis=-1, keepdims=True)
        spread_c = jnp.sqrt(jnp.mean(centred * centred, axis=-1, keepdims=True) + 1e-05)
        shapes_ref[c] = (centred * (1.0 / spread_c)).astype(jnp.bfloat16)

    tile = SOURCES * rows
    copies = []
    for step in range(devices // SOURCES):
        top = step * tile
        line = iota((tile, pairs), 0).astype(jnp.float32) + float(top)
        total = jnp.zeros((tile, length), jnp.float32)
        for c in range(comps):
            pick = jnp.where(line == goal + float(c * count), 1.0, 0.0).astype(jnp.bfloat16)
            total = total + dot(pick, shapes_ref[c])
        if codes is not None:
            width = codes.shape[1]
            mine = codes[step * SOURCES : (step + 1) * SOURCES].reshape(SOURCES, 1, width)
            last = iota((SOURCES, rows, 1), 1) == rows - 1
            mine = jnp.where(last, mine, 0.0).reshape(tile, width)
            total = jnp.concatenate([total[:, :width] + mine, total[:, width:]], axis=1)
        part = pl.ds(top, tile)
        packed_ref[part, :] = total.astype(jnp.bfloat16)
        copies.append(pltpu.make_async_copy(packed_ref.at[part], packed_hbm.at[part], out_sems.at[step]))
        copies[-1].start()
    for copy in copies:
        copy.wait()


def read_codes(block):
    width = DIGITS * LANES
    rows = block.shape[0] // SOURCES
    values = block[:, :width].astype(jnp.float32).reshape(SOURCES, rows, width)
    last = iota((1, rows, 1), 1) == rows - 1
    digits = jnp.sum(jnp.where(last, values, 0.0), axis=1)
    return sum(digits[:, d * LANES : (d + 1) * LANES] * float(256**d) for d in range(DIGITS))


def block_lines(cfg, codes, comps, first, count, rows):
    tile = SOURCES * rows
    line = iota((SOURCES, rows, 1), 1).reshape(tile, 1)
    owner = iota((SOURCES, rows, 1), 0).reshape(tile, 1)
    comp = jnp.zeros((tile, 1), jnp.int32)
    for c in range(1, comps + 1):
        comp = comp + jnp.where(line >= c * count, 1, 0)
    slot = line - comp * count + first
    repeated = jnp.broadcast_to(codes.reshape(SOURCES, 1, LANES), (SOURCES, rows, LANES)).reshape(tile, LANES)
    chosen = (iota((tile, LANES), 1) == slot) & (comp < comps)
    code = jnp.sum(jnp.where(chosen, repeated, 0.0), axis=1, keepdims=True).astype(jnp.int32)
    shift_bits, row_bits = cfg["shift_bits"], cfg["row_bits"]
    shift = code & ((1 << shift_bits) - 1)
    row = lax.shift_right_logical(code, shift_bits) & ((1 << row_bits) - 1)
    tpl = lax.shift_right_logical(code, shift_bits + row_bits) - 1
    goal = jnp.where(tpl >= 0, comp * cfg["station_dev"] + row, -1)
    return shift, goal, jnp.where(tpl >= 0, owner * cfg["tpl_count"] + tpl, -1)


def cut_traces(cfg, shift, goal, waves):
    tile, seg_len, shift_bits = shift.shape[0], cfg["seg_len"], cfg["shift_bits"]
    pick = jnp.where(iota((tile, waves.shape[0]), 1) == goal, 1.0, 0.0).astype(jnp.bfloat16)
    x = dot(pick, waves)

    for bit in range(shift_bits - 1, 6, -1):
        step = 1 << bit
        width = seg_len + step
        if x.shape[1] < width + step:
            x = jnp.concatenate([x, jnp.zeros((tile, width + step - x.shape[1]), jnp.float32)], axis=1)
        x = jnp.where((shift & step) != 0, x[:, step : step + width], x[:, :width])
    for bit in range(min(shift_bits, 7) - 1, -1, -1):
        step = 1 << bit
        x = jnp.where((shift & step) != 0, pltpu.roll(x, x.shape[1] - step, 1), x)
    return x[:, :seg_len]


def line_sums(cfg, column):
    groups = SOURCES * cfg["tpl_count"]
    return jnp.where(iota((column.shape[0], groups), 1) == column, 1.0, 0.0).T.astype(jnp.bfloat16)


def levels_scale(cfg, segment, band):
    length = cfg["length"]
    power = segment * segment
    high = power.astype(jnp.bfloat16)
    low = (power - high.astype(jnp.float32)).astype(jnp.bfloat16)
    energy = dot(high, band) + dot(low, band)
    return 1.0 / (length * jnp.sqrt(energy * (1.0 / length) + 1e-05))


def match_lines(shapes, spectrum_of, scale, forward, inverse):
    real = imag = 0.0
    for h in range(shapes.shape[1] // LAGS):
        part = shapes[:, h * LAGS : (h + 1) * LAGS]
        mine = dot(jnp.concatenate([part, part], axis=1), forward)
        theirs = spectrum_of(h)
        mine_r, mine_i = mine[:, :LAGS], mine[:, LAGS:]
        theirs_r, theirs_i = theirs[:, :LAGS], theirs[:, LAGS:]
        real = real + (theirs_r * mine_r + theirs_i * mine_i)
        imag = imag + (theirs_i * mine_r - theirs_r * mine_i)
    product = jnp.concatenate([real, imag], axis=1)
    high = product.astype(jnp.bfloat16)
    low = (product - high.astype(jnp.float32)).astype(jnp.bfloat16)
    return dot(jnp.concatenate([high, high, low], axis=1), inverse) * scale


def sum_lines(sums, left):
    total = 0.0
    for _ in range(3):
        part = left.astype(jnp.bfloat16)
        left = left - part.astype(jnp.float32)
        total = total + dot(sums, part)
    return total


def hold_kernel(cfg, later, shapes_ref, waves_ref, forward_ref, short_ref, inverse_ref, band_ref, sent_ref, *later_refs):
    codes = read_codes(shapes_ref[...])
    comps, station_dev, samples = waves_ref.shape
    blocks = [(0, cfg["per_block"], ROWS)] + ([later] if later else [])
    columns = [block_lines(cfg, codes, comps, *block) for block in blocks]
    shift, goal = (jnp.concatenate([column[q] for column in columns], axis=0) for q in range(2))
    segment = cut_traces(cfg, shift, goal, waves_ref[...].reshape(comps * station_dev, samples))
    scale = levels_scale(cfg, segment, band_ref[...])
    narrow = segment.astype(jnp.bfloat16)
    forward = forward_ref[...]
    tile = SOURCES * ROWS
    if later:
        spectra_ref, scale_ref, sums_ref = later_refs
        scale_ref[...] = scale[tile:]
        sums_ref[...] = line_sums(cfg, columns[1][2])

    def spectrum_of(h):
        part = narrow[:, h * LAGS : (h + 2) * LAGS]
        both = dot(jnp.concatenate([part, part], axis=1), forward)
        if later:
            spectra_ref[:, h * 2 * LAGS : (h + 1) * 2 * LAGS] = both[tile:]
        return both[:tile]

    left = match_lines(shapes_ref[...], spectrum_of, scale[:tile], short_ref[...], inverse_ref[...])
    sent_ref[...] = sum_lines(line_sums(cfg, columns[0][2]), left)


def match_kernel(shapes_hbm, spectra_hbm, scale_hbm, sums_hbm, short_hbm, inverse_hbm, before_hbm, sent_hbm, *scratch):
    bufs, sent_ref, sems, sent_sems = scratch[:7], scratch[7], scratch[8], scratch[9]
    shapes_ref, spectra_ref, scale_ref, sums_ref, short_ref, inverse_ref, before_ref = bufs
    tiles = sent_sems.shape[0]

    def fetch(source, buffer, sem):
        copy = pltpu.make_async_copy(source, buffer, sem)
        copy.start()
        return copy

    def tile_of(ref, step):
        size = ref.shape[0] // tiles
        return ref.at[pl.ds(step * size, size)]

    short_copy = fetch(short_hbm, short_ref, sems.at[0])
    tiled = (
        (shapes_hbm, shapes_ref),
        (spectra_hbm, spectra_ref),
        (scale_hbm, scale_ref),
        (sums_hbm, sums_ref),
        (before_hbm, before_ref),
    )
    copies = []
    for step in range(tiles):
        row = []
        for q, (source, buffer) in enumerate(tiled):
            row.append(fetch(tile_of(source, step), tile_of(buffer, step), sems.at[2 + step * len(tiled) + q]))
            if step == 0 and q == 1:
                inverse_copy = fetch(inverse_hbm, inverse_ref, sems.at[1])
        copies.append(row)
    short_copy.wait()
    out = []
    for step in range(tiles):
        for copy in copies[step]:
            copy.wait()
        if step == 0:
            inverse_copy.wait()
        spectra = tile_of(spectra_ref, step)
        left = match_lines(
            tile_of(shapes_ref, step)[...],
            lambda h: spectra[:, h * 2 * LAGS : (h + 1) * 2 * LAGS],
            tile_of(scale_ref, step)[...],
            short_ref[...],
            inverse_ref[...],
        )
        tile_of(sent_ref, step)[...] = tile_of(before_ref, step)[...] + sum_lines(tile_of(sums_ref, step)[...], left)
        out.append(fetch(tile_of(sent_ref, step), tile_of(sent_hbm, step), sent_sems.at[step]))
    for copy in out:
        copy.wait()


def stack_kernel(factor, parts_ref, stacks_ref, top_ref):
    stacks = jnp.sum(parts_ref[...], axis=0) * factor
    stacks_ref[...] = stacks
    top_ref[...] = jnp.broadcast_to(jnp.max(stacks, axis=0, keepdims=True), top_ref.shape)


def body(waveforms, templates, stations, moveouts):
    devices = lax.axis_size(AXES)
    tpl_count, slot_count = stations.shape
    comps, length = templates.shape[2:]
    station_dev, _, samples = waveforms.shape
    seg_len = length + LAGS
    pairs = tpl_count * slot_count
    capacity = (2 * pairs + devices - 1) // devices
    per_block = (ROWS - 1) // comps
    cfg = dict(
        devices=devices,
        station_dev=station_dev,
        tpl_count=tpl_count,
        per_block=per_block,
        length=length,
        seg_len=seg_len,
        shift_bits=bits_of(samples - seg_len + 1),
        row_bits=bits_of(station_dev),
    )
    forward, short, inverse = (jnp.asarray(t) for t in transform_tables(LAGS))
    band = jnp.asarray(band_table(length, LAGS))
    groups = SOURCES * tpl_count
    tiles = devices // SOURCES
    spectrum = length // LAGS * 2 * LAGS
    rest = max(0, capacity - per_block)
    rest_rows = -(-comps * rest // 16) * 16
    later = (per_block, rest, rest_rows) if rest else ()
    whole = pl.BlockSpec(memory_space=pltpu.VMEM)
    anywhere = pl.BlockSpec(memory_space=pl.ANY)
    params = pltpu.CompilerParams(vmem_limit_bytes=60 * MIB)
    by_slot = templates.transpose(1, 2, 0, 3)

    def exchange(x):
        return lax.all_to_all(x, AXES, split_axis=0, concat_axis=0, tiled=True)

    def pack_slots(first, count, rows):
        lines = devices * rows
        packed = pl.pallas_call(
            functools.partial(pack_kernel, cfg, first, count, rows),
            out_shape=jax.ShapeDtypeStruct((lines, length), jnp.bfloat16),
            in_specs=[whole, whole, anywhere],
            out_specs=anywhere,
            scratch_shapes=[
                pltpu.VMEM(by_slot.shape, jnp.bfloat16),
                pltpu.VMEM((comps, pairs, length), jnp.bfloat16),
                pltpu.VMEM((lines, length), jnp.bfloat16),
                pltpu.SemaphoreType.DMA,
                pltpu.SemaphoreType.DMA((tiles,)),
            ],
            compiler_params=params,
            cost_estimate=work(2 * lines * pairs * comps * length, 2 * (by_slot.size + lines * length)),
            name="pack",
        )(stations, moveouts, by_slot)
        return packed.reshape(devices, rows, length)

    def same(shape):
        return pl.BlockSpec(shape, lambda i: (0,) * len(shape))

    def tiled(*shape):
        return pl.BlockSpec(shape, lambda i: (i, 0))

    def work(flops, size):
        return pl.CostEstimate(flops=flops, bytes_accessed=size, transcendentals=0)

    first_rows = exchange(pack_slots(0, per_block, ROWS))
    if later:
        first_rows, later_rows = lax.optimization_barrier((first_rows, pack_slots(*later)))
        later_rows = exchange(later_rows).reshape(devices * rest_rows, length)
    first_rows = first_rows.reshape(devices * ROWS, length)
    tile = SOURCES * rest_rows
    sent, *kept = pl.pallas_call(
        functools.partial(hold_kernel, cfg, later),
        grid=(tiles,),
        out_shape=[jax.ShapeDtypeStruct((devices * tpl_count, LAGS), jnp.float32)]
        + [
            jax.ShapeDtypeStruct((devices * rest_rows, spectrum), jnp.float32),
            jax.ShapeDtypeStruct((devices * rest_rows, LAGS), jnp.float32),
            jax.ShapeDtypeStruct((devices * tpl_count, tile), jnp.bfloat16),
        ][: 3 if later else 0],
        in_specs=[
            tiled(SOURCES * ROWS, length),
            same((comps, station_dev, samples)),
            same(forward.shape),
            same(short.shape),
            same(inverse.shape),
            same(band.shape),
        ],
        out_specs=[tiled(groups, LAGS)]
        + [tiled(tile, spectrum), tiled(tile, LAGS), tiled(groups, tile)][: 3 if later else 0],
        compiler_params=params,
        cost_estimate=work(
            2 * devices * (ROWS + rest_rows) * (length // LAGS * 8 * LAGS * LAGS + 2 * seg_len * LAGS),
            devices * (ROWS + rest_rows) * spectrum * 4,
        ),
        name="hold",
    )(first_rows, waveforms.transpose(1, 0, 2), forward, short, inverse, band)
    if later:
        operands = (later_rows, *kept, short, inverse, sent)
        sent = pl.pallas_call(
            match_kernel,
            out_shape=jax.ShapeDtypeStruct(sent.shape, jnp.float32),
            in_specs=[anywhere] * len(operands),
            out_specs=anywhere,
            scratch_shapes=[pltpu.VMEM(x.shape, x.dtype) for x in operands]
            + [
                pltpu.VMEM(sent.shape, jnp.float32),
                pltpu.SemaphoreType.DMA((2 + 5 * tiles,)),
                pltpu.SemaphoreType.DMA((tiles,)),
            ],
            compiler_params=params,
            name="match",
        )(*operands)

    parts = exchange(sent.reshape(devices, tpl_count, LAGS))
    stacks, top = pl.pallas_call(
        functools.partial(stack_kernel, math.sqrt(length / (comps * slot_count))),
        out_shape=[
            jax.ShapeDtypeStruct((tpl_count, LAGS), jnp.float32),
            jax.ShapeDtypeStruct((lax.axis_size(AXES[-1]), 1, LAGS), jnp.float32),
        ],
        in_specs=[whole],
        out_specs=[whole, whole],
        compiler_params=pltpu.CompilerParams(vmem_limit_bytes=16 * MIB),
        name="stack",
    )(parts)
    for axis in reversed(AXES):
        spread = jnp.broadcast_to(top[:1], (lax.axis_size(axis), 1, LAGS)) if axis != AXES[-1] else top
        tops = lax.all_to_all(spread, axis, split_axis=0, concat_axis=0, tiled=True)
        top = jnp.max(tops, axis=0, keepdims=True)
    return stacks, top.reshape(LAGS)


def solution(mesh):
    placed = (
        P(AXES, None, None),
        P(AXES, None, None, None),
        P(AXES, None),
        P(AXES, None),
    )
    return jax.shard_map(body, mesh=mesh, in_specs=placed, out_specs=(P(AXES, None), P()), check_vma=False)
```

```python
import functools
import math

import jax
import jax.numpy as jnp
import ml_dtypes
import numpy as np
from jax import lax
from jax.experimental import pallas as pl
from jax.experimental.pallas import tpu as pltpu
from jax.sharding import PartitionSpec as P

LAGS = 256
HALF = "half"
GROUP = ("tmpl", "sta")
AXES = (HALF,) + GROUP
SOURCES = 8
DIGITS = 3
LANES = 128
MIB = 1024 * 1024


def bits_of(limit):
    return max(1, (limit - 1).bit_length())


def split_table(table):
    high = table.astype(ml_dtypes.bfloat16)
    low = (table - high.astype(np.float64)).astype(ml_dtypes.bfloat16)
    return np.concatenate([high, low], axis=0)


def transform_tables(piece):
    size = 2 * piece
    angle = 2.0 * np.pi * (np.arange(piece) + 0.5) / size
    phase = np.arange(size)[:, None] * angle[None, :]
    forward = np.concatenate([np.cos(phase), -np.sin(phase)], axis=1)
    short = split_table(forward[:piece])
    back = angle[:, None] * np.arange(piece)[None, :]
    inverse = np.concatenate([np.cos(back), -np.sin(back)], axis=0) * (2.0 / size)
    inverse = split_table(inverse)
    return split_table(forward), short, np.concatenate([inverse, inverse[:size]], axis=0)


def band_table(length, lag_count):
    sample = np.arange(length + lag_count)[:, None]
    lag = np.arange(lag_count)[None, :]
    return ((sample >= lag) & (sample < lag + length)).astype(ml_dtypes.bfloat16)


def iota(shape, axis):
    return lax.broadcasted_iota(jnp.int32, shape, axis)


def dot(a, b):
    return jnp.dot(a, b, preferred_element_type=jnp.float32)


def exact_dot(a, b):
    return jnp.dot(a, b, precision=lax.Precision.HIGHEST, preferred_element_type=jnp.float32)


def entry_lanes(tpl_count, slot_count):
    pairs = tpl_count * slot_count
    first = iota((slot_count, pairs), 0) * tpl_count
    entry = iota((slot_count, pairs), 1)
    spread = jnp.where((entry >= first) & (entry < first + tpl_count), 1.0, 0.0)
    start = jnp.sum(spread * first.astype(jnp.float32), axis=0, keepdims=True)
    return spread, iota((1, pairs), 1).astype(jnp.float32) - start


def as_lanes(values, spread, place, tpl_count):
    owners = values.shape[0] // tpl_count
    pairs = spread.shape[1]
    wide = exact_dot(values.astype(jnp.float32), spread).reshape(owners, tpl_count, pairs)
    own = iota((1, tpl_count, pairs), 1).astype(jnp.float32) == place.reshape(1, 1, pairs)
    return jnp.sum(jnp.where(own, wide, 0.0), axis=1)


def count_before(hits):
    pairs = hits.shape[1]
    earlier = jnp.where(iota((pairs, pairs), 0) < iota((pairs, pairs), 1), 1.0, 0.0)
    return dot(hits.astype(jnp.bfloat16), earlier.astype(jnp.bfloat16))


def pack_kernel(cfg, block, half_ref, stations_ref, moveouts_ref, templates_hbm, packed_hbm, raw_ref, shapes_ref, packed_ref, in_sem, out_sems):
    load = pltpu.make_async_copy(templates_hbm, raw_ref, in_sem)
    load.start()
    tpl_count, slot_count = stations_ref.shape
    pairs = tpl_count * slot_count
    devices, group, halves = cfg["devices"], cfg["group"], cfg["halves"]
    station_dev, rows, capacity = cfg["station_dev"], cfg["rows"], cfg["capacity"]
    spread, place = entry_lanes(tpl_count, slot_count)
    station = as_lanes(stations_ref[...], spread, place, tpl_count)
    device = jnp.floor((station + 0.5) * (1.0 / station_dev))
    onehot = jnp.where(iota((devices, pairs), 0).astype(jnp.float32) == device, 1.0, 0.0)
    rank = jnp.sum(onehot * count_before(onehot), axis=0, keepdims=True)
    half = jnp.floor((device + 0.5) * (1.0 / group))
    holder = device - half * group
    mine = half_ref[0].astype(jnp.float32)
    away = jnp.where(half == mine, 0.0, 1.0)
    inside = (away == float(block)) & (rank < float(capacity))
    goal = jnp.where(inside, holder * rows + rank, -float(group * rows))

    codes = None
    if block == 0:
        shift = as_lanes(moveouts_ref[...], spread, place, tpl_count)
        row = station - device * station_dev
        code = ((place + 1.0) * (1 << cfg["row_bits"]) + row) * (1 << cfg["shift_bits"]) + shift
        code = code.astype(jnp.int32)
        at_rank = jnp.where(iota((LANES, pairs), 0).astype(jnp.float32) == rank, 1.0, 0.0).astype(jnp.bfloat16)
        at_holder = iota((group, pairs), 0).astype(jnp.float32) == holder
        digits = []
        for q in range(halves):
            for d in range(DIGITS):
                digit = (lax.shift_right_logical(code, 8 * d) & 255).astype(jnp.float32)
                marked = jnp.where(at_holder & (away == float(q)), digit, 0.0).astype(jnp.bfloat16)
                digits.append(
                    lax.dot_general(marked, at_rank, (((1,), (1,)), ((), ())), preferred_element_type=jnp.float32)
                )
        codes = jnp.concatenate(digits, axis=1)

    load.wait()
    comps, length = raw_ref.shape[1], raw_ref.shape[3]
    for c in range(comps):
        values = raw_ref[:, c].astype(jnp.float32).reshape(pairs, length)
        centred = values - jnp.mean(values, axis=-1, keepdims=True)
        spread_c = jnp.sqrt(jnp.mean(centred * centred, axis=-1, keepdims=True) + 1e-05)
        shapes_ref[c] = (centred * (1.0 / spread_c)).astype(jnp.bfloat16)

    tile = SOURCES * rows
    copies = []
    for step in range(group // SOURCES):
        top = step * tile
        line = iota((tile, pairs), 0).astype(jnp.float32) + float(top)
        total = jnp.zeros((tile, length), jnp.float32)
        for c in range(comps):
            pick = jnp.where(line == goal + float(c * capacity), 1.0, 0.0).astype(jnp.bfloat16)
            total = total + dot(pick, shapes_ref[c])
        if codes is not None:
            width = codes.shape[1]
            here = codes[step * SOURCES : (step + 1) * SOURCES].reshape(SOURCES, 1, width)
            last = iota((SOURCES, rows, 1), 1) == rows - 1
            here = jnp.where(last, here, 0.0).reshape(tile, width)
            total = jnp.concatenate([total[:, :width] + here, total[:, width:]], axis=1)
        part = pl.ds(top, tile)
        packed_ref[part, :] = total.astype(jnp.bfloat16)
        copies.append(pltpu.make_async_copy(packed_ref.at[part], packed_hbm.at[part], out_sems.at[step]))
        copies[-1].start()
    for copy in copies:
        copy.wait()


def read_codes(first_block, block):
    width = DIGITS * LANES
    rows = first_block.shape[0] // SOURCES
    values = first_block[:, block * width : (block + 1) * width].astype(jnp.float32).reshape(SOURCES, rows, width)
    last = iota((1, rows, 1), 1) == rows - 1
    digits = jnp.sum(jnp.where(last, values, 0.0), axis=1)
    return sum(digits[:, d * LANES : (d + 1) * LANES] * float(256**d) for d in range(DIGITS))


def block_lines(cfg, codes, comps):
    capacity, rows = cfg["capacity"], cfg["rows"]
    tile = SOURCES * rows
    line = iota((SOURCES, rows, 1), 1).reshape(tile, 1)
    owner = iota((SOURCES, rows, 1), 0).reshape(tile, 1)
    comp = jnp.zeros((tile, 1), jnp.int32)
    for c in range(1, comps + 1):
        comp = comp + jnp.where(line >= c * capacity, 1, 0)
    slot = line - comp * capacity
    repeated = jnp.broadcast_to(codes.reshape(SOURCES, 1, LANES), (SOURCES, rows, LANES)).reshape(tile, LANES)
    chosen = (iota((tile, LANES), 1) == slot) & (comp < comps)
    code = jnp.sum(jnp.where(chosen, repeated, 0.0), axis=1, keepdims=True).astype(jnp.int32)
    shift_bits, row_bits = cfg["shift_bits"], cfg["row_bits"]
    shift = code & ((1 << shift_bits) - 1)
    row = lax.shift_right_logical(code, shift_bits) & ((1 << row_bits) - 1)
    tpl = lax.shift_right_logical(code, shift_bits + row_bits) - 1
    goal = jnp.where(tpl >= 0, comp * cfg["station_dev"] + row, -1)
    return shift, goal, jnp.where(tpl >= 0, owner * cfg["tpl_count"] + tpl, -1)


def cut_traces(cfg, shift, goal, waves):
    tile, seg_len, shift_bits = shift.shape[0], cfg["seg_len"], cfg["shift_bits"]
    pick = jnp.where(iota((tile, waves.shape[0]), 1) == goal, 1.0, 0.0).astype(jnp.bfloat16)
    x = dot(pick, waves)

    for bit in range(shift_bits - 1, 6, -1):
        step = 1 << bit
        width = seg_len + step
        if x.shape[1] < width + step:
            x = jnp.concatenate([x, jnp.zeros((tile, width + step - x.shape[1]), jnp.float32)], axis=1)
        x = jnp.where((shift & step) != 0, x[:, step : step + width], x[:, :width])
    for bit in range(min(shift_bits, 7) - 1, -1, -1):
        step = 1 << bit
        x = jnp.where((shift & step) != 0, pltpu.roll(x, x.shape[1] - step, 1), x)
    return x[:, :seg_len]


def line_sums(cfg, column):
    groups = SOURCES * cfg["tpl_count"]
    return jnp.where(iota((column.shape[0], groups), 1) == column, 1.0, 0.0).T.astype(jnp.bfloat16)


def levels_scale(cfg, segment, band):
    length = cfg["length"]
    power = segment * segment
    high = power.astype(jnp.bfloat16)
    low = (power - high.astype(jnp.float32)).astype(jnp.bfloat16)
    energy = dot(high, band) + dot(low, band)
    return 1.0 / (length * jnp.sqrt(energy * (1.0 / length) + 1e-05))


def match_lines(shapes, spectrum_of, scale, forward, inverse):
    real = imag = 0.0
    for h in range(shapes.shape[1] // LAGS):
        part = shapes[:, h * LAGS : (h + 1) * LAGS]
        mine = dot(jnp.concatenate([part, part], axis=1), forward)
        theirs = spectrum_of(h)
        mine_r, mine_i = mine[:, :LAGS], mine[:, LAGS:]
        theirs_r, theirs_i = theirs[:, :LAGS], theirs[:, LAGS:]
        real = real + (theirs_r * mine_r + theirs_i * mine_i)
        imag = imag + (theirs_i * mine_r - theirs_r * mine_i)
    product = jnp.concatenate([real, imag], axis=1)
    high = product.astype(jnp.bfloat16)
    low = (product - high.astype(jnp.float32)).astype(jnp.bfloat16)
    return dot(jnp.concatenate([high, high, low], axis=1), inverse) * scale


def sum_lines(sums, left):
    total = 0.0
    for _ in range(3):
        part = left.astype(jnp.bfloat16)
        left = left - part.astype(jnp.float32)
        total = total + dot(sums, part)
    return total


def traces_of(cfg, block, first_ref, waves_ref, band_ref):
    codes = read_codes(first_ref[...], block)
    comps, station_dev, samples = waves_ref.shape
    shift, goal, column = block_lines(cfg, codes, comps)
    segment = cut_traces(cfg, shift, goal, waves_ref[...].reshape(comps * station_dev, samples))
    return segment.astype(jnp.bfloat16), levels_scale(cfg, segment, band_ref[...]), line_sums(cfg, column)


def spectrum(narrow, h, forward):
    part = narrow[:, h * LAGS : (h + 2) * LAGS]
    return dot(jnp.concatenate([part, part], axis=1), forward)


def near_kernel(cfg, first_ref, waves_ref, forward_ref, short_ref, inverse_ref, band_ref, sent_ref):
    narrow, scale, sums = traces_of(cfg, 0, first_ref, waves_ref, band_ref)
    forward = forward_ref[...]
    left = match_lines(first_ref[...], lambda h: spectrum(narrow, h, forward), scale, short_ref[...], inverse_ref[...])
    sent_ref[...] = sum_lines(sums, left)


def far_kernel(cfg, first_ref, waves_ref, forward_ref, band_ref, spectra_ref, scale_ref, sums_ref):
    narrow, scale, sums = traces_of(cfg, 1, first_ref, waves_ref, band_ref)
    scale_ref[...] = scale
    sums_ref[...] = sums
    forward = forward_ref[...]
    for h in range(cfg["length"] // LAGS):
        spectra_ref[:, h * 2 * LAGS : (h + 1) * 2 * LAGS] = spectrum(narrow, h, forward)


def match_kernel(shapes_ref, spectra_ref, scale_ref, sums_ref, short_ref, inverse_ref, before_ref, sent_ref):
    groups, tile = sums_ref.shape
    tiles = shapes_ref.shape[0] // tile
    groups = groups // tiles

    def one_tile(step):
        lines = pl.ds(pl.multiple_of(step * tile, tile), tile)
        ends = pl.ds(pl.multiple_of(step * groups, groups), groups)
        left = match_lines(
            shapes_ref[lines, :],
            lambda h: spectra_ref[lines, h * 2 * LAGS : (h + 1) * 2 * LAGS],
            scale_ref[lines, :],
            short_ref[...],
            inverse_ref[...],
        )
        sent_ref[ends, :] = before_ref[ends, :] + sum_lines(sums_ref[ends, :], left)

    if tiles <= 4:
        for step in range(tiles):
            one_tile(step)
    else:
        pl.loop(0, tiles)(one_tile)


def stack_kernel(factor, parts_ref, stacks_ref, top_ref):
    stacks = jnp.sum(parts_ref[...], axis=0) * factor
    stacks_ref[...] = stacks
    top_ref[...] = jnp.broadcast_to(jnp.max(stacks, axis=0, keepdims=True), top_ref.shape)


def body(waveforms, templates, stations, moveouts):
    devices, group, halves = lax.axis_size(AXES), lax.axis_size(GROUP), lax.axis_size(HALF)
    tpl_count, slot_count = stations.shape
    comps, length = templates.shape[2:]
    station_dev, _, samples = waveforms.shape
    seg_len = length + LAGS
    pairs = tpl_count * slot_count
    capacity = (2 * pairs + devices - 1) // devices
    rows = -(-(comps * capacity + 1) // 16) * 16
    cfg = dict(
        devices=devices,
        group=group,
        halves=halves,
        station_dev=station_dev,
        tpl_count=tpl_count,
        capacity=capacity,
        rows=rows,
        length=length,
        seg_len=seg_len,
        shift_bits=bits_of(samples - seg_len + 1),
        row_bits=bits_of(station_dev),
    )
    forward, short, inverse = (jnp.asarray(t) for t in transform_tables(LAGS))
    band = jnp.asarray(band_table(length, LAGS))
    tiles = group // SOURCES
    tile = SOURCES * rows
    lines = group * rows
    sums_tile = SOURCES * tpl_count
    spectrum_len = length // LAGS * 2 * LAGS
    whole = pl.BlockSpec(memory_space=pltpu.VMEM)
    anywhere = pl.BlockSpec(memory_space=pl.ANY)
    params = pltpu.CompilerParams(vmem_limit_bytes=32 * MIB)
    by_slot = templates.transpose(1, 2, 0, 3)
    waves = waveforms.transpose(1, 0, 2)
    half = lax.axis_index(HALF).reshape(1)

    def work(flops, size):
        return pl.CostEstimate(flops=flops, bytes_accessed=size, transcendentals=0)

    def exchange(x, axes):
        return lax.all_to_all(x, axes, split_axis=0, concat_axis=0, tiled=True)

    def pack(block):
        return pl.pallas_call(
            functools.partial(pack_kernel, cfg, block),
            out_shape=jax.ShapeDtypeStruct((lines, length), jnp.bfloat16),
            in_specs=[pl.BlockSpec(memory_space=pltpu.SMEM), whole, whole, anywhere],
            out_specs=anywhere,
            scratch_shapes=[
                pltpu.VMEM(by_slot.shape, jnp.bfloat16),
                pltpu.VMEM((comps, pairs, length), jnp.bfloat16),
                pltpu.VMEM((lines, length), jnp.bfloat16),
                pltpu.SemaphoreType.DMA,
                pltpu.SemaphoreType.DMA((tiles,)),
            ],
            compiler_params=pltpu.CompilerParams(vmem_limit_bytes=60 * MIB),
            cost_estimate=work(2 * lines * pairs * comps * length, 2 * (by_slot.size + lines * length)),
            name="pack",
        )(half, stations, moveouts, by_slot).reshape(group, rows, length)

    def same(shape):
        return pl.BlockSpec(shape, lambda i: (0,) * len(shape))

    def tiled(*shape):
        return pl.BlockSpec(shape, lambda i: (i, 0))

    trace_flops = 2 * lines * (length // LAGS * 8 * LAGS * LAGS + 2 * seg_len * LAGS)
    swapped = lax.ppermute(waves, HALF, [(0, 1), (1, 0)]) if halves == 2 else None
    first = exchange(pack(0), GROUP)
    if halves == 2:
        first, second = lax.optimization_barrier((first, pack(1)))
        second = exchange(second, GROUP).reshape(lines, length)
    first = first.reshape(lines, length)

    sent = pl.pallas_call(
        functools.partial(near_kernel, cfg),
        grid=(tiles,),
        out_shape=jax.ShapeDtypeStruct((group * tpl_count, LAGS), jnp.float32),
        in_specs=[
            tiled(tile, length),
            same(waves.shape),
            same(forward.shape),
            same(short.shape),
            same(inverse.shape),
            same(band.shape),
        ],
        out_specs=tiled(sums_tile, LAGS),
        compiler_params=params,
        cost_estimate=work(trace_flops, lines * length * 2),
        name="near",
    )(first, waves, forward, short, inverse, band)
    if halves == 2:
        kept = pl.pallas_call(
            functools.partial(far_kernel, cfg),
            grid=(tiles,),
            out_shape=[
                jax.ShapeDtypeStruct((lines, spectrum_len), jnp.float32),
                jax.ShapeDtypeStruct((lines, LAGS), jnp.float32),
                jax.ShapeDtypeStruct((group * tpl_count, tile), jnp.bfloat16),
            ],
            in_specs=[tiled(tile, length), same(waves.shape), same(forward.shape), same(band.shape)],
            out_specs=[tiled(tile, spectrum_len), tiled(tile, LAGS), tiled(sums_tile, tile)],
            compiler_params=params,
            cost_estimate=work(trace_flops, lines * spectrum_len * 4),
            name="far",
        )(first, swapped, forward, band)
        operands = (second, *kept, short, inverse, sent)
        sent = pl.pallas_call(
            match_kernel,
            out_shape=jax.ShapeDtypeStruct(sent.shape, jnp.float32),
            in_specs=[whole] * len(operands),
            out_specs=whole,
            compiler_params=params,
            name="match",
        )(*operands)

    parts = exchange(sent.reshape(group, tpl_count, LAGS), GROUP)
    stacks, top = pl.pallas_call(
        functools.partial(stack_kernel, math.sqrt(length / (comps * slot_count))),
        out_shape=[
            jax.ShapeDtypeStruct((tpl_count, LAGS), jnp.float32),
            jax.ShapeDtypeStruct((devices, 1, LAGS), jnp.float32),
        ],
        in_specs=[whole],
        out_specs=[whole, whole],
        compiler_params=pltpu.CompilerParams(vmem_limit_bytes=16 * MIB),
        name="stack",
    )(parts)
    return stacks, jnp.max(exchange(top, AXES), axis=(0, 1))


def solution(mesh):
    slow, fast = (mesh.shape[name] for name in GROUP)
    halves = 2 if slow % 2 == 0 else 1
    split = jax.sharding.Mesh(mesh.devices.reshape(halves, slow // halves, fast), AXES)
    placed = (
        P(AXES, None, None),
        P(AXES, None, None, None),
        P(AXES, None),
        P(AXES, None),
    )
    return jax.shard_map(body, mesh=split, in_specs=placed, out_specs=(P(AXES, None), P()), check_vma=False)
```

```python
import functools
import math

import jax
import jax.numpy as jnp
import ml_dtypes
import numpy as np
from jax import lax
from jax.experimental import pallas as pl
from jax.experimental.pallas import tpu as pltpu
from jax.sharding import PartitionSpec as P

LAGS = 256
HALF = "half"
GROUP = ("tmpl", "sta")
AXES = (HALF,) + GROUP
SOURCES = 8
LANES = 128
MIB = 1024 * 1024


def bits_of(limit):
    return max(1, (limit - 1).bit_length())


def split_table(table):
    high = table.astype(ml_dtypes.bfloat16)
    low = (table - high.astype(np.float64)).astype(ml_dtypes.bfloat16)
    return np.concatenate([high, low], axis=0)


def transform_tables(piece):
    size = 2 * piece
    angle = 2.0 * np.pi * (np.arange(piece) + 0.5) / size
    phase = np.arange(size)[:, None] * angle[None, :]
    forward = np.concatenate([np.cos(phase), -np.sin(phase)], axis=1)
    short = split_table(forward[:piece])
    back = angle[:, None] * np.arange(piece)[None, :]
    inverse = np.concatenate([np.cos(back), -np.sin(back)], axis=0) * (2.0 / size)
    inverse = split_table(inverse)
    return split_table(forward), short, np.concatenate([inverse, inverse[:size]], axis=0)


def band_table(length, lag_count):
    sample = np.arange(length + lag_count)[:, None]
    lag = np.arange(lag_count)[None, :]
    return ((sample >= lag) & (sample < lag + length)).astype(ml_dtypes.bfloat16)


def iota(shape, axis):
    return lax.broadcasted_iota(jnp.int32, shape, axis)


def dot(a, b):
    return jnp.dot(a, b, preferred_element_type=jnp.float32)


def exact_dot(a, b):
    return jnp.dot(a, b, precision=lax.Precision.HIGHEST, preferred_element_type=jnp.float32)


def entry_lanes(tpl_count, slot_count):
    pairs = tpl_count * slot_count
    first = iota((slot_count, pairs), 0) * tpl_count
    entry = iota((slot_count, pairs), 1)
    spread = jnp.where((entry >= first) & (entry < first + tpl_count), 1.0, 0.0)
    start = jnp.sum(spread * first.astype(jnp.float32), axis=0, keepdims=True)
    return spread, iota((1, pairs), 1).astype(jnp.float32) - start


def as_lanes(values, spread, place, tpl_count):
    owners = values.shape[0] // tpl_count
    pairs = spread.shape[1]
    wide = exact_dot(values.astype(jnp.float32), spread).reshape(owners, tpl_count, pairs)
    own = iota((1, tpl_count, pairs), 1).astype(jnp.float32) == place.reshape(1, 1, pairs)
    return jnp.sum(jnp.where(own, wide, 0.0), axis=1)


def count_before(hits):
    pairs = hits.shape[1]
    earlier = jnp.where(iota((pairs, pairs), 0) < iota((pairs, pairs), 1), 1.0, 0.0)
    return dot(hits.astype(jnp.bfloat16), earlier.astype(jnp.bfloat16))


def list_kernel(cfg, half_ref, stations_ref, moveouts_ref, codes_ref, goal_ref):
    tpl_count, slot_count = stations_ref.shape
    pairs = tpl_count * slot_count
    devices, group, halves = cfg["devices"], cfg["group"], cfg["halves"]
    station_dev, rows, capacity = cfg["station_dev"], cfg["rows"], cfg["capacity"]
    spread, place = entry_lanes(tpl_count, slot_count)
    station = as_lanes(stations_ref[...], spread, place, tpl_count)
    shift = as_lanes(moveouts_ref[...], spread, place, tpl_count)
    device = jnp.floor((station + 0.5) * (1.0 / station_dev))
    onehot = jnp.where(iota((devices, pairs), 0).astype(jnp.float32) == device, 1.0, 0.0)
    rank = jnp.sum(onehot * count_before(onehot), axis=0, keepdims=True)
    half = jnp.floor((device + 0.5) * (1.0 / group))
    away = jnp.where(half == half_ref[0].astype(jnp.float32), 0.0, 1.0)
    place_of = (device - half * group) * halves + away
    goal_ref[...] = jnp.where(rank < float(capacity), place_of * rows + rank, -float(group * halves * rows))

    row = station - device * station_dev
    code = ((place + 1.0) * (1 << cfg["row_bits"]) + row) * (1 << cfg["shift_bits"]) + shift
    marked = jnp.where(iota((group * halves, pairs), 0).astype(jnp.float32) == place_of, code, 0.0)
    at_rank = jnp.where(iota((LANES, pairs), 0).astype(jnp.float32) == rank, 1.0, 0.0)
    codes = lax.dot_general(
        marked,
        at_rank,
        (((1,), (1,)), ((), ())),
        precision=lax.Precision.HIGHEST,
        preferred_element_type=jnp.float32,
    )
    codes_ref[...] = codes.astype(jnp.int32)


def pack_kernel(cfg, goal_ref, templates_hbm, packed_hbm, raw_ref, shapes_ref, packed_ref, in_sem, out_sems):
    load = pltpu.make_async_copy(templates_hbm, raw_ref, in_sem)
    load.start()
    goal = goal_ref[...]
    pairs = goal.shape[1]
    comps, length = raw_ref.shape[1], raw_ref.shape[3]
    load.wait()
    for c in range(comps):
        values = raw_ref[:, c].astype(jnp.float32).reshape(pairs, length)
        centred = values - jnp.mean(values, axis=-1, keepdims=True)
        spread_c = jnp.sqrt(jnp.mean(centred * centred, axis=-1, keepdims=True) + 1e-05)
        shapes_ref[c] = (centred * (1.0 / spread_c)).astype(jnp.bfloat16)

    tiles = out_sems.shape[0]
    tile = packed_ref.shape[0] // tiles
    copies = []
    for step in range(tiles):
        line = iota((tile, pairs), 0).astype(jnp.float32) + float(step * tile)
        total = jnp.zeros((tile, length), jnp.float32)
        for c in range(comps):
            pick = jnp.where(line == goal + float(c * cfg["capacity"]), 1.0, 0.0).astype(jnp.bfloat16)
            total = total + dot(pick, shapes_ref[c])
        part = pl.ds(step * tile, tile)
        packed_ref[part, :] = total.astype(jnp.bfloat16)
        copies.append(pltpu.make_async_copy(packed_ref.at[part], packed_hbm.at[part], out_sems.at[step]))
        copies[-1].start()
    for copy in copies:
        copy.wait()


def block_lines(cfg, block, codes):
    capacity, rows, comps, halves = cfg["capacity"], cfg["rows"], cfg["comps"], cfg["halves"]
    codes = codes.reshape(SOURCES, halves, LANES)
    codes = jnp.sum(jnp.where(iota((1, halves, 1), 1) == block, codes, 0), axis=1).astype(jnp.float32)
    tile = SOURCES * rows
    line = iota((SOURCES, rows, 1), 1).reshape(tile, 1)
    owner = iota((SOURCES, rows, 1), 0).reshape(tile, 1)
    comp = jnp.zeros((tile, 1), jnp.int32)
    for c in range(1, comps + 1):
        comp = comp + jnp.where(line >= c * capacity, 1, 0)
    slot = line - comp * capacity
    repeated = jnp.broadcast_to(codes.reshape(SOURCES, 1, LANES), (SOURCES, rows, LANES)).reshape(tile, LANES)
    chosen = (iota((tile, LANES), 1) == slot) & (comp < comps)
    code = jnp.sum(jnp.where(chosen, repeated, 0.0), axis=1, keepdims=True).astype(jnp.int32)
    shift_bits, row_bits = cfg["shift_bits"], cfg["row_bits"]
    shift = code & ((1 << shift_bits) - 1)
    row = lax.shift_right_logical(code, shift_bits) & ((1 << row_bits) - 1)
    tpl = lax.shift_right_logical(code, shift_bits + row_bits) - 1
    goal = jnp.where(tpl >= 0, comp * cfg["station_dev"] + row, -1)
    return shift, goal, jnp.where(tpl >= 0, owner * cfg["tpl_count"] + tpl, -1)


def cut_traces(cfg, shift, goal, waves):
    tile, seg_len, shift_bits = shift.shape[0], cfg["seg_len"], cfg["shift_bits"]
    pick = jnp.where(iota((tile, waves.shape[0]), 1) == goal, 1.0, 0.0).astype(jnp.bfloat16)
    x = dot(pick, waves)

    for bit in range(shift_bits - 1, 6, -1):
        step = 1 << bit
        width = seg_len + step
        if x.shape[1] < width + step:
            x = jnp.concatenate([x, jnp.zeros((tile, width + step - x.shape[1]), jnp.float32)], axis=1)
        x = jnp.where((shift & step) != 0, x[:, step : step + width], x[:, :width])
    for bit in range(min(shift_bits, 7) - 1, -1, -1):
        step = 1 << bit
        x = jnp.where((shift & step) != 0, pltpu.roll(x, x.shape[1] - step, 1), x)
    return x[:, :seg_len]


def line_sums(cfg, column):
    groups = SOURCES * cfg["tpl_count"]
    return jnp.where(iota((column.shape[0], groups), 1) == column, 1.0, 0.0).T.astype(jnp.bfloat16)


def levels_scale(cfg, segment, band):
    length = cfg["length"]
    power = segment * segment
    high = power.astype(jnp.bfloat16)
    low = (power - high.astype(jnp.float32)).astype(jnp.bfloat16)
    energy = dot(high, band) + dot(low, band)
    return 1.0 / (length * jnp.sqrt(energy * (1.0 / length) + 1e-05))


def match_lines(shapes, spectrum_of, scale, forward, inverse):
    real = imag = 0.0
    for h in range(shapes.shape[1] // LAGS):
        part = shapes[:, h * LAGS : (h + 1) * LAGS]
        mine = dot(jnp.concatenate([part, part], axis=1), forward)
        theirs = spectrum_of(h)
        mine_r, mine_i = mine[:, :LAGS], mine[:, LAGS:]
        theirs_r, theirs_i = theirs[:, :LAGS], theirs[:, LAGS:]
        real = real + (theirs_r * mine_r + theirs_i * mine_i)
        imag = imag + (theirs_i * mine_r - theirs_r * mine_i)
    product = jnp.concatenate([real, imag], axis=1)
    high = product.astype(jnp.bfloat16)
    low = (product - high.astype(jnp.float32)).astype(jnp.bfloat16)
    return dot(jnp.concatenate([high, high, low], axis=1), inverse) * scale


def sum_lines(sums, left):
    total = 0.0
    for _ in range(3):
        part = left.astype(jnp.bfloat16)
        left = left - part.astype(jnp.float32)
        total = total + dot(sums, part)
    return total


def spectrum(narrow, h, forward):
    part = narrow[:, h * LAGS : (h + 2) * LAGS]
    return dot(jnp.concatenate([part, part], axis=1), forward)


def trace_kernel(cfg, block, codes_ref, waves_ref, forward_ref, band_ref, spectra_ref, scale_ref):
    comps, station_dev, samples = waves_ref.shape
    shift, goal, _ = block_lines(cfg, block, codes_ref[...])
    segment = cut_traces(cfg, shift, goal, waves_ref[...].reshape(comps * station_dev, samples))
    scale_ref[...] = levels_scale(cfg, segment, band_ref[...])
    narrow = segment.astype(jnp.bfloat16)
    forward = forward_ref[...]
    for h in range(cfg["length"] // LAGS):
        spectra_ref[:, h * 2 * LAGS : (h + 1) * 2 * LAGS] = spectrum(narrow, h, forward)


def sums_kernel(cfg, codes_ref, scale_hbm, sums_ref):
    step = SOURCES * cfg["halves"]
    for t in range(sums_ref.shape[0]):
        for block in range(cfg["halves"]):
            column = block_lines(cfg, block, codes_ref[t * step : (t + 1) * step, :])[2]
            sums_ref[t, block] = line_sums(cfg, column)


def match_kernel(cfg, shapes_ref, sums_ref, short_ref, inverse_ref, *rest):
    spectra_refs, scale_refs, sent_ref = rest[0:-1:2], rest[1:-1:2], rest[-1]
    tile, length = SOURCES * cfg["rows"], cfg["length"]
    groups = SOURCES * cfg["tpl_count"]

    def one_tile(step):
        lines = pl.ds(pl.multiple_of(step * tile, tile), tile)
        total = 0.0
        for block, (spectra_ref, scale_ref) in enumerate(zip(spectra_refs, scale_refs)):
            shapes = shapes_ref[pl.ds(step * SOURCES, SOURCES), block].reshape(tile, length)
            left = match_lines(
                shapes,
                lambda h: spectra_ref[lines, h * 2 * LAGS : (h + 1) * 2 * LAGS],
                scale_ref[lines, :],
                short_ref[...],
                inverse_ref[...],
            )
            total = total + sum_lines(sums_ref[step, block], left)
        sent_ref[pl.ds(pl.multiple_of(step * groups, groups), groups), :] = total

    tiles = sums_ref.shape[0]
    if tiles <= 4:
        for step in range(tiles):
            one_tile(step)
    else:
        pl.loop(0, tiles)(one_tile)


def stack_kernel(factor, parts_ref, stacks_ref, top_ref):
    stacks = jnp.sum(parts_ref[...], axis=0) * factor
    stacks_ref[...] = stacks
    top_ref[...] = jnp.broadcast_to(jnp.max(stacks, axis=0, keepdims=True), top_ref.shape)


def body(waveforms, templates, stations, moveouts):
    devices, group, halves = lax.axis_size(AXES), lax.axis_size(GROUP), lax.axis_size(HALF)
    tpl_count, slot_count = stations.shape
    comps, length = templates.shape[2:]
    station_dev, _, samples = waveforms.shape
    seg_len = length + LAGS
    pairs = tpl_count * slot_count
    capacity = (2 * pairs + devices - 1) // devices
    rows = -(-comps * capacity // 16) * 16
    cfg = dict(
        devices=devices,
        group=group,
        halves=halves,
        station_dev=station_dev,
        tpl_count=tpl_count,
        comps=comps,
        capacity=capacity,
        rows=rows,
        length=length,
        seg_len=seg_len,
        shift_bits=bits_of(samples - seg_len + 1),
        row_bits=bits_of(station_dev),
    )
    forward, short, inverse = (jnp.asarray(t) for t in transform_tables(LAGS))
    band = jnp.asarray(band_table(length, LAGS))
    tiles = group // SOURCES
    tile = SOURCES * rows
    lines = group * rows
    sums_tile = SOURCES * tpl_count
    spectrum_len = length // LAGS * 2 * LAGS
    whole = pl.BlockSpec(memory_space=pltpu.VMEM)
    anywhere = pl.BlockSpec(memory_space=pl.ANY)
    params = pltpu.CompilerParams(vmem_limit_bytes=32 * MIB)
    by_slot = templates.transpose(1, 2, 0, 3)
    waves = waveforms.transpose(1, 0, 2)
    half = lax.axis_index(HALF).reshape(1)

    def work(flops, size):
        return pl.CostEstimate(flops=flops, bytes_accessed=size, transcendentals=0)

    def exchange(x, axes):
        return lax.all_to_all(x, axes, split_axis=0, concat_axis=0, tiled=True)

    def same(shape):
        return pl.BlockSpec(shape, lambda i: (0,) * len(shape))

    def tiled(*shape):
        return pl.BlockSpec(shape, lambda i: (i, 0))

    swapped = lax.ppermute(waves, HALF, [(0, 1), (1, 0)]) if halves == 2 else None
    codes, goal = pl.pallas_call(
        functools.partial(list_kernel, cfg),
        out_shape=[
            jax.ShapeDtypeStruct((group * halves, LANES), jnp.int32),
            jax.ShapeDtypeStruct((1, pairs), jnp.float32),
        ],
        in_specs=[pl.BlockSpec(memory_space=pltpu.SMEM), whole, whole],
        out_specs=[whole, whole],
        compiler_params=pltpu.CompilerParams(vmem_limit_bytes=60 * MIB),
        name="lists",
    )(half, stations, moveouts)
    codes = exchange(codes.reshape(group, halves, LANES), GROUP).reshape(group * halves, LANES)

    pack_tiles = 4
    packed = pl.pallas_call(
        functools.partial(pack_kernel, cfg),
        out_shape=jax.ShapeDtypeStruct((halves * lines, length), jnp.bfloat16),
        in_specs=[whole, anywhere],
        out_specs=anywhere,
        scratch_shapes=[
            pltpu.VMEM(by_slot.shape, jnp.bfloat16),
            pltpu.VMEM((comps, pairs, length), jnp.bfloat16),
            pltpu.VMEM((halves * lines, length), jnp.bfloat16),
            pltpu.SemaphoreType.DMA,
            pltpu.SemaphoreType.DMA((pack_tiles,)),
        ],
        compiler_params=pltpu.CompilerParams(vmem_limit_bytes=60 * MIB),
        cost_estimate=work(2 * halves * lines * pairs * comps * length, 2 * (by_slot.size + lines * length)),
        name="pack",
    )(goal, by_slot)
    codes, packed = lax.optimization_barrier((codes, packed))
    arrived = exchange(packed.reshape(group, halves * rows, length), GROUP).reshape(group, halves, rows, length)

    kept = []
    for block, traces in enumerate([waves, swapped][:halves]):
        kept += pl.pallas_call(
            functools.partial(trace_kernel, cfg, block),
            grid=(tiles,),
            out_shape=[
                jax.ShapeDtypeStruct((lines, spectrum_len), jnp.float32),
                jax.ShapeDtypeStruct((lines, LAGS), jnp.float32),
            ],
            in_specs=[tiled(SOURCES * halves, LANES), same(waves.shape), same(forward.shape), same(band.shape)],
            out_specs=[tiled(tile, spectrum_len), tiled(tile, LAGS)],
            compiler_params=params,
            cost_estimate=work(1, 1),
            name="traces",
        )(codes, traces, forward, band)
    sums = pl.pallas_call(
        functools.partial(sums_kernel, cfg),
        out_shape=jax.ShapeDtypeStruct((tiles, halves, sums_tile, tile), jnp.bfloat16),
        in_specs=[whole, anywhere],
        out_specs=whole,
        compiler_params=params,
        cost_estimate=work(1, 1),
        name="sums",
    )(codes, kept[-1])
    operands = (arrived, sums, short, inverse, *kept)
    sent = pl.pallas_call(
        functools.partial(match_kernel, cfg),
        out_shape=jax.ShapeDtypeStruct((group * tpl_count, LAGS), jnp.float32),
        in_specs=[whole] * len(operands),
        out_specs=whole,
        compiler_params=params,
        name="match",
    )(*operands)

    parts = exchange(sent.reshape(group, tpl_count, LAGS), GROUP)
    stacks, top = pl.pallas_call(
        functools.partial(stack_kernel, math.sqrt(length / (comps * slot_count))),
        out_shape=[
            jax.ShapeDtypeStruct((tpl_count, LAGS), jnp.float32),
            jax.ShapeDtypeStruct((devices, 1, LAGS), jnp.float32),
        ],
        in_specs=[whole],
        out_specs=[whole, whole],
        compiler_params=pltpu.CompilerParams(vmem_limit_bytes=16 * MIB),
        name="stack",
    )(parts)
    return stacks, jnp.max(exchange(top, AXES), axis=(0, 1))


def solution(mesh):
    slow, fast = (mesh.shape[name] for name in GROUP)
    halves = 2 if slow % 2 == 0 else 1
    split = jax.sharding.Mesh(mesh.devices.reshape(halves, slow // halves, fast), AXES)
    placed = (
        P(AXES, None, None),
        P(AXES, None, None, None),
        P(AXES, None),
        P(AXES, None),
    )
    return jax.shard_map(body, mesh=split, in_specs=placed, out_specs=(P(AXES, None), P()), check_vma=False)
```

```python
import functools
import math

import jax
import jax.numpy as jnp
import ml_dtypes
import numpy as np
from jax import lax
from jax.experimental import pallas as pl
from jax.experimental.pallas import tpu as pltpu
from jax.sharding import PartitionSpec as P

LAGS = 256
HALF = "half"
GROUP = ("tmpl", "sta")
AXES = (HALF,) + GROUP
SOURCES = 4
LANES = 128
MIB = 1024 * 1024


def bits_of(limit):
    return max(1, (limit - 1).bit_length())


def split_table(table):
    high = table.astype(ml_dtypes.bfloat16)
    low = (table - high.astype(np.float64)).astype(ml_dtypes.bfloat16)
    return np.concatenate([high, low], axis=0)


def transform_tables(piece):
    size = 2 * piece
    angle = 2.0 * np.pi * (np.arange(piece) + 0.5) / size
    phase = np.arange(size)[:, None] * angle[None, :]
    forward = np.concatenate([np.cos(phase), -np.sin(phase)], axis=1)
    short = split_table(forward[:piece])
    back = angle[:, None] * np.arange(piece)[None, :]
    inverse = np.concatenate([np.cos(back), -np.sin(back)], axis=0) * (2.0 / size)
    inverse = split_table(inverse)
    return split_table(forward), short, np.concatenate([inverse, inverse[:size]], axis=0)


def band_table(length, lag_count):
    sample = np.arange(length + lag_count)[:, None]
    lag = np.arange(lag_count)[None, :]
    return ((sample >= lag) & (sample < lag + length)).astype(ml_dtypes.bfloat16)


def iota(shape, axis):
    return lax.broadcasted_iota(jnp.int32, shape, axis)


def dot(a, b):
    return jnp.dot(a, b, preferred_element_type=jnp.float32)


def exact_dot(a, b):
    return jnp.dot(a, b, precision=lax.Precision.HIGHEST, preferred_element_type=jnp.float32)


def entry_lanes(tpl_count, slot_count):
    pairs = tpl_count * slot_count
    first = iota((slot_count, pairs), 0) * tpl_count
    entry = iota((slot_count, pairs), 1)
    spread = jnp.where((entry >= first) & (entry < first + tpl_count), 1.0, 0.0)
    start = jnp.sum(spread * first.astype(jnp.float32), axis=0, keepdims=True)
    return spread, iota((1, pairs), 1).astype(jnp.float32) - start


def as_lanes(values, spread, place, tpl_count):
    owners = values.shape[0] // tpl_count
    pairs = spread.shape[1]
    wide = exact_dot(values.astype(jnp.float32), spread).reshape(owners, tpl_count, pairs)
    own = iota((1, tpl_count, pairs), 1).astype(jnp.float32) == place.reshape(1, 1, pairs)
    return jnp.sum(jnp.where(own, wide, 0.0), axis=1)


def count_before(hits):
    pairs = hits.shape[1]
    earlier = jnp.where(iota((pairs, pairs), 0) < iota((pairs, pairs), 1), 1.0, 0.0)
    return dot(hits.astype(jnp.bfloat16), earlier.astype(jnp.bfloat16))


def list_kernel(cfg, half_ref, stations_ref, moveouts_ref, codes_ref, goal_ref):
    tpl_count, slot_count = stations_ref.shape
    pairs = tpl_count * slot_count
    devices, group, halves = cfg["devices"], cfg["group"], cfg["halves"]
    station_dev, rows, capacity = cfg["station_dev"], cfg["rows"], cfg["capacity"]
    spread, place = entry_lanes(tpl_count, slot_count)
    station = as_lanes(stations_ref[...], spread, place, tpl_count)
    shift = as_lanes(moveouts_ref[...], spread, place, tpl_count)
    device = jnp.floor((station + 0.5) * (1.0 / station_dev))
    onehot = jnp.where(iota((devices, pairs), 0).astype(jnp.float32) == device, 1.0, 0.0)
    rank = jnp.sum(onehot * count_before(onehot), axis=0, keepdims=True)
    half = jnp.floor((device + 0.5) * (1.0 / group))
    away = jnp.where(half == half_ref[0].astype(jnp.float32), 0.0, 1.0)
    place_of = (device - half * group) * halves + away
    goal_ref[...] = jnp.where(rank < float(capacity), place_of * rows + rank, -float(group * halves * rows))

    row = station - device * station_dev
    code = ((place + 1.0) * (1 << cfg["row_bits"]) + row) * (1 << cfg["shift_bits"]) + shift
    marked = jnp.where(iota((group * halves, pairs), 0).astype(jnp.float32) == place_of, code, 0.0)
    at_rank = jnp.where(iota((LANES, pairs), 0).astype(jnp.float32) == rank, 1.0, 0.0)
    codes = lax.dot_general(
        marked,
        at_rank,
        (((1,), (1,)), ((), ())),
        precision=lax.Precision.HIGHEST,
        preferred_element_type=jnp.float32,
    )
    codes_ref[...] = codes.astype(jnp.int32)


def pack_kernel(cfg, goal_ref, templates_hbm, packed_hbm, raw_ref, shapes_ref, packed_ref, in_sem, out_sems):
    load = pltpu.make_async_copy(templates_hbm, raw_ref, in_sem)
    load.start()
    goal = goal_ref[...]
    pairs = goal.shape[1]
    comps, length = raw_ref.shape[1], raw_ref.shape[3]
    load.wait()
    for c in range(comps):
        values = raw_ref[:, c].astype(jnp.float32).reshape(pairs, length)
        centred = values - jnp.mean(values, axis=-1, keepdims=True)
        spread_c = jnp.sqrt(jnp.mean(centred * centred, axis=-1, keepdims=True) + 1e-05)
        shapes_ref[c] = (centred * (1.0 / spread_c)).astype(jnp.bfloat16)

    tiles = out_sems.shape[0]
    tile = packed_ref.shape[0] // tiles
    copies = []
    for step in range(tiles):
        line = iota((tile, pairs), 0).astype(jnp.float32) + float(step * tile)
        total = jnp.zeros((tile, length), jnp.float32)
        for c in range(comps):
            pick = jnp.where(line == goal + float(c * cfg["capacity"]), 1.0, 0.0).astype(jnp.bfloat16)
            total = total + dot(pick, shapes_ref[c])
        part = pl.ds(step * tile, tile)
        packed_ref[part, :] = total.astype(jnp.bfloat16)
        copies.append(pltpu.make_async_copy(packed_ref.at[part], packed_hbm.at[part], out_sems.at[step]))
        copies[-1].start()
    for copy in copies:
        copy.wait()


def tile_lines(cfg, codes):
    capacity, rows, comps, halves = cfg["capacity"], cfg["rows"], cfg["comps"], cfg["halves"]
    blocks = SOURCES * halves
    tile = blocks * rows
    line = iota((blocks, rows, 1), 1).reshape(tile, 1)
    block = iota((blocks, rows, 1), 0).reshape(tile, 1)
    comp = jnp.zeros((tile, 1), jnp.int32)
    for c in range(1, comps + 1):
        comp = comp + jnp.where(line >= c * capacity, 1, 0)
    slot = line - comp * capacity
    owner = jnp.zeros((tile, 1), jnp.int32)
    for k in range(1, SOURCES):
        owner = owner + jnp.where(block >= k * halves, 1, 0)
    repeated = codes.astype(jnp.float32).reshape(blocks, 1, LANES)
    repeated = jnp.broadcast_to(repeated, (blocks, rows, LANES)).reshape(tile, LANES)
    chosen = (iota((tile, LANES), 1) == slot) & (comp < comps)
    code = jnp.sum(jnp.where(chosen, repeated, 0.0), axis=1, keepdims=True).astype(jnp.int32)
    shift_bits, row_bits = cfg["shift_bits"], cfg["row_bits"]
    shift = code & ((1 << shift_bits) - 1)
    row = lax.shift_right_logical(code, shift_bits) & ((1 << row_bits) - 1)
    tpl = lax.shift_right_logical(code, shift_bits + row_bits) - 1
    goal = ((block - owner * halves) * comps + comp) * cfg["station_dev"] + row
    return shift, jnp.where(tpl >= 0, goal, -1), jnp.where(tpl >= 0, owner * cfg["tpl_count"] + tpl, -1)


def cut_traces(cfg, shift, goal, waves):
    tile, seg_len, shift_bits = shift.shape[0], cfg["seg_len"], cfg["shift_bits"]
    pick = jnp.where(iota((tile, waves.shape[0]), 1) == goal, 1.0, 0.0).astype(jnp.bfloat16)
    x = dot(pick, waves)

    for bit in range(shift_bits - 1, 6, -1):
        step = 1 << bit
        width = seg_len + step
        if x.shape[1] < width + step:
            x = jnp.concatenate([x, jnp.zeros((tile, width + step - x.shape[1]), jnp.float32)], axis=1)
        x = jnp.where((shift & step) != 0, x[:, step : step + width], x[:, :width])
    for bit in range(min(shift_bits, 7) - 1, -1, -1):
        step = 1 << bit
        x = jnp.where((shift & step) != 0, pltpu.roll(x, x.shape[1] - step, 1), x)
    return x[:, :seg_len]


def line_sums(cfg, column):
    groups = SOURCES * cfg["tpl_count"]
    return jnp.where(iota((column.shape[0], groups), 1) == column, 1.0, 0.0).T.astype(jnp.bfloat16)


def levels_scale(cfg, segment, band):
    length = cfg["length"]
    power = segment * segment
    high = power.astype(jnp.bfloat16)
    low = (power - high.astype(jnp.float32)).astype(jnp.bfloat16)
    energy = dot(high, band) + dot(low, band)
    return 1.0 / (length * jnp.sqrt(energy * (1.0 / length) + 1e-05))


def match_lines(shapes, spectrum_of, forward, rest):
    real = imag = 0.0
    for h in range(shapes.shape[1] // LAGS):
        part = shapes[:, h * LAGS : (h + 1) * LAGS]
        mine = dot(jnp.concatenate([part, part], axis=1), forward)
        theirs = spectrum_of(h)
        mine_r, mine_i = mine[:, :LAGS], mine[:, LAGS:]
        theirs_r, theirs_i = theirs[:, :LAGS], theirs[:, LAGS:]
        real = real + (theirs_r * mine_r + theirs_i * mine_i)
        imag = imag + (theirs_i * mine_r - theirs_r * mine_i)
    product = jnp.concatenate([real, imag], axis=1)
    high = product.astype(jnp.bfloat16)
    low = (product - high.astype(jnp.float32)).astype(jnp.bfloat16)
    inverse, scale = rest()
    return dot(jnp.concatenate([high, high, low], axis=1), inverse) * scale


def sum_lines(sums, left):
    total = 0.0
    for _ in range(3):
        part = left.astype(jnp.bfloat16)
        left = left - part.astype(jnp.float32)
        total = total + dot(sums, part)
    return total


def spectrum(narrow, h, forward):
    part = narrow[:, h * LAGS : (h + 2) * LAGS]
    return dot(jnp.concatenate([part, part], axis=1), forward)


def trace_kernel(cfg, codes_ref, *refs):
    waves_refs, (forward_ref, band_ref, spectra_ref, scale_ref, sums_ref) = refs[:-5], refs[-5:]
    shift, goal, column = tile_lines(cfg, codes_ref[...])
    waves = [ref[...].reshape(-1, ref.shape[2]) for ref in waves_refs]
    segment = cut_traces(cfg, shift, goal, jnp.concatenate(waves, axis=0))
    scale_ref[...] = levels_scale(cfg, segment, band_ref[...])
    sums_ref[...] = line_sums(cfg, column)
    narrow = segment.astype(jnp.bfloat16)
    forward = forward_ref[...]
    for h in range(cfg["length"] // LAGS):
        spectra_ref[:, h * 2 * LAGS : (h + 1) * 2 * LAGS] = spectrum(narrow, h, forward)


def match_kernel(shapes_hbm, spectra_hbm, scale_hbm, sums_hbm, short_hbm, inverse_hbm, sent_hbm, *scratch):
    shapes_ref, spectra_ref, scale_ref, sums_ref, short_ref, inverse_ref, sent_ref, sems, out_sems = scratch
    tiles = out_sems.shape[0]
    tile = shapes_ref.shape[0] // tiles
    groups = sent_ref.shape[0] // tiles
    pieces = shapes_ref.shape[1] // LAGS
    width = 2 * LAGS
    used = []

    def fetch(source, buffer):
        copy = pltpu.make_async_copy(source, buffer, sems.at[len(used)])
        copy.start()
        used.append(copy)
        return copy

    short = fetch(short_hbm, short_ref)
    inverse = None
    loads = []
    for t in range(tiles):
        lines, ends = pl.ds(t * tile, tile), pl.ds(t * groups, groups)
        load = [fetch(shapes_hbm.at[lines], shapes_ref.at[lines])]
        for h in range(pieces):
            part = pl.ds(h * width, width)
            load.append(fetch(spectra_hbm.at[lines, part], spectra_ref.at[lines, part]))
        inverse = inverse or fetch(inverse_hbm, inverse_ref)
        load.append(fetch(scale_hbm.at[lines], scale_ref.at[lines]))
        load.append(fetch(sums_hbm.at[ends], sums_ref.at[ends]))
        loads.append(load)
    short.wait()
    sends = []
    for t, load in enumerate(loads):
        lines, ends = pl.ds(t * tile, tile), pl.ds(t * groups, groups)
        load[0].wait()

        def piece(h):
            load[1 + h].wait()
            return spectra_ref[lines, h * width : (h + 1) * width]

        def rest():
            if t == 0:
                inverse.wait()
            for copy in load[-2:]:
                copy.wait()
            return inverse_ref[...], scale_ref[lines, :]

        left = match_lines(shapes_ref[lines, :], piece, short_ref[...], rest)
        sent_ref[ends, :] = sum_lines(sums_ref[ends, :], left)
        sends.append(pltpu.make_async_copy(sent_ref.at[ends], sent_hbm.at[ends], out_sems.at[t]))
        sends[-1].start()
    for copy in sends:
        copy.wait()


def stack_kernel(factor, parts_ref, stacks_ref, top_ref):
    stacks = jnp.sum(parts_ref[...], axis=0) * factor
    stacks_ref[...] = stacks
    top_ref[...] = jnp.broadcast_to(jnp.max(stacks, axis=0, keepdims=True), top_ref.shape)


def body(waveforms, templates, stations, moveouts):
    devices, group, halves = lax.axis_size(AXES), lax.axis_size(GROUP), lax.axis_size(HALF)
    tpl_count, slot_count = stations.shape
    comps, length = templates.shape[2:]
    station_dev, _, samples = waveforms.shape
    seg_len = length + LAGS
    pairs = tpl_count * slot_count
    capacity = (2 * pairs + devices - 1) // devices
    rows = -(-comps * capacity // 16) * 16
    cfg = dict(
        devices=devices,
        group=group,
        halves=halves,
        station_dev=station_dev,
        tpl_count=tpl_count,
        comps=comps,
        capacity=capacity,
        rows=rows,
        length=length,
        seg_len=seg_len,
        shift_bits=bits_of(samples - seg_len + 1),
        row_bits=bits_of(station_dev),
    )
    forward, short, inverse = (jnp.asarray(t) for t in transform_tables(LAGS))
    band = jnp.asarray(band_table(length, LAGS))
    tiles = group // SOURCES
    tile = SOURCES * halves * rows
    lines = group * halves * rows
    sums_tile = SOURCES * tpl_count
    spectrum_len = length // LAGS * 2 * LAGS
    whole = pl.BlockSpec(memory_space=pltpu.VMEM)
    anywhere = pl.BlockSpec(memory_space=pl.ANY)
    params = pltpu.CompilerParams(vmem_limit_bytes=60 * MIB)
    by_slot = templates.transpose(1, 2, 0, 3)
    waves = waveforms.transpose(1, 0, 2)
    half = lax.axis_index(HALF).reshape(1)

    def work(flops, size):
        return pl.CostEstimate(flops=flops, bytes_accessed=size, transcendentals=0)

    def exchange(x, axes):
        return lax.all_to_all(x, axes, split_axis=0, concat_axis=0, tiled=True)

    def same(shape):
        return pl.BlockSpec(shape, lambda i: (0,) * len(shape))

    def tiled(*shape):
        return pl.BlockSpec(shape, lambda i: (i, 0))

    traces = [waves] + [lax.ppermute(waves, HALF, [(0, 1), (1, 0)])] * (halves - 1)
    codes, goal = pl.pallas_call(
        functools.partial(list_kernel, cfg),
        out_shape=[
            jax.ShapeDtypeStruct((group * halves, LANES), jnp.int32),
            jax.ShapeDtypeStruct((1, pairs), jnp.float32),
        ],
        in_specs=[pl.BlockSpec(memory_space=pltpu.SMEM), whole, whole],
        out_specs=[whole, whole],
        compiler_params=params,
        cost_estimate=work(1, 1),
        name="lists",
    )(half, stations, moveouts)
    codes = exchange(codes.reshape(group, halves, LANES), GROUP).reshape(group * halves, LANES)

    pack_tiles = 4
    packed = pl.pallas_call(
        functools.partial(pack_kernel, cfg),
        out_shape=jax.ShapeDtypeStruct((lines, length), jnp.bfloat16),
        in_specs=[whole, anywhere],
        out_specs=anywhere,
        scratch_shapes=[
            pltpu.VMEM(by_slot.shape, jnp.bfloat16),
            pltpu.VMEM((comps, pairs, length), jnp.bfloat16),
            pltpu.VMEM((lines, length), jnp.bfloat16),
            pltpu.SemaphoreType.DMA,
            pltpu.SemaphoreType.DMA((pack_tiles,)),
        ],
        compiler_params=params,
        cost_estimate=work(1, 1),
        name="pack",
    )(goal, by_slot)
    codes, packed = lax.optimization_barrier((codes, packed))
    arrived = exchange(packed.reshape(group, halves * rows, length), GROUP).reshape(lines, length)

    kept = pl.pallas_call(
        functools.partial(trace_kernel, cfg),
        grid=(tiles,),
        out_shape=[
            jax.ShapeDtypeStruct((lines, spectrum_len), jnp.float32),
            jax.ShapeDtypeStruct((lines, LAGS), jnp.float32),
            jax.ShapeDtypeStruct((group * tpl_count, tile), jnp.bfloat16),
        ],
        in_specs=[tiled(SOURCES * halves, LANES)]
        + [same(waves.shape)] * halves
        + [same(forward.shape), same(band.shape)],
        out_specs=[tiled(tile, spectrum_len), tiled(tile, LAGS), tiled(sums_tile, tile)],
        compiler_params=params,
        cost_estimate=work(1, 1),
        name="traces",
    )(codes, *traces, forward, band)
    operands = (arrived, *kept, short, inverse)
    sent_shape = jax.ShapeDtypeStruct((group * tpl_count, LAGS), jnp.float32)
    sent = pl.pallas_call(
        match_kernel,
        out_shape=sent_shape,
        in_specs=[anywhere] * len(operands),
        out_specs=anywhere,
        scratch_shapes=[pltpu.VMEM(x.shape, x.dtype) for x in (*operands, sent_shape)]
        + [
            pltpu.SemaphoreType.DMA((2 + tiles * (3 + length // LAGS),)),
            pltpu.SemaphoreType.DMA((tiles,)),
        ],
        compiler_params=pltpu.CompilerParams(vmem_limit_bytes=58 * MIB),
        name="match",
    )(*operands)

    parts = exchange(sent.reshape(group, tpl_count, LAGS), GROUP)
    stacks, top = pl.pallas_call(
        functools.partial(stack_kernel, math.sqrt(length / (comps * slot_count))),
        out_shape=[
            jax.ShapeDtypeStruct((tpl_count, LAGS), jnp.float32),
            jax.ShapeDtypeStruct((devices, 1, LAGS), jnp.float32),
        ],
        in_specs=[whole],
        out_specs=[whole, whole],
        compiler_params=pltpu.CompilerParams(vmem_limit_bytes=16 * MIB),
        name="stack",
    )(parts)
    return stacks, jnp.max(exchange(top, AXES), axis=(0, 1))


def solution(mesh):
    slow, fast = (mesh.shape[name] for name in GROUP)
    halves = 2 if slow % 2 == 0 else 1
    split = jax.sharding.Mesh(mesh.devices.reshape(halves, slow // halves, fast), AXES)
    placed = (
        P(AXES, None, None),
        P(AXES, None, None, None),
        P(AXES, None),
        P(AXES, None),
    )
    return jax.shard_map(body, mesh=split, in_specs=placed, out_specs=(P(AXES, None), P()), check_vma=False)
```

```python
import functools
import math

import jax
import jax.numpy as jnp
import ml_dtypes
import numpy as np
from jax import lax
from jax.experimental import pallas as pl
from jax.experimental.pallas import tpu as pltpu
from jax.sharding import PartitionSpec as P

LAGS = 256
HALF = "half"
GROUP = ("tmpl", "sta")
AXES = (HALF,) + GROUP
SOURCES = 8
DIGITS = 3
LANES = 128
MIB = 1024 * 1024


def bits_of(limit):
    return max(1, (limit - 1).bit_length())


def split_table(table):
    high = table.astype(ml_dtypes.bfloat16)
    return high, (table - high.astype(np.float64)).astype(ml_dtypes.bfloat16)


def transform_table(piece):
    size = 2 * piece
    angle = 2.0 * np.pi * (np.arange(piece) + 0.5) / size
    phase = np.arange(piece)[:, None] * angle[None, :]
    forward = np.concatenate([np.cos(phase), -np.sin(phase)], axis=1)
    inverse = np.concatenate([np.cos(phase.T), -np.sin(phase.T)], axis=0) * (2.0 / size)
    return np.concatenate([*split_table(forward), np.concatenate(split_table(inverse), axis=1)], axis=0)


def edge_table(lag_count):
    sample = np.arange(lag_count)[:, None]
    lag = np.arange(lag_count)[None, :]
    return np.concatenate([sample >= lag, sample < lag], axis=0).astype(ml_dtypes.bfloat16)


def iota(shape, axis):
    return lax.broadcasted_iota(jnp.int32, shape, axis)


def dot(a, b):
    return jnp.dot(a, b, preferred_element_type=jnp.float32)


def exact_dot(a, b):
    return jnp.dot(a, b, precision=lax.Precision.HIGHEST, preferred_element_type=jnp.float32)


def entry_lanes(tpl_count, slot_count):
    pairs = tpl_count * slot_count
    first = iota((slot_count, pairs), 0) * tpl_count
    entry = iota((slot_count, pairs), 1)
    spread = jnp.where((entry >= first) & (entry < first + tpl_count), 1.0, 0.0)
    start = jnp.sum(spread * first.astype(jnp.float32), axis=0, keepdims=True)
    return spread, iota((1, pairs), 1).astype(jnp.float32) - start


def as_lanes(values, spread, place, tpl_count):
    owners = values.shape[0] // tpl_count
    pairs = spread.shape[1]
    wide = exact_dot(values.astype(jnp.float32), spread).reshape(owners, tpl_count, pairs)
    own = iota((1, tpl_count, pairs), 1).astype(jnp.float32) == place.reshape(1, 1, pairs)
    return jnp.sum(jnp.where(own, wide, 0.0), axis=1)


def count_before(hits):
    pairs = hits.shape[1]
    earlier = jnp.where(iota((pairs, pairs), 0) < iota((pairs, pairs), 1), 1.0, 0.0)
    return dot(hits.astype(jnp.bfloat16), earlier.astype(jnp.bfloat16))


def pack_kernel(cfg, half_ref, stations_ref, moveouts_ref, templates_hbm, *refs):
    blocks_hbm, (raw_ref, shapes_ref, packed_ref, in_sem, out_sems) = refs[:-5], refs[-5:]
    load = pltpu.make_async_copy(templates_hbm, raw_ref, in_sem)
    load.start()
    tpl_count, slot_count = stations_ref.shape
    pairs = tpl_count * slot_count
    devices, group, halves = cfg["devices"], cfg["group"], cfg["halves"]
    station_dev, rows, capacity = cfg["station_dev"], cfg["rows"], cfg["capacity"]
    spread, place = entry_lanes(tpl_count, slot_count)
    station = as_lanes(stations_ref[...], spread, place, tpl_count)
    device = jnp.floor((station + 0.5) * (1.0 / station_dev))
    onehot = jnp.where(iota((devices, pairs), 0).astype(jnp.float32) == device, 1.0, 0.0)
    rank = jnp.sum(onehot * count_before(onehot), axis=0, keepdims=True)
    half = jnp.floor((device + 0.5) * (1.0 / group))
    holder = device - half * group
    mine = half_ref[0].astype(jnp.float32)
    away = jnp.where(half == mine, 0.0, 1.0)
    fits = rank < float(capacity)

    shift = as_lanes(moveouts_ref[...], spread, place, tpl_count)
    row = station - device * station_dev
    code = ((place + 1.0) * (1 << cfg["row_bits"]) + row) * (1 << cfg["shift_bits"]) + shift
    code = code.astype(jnp.int32)
    at_rank = jnp.where(iota((LANES, pairs), 0).astype(jnp.float32) == rank, 1.0, 0.0).astype(jnp.bfloat16)
    at_holder = iota((group, pairs), 0).astype(jnp.float32) == holder
    digits = []
    for q in range(halves):
        for d in range(DIGITS):
            digit = (lax.shift_right_logical(code, 8 * d) & 255).astype(jnp.float32)
            marked = jnp.where(at_holder & (away == float(q)), digit, 0.0).astype(jnp.bfloat16)
            digits.append(
                lax.dot_general(marked, at_rank, (((1,), (1,)), ((), ())), preferred_element_type=jnp.float32)
            )
    codes = jnp.concatenate(digits, axis=1)

    load.wait()
    comps, length = raw_ref.shape[1], raw_ref.shape[3]
    for c in range(comps):
        values = raw_ref[:, c].astype(jnp.float32).reshape(pairs, length)
        centred = values - jnp.mean(values, axis=-1, keepdims=True)
        spread_c = jnp.sqrt(jnp.mean(centred * centred, axis=-1, keepdims=True) + 1e-05)
        shapes_ref[c] = (centred * (1.0 / spread_c)).astype(jnp.bfloat16)

    tile = SOURCES * rows
    tiles = group // SOURCES
    width = codes.shape[1]
    copies = []
    for block, block_hbm in enumerate(blocks_hbm):
        goal = jnp.where(fits & (away == float(block)), holder * rows + rank, -float(group * rows))
        for step in range(tiles):
            line = iota((tile, pairs), 0).astype(jnp.float32) + float(step * tile)
            total = jnp.zeros((tile, length), jnp.float32)
            for c in range(comps):
                pick = jnp.where(line == goal + float(c * capacity), 1.0, 0.0).astype(jnp.bfloat16)
                total = total + dot(pick, shapes_ref[c])
            if block == 0:
                here = codes[step * SOURCES : (step + 1) * SOURCES].reshape(SOURCES, 1, width)
                last = iota((SOURCES, rows, 1), 1) == rows - 1
                here = jnp.where(last, here, 0.0).reshape(tile, width)
                total = jnp.concatenate([total[:, :width] + here, total[:, width:]], axis=1)
            place_in = pl.ds(step * tile, tile)
            packed_ref[block, place_in, :] = total.astype(jnp.bfloat16)
            copies.append(
                pltpu.make_async_copy(
                    packed_ref.at[block, place_in], block_hbm.at[place_in], out_sems.at[block * tiles + step]
                )
            )
            copies[-1].start()
    for copy in copies:
        copy.wait()


def read_codes(first_block, block):
    width = DIGITS * LANES
    rows = first_block.shape[0] // SOURCES
    values = first_block[:, block * width : (block + 1) * width].astype(jnp.float32).reshape(SOURCES, rows, width)
    last = iota((1, rows, 1), 1) == rows - 1
    digits = jnp.sum(jnp.where(last, values, 0.0), axis=1)
    return sum(digits[:, d * LANES : (d + 1) * LANES] * float(256**d) for d in range(DIGITS))


def block_lines(cfg, codes, comps):
    capacity, rows = cfg["capacity"], cfg["rows"]
    tile = SOURCES * rows
    line = iota((SOURCES, rows, 1), 1).reshape(tile, 1)
    owner = iota((SOURCES, rows, 1), 0).reshape(tile, 1)
    comp = jnp.zeros((tile, 1), jnp.int32)
    for c in range(1, comps + 1):
        comp = comp + jnp.where(line >= c * capacity, 1, 0)
    slot = line - comp * capacity
    repeated = jnp.broadcast_to(codes.reshape(SOURCES, 1, LANES), (SOURCES, rows, LANES)).reshape(tile, LANES)
    chosen = (iota((tile, LANES), 1) == slot) & (comp < comps)
    code = jnp.sum(jnp.where(chosen, repeated, 0.0), axis=1, keepdims=True).astype(jnp.int32)
    shift_bits, row_bits = cfg["shift_bits"], cfg["row_bits"]
    shift = code & ((1 << shift_bits) - 1)
    row = lax.shift_right_logical(code, shift_bits) & ((1 << row_bits) - 1)
    tpl = lax.shift_right_logical(code, shift_bits + row_bits) - 1
    goal = jnp.where(tpl >= 0, comp * cfg["station_dev"] + row, -1)
    return shift, goal, jnp.where(tpl >= 0, owner * cfg["tpl_count"] + tpl, -1)


def cut_traces(cfg, shift, goal, waves):
    tile, seg_len, shift_bits = shift.shape[0], cfg["seg_len"], cfg["shift_bits"]
    pick = jnp.where(iota((tile, waves.shape[0]), 1) == goal, 1.0, 0.0).astype(jnp.bfloat16)
    x = dot(pick, waves)

    for bit in range(shift_bits - 1, 6, -1):
        step = 1 << bit
        width = seg_len + step
        if x.shape[1] < width + step:
            x = jnp.concatenate([x, jnp.zeros((tile, width + step - x.shape[1]), jnp.float32)], axis=1)
        x = jnp.where((shift & step) != 0, x[:, step : step + width], x[:, :width])
    for bit in range(min(shift_bits, 7) - 1, -1, -1):
        step = 1 << bit
        x = jnp.where((shift & step) != 0, pltpu.roll(x, x.shape[1] - step, 1), x)
    return x[:, :seg_len]


def line_sums(cfg, column):
    groups = SOURCES * cfg["tpl_count"]
    return jnp.where(iota((column.shape[0], groups), 1) == column, 1.0, 0.0).T.astype(jnp.bfloat16)


def levels_scale(cfg, segment, edges):
    length = cfg["length"]
    power = segment * segment
    ends = jnp.concatenate([power[:, :LAGS], power[:, length:]], axis=1)
    high = ends.astype(jnp.bfloat16)
    low = (ends - high.astype(jnp.float32)).astype(jnp.bfloat16)
    energy = dot(high, edges) + dot(low, edges) + jnp.sum(power[:, LAGS:length], axis=1, keepdims=True)
    return 1.0 / (length * jnp.sqrt(energy * (1.0 / length) + 1e-05))


def match_lines(shapes, spectra, scale, forward, inverse):
    real = imag = 0.0
    for h, (theirs_r, theirs_i) in enumerate(spectra):
        part = shapes[:, h * LAGS : (h + 1) * LAGS]
        mine = dot(jnp.concatenate([part, part], axis=1), forward)
        mine_r, mine_i = mine[:, :LAGS], mine[:, LAGS:]
        real = real + (theirs_r * mine_r + theirs_i * mine_i)
        imag = imag + (theirs_i * mine_r - theirs_r * mine_i)
    product = jnp.concatenate([real, imag], axis=1)
    high = product.astype(jnp.bfloat16)
    low = (product - high.astype(jnp.float32)).astype(jnp.bfloat16)
    return dot(jnp.concatenate([high, high, low], axis=1), inverse) * scale


def sum_lines(sums, left):
    total = 0.0
    for _ in range(3):
        part = left.astype(jnp.bfloat16)
        left = left - part.astype(jnp.float32)
        total = total + dot(sums, part)
    return total


def tables_of(table_ref):
    back = table_ref[2 * LAGS :, :]
    high, low = back[:, :LAGS], back[:, LAGS:]
    return table_ref[: 2 * LAGS, :], jnp.concatenate([high, low, high], axis=0)


def traces_of(cfg, block, first_ref, waves_ref, edges_ref, forward):
    codes = read_codes(first_ref[...], block)
    comps, station_dev, samples = waves_ref.shape
    shift, goal, column = block_lines(cfg, codes, comps)
    segment = cut_traces(cfg, shift, goal, waves_ref[...].reshape(comps * station_dev, samples))
    narrow = segment.astype(jnp.bfloat16)
    sign = (1 - 2 * (iota((1, LAGS), 1) & 1)).astype(jnp.float32)

    def spectra():
        before = None
        for h in range(cfg["length"] // LAGS + 1):
            part = narrow[:, h * LAGS : (h + 1) * LAGS]
            here = dot(jnp.concatenate([part, part], axis=1), forward)
            here = here[:, :LAGS], here[:, LAGS:]
            if before is not None:
                yield before[0] + sign * here[1], before[1] - sign * here[0]
            before = here

    return spectra(), levels_scale(cfg, segment, edges_ref[...]), line_sums(cfg, column)


def near_kernel(cfg, first_ref, waves_ref, table_ref, edges_ref, sent_ref):
    forward, inverse = tables_of(table_ref)
    spectra, scale, sums = traces_of(cfg, 0, first_ref, waves_ref, edges_ref, forward)
    sent_ref[...] = sum_lines(sums, match_lines(first_ref[...], spectra, scale, forward, inverse))


def far_kernel(cfg, first_ref, waves_ref, table_ref, edges_ref, kept_ref, sums_ref):
    forward, _ = tables_of(table_ref)
    spectra, scale, sums = traces_of(cfg, 1, first_ref, waves_ref, edges_ref, forward)
    sums_ref[...] = sums
    kept_ref[:, 2 * cfg["length"] :] = scale
    for h, (real, imag) in enumerate(spectra):
        kept_ref[:, 2 * h * LAGS : (2 * h + 1) * LAGS] = real
        kept_ref[:, (2 * h + 1) * LAGS : (2 * h + 2) * LAGS] = imag


def match_kernel(tiles, shapes_ref, kept_hbm, sums_hbm, table_hbm, before_hbm, sent_ref, *scratch):
    kept_ref, sums_ref, table_ref, before_ref, sems = scratch
    tile = shapes_ref.shape[0] // tiles
    groups = sent_ref.shape[0] // tiles
    length = shapes_ref.shape[1]

    def fetch(source, buffer, sem):
        copy = pltpu.make_async_copy(source, buffer, sems.at[sem])
        copy.start()
        return copy

    def lines(t):
        return pl.ds(t * tile, tile)

    table = fetch(table_hbm, table_ref, 0)
    kept = [fetch(kept_hbm.at[lines(0)], kept_ref.at[lines(0)], 3)]
    sums = fetch(sums_hbm, sums_ref, 1)
    before = fetch(before_hbm, before_ref, 2)
    kept += [fetch(kept_hbm.at[lines(t)], kept_ref.at[lines(t)], 3 + t) for t in range(1, tiles)]
    table.wait()
    forward, inverse = tables_of(table_ref)
    for t in range(tiles):
        kept[t].wait()
        theirs = kept_ref[lines(t), :]
        spectra = [
            (theirs[:, 2 * h * LAGS : (2 * h + 1) * LAGS], theirs[:, (2 * h + 1) * LAGS : (2 * h + 2) * LAGS])
            for h in range(length // LAGS)
        ]
        left = match_lines(shapes_ref[lines(t), :], spectra, theirs[:, 2 * length :], forward, inverse)
        if t == 0:
            sums.wait()
            before.wait()
        ends = pl.ds(t * groups, groups)
        sent_ref[ends, :] = before_ref[ends, :] + sum_lines(sums_ref[ends, :], left)


def stack_kernel(factor, parts_ref, stacks_ref, top_ref):
    stacks = jnp.sum(parts_ref[...], axis=0) * factor
    stacks_ref[...] = stacks
    top_ref[...] = jnp.broadcast_to(jnp.max(stacks, axis=0, keepdims=True), top_ref.shape)


def body(waveforms, templates, stations, moveouts):
    devices, group, halves = lax.axis_size(AXES), lax.axis_size(GROUP), lax.axis_size(HALF)
    tpl_count, slot_count = stations.shape
    comps, length = templates.shape[2:]
    station_dev, _, samples = waveforms.shape
    seg_len = length + LAGS
    pairs = tpl_count * slot_count
    capacity = (2 * pairs + devices - 1) // devices
    rows = -(-(comps * capacity + 1) // 16) * 16
    cfg = dict(
        devices=devices,
        group=group,
        halves=halves,
        station_dev=station_dev,
        tpl_count=tpl_count,
        capacity=capacity,
        rows=rows,
        length=length,
        seg_len=seg_len,
        shift_bits=bits_of(samples - seg_len + 1),
        row_bits=bits_of(station_dev),
    )
    table = jnp.asarray(transform_table(LAGS))
    edges = jnp.asarray(edge_table(LAGS))
    tiles = group // SOURCES
    tile = SOURCES * rows
    lines = group * rows
    sums_tile = SOURCES * tpl_count
    kept_len = 2 * length + LAGS
    whole = pl.BlockSpec(memory_space=pltpu.VMEM)
    anywhere = pl.BlockSpec(memory_space=pl.ANY)
    params = pltpu.CompilerParams(vmem_limit_bytes=60 * MIB)
    by_slot = templates.transpose(1, 2, 0, 3)
    waves = waveforms.transpose(1, 0, 2)
    half = lax.axis_index(HALF).reshape(1)

    def work(flops, size):
        return pl.CostEstimate(flops=flops, bytes_accessed=size, transcendentals=0)

    def exchange(x, axes):
        return lax.all_to_all(x, axes, split_axis=0, concat_axis=0, tiled=True)

    def same(shape):
        return pl.BlockSpec(shape, lambda i: (0,) * len(shape))

    def tiled(*shape):
        return pl.BlockSpec(shape, lambda i: (i, 0))

    block_shape = jax.ShapeDtypeStruct((lines, length), jnp.bfloat16)
    first, *second = pl.pallas_call(
        functools.partial(pack_kernel, cfg),
        out_shape=[block_shape] * halves,
        in_specs=[pl.BlockSpec(memory_space=pltpu.SMEM), whole, whole, anywhere],
        out_specs=[anywhere] * halves,
        scratch_shapes=[
            pltpu.VMEM(by_slot.shape, jnp.bfloat16),
            pltpu.VMEM((comps, pairs, length), jnp.bfloat16),
            pltpu.VMEM((halves, lines, length), jnp.bfloat16),
            pltpu.SemaphoreType.DMA,
            pltpu.SemaphoreType.DMA((halves * tiles,)),
        ],
        compiler_params=params,
        name="pack",
    )(half, stations, moveouts, by_slot)

    def exchange_rows(x):
        return exchange(x.reshape(group, rows, length), GROUP).reshape(lines, length)

    first = exchange_rows(first)
    if halves == 2:
        swapped = lax.ppermute(waves, HALF, [(0, 1), (1, 0)])
        first, swapped, second = lax.optimization_barrier((first, swapped, second[0]))
        second = exchange_rows(second)

    trace_flops = 2 * lines * (length // LAGS * 6 * LAGS * LAGS + 4 * LAGS * LAGS + comps * station_dev * samples)
    trace_specs = [tiled(tile, length), same(waves.shape), same(table.shape), same(edges.shape)]
    sent = pl.pallas_call(
        functools.partial(near_kernel, cfg),
        grid=(tiles,),
        out_shape=jax.ShapeDtypeStruct((group * tpl_count, LAGS), jnp.float32),
        in_specs=trace_specs,
        out_specs=tiled(sums_tile, LAGS),
        compiler_params=params,
        cost_estimate=work(trace_flops, lines * length * 2),
        name="near",
    )(first, waves, table, edges)
    if halves == 2:
        kept, sums = pl.pallas_call(
            functools.partial(far_kernel, cfg),
            grid=(tiles,),
            out_shape=[
                jax.ShapeDtypeStruct((lines, kept_len), jnp.float32),
                jax.ShapeDtypeStruct((group * tpl_count, tile), jnp.bfloat16),
            ],
            in_specs=trace_specs,
            out_specs=[tiled(tile, kept_len), tiled(sums_tile, tile)],
            compiler_params=params,
            cost_estimate=work(trace_flops, lines * kept_len * 4),
            name="far",
        )(first, swapped, table, edges)
        operands = (kept, sums, table, sent)
        sent = pl.pallas_call(
            functools.partial(match_kernel, tiles),
            out_shape=jax.ShapeDtypeStruct(sent.shape, jnp.float32),
            in_specs=[whole] + [anywhere] * len(operands),
            out_specs=whole,
            scratch_shapes=[pltpu.VMEM(x.shape, x.dtype) for x in operands]
            + [pltpu.SemaphoreType.DMA((3 + tiles,))],
            compiler_params=pltpu.CompilerParams(vmem_limit_bytes=58 * MIB),
            name="match",
        )(second, *operands)

    parts = exchange(sent.reshape(group, tpl_count, LAGS), GROUP)
    stacks, top = pl.pallas_call(
        functools.partial(stack_kernel, math.sqrt(length / (comps * slot_count))),
        out_shape=[
            jax.ShapeDtypeStruct((tpl_count, LAGS), jnp.float32),
            jax.ShapeDtypeStruct((devices, 1, LAGS), jnp.float32),
        ],
        in_specs=[whole],
        out_specs=[whole, whole],
        compiler_params=pltpu.CompilerParams(vmem_limit_bytes=16 * MIB),
        name="stack",
    )(parts)
    return stacks, jnp.max(exchange(top, AXES), axis=(0, 1))


def solution(mesh):
    slow, fast = (mesh.shape[name] for name in GROUP)
    halves = 2 if slow % 2 == 0 else 1
    split = jax.sharding.Mesh(mesh.devices.reshape(halves, slow // halves, fast), AXES)
    placed = (
        P(AXES, None, None),
        P(AXES, None, None, None),
        P(AXES, None),
        P(AXES, None),
    )
    return jax.shard_map(body, mesh=split, in_specs=placed, out_specs=(P(AXES, None), P()), check_vma=False)
```

```python
import functools
import math

import jax
import jax.numpy as jnp
import ml_dtypes
import numpy as np
from jax import lax
from jax.experimental import pallas as pl
from jax.experimental.pallas import tpu as pltpu
from jax.sharding import PartitionSpec as P

LAGS = 256
HALF = "half"
GROUP = ("tmpl", "sta")
AXES = (HALF,) + GROUP
SOURCES = 8
DIGITS = 3
LANES = 128
MIB = 1024 * 1024


def bits_of(limit):
    return max(1, (limit - 1).bit_length())


def split_table(table):
    high = table.astype(ml_dtypes.bfloat16)
    return high, (table - high.astype(np.float64)).astype(ml_dtypes.bfloat16)


def transform_table(piece):
    size = 2 * piece
    angle = 2.0 * np.pi * (np.arange(piece) + 0.5) / size
    phase = np.arange(piece)[:, None] * angle[None, :]
    forward = np.concatenate([np.cos(phase), -np.sin(phase)], axis=1)
    inverse = np.concatenate([np.cos(phase.T), -np.sin(phase.T)], axis=0) * (2.0 / size)
    return np.concatenate([*split_table(forward), np.concatenate(split_table(inverse), axis=1)], axis=0)


def edge_table(lag_count):
    sample = np.arange(lag_count)[:, None]
    lag = np.arange(lag_count)[None, :]
    return np.concatenate([sample >= lag, sample < lag], axis=0).astype(ml_dtypes.bfloat16)


def iota(shape, axis):
    return lax.broadcasted_iota(jnp.int32, shape, axis)


def dot(a, b):
    return jnp.dot(a, b, preferred_element_type=jnp.float32)


def exact_dot(a, b):
    return jnp.dot(a, b, precision=lax.Precision.HIGHEST, preferred_element_type=jnp.float32)


def entry_lanes(tpl_count, slot_count):
    pairs = tpl_count * slot_count
    first = iota((slot_count, pairs), 0) * tpl_count
    entry = iota((slot_count, pairs), 1)
    spread = jnp.where((entry >= first) & (entry < first + tpl_count), 1.0, 0.0)
    start = jnp.sum(spread * first.astype(jnp.float32), axis=0, keepdims=True)
    return spread, iota((1, pairs), 1).astype(jnp.float32) - start


def as_lanes(values, spread, place, tpl_count):
    owners = values.shape[0] // tpl_count
    pairs = spread.shape[1]
    wide = exact_dot(values.astype(jnp.float32), spread).reshape(owners, tpl_count, pairs)
    own = iota((1, tpl_count, pairs), 1).astype(jnp.float32) == place.reshape(1, 1, pairs)
    return jnp.sum(jnp.where(own, wide, 0.0), axis=1)


def count_before(hits):
    pairs = hits.shape[1]
    earlier = jnp.where(iota((pairs, pairs), 0) < iota((pairs, pairs), 1), 1.0, 0.0)
    return dot(hits.astype(jnp.bfloat16), earlier.astype(jnp.bfloat16))


def pack_kernel(cfg, half_ref, stations_ref, moveouts_ref, templates_hbm, *refs):
    blocks_hbm, (raw_ref, shapes_ref, packed_ref, in_sem, out_sems) = refs[:-5], refs[-5:]
    load = pltpu.make_async_copy(templates_hbm, raw_ref, in_sem)
    load.start()
    tpl_count, slot_count = stations_ref.shape
    pairs = tpl_count * slot_count
    devices, group, halves = cfg["devices"], cfg["group"], cfg["halves"]
    station_dev, rows, capacity = cfg["station_dev"], cfg["rows"], cfg["capacity"]
    spread, place = entry_lanes(tpl_count, slot_count)
    station = as_lanes(stations_ref[...], spread, place, tpl_count)
    device = jnp.floor((station + 0.5) * (1.0 / station_dev))
    onehot = jnp.where(iota((devices, pairs), 0).astype(jnp.float32) == device, 1.0, 0.0)
    rank = jnp.sum(onehot * count_before(onehot), axis=0, keepdims=True)
    half = jnp.floor((device + 0.5) * (1.0 / group))
    holder = device - half * group
    mine = half_ref[0].astype(jnp.float32)
    away = jnp.where(half == mine, 0.0, 1.0)
    fits = rank < float(capacity)

    shift = as_lanes(moveouts_ref[...], spread, place, tpl_count)
    row = station - device * station_dev
    code = ((place + 1.0) * (1 << cfg["row_bits"]) + row) * (1 << cfg["shift_bits"]) + shift
    code = code.astype(jnp.int32)
    at_rank = jnp.where(iota((LANES, pairs), 0).astype(jnp.float32) == rank, 1.0, 0.0).astype(jnp.bfloat16)
    at_holder = iota((group, pairs), 0).astype(jnp.float32) == holder
    digits = []
    for q in range(halves):
        for d in range(DIGITS):
            digit = (lax.shift_right_logical(code, 8 * d) & 255).astype(jnp.float32)
            marked = jnp.where(at_holder & (away == float(q)), digit, 0.0).astype(jnp.bfloat16)
            digits.append(
                lax.dot_general(marked, at_rank, (((1,), (1,)), ((), ())), preferred_element_type=jnp.float32)
            )
    codes = jnp.concatenate(digits, axis=1)

    load.wait()
    comps, length = raw_ref.shape[1], raw_ref.shape[3]
    for c in range(comps):
        values = raw_ref[:, c].astype(jnp.float32).reshape(pairs, length)
        centred = values - jnp.mean(values, axis=-1, keepdims=True)
        spread_c = jnp.sqrt(jnp.mean(centred * centred, axis=-1, keepdims=True) + 1e-05)
        shapes_ref[c] = (centred * (1.0 / spread_c)).astype(jnp.bfloat16)

    tile = SOURCES * rows
    tiles = group // SOURCES
    width = codes.shape[1]
    copies = []
    for block, block_hbm in enumerate(blocks_hbm):
        goal = jnp.where(fits & (away == float(block)), holder * rows + rank, -float(group * rows))
        for step in range(tiles):
            line = iota((tile, pairs), 0).astype(jnp.float32) + float(step * tile)
            total = jnp.zeros((tile, length), jnp.float32)
            for c in range(comps):
                pick = jnp.where(line == goal + float(c * capacity), 1.0, 0.0).astype(jnp.bfloat16)
                total = total + dot(pick, shapes_ref[c])
            if block == 0:
                here = codes[step * SOURCES : (step + 1) * SOURCES].reshape(SOURCES, 1, width)
                last = iota((SOURCES, rows, 1), 1) == rows - 1
                here = jnp.where(last, here, 0.0).reshape(tile, width)
                total = jnp.concatenate([total[:, :width] + here, total[:, width:]], axis=1)
            place_in = pl.ds(step * tile, tile)
            packed_ref[block, place_in, :] = total.astype(jnp.bfloat16)
            copies.append(
                pltpu.make_async_copy(
                    packed_ref.at[block, place_in], block_hbm.at[place_in], out_sems.at[block * tiles + step]
                )
            )
            copies[-1].start()
    for copy in copies:
        copy.wait()


def read_codes(first_block, block):
    width = DIGITS * LANES
    rows = first_block.shape[0] // SOURCES
    values = first_block[:, block * width : (block + 1) * width].astype(jnp.float32).reshape(SOURCES, rows, width)
    last = iota((1, rows, 1), 1) == rows - 1
    digits = jnp.sum(jnp.where(last, values, 0.0), axis=1)
    return sum(digits[:, d * LANES : (d + 1) * LANES] * float(256**d) for d in range(DIGITS))


def block_lines(cfg, codes):
    capacity, rows, comps = cfg["capacity"], cfg["rows"], cfg["comps"]
    tile = SOURCES * rows
    line = iota((SOURCES, rows, 1), 1).reshape(tile, 1)
    owner = iota((SOURCES, rows, 1), 0).reshape(tile, 1)
    comp = jnp.zeros((tile, 1), jnp.int32)
    for c in range(1, comps + 1):
        comp = comp + jnp.where(line >= c * capacity, 1, 0)
    slot = line - comp * capacity
    repeated = jnp.broadcast_to(codes.reshape(SOURCES, 1, LANES), (SOURCES, rows, LANES)).reshape(tile, LANES)
    chosen = (iota((tile, LANES), 1) == slot) & (comp < comps)
    code = jnp.sum(jnp.where(chosen, repeated, 0.0), axis=1, keepdims=True).astype(jnp.int32)
    shift_bits, row_bits = cfg["shift_bits"], cfg["row_bits"]
    shift = code & ((1 << shift_bits) - 1)
    row = lax.shift_right_logical(code, shift_bits) & ((1 << row_bits) - 1)
    tpl = lax.shift_right_logical(code, shift_bits + row_bits) - 1
    goal = jnp.where(tpl >= 0, comp * cfg["station_dev"] + row, -1)
    return shift, goal, jnp.where(tpl >= 0, owner * cfg["tpl_count"] + tpl, -1)


def cut_traces(cfg, shift, goal, waves, x_ref, shift_ref, narrow_ref, ends_ref, middle_ref):
    tile, samples = x_ref.shape
    seg_len, length, shift_bits = cfg["seg_len"], cfg["length"], cfg["shift_bits"]
    pick = jnp.where(iota((tile, waves.shape[0]), 1) == goal, 1.0, 0.0).astype(jnp.bfloat16)
    x_ref[...] = dot(pick, waves)
    shift_ref[...] = jnp.broadcast_to(shift, (tile, LANES))
    parts = seg_len // LANES
    edge = LAGS // LANES
    lane = iota((8, LANES), 1)
    zero = jnp.zeros((8, LANES), jnp.float32)

    def cut(rows):
        by = shift_ref[rows, :]
        x = [x_ref[rows, j * LANES : (j + 1) * LANES] for j in range(samples // LANES)]
        for bit in range(shift_bits - 1, -1, -1):
            step = 1 << bit
            flag = (by & step) != 0
            if step >= LANES:
                hop = step // LANES
                moved = (x + [zero] * hop)[hop:]
            else:
                x = x[: parts + 1]
                turned = [pltpu.roll(v, LANES - step, 1) for v in x]
                inner = lane < LANES - step
                moved = [jnp.where(inner, u, v) for u, v in zip(turned, turned[1:] + turned[:1])]
            x = [jnp.where(flag, u, v) for u, v in zip(moved, x)]
        return x[:parts]

    def one_group(i):
        top = pl.multiple_of(i * 16, 16)
        two = [cut(pl.ds(top + 8 * k, 8)) for k in range(2)]
        rows = pl.ds(top, 16)
        middle = [zero, zero]
        for j in range(parts):
            value = jnp.concatenate([two[0][j], two[1][j]], axis=0)
            narrow_ref[rows, j * LANES : (j + 1) * LANES] = value.astype(jnp.bfloat16)
            if edge <= j < parts - edge:
                middle = [m + x[j] * x[j] for m, x in zip(middle, two)]
            else:
                power = value * value
                high = power.astype(jnp.bfloat16)
                at = j if j < edge else j - (parts - 2 * edge)
                ends_ref[0, rows, at * LANES : (at + 1) * LANES] = high
                ends_ref[1, rows, at * LANES : (at + 1) * LANES] = (power - high.astype(jnp.float32)).astype(jnp.bfloat16)
        middle_ref[rows, :] = jnp.concatenate(middle, axis=0)

    pl.loop(0, tile // 16)(one_group)


def line_sums(cfg, column):
    groups = SOURCES * cfg["tpl_count"]
    return jnp.where(iota((column.shape[0], groups), 1) == column, 1.0, 0.0).T.astype(jnp.bfloat16)


def levels_scale(cfg, ends_ref, middle_ref, edges):
    length = cfg["length"]
    energy = dot(ends_ref[0], edges) + dot(ends_ref[1], edges)
    energy = energy + jnp.sum(middle_ref[...], axis=1, keepdims=True)
    return 1.0 / (length * jnp.sqrt(energy * (1.0 / length) + 1e-05))


def match_lines(shapes, spectra, scale, forward, inverse):
    real = imag = 0.0
    for h, (theirs_r, theirs_i) in enumerate(spectra):
        part = shapes[:, h * LAGS : (h + 1) * LAGS]
        mine = dot(jnp.concatenate([part, part], axis=1), forward)
        mine_r, mine_i = mine[:, :LAGS], mine[:, LAGS:]
        real = real + (theirs_r * mine_r + theirs_i * mine_i)
        imag = imag + (theirs_i * mine_r - theirs_r * mine_i)
    product = jnp.concatenate([real, imag], axis=1)
    high = product.astype(jnp.bfloat16)
    low = (product - high.astype(jnp.float32)).astype(jnp.bfloat16)
    return dot(jnp.concatenate([high, high, low], axis=1), inverse) * scale


def sum_lines(sums, left):
    total = 0.0
    for _ in range(3):
        part = left.astype(jnp.bfloat16)
        left = left - part.astype(jnp.float32)
        total = total + dot(sums, part)
    return total


def tables_of(table_ref):
    back = table_ref[2 * LAGS :, :]
    high, low = back[:, :LAGS], back[:, LAGS:]
    return table_ref[: 2 * LAGS, :], jnp.concatenate([high, low, high], axis=0)


def traces_of(cfg, block, first_ref, waves_refs, edges_ref, forward, scratch):
    codes = read_codes(first_ref[...], block)
    shift, goal, column = block_lines(cfg, codes)
    waves = [ref[...].reshape(-1, ref.shape[2]) for ref in waves_refs]
    cut_traces(cfg, shift, goal, jnp.concatenate(waves, axis=0), *scratch)
    _, _, narrow_ref, ends_ref, middle_ref = scratch
    sign = (1 - 2 * (iota((1, LAGS), 1) & 1)).astype(jnp.float32)

    def spectra():
        before = None
        for h in range(cfg["length"] // LAGS + 1):
            part = narrow_ref[:, h * LAGS : (h + 1) * LAGS]
            here = dot(jnp.concatenate([part, part], axis=1), forward)
            here = here[:, :LAGS], here[:, LAGS:]
            if before is not None:
                yield before[0] + sign * here[1], before[1] - sign * here[0]
            before = here

    return spectra(), levels_scale(cfg, ends_ref, middle_ref, edges_ref[...]), line_sums(cfg, column)


def near_kernel(cfg, first_ref, waves_ref, table_ref, edges_ref, sent_ref, *scratch):
    forward, inverse = tables_of(table_ref)
    spectra, scale, sums = traces_of(cfg, 0, first_ref, [waves_ref], edges_ref, forward, scratch)
    sent_ref[...] = sum_lines(sums, match_lines(first_ref[...], spectra, scale, forward, inverse))


def far_kernel(cfg, first_ref, waves_ref, last_waves_ref, table_ref, edges_ref, kept_ref, sums_ref, *scratch):
    forward, _ = tables_of(table_ref)
    spectra, scale, sums = traces_of(cfg, 1, first_ref, [waves_ref, last_waves_ref], edges_ref, forward, scratch)
    sums_ref[...] = sums
    kept_ref[:, 2 * cfg["length"] :] = scale
    for h, (real, imag) in enumerate(spectra):
        kept_ref[:, 2 * h * LAGS : (2 * h + 1) * LAGS] = real
        kept_ref[:, (2 * h + 1) * LAGS : (2 * h + 2) * LAGS] = imag


def match_kernel(tiles, shapes_hbm, kept_hbm, sums_hbm, table_hbm, before_hbm, sent_ref, *scratch):
    shapes_ref, kept_ref, sums_ref, table_ref, before_ref, sems = scratch
    tile = shapes_ref.shape[0] // tiles
    groups = sent_ref.shape[0] // tiles
    length = shapes_ref.shape[1]

    def fetch(source, buffer, sem):
        copy = pltpu.make_async_copy(source, buffer, sems.at[sem])
        copy.start()
        return copy

    def lines(t):
        return pl.ds(t * tile, tile)

    table = fetch(table_hbm, table_ref, 0)
    shapes = fetch(shapes_hbm, shapes_ref, 3)
    kept = [fetch(kept_hbm.at[lines(0)], kept_ref.at[lines(0)], 4)]
    sums = fetch(sums_hbm, sums_ref, 1)
    before = fetch(before_hbm, before_ref, 2)
    kept += [fetch(kept_hbm.at[lines(t)], kept_ref.at[lines(t)], 4 + t) for t in range(1, tiles)]
    table.wait()
    shapes.wait()
    forward, inverse = tables_of(table_ref)
    for t in range(tiles):
        kept[t].wait()
        theirs = kept_ref[lines(t), :]
        spectra = [
            (theirs[:, 2 * h * LAGS : (2 * h + 1) * LAGS], theirs[:, (2 * h + 1) * LAGS : (2 * h + 2) * LAGS])
            for h in range(length // LAGS)
        ]
        left = match_lines(shapes_ref[lines(t), :], spectra, theirs[:, 2 * length :], forward, inverse)
        if t == 0:
            sums.wait()
            before.wait()
        ends = pl.ds(t * groups, groups)
        sent_ref[ends, :] = before_ref[ends, :] + sum_lines(sums_ref[ends, :], left)


def stack_kernel(factor, parts_ref, stacks_ref, top_ref):
    stacks = jnp.sum(parts_ref[...], axis=0) * factor
    stacks_ref[...] = stacks
    top_ref[...] = jnp.broadcast_to(jnp.max(stacks, axis=0, keepdims=True), top_ref.shape)


def body(waveforms, templates, stations, moveouts):
    devices, group, halves = lax.axis_size(AXES), lax.axis_size(GROUP), lax.axis_size(HALF)
    tpl_count, slot_count = stations.shape
    comps, length = templates.shape[2:]
    station_dev, _, samples = waveforms.shape
    seg_len = length + LAGS
    pairs = tpl_count * slot_count
    capacity = (2 * pairs + devices - 1) // devices
    rows = -(-(comps * capacity + 1) // 16) * 16
    cfg = dict(
        devices=devices,
        group=group,
        halves=halves,
        station_dev=station_dev,
        tpl_count=tpl_count,
        comps=comps,
        capacity=capacity,
        rows=rows,
        length=length,
        seg_len=seg_len,
        shift_bits=bits_of(samples - seg_len + 1),
        row_bits=bits_of(station_dev),
    )
    table = jnp.asarray(transform_table(LAGS))
    edges = jnp.asarray(edge_table(LAGS))
    tiles = group // SOURCES
    tile = SOURCES * rows
    lines = group * rows
    sums_tile = SOURCES * tpl_count
    kept_len = 2 * length + LAGS
    whole = pl.BlockSpec(memory_space=pltpu.VMEM)
    anywhere = pl.BlockSpec(memory_space=pl.ANY)
    params = pltpu.CompilerParams(vmem_limit_bytes=60 * MIB)
    by_slot = templates.transpose(1, 2, 0, 3)
    waves = waveforms.transpose(1, 0, 2)
    half = lax.axis_index(HALF).reshape(1)

    def work(flops, size):
        return pl.CostEstimate(flops=flops, bytes_accessed=size, transcendentals=0)

    def exchange(x, axes):
        return lax.all_to_all(x, axes, split_axis=0, concat_axis=0, tiled=True)

    def same(shape):
        return pl.BlockSpec(shape, lambda i: (0,) * len(shape))

    def tiled(*shape):
        return pl.BlockSpec(shape, lambda i: (i, 0))

    block_shape = jax.ShapeDtypeStruct((lines, length), jnp.bfloat16)
    first, *second = pl.pallas_call(
        functools.partial(pack_kernel, cfg),
        out_shape=[block_shape] * halves,
        in_specs=[pl.BlockSpec(memory_space=pltpu.SMEM), whole, whole, anywhere],
        out_specs=[anywhere] * halves,
        scratch_shapes=[
            pltpu.VMEM(by_slot.shape, jnp.bfloat16),
            pltpu.VMEM((comps, pairs, length), jnp.bfloat16),
            pltpu.VMEM((halves, lines, length), jnp.bfloat16),
            pltpu.SemaphoreType.DMA,
            pltpu.SemaphoreType.DMA((halves * tiles,)),
        ],
        compiler_params=params,
        name="pack",
    )(half, stations, moveouts, by_slot)

    def exchange_rows(x):
        return exchange(x.reshape(group, rows, length), GROUP).reshape(lines, length)

    first = exchange_rows(first)
    if halves == 2:
        early = -(-2 * comps // 3)
        swapped = [lax.ppermute(x, HALF, [(0, 1), (1, 0)]) for x in (waves[:early], waves[early:])]
        first, swapped[0], second = lax.optimization_barrier((first, swapped[0], second[0]))
        second = exchange_rows(second)

    trace_flops = 2 * lines * (length // LAGS * 6 * LAGS * LAGS + 4 * LAGS * LAGS + comps * station_dev * samples)
    trace_scratch = [
        pltpu.VMEM((tile, samples), jnp.float32),
        pltpu.VMEM((tile, LANES), jnp.int32),
        pltpu.VMEM((tile, seg_len), jnp.bfloat16),
        pltpu.VMEM((2, tile, 2 * LAGS), jnp.bfloat16),
        pltpu.VMEM((tile, LANES), jnp.float32),
    ]

    def trace_specs(*traces):
        return [tiled(tile, length)] + [same(x.shape) for x in (*traces, table, edges)]

    sent = pl.pallas_call(
        functools.partial(near_kernel, cfg),
        grid=(tiles,),
        out_shape=jax.ShapeDtypeStruct((group * tpl_count, LAGS), jnp.float32),
        in_specs=trace_specs(waves),
        out_specs=tiled(sums_tile, LAGS),
        scratch_shapes=trace_scratch,
        compiler_params=params,
        cost_estimate=work(trace_flops, lines * length * 2),
        name="near",
    )(first, waves, table, edges)
    if halves == 2:
        kept, sums = pl.pallas_call(
            functools.partial(far_kernel, cfg),
            grid=(tiles,),
            out_shape=[
                jax.ShapeDtypeStruct((lines, kept_len), jnp.float32),
                jax.ShapeDtypeStruct((group * tpl_count, tile), jnp.bfloat16),
            ],
            in_specs=trace_specs(*swapped),
            out_specs=[tiled(tile, kept_len), tiled(sums_tile, tile)],
            scratch_shapes=trace_scratch,
            compiler_params=params,
            cost_estimate=work(trace_flops, lines * kept_len * 4),
            name="far",
        )(first, *swapped, table, edges)
        operands = (second, kept, sums, table, sent)
        sent = pl.pallas_call(
            functools.partial(match_kernel, tiles),
            out_shape=jax.ShapeDtypeStruct(sent.shape, jnp.float32),
            in_specs=[anywhere] * len(operands),
            out_specs=whole,
            scratch_shapes=[pltpu.VMEM(x.shape, x.dtype) for x in operands]
            + [pltpu.SemaphoreType.DMA((4 + tiles,))],
            compiler_params=pltpu.CompilerParams(vmem_limit_bytes=57 * MIB),
            name="match",
        )(*operands)

    parts = exchange(sent.reshape(group, tpl_count, LAGS), GROUP)
    stacks, top = pl.pallas_call(
        functools.partial(stack_kernel, math.sqrt(length / (comps * slot_count))),
        out_shape=[
            jax.ShapeDtypeStruct((tpl_count, LAGS), jnp.float32),
            jax.ShapeDtypeStruct((devices, 1, LAGS), jnp.float32),
        ],
        in_specs=[whole],
        out_specs=[whole, whole],
        compiler_params=pltpu.CompilerParams(vmem_limit_bytes=16 * MIB),
        name="stack",
    )(parts)
    return stacks, jnp.max(exchange(top, AXES), axis=(0, 1))


def solution(mesh):
    slow, fast = (mesh.shape[name] for name in GROUP)
    halves = 2 if slow % 2 == 0 else 1
    split = jax.sharding.Mesh(mesh.devices.reshape(halves, slow // halves, fast), AXES)
    placed = (
        P(AXES, None, None),
        P(AXES, None, None, None),
        P(AXES, None),
        P(AXES, None),
    )
    return jax.shard_map(body, mesh=split, in_specs=placed, out_specs=(P(AXES, None), P()), check_vma=False)
```

```python
import functools
import math

import jax
import jax.numpy as jnp
import ml_dtypes
import numpy as np
from jax import lax
from jax.experimental import pallas as pl
from jax.experimental.pallas import tpu as pltpu
from jax.sharding import PartitionSpec as P

LAGS = 256
HALF = "half"
GROUP = ("tmpl", "sta")
AXES = (HALF,) + GROUP
SOURCES = 8
DIGITS = 3
LANES = 128
MIB = 1024 * 1024


def bits_of(limit):
    return max(1, (limit - 1).bit_length())


def split_table(table):
    high = table.astype(ml_dtypes.bfloat16)
    return high, (table - high.astype(np.float64)).astype(ml_dtypes.bfloat16)


def transform_table(piece):
    size = 2 * piece
    angle = 2.0 * np.pi * (np.arange(piece) + 0.5) / size
    phase = np.arange(piece)[:, None] * angle[None, :]
    forward = np.concatenate([np.cos(phase), -np.sin(phase)], axis=1)
    inverse = np.concatenate([np.cos(phase.T), -np.sin(phase.T)], axis=0) * (2.0 / size)
    return np.concatenate([*split_table(forward), np.concatenate(split_table(inverse), axis=1)], axis=0)


def edge_table(lag_count):
    sample = np.arange(lag_count)[:, None]
    lag = np.arange(lag_count)[None, :]
    return np.concatenate([sample >= lag, sample < lag], axis=0).astype(ml_dtypes.bfloat16)


def iota(shape, axis):
    return lax.broadcasted_iota(jnp.int32, shape, axis)


def dot(a, b):
    return jnp.dot(a, b, preferred_element_type=jnp.float32)


def exact_dot(a, b):
    return jnp.dot(a, b, precision=lax.Precision.HIGHEST, preferred_element_type=jnp.float32)


def entry_lanes(tpl_count, slot_count):
    pairs = tpl_count * slot_count
    first = iota((slot_count, pairs), 0) * tpl_count
    entry = iota((slot_count, pairs), 1)
    spread = jnp.where((entry >= first) & (entry < first + tpl_count), 1.0, 0.0)
    start = jnp.sum(spread * first.astype(jnp.float32), axis=0, keepdims=True)
    return spread, iota((1, pairs), 1).astype(jnp.float32) - start


def as_lanes(values, spread, place, tpl_count):
    owners = values.shape[0] // tpl_count
    pairs = spread.shape[1]
    wide = exact_dot(values.astype(jnp.float32), spread).reshape(owners, tpl_count, pairs)
    own = iota((1, tpl_count, pairs), 1).astype(jnp.float32) == place.reshape(1, 1, pairs)
    return jnp.sum(jnp.where(own, wide, 0.0), axis=1)


def count_before(hits):
    pairs = hits.shape[1]
    earlier = jnp.where(iota((pairs, pairs), 0) < iota((pairs, pairs), 1), 1.0, 0.0)
    return dot(hits.astype(jnp.bfloat16), earlier.astype(jnp.bfloat16))


def pack_kernel(cfg, half_ref, stations_ref, moveouts_ref, templates_hbm, *refs):
    blocks_hbm, (raw_ref, shapes_ref, packed_ref, in_sem, out_sems) = refs[:-5], refs[-5:]
    load = pltpu.make_async_copy(templates_hbm, raw_ref, in_sem)
    load.start()
    tpl_count, slot_count = stations_ref.shape
    pairs = tpl_count * slot_count
    devices, group, halves = cfg["devices"], cfg["group"], cfg["halves"]
    station_dev, rows, capacity = cfg["station_dev"], cfg["rows"], cfg["capacity"]
    spread, place = entry_lanes(tpl_count, slot_count)
    station = as_lanes(stations_ref[...], spread, place, tpl_count)
    device = jnp.floor((station + 0.5) * (1.0 / station_dev))
    onehot = jnp.where(iota((devices, pairs), 0).astype(jnp.float32) == device, 1.0, 0.0)
    rank = jnp.sum(onehot * count_before(onehot), axis=0, keepdims=True)
    half = jnp.floor((device + 0.5) * (1.0 / group))
    holder = device - half * group
    mine = half_ref[0].astype(jnp.float32)
    away = jnp.where(half == mine, 0.0, 1.0)
    fits = rank < float(capacity)

    shift = as_lanes(moveouts_ref[...], spread, place, tpl_count)
    row = station - device * station_dev
    code = ((place + 1.0) * (1 << cfg["row_bits"]) + row) * (1 << cfg["shift_bits"]) + shift
    code = code.astype(jnp.int32)
    at_rank = jnp.where(iota((LANES, pairs), 0).astype(jnp.float32) == rank, 1.0, 0.0).astype(jnp.bfloat16)
    at_holder = iota((group, pairs), 0).astype(jnp.float32) == holder
    digits = []
    for q in range(halves):
        for d in range(DIGITS):
            digit = (lax.shift_right_logical(code, 8 * d) & 255).astype(jnp.float32)
            marked = jnp.where(at_holder & (away == float(q)), digit, 0.0).astype(jnp.bfloat16)
            digits.append(
                lax.dot_general(marked, at_rank, (((1,), (1,)), ((), ())), preferred_element_type=jnp.float32)
            )
    codes = jnp.concatenate(digits, axis=1)

    load.wait()
    comps, length = raw_ref.shape[1], raw_ref.shape[3]
    for c in range(comps):
        values = raw_ref[:, c].astype(jnp.float32).reshape(pairs, length)
        centred = values - jnp.mean(values, axis=-1, keepdims=True)
        spread_c = jnp.sqrt(jnp.mean(centred * centred, axis=-1, keepdims=True) + 1e-05)
        shapes_ref[c] = (centred * (1.0 / spread_c)).astype(jnp.bfloat16)

    tile = SOURCES * rows
    tiles = group // SOURCES
    width = codes.shape[1]
    copies = []
    for block, block_hbm in enumerate(blocks_hbm):
        goal = jnp.where(fits & (away == float(block)), holder * rows + rank, -float(group * rows))
        for step in range(tiles):
            line = iota((tile, pairs), 0).astype(jnp.float32) + float(step * tile)
            total = jnp.zeros((tile, length), jnp.float32)
            for c in range(comps):
                pick = jnp.where(line == goal + float(c * capacity), 1.0, 0.0).astype(jnp.bfloat16)
                total = total + dot(pick, shapes_ref[c])
            if block == 0:
                here = codes[step * SOURCES : (step + 1) * SOURCES].reshape(SOURCES, 1, width)
                last = iota((SOURCES, rows, 1), 1) == rows - 1
                here = jnp.where(last, here, 0.0).reshape(tile, width)
                total = jnp.concatenate([total[:, :width] + here, total[:, width:]], axis=1)
            place_in = pl.ds(step * tile, tile)
            packed_ref[block, place_in, :] = total.astype(jnp.bfloat16)
            copies.append(
                pltpu.make_async_copy(
                    packed_ref.at[block, place_in], block_hbm.at[place_in], out_sems.at[block * tiles + step]
                )
            )
            copies[-1].start()
    for copy in copies:
        copy.wait()


def read_codes(first_block, block):
    width = DIGITS * LANES
    rows = first_block.shape[0] // SOURCES
    values = first_block[:, block * width : (block + 1) * width].astype(jnp.float32).reshape(SOURCES, rows, width)
    last = iota((1, rows, 1), 1) == rows - 1
    digits = jnp.sum(jnp.where(last, values, 0.0), axis=1)
    return sum(digits[:, d * LANES : (d + 1) * LANES] * float(256**d) for d in range(DIGITS))


def block_lines(cfg, codes, comps):
    capacity, rows = cfg["capacity"], cfg["rows"]
    tile = SOURCES * rows
    line = iota((SOURCES, rows, 1), 1).reshape(tile, 1)
    owner = iota((SOURCES, rows, 1), 0).reshape(tile, 1)
    comp = jnp.zeros((tile, 1), jnp.int32)
    for c in range(1, comps + 1):
        comp = comp + jnp.where(line >= c * capacity, 1, 0)
    slot = line - comp * capacity
    repeated = jnp.broadcast_to(codes.reshape(SOURCES, 1, LANES), (SOURCES, rows, LANES)).reshape(tile, LANES)
    chosen = (iota((tile, LANES), 1) == slot) & (comp < comps)
    code = jnp.sum(jnp.where(chosen, repeated, 0.0), axis=1, keepdims=True).astype(jnp.int32)
    shift_bits, row_bits = cfg["shift_bits"], cfg["row_bits"]
    shift = code & ((1 << shift_bits) - 1)
    row = lax.shift_right_logical(code, shift_bits) & ((1 << row_bits) - 1)
    tpl = lax.shift_right_logical(code, shift_bits + row_bits) - 1
    goal = jnp.where(tpl >= 0, comp * cfg["station_dev"] + row, -1)
    return shift, goal, jnp.where(tpl >= 0, owner * cfg["tpl_count"] + tpl, -1)


def cut_traces(cfg, shift, goal, waves):
    tile, seg_len, shift_bits = shift.shape[0], cfg["seg_len"], cfg["shift_bits"]
    pick = jnp.where(iota((tile, waves.shape[0]), 1) == goal, 1.0, 0.0).astype(jnp.bfloat16)
    x = dot(pick, waves)

    for bit in range(shift_bits - 1, 6, -1):
        step = 1 << bit
        width = seg_len + step
        if x.shape[1] < width + step:
            x = jnp.concatenate([x, jnp.zeros((tile, width + step - x.shape[1]), jnp.float32)], axis=1)
        x = jnp.where((shift & step) != 0, x[:, step : step + width], x[:, :width])
    for bit in range(min(shift_bits, 7) - 1, -1, -1):
        step = 1 << bit
        x = jnp.where((shift & step) != 0, pltpu.roll(x, x.shape[1] - step, 1), x)
    return x[:, :seg_len]


def line_sums(cfg, column):
    groups = SOURCES * cfg["tpl_count"]
    return jnp.where(iota((column.shape[0], groups), 1) == column, 1.0, 0.0).T.astype(jnp.bfloat16)


def levels_scale(cfg, segment, edges):
    length = cfg["length"]
    power = segment * segment
    ends = jnp.concatenate([power[:, :LAGS], power[:, length:]], axis=1)
    high = ends.astype(jnp.bfloat16)
    low = (ends - high.astype(jnp.float32)).astype(jnp.bfloat16)
    energy = dot(high, edges) + dot(low, edges) + jnp.sum(power[:, LAGS:length], axis=1, keepdims=True)
    return 1.0 / (length * jnp.sqrt(energy * (1.0 / length) + 1e-05))


def shape_spectra(shapes, forward):
    spectra = []
    for h in range(shapes.shape[1] // LAGS):
        part = shapes[:, h * LAGS : (h + 1) * LAGS]
        mine = dot(jnp.concatenate([part, part], axis=1), forward)
        spectra.append((mine[:, :LAGS], mine[:, LAGS:]))
    return spectra


def match_lines(mine, theirs, scale, inverse):
    real = imag = 0.0
    for (mine_r, mine_i), (theirs_r, theirs_i) in zip(mine, theirs):
        real = real + (theirs_r * mine_r + theirs_i * mine_i)
        imag = imag + (theirs_i * mine_r - theirs_r * mine_i)
    product = jnp.concatenate([real, imag], axis=1)
    high = product.astype(jnp.bfloat16)
    low = (product - high.astype(jnp.float32)).astype(jnp.bfloat16)
    return dot(jnp.concatenate([high, high, low], axis=1), inverse) * scale


def sum_lines(sums, left):
    total = 0.0
    for _ in range(3):
        part = left.astype(jnp.bfloat16)
        left = left - part.astype(jnp.float32)
        total = total + dot(sums, part)
    return total


def tables_of(table_ref):
    back = table_ref[2 * LAGS :, :]
    high, low = back[:, :LAGS], back[:, LAGS:]
    return table_ref[: 2 * LAGS, :], jnp.concatenate([high, low, high], axis=0)


def traces_of(cfg, codes, waves_ref, edges_ref, forward):
    comps, station_dev, samples = waves_ref.shape
    shift, goal, column = block_lines(cfg, codes, comps)
    segment = cut_traces(cfg, shift, goal, waves_ref[...].reshape(comps * station_dev, samples))
    narrow = segment.astype(jnp.bfloat16)
    sign = (1 - 2 * (iota((1, LAGS), 1) & 1)).astype(jnp.float32)

    def spectra():
        before = None
        for h in range(cfg["length"] // LAGS + 1):
            part = narrow[:, h * LAGS : (h + 1) * LAGS]
            here = dot(jnp.concatenate([part, part], axis=1), forward)
            here = here[:, :LAGS], here[:, LAGS:]
            if before is not None:
                yield before[0] + sign * here[1], before[1] - sign * here[0]
            before = here

    return spectra(), levels_scale(cfg, segment, edges_ref[...]), line_sums(cfg, column)


def near_kernel(cfg, first_ref, waves_ref, table_ref, edges_ref, sent_ref, *codes_ref):
    forward, inverse = tables_of(table_ref)
    if codes_ref:
        codes_ref[0][...] = read_codes(first_ref[...], 1)
    codes = read_codes(first_ref[...], 0)
    spectra, scale, sums = traces_of(cfg, codes, waves_ref, edges_ref, forward)
    sent_ref[...] = sum_lines(sums, match_lines(shape_spectra(first_ref[...], forward), spectra, scale, inverse))


def far_kernel(cfg, codes_ref, waves_ref, forward_ref, edges_ref, kept_ref, sums_ref):
    spectra, scale, sums = traces_of(cfg, codes_ref[...], waves_ref, edges_ref, forward_ref[...])
    sums_ref[...] = sums
    kept_ref[:, 2 * cfg["length"] :] = scale
    for h, (real, imag) in enumerate(spectra):
        kept_ref[:, 2 * h * LAGS : (2 * h + 1) * LAGS] = real
        kept_ref[:, (2 * h + 1) * LAGS : (2 * h + 2) * LAGS] = imag


def match_kernel(tiles, shapes_hbm, kept_hbm, sums_hbm, table_hbm, before_hbm, sent_ref, *scratch):
    shapes_ref, kept_ref, sums_ref, table_ref, before_ref, sems = scratch
    tile = shapes_ref.shape[0] // tiles
    groups = sent_ref.shape[0] // tiles
    length = shapes_ref.shape[1]

    def fetch(source, buffer, sem):
        copy = pltpu.make_async_copy(source, buffer, sems.at[sem])
        copy.start()
        return copy

    def lines(t):
        return pl.ds(t * tile, tile)

    table = fetch(table_hbm, table_ref, 0)
    shapes = fetch(shapes_hbm, shapes_ref, 1)
    kept = [fetch(kept_hbm.at[lines(0)], kept_ref.at[lines(0)], 4)]
    sums = fetch(sums_hbm, sums_ref, 2)
    before = fetch(before_hbm, before_ref, 3)
    kept += [fetch(kept_hbm.at[lines(t)], kept_ref.at[lines(t)], 4 + t) for t in range(1, tiles)]
    table.wait()
    shapes.wait()
    forward, inverse = tables_of(table_ref)
    for t in range(tiles):
        mine = shape_spectra(shapes_ref[lines(t), :], forward)
        kept[t].wait()
        theirs = kept_ref[lines(t), :]
        spectra = [
            (theirs[:, 2 * h * LAGS : (2 * h + 1) * LAGS], theirs[:, (2 * h + 1) * LAGS : (2 * h + 2) * LAGS])
            for h in range(length // LAGS)
        ]
        left = match_lines(mine, spectra, theirs[:, 2 * length :], inverse)
        if t == 0:
            sums.wait()
            before.wait()
        ends = pl.ds(t * groups, groups)
        sent_ref[ends, :] = before_ref[ends, :] + sum_lines(sums_ref[ends, :], left)


def stack_kernel(factor, parts_ref, stacks_ref, top_ref):
    stacks = jnp.sum(parts_ref[...], axis=0) * factor
    stacks_ref[...] = stacks
    top_ref[...] = jnp.broadcast_to(jnp.max(stacks, axis=0, keepdims=True), top_ref.shape)


def body(waveforms, templates, stations, moveouts):
    devices, group, halves = lax.axis_size(AXES), lax.axis_size(GROUP), lax.axis_size(HALF)
    tpl_count, slot_count = stations.shape
    comps, length = templates.shape[2:]
    station_dev, _, samples = waveforms.shape
    seg_len = length + LAGS
    pairs = tpl_count * slot_count
    capacity = (2 * pairs + devices - 1) // devices
    rows = -(-(comps * capacity + 1) // 16) * 16
    cfg = dict(
        devices=devices,
        group=group,
        halves=halves,
        station_dev=station_dev,
        tpl_count=tpl_count,
        capacity=capacity,
        rows=rows,
        length=length,
        seg_len=seg_len,
        shift_bits=bits_of(samples - seg_len + 1),
        row_bits=bits_of(station_dev),
    )
    table = jnp.asarray(transform_table(LAGS))
    edges = jnp.asarray(edge_table(LAGS))
    tiles = group // SOURCES
    tile = SOURCES * rows
    lines = group * rows
    sums_tile = SOURCES * tpl_count
    kept_len = 2 * length + LAGS
    whole = pl.BlockSpec(memory_space=pltpu.VMEM)
    anywhere = pl.BlockSpec(memory_space=pl.ANY)
    params = pltpu.CompilerParams(vmem_limit_bytes=60 * MIB)
    by_slot = templates.transpose(1, 2, 0, 3)
    waves = waveforms.transpose(1, 0, 2)
    half = lax.axis_index(HALF).reshape(1)

    def work(flops, size):
        return pl.CostEstimate(flops=flops, bytes_accessed=size, transcendentals=0)

    def exchange(x, axes):
        return lax.all_to_all(x, axes, split_axis=0, concat_axis=0, tiled=True)

    def same(shape):
        return pl.BlockSpec(shape, lambda i: (0,) * len(shape))

    def tiled(*shape):
        return pl.BlockSpec(shape, lambda i: (i, 0))

    block_shape = jax.ShapeDtypeStruct((lines, length), jnp.bfloat16)
    first, *second = pl.pallas_call(
        functools.partial(pack_kernel, cfg),
        out_shape=[block_shape] * halves,
        in_specs=[pl.BlockSpec(memory_space=pltpu.SMEM), whole, whole, anywhere],
        out_specs=[anywhere] * halves,
        scratch_shapes=[
            pltpu.VMEM(by_slot.shape, jnp.bfloat16),
            pltpu.VMEM((comps, pairs, length), jnp.bfloat16),
            pltpu.VMEM((halves, lines, length), jnp.bfloat16),
            pltpu.SemaphoreType.DMA,
            pltpu.SemaphoreType.DMA((halves * tiles,)),
        ],
        compiler_params=params,
        name="pack",
    )(half, stations, moveouts, by_slot)

    def exchange_rows(x):
        return exchange(x.reshape(group, rows, length), GROUP).reshape(lines, length)

    trace_flops = 2 * lines * (length // LAGS * 6 * LAGS * LAGS + 4 * LAGS * LAGS + comps * station_dev * samples)
    sent, *codes = pl.pallas_call(
        functools.partial(near_kernel, cfg),
        grid=(tiles,),
        out_shape=[jax.ShapeDtypeStruct((group * tpl_count, LAGS), jnp.float32)]
        + [jax.ShapeDtypeStruct((group, LANES), jnp.float32)] * (halves - 1),
        in_specs=[tiled(tile, length), same(waves.shape), same(table.shape), same(edges.shape)],
        out_specs=[tiled(sums_tile, LAGS)] + [tiled(SOURCES, LANES)] * (halves - 1),
        compiler_params=params,
        cost_estimate=work(1, 1),
        name="near",
    )(exchange_rows(first), waves, table, edges)
    if halves == 2:
        swapped = lax.ppermute(waves, HALF, [(0, 1), (1, 0)])
        sent, codes, swapped, second = lax.optimization_barrier((sent, codes[0], swapped, second[0]))
        second = exchange_rows(second)
        kept, sums = pl.pallas_call(
            functools.partial(far_kernel, cfg),
            grid=(tiles,),
            out_shape=[
                jax.ShapeDtypeStruct((lines, kept_len), jnp.float32),
                jax.ShapeDtypeStruct((group * tpl_count, tile), jnp.bfloat16),
            ],
            in_specs=[
                tiled(SOURCES, LANES),
                same(waves.shape),
                same((2 * LAGS, 2 * LAGS)),
                same(edges.shape),
            ],
            out_specs=[tiled(tile, kept_len), tiled(sums_tile, tile)],
            compiler_params=params,
            cost_estimate=work(trace_flops, lines * kept_len * 4),
            name="far",
        )(codes, swapped, table, edges)
        operands = (second, kept, sums, table, sent)
        sent = pl.pallas_call(
            functools.partial(match_kernel, tiles),
            out_shape=jax.ShapeDtypeStruct(sent.shape, jnp.float32),
            in_specs=[anywhere] * len(operands),
            out_specs=whole,
            scratch_shapes=[pltpu.VMEM(x.shape, x.dtype) for x in operands]
            + [pltpu.SemaphoreType.DMA((4 + tiles,))],
            compiler_params=pltpu.CompilerParams(vmem_limit_bytes=57 * MIB),
            name="match",
        )(*operands)

    parts = exchange(sent.reshape(group, tpl_count, LAGS), GROUP)
    stacks, top = pl.pallas_call(
        functools.partial(stack_kernel, math.sqrt(length / (comps * slot_count))),
        out_shape=[
            jax.ShapeDtypeStruct((tpl_count, LAGS), jnp.float32),
            jax.ShapeDtypeStruct((devices, 1, LAGS), jnp.float32),
        ],
        in_specs=[whole],
        out_specs=[whole, whole],
        compiler_params=pltpu.CompilerParams(vmem_limit_bytes=16 * MIB),
        name="stack",
    )(parts)
    return stacks, jnp.max(exchange(top, AXES), axis=(0, 1))


def solution(mesh):
    slow, fast = (mesh.shape[name] for name in GROUP)
    halves = 2 if slow % 2 == 0 else 1
    split = jax.sharding.Mesh(mesh.devices.reshape(halves, slow // halves, fast), AXES)
    placed = (
        P(AXES, None, None),
        P(AXES, None, None, None),
        P(AXES, None),
        P(AXES, None),
    )
    return jax.shard_map(body, mesh=split, in_specs=placed, out_specs=(P(AXES, None), P()), check_vma=False)
```

```python
import functools
import math

import jax
import jax.numpy as jnp
import ml_dtypes
import numpy as np
from jax import lax
from jax.experimental import pallas as pl
from jax.experimental.pallas import tpu as pltpu
from jax.sharding import PartitionSpec as P

LAGS = 256
HALF = "half"
GROUP = ("tmpl", "sta")
AXES = (HALF,) + GROUP
SOURCES = 8
DIGITS = 3
LANES = 128
MIB = 1024 * 1024


def bits_of(limit):
    return max(1, (limit - 1).bit_length())


def split_table(table):
    high = table.astype(ml_dtypes.bfloat16)
    return high, (table - high.astype(np.float64)).astype(ml_dtypes.bfloat16)


def transform_table(piece):
    size = 2 * piece
    angle = 2.0 * np.pi * (np.arange(piece) + 0.5) / size
    phase = np.arange(piece)[:, None] * angle[None, :]
    forward = np.concatenate([np.cos(phase), -np.sin(phase)], axis=1)
    inverse = np.concatenate([np.cos(phase.T), -np.sin(phase.T)], axis=0) * (2.0 / size)
    return np.concatenate([*split_table(forward), np.concatenate(split_table(inverse), axis=1)], axis=0)


def edge_table(lag_count):
    sample = np.arange(lag_count)[:, None]
    lag = np.arange(lag_count)[None, :]
    return np.concatenate([sample >= lag, sample < lag], axis=0).astype(ml_dtypes.bfloat16)


def iota(shape, axis):
    return lax.broadcasted_iota(jnp.int32, shape, axis)


def dot(a, b):
    return jnp.dot(a, b, preferred_element_type=jnp.float32)


def exact_dot(a, b):
    return jnp.dot(a, b, precision=lax.Precision.HIGHEST, preferred_element_type=jnp.float32)


def entry_lanes(tpl_count, slot_count):
    pairs = tpl_count * slot_count
    first = iota((slot_count, pairs), 0) * tpl_count
    entry = iota((slot_count, pairs), 1)
    spread = jnp.where((entry >= first) & (entry < first + tpl_count), 1.0, 0.0)
    start = jnp.sum(spread * first.astype(jnp.float32), axis=0, keepdims=True)
    return spread, iota((1, pairs), 1).astype(jnp.float32) - start


def as_lanes(values, spread, place, tpl_count):
    owners = values.shape[0] // tpl_count
    pairs = spread.shape[1]
    wide = exact_dot(values.astype(jnp.float32), spread).reshape(owners, tpl_count, pairs)
    own = iota((1, tpl_count, pairs), 1).astype(jnp.float32) == place.reshape(1, 1, pairs)
    return jnp.sum(jnp.where(own, wide, 0.0), axis=1)


def count_before(hits):
    pairs = hits.shape[1]
    earlier = jnp.where(iota((pairs, pairs), 0) < iota((pairs, pairs), 1), 1.0, 0.0)
    return dot(hits.astype(jnp.bfloat16), earlier.astype(jnp.bfloat16))


def pack_kernel(cfg, half_ref, stations_ref, moveouts_ref, templates_hbm, *refs):
    blocks_hbm, (raw_ref, shapes_ref, packed_ref, in_sem, out_sems) = refs[:-5], refs[-5:]
    load = pltpu.make_async_copy(templates_hbm, raw_ref, in_sem)
    load.start()
    tpl_count, slot_count = stations_ref.shape
    pairs = tpl_count * slot_count
    devices, group, halves = cfg["devices"], cfg["group"], cfg["halves"]
    station_dev, rows, capacity = cfg["station_dev"], cfg["rows"], cfg["capacity"]
    spread, place = entry_lanes(tpl_count, slot_count)
    station = as_lanes(stations_ref[...], spread, place, tpl_count)
    device = jnp.floor((station + 0.5) * (1.0 / station_dev))
    onehot = jnp.where(iota((devices, pairs), 0).astype(jnp.float32) == device, 1.0, 0.0)
    rank = jnp.sum(onehot * count_before(onehot), axis=0, keepdims=True)
    half = jnp.floor((device + 0.5) * (1.0 / group))
    holder = device - half * group
    mine = half_ref[0].astype(jnp.float32)
    away = jnp.where(half == mine, 0.0, 1.0)
    fits = rank < float(capacity)

    shift = as_lanes(moveouts_ref[...], spread, place, tpl_count)
    row = station - device * station_dev
    code = ((place + 1.0) * (1 << cfg["row_bits"]) + row) * (1 << cfg["shift_bits"]) + shift
    code = code.astype(jnp.int32)
    at_rank = jnp.where(iota((LANES, pairs), 0).astype(jnp.float32) == rank, 1.0, 0.0).astype(jnp.bfloat16)
    at_holder = iota((group, pairs), 0).astype(jnp.float32) == holder
    digits = []
    for q in range(halves):
        for d in range(DIGITS):
            digit = (lax.shift_right_logical(code, 8 * d) & 255).astype(jnp.float32)
            marked = jnp.where(at_holder & (away == float(q)), digit, 0.0).astype(jnp.bfloat16)
            digits.append(
                lax.dot_general(marked, at_rank, (((1,), (1,)), ((), ())), preferred_element_type=jnp.float32)
            )
    codes = jnp.concatenate(digits, axis=1)

    load.wait()
    comps, length = raw_ref.shape[1], raw_ref.shape[3]
    for c in range(comps):
        values = raw_ref[:, c].astype(jnp.float32).reshape(pairs, length)
        centred = values - jnp.mean(values, axis=-1, keepdims=True)
        spread_c = jnp.sqrt(jnp.mean(centred * centred, axis=-1, keepdims=True) + 1e-05)
        shapes_ref[c] = (centred * (1.0 / spread_c)).astype(jnp.bfloat16)

    tile = SOURCES * rows
    tiles = group // SOURCES
    width = codes.shape[1]
    copies = []
    for block, block_hbm in enumerate(blocks_hbm):
        goal = jnp.where(fits & (away == float(block)), holder * rows + rank, -float(group * rows))
        for step in range(tiles):
            line = iota((tile, pairs), 0).astype(jnp.float32) + float(step * tile)
            total = jnp.zeros((tile, length), jnp.float32)
            for c in range(comps):
                pick = jnp.where(line == goal + float(c * capacity), 1.0, 0.0).astype(jnp.bfloat16)
                total = total + dot(pick, shapes_ref[c])
            if block == 0:
                here = codes[step * SOURCES : (step + 1) * SOURCES].reshape(SOURCES, 1, width)
                last = iota((SOURCES, rows, 1), 1) == rows - 1
                here = jnp.where(last, here, 0.0).reshape(tile, width)
                total = jnp.concatenate([total[:, :width] + here, total[:, width:]], axis=1)
            place_in = pl.ds(step * tile, tile)
            packed_ref[block, place_in, :] = total.astype(jnp.bfloat16)
            copies.append(
                pltpu.make_async_copy(
                    packed_ref.at[block, place_in], block_hbm.at[place_in], out_sems.at[block * tiles + step]
                )
            )
            copies[-1].start()
    for copy in copies:
        copy.wait()


def read_codes(first_block, block):
    width = DIGITS * LANES
    rows = first_block.shape[0] // SOURCES
    values = first_block[:, block * width : (block + 1) * width].astype(jnp.float32).reshape(SOURCES, rows, width)
    last = iota((1, rows, 1), 1) == rows - 1
    digits = jnp.sum(jnp.where(last, values, 0.0), axis=1)
    return sum(digits[:, d * LANES : (d + 1) * LANES] * float(256**d) for d in range(DIGITS))


def block_lines(cfg, codes):
    capacity, rows, comps = cfg["capacity"], cfg["rows"], cfg["comps"]
    tile = SOURCES * rows
    line = iota((SOURCES, rows, 1), 1).reshape(tile, 1)
    owner = iota((SOURCES, rows, 1), 0).reshape(tile, 1)
    comp = jnp.zeros((tile, 1), jnp.int32)
    for c in range(1, comps + 1):
        comp = comp + jnp.where(line >= c * capacity, 1, 0)
    slot = line - comp * capacity
    repeated = jnp.broadcast_to(codes.reshape(SOURCES, 1, LANES), (SOURCES, rows, LANES)).reshape(tile, LANES)
    chosen = (iota((tile, LANES), 1) == slot) & (comp < comps)
    code = jnp.sum(jnp.where(chosen, repeated, 0.0), axis=1, keepdims=True).astype(jnp.int32)
    shift_bits, row_bits = cfg["shift_bits"], cfg["row_bits"]
    shift = code & ((1 << shift_bits) - 1)
    row = lax.shift_right_logical(code, shift_bits) & ((1 << row_bits) - 1)
    tpl = lax.shift_right_logical(code, shift_bits + row_bits) - 1
    goal = jnp.where(tpl >= 0, comp * cfg["station_dev"] + row, -1)
    return shift, goal, jnp.where(tpl >= 0, owner * cfg["tpl_count"] + tpl, -1)


def cut_traces(cfg, shift, goal, waves):
    tile, seg_len, shift_bits = shift.shape[0], cfg["seg_len"], cfg["shift_bits"]
    pick = jnp.where(iota((tile, waves.shape[0]), 1) == goal, 1.0, 0.0).astype(jnp.bfloat16)
    x = dot(pick, waves).astype(jnp.bfloat16)

    def choose(step, moved, still):
        flag = jnp.where((shift & step) != 0, 1.0, 0.0)
        return moved * flag.astype(jnp.bfloat16) + still * (1.0 - flag).astype(jnp.bfloat16)

    for bit in range(shift_bits - 1, 6, -1):
        step = 1 << bit
        width = seg_len + step
        if x.shape[1] < width + step:
            x = jnp.concatenate([x, jnp.zeros((tile, width + step - x.shape[1]), jnp.bfloat16)], axis=1)
        x = choose(step, x[:, step : step + width], x[:, :width])
    for bit in range(min(shift_bits, 7) - 1, -1, -1):
        step = 1 << bit
        x = choose(step, pltpu.roll(x, x.shape[1] - step, 1), x)
    return x[:, :seg_len]


def line_sums(cfg, column):
    groups = SOURCES * cfg["tpl_count"]
    return jnp.where(iota((column.shape[0], groups), 1) == column, 1.0, 0.0).T.astype(jnp.bfloat16)


def levels_scale(cfg, narrow, edges):
    length = cfg["length"]
    ends = jnp.concatenate([narrow[:, :LAGS], narrow[:, length:]], axis=1).astype(jnp.float32)
    ends = ends * ends
    high = ends.astype(jnp.bfloat16)
    low = (ends - high.astype(jnp.float32)).astype(jnp.bfloat16)
    middle = narrow[:, LAGS:length].astype(jnp.float32)
    energy = dot(high, edges) + dot(low, edges) + jnp.sum(middle * middle, axis=1, keepdims=True)
    return 1.0 / (length * jnp.sqrt(energy * (1.0 / length) + 1e-05))


def shape_spectra(shapes, forward):
    spectra = []
    for h in range(shapes.shape[1] // LAGS):
        part = shapes[:, h * LAGS : (h + 1) * LAGS]
        mine = dot(jnp.concatenate([part, part], axis=1), forward)
        spectra.append((mine[:, :LAGS], mine[:, LAGS:]))
    return spectra


def match_lines(mine, theirs, scale, inverse):
    real = imag = 0.0
    for (mine_r, mine_i), (theirs_r, theirs_i) in zip(mine, theirs):
        real = real + (theirs_r * mine_r + theirs_i * mine_i)
        imag = imag + (theirs_i * mine_r - theirs_r * mine_i)
    product = jnp.concatenate([real, imag], axis=1)
    high = product.astype(jnp.bfloat16)
    low = (product - high.astype(jnp.float32)).astype(jnp.bfloat16)
    return dot(jnp.concatenate([high, high, low], axis=1), inverse) * scale


def sum_lines(sums, left):
    total = 0.0
    for _ in range(3):
        part = left.astype(jnp.bfloat16)
        left = left - part.astype(jnp.float32)
        total = total + dot(sums, part)
    return total


def tables_of(table_ref):
    back = table_ref[2 * LAGS :, :]
    high, low = back[:, :LAGS], back[:, LAGS:]
    return table_ref[: 2 * LAGS, :], jnp.concatenate([high, low, high], axis=0)


def traces_of(cfg, codes, waves_refs, edges_ref, forward):
    shift, goal, column = block_lines(cfg, codes)
    waves = [ref[...].reshape(-1, ref.shape[2]) for ref in waves_refs]
    narrow = cut_traces(cfg, shift, goal, jnp.concatenate(waves, axis=0))
    sign = (1 - 2 * (iota((1, LAGS), 1) & 1)).astype(jnp.float32)

    def spectra():
        before = None
        for h in range(cfg["length"] // LAGS + 1):
            part = narrow[:, h * LAGS : (h + 1) * LAGS]
            here = dot(jnp.concatenate([part, part], axis=1), forward)
            here = here[:, :LAGS], here[:, LAGS:]
            if before is not None:
                yield before[0] + sign * here[1], before[1] - sign * here[0]
            before = here

    return spectra(), levels_scale(cfg, narrow, edges_ref[...]), line_sums(cfg, column)


def near_kernel(cfg, first_ref, waves_ref, table_ref, edges_ref, sent_ref, *codes_ref):
    forward, inverse = tables_of(table_ref)
    if codes_ref:
        codes_ref[0][...] = read_codes(first_ref[...], 1)
    codes = read_codes(first_ref[...], 0)
    spectra, scale, sums = traces_of(cfg, codes, [waves_ref], edges_ref, forward)
    sent_ref[...] = sum_lines(sums, match_lines(shape_spectra(first_ref[...], forward), spectra, scale, inverse))


def far_kernel(cfg, codes_ref, *refs):
    waves_refs, (forward_ref, edges_ref, kept_ref, sums_ref) = refs[:-4], refs[-4:]
    spectra, scale, sums = traces_of(cfg, codes_ref[...], waves_refs, edges_ref, forward_ref[...])
    sums_ref[...] = sums
    kept_ref[:, 2 * cfg["length"] :] = scale
    for h, (real, imag) in enumerate(spectra):
        kept_ref[:, 2 * h * LAGS : (2 * h + 1) * LAGS] = real
        kept_ref[:, (2 * h + 1) * LAGS : (2 * h + 2) * LAGS] = imag


def match_kernel(tiles, shapes_hbm, kept_hbm, sums_hbm, table_hbm, before_hbm, sent_ref, *scratch):
    shapes_ref, kept_ref, sums_ref, table_ref, before_ref, sems = scratch
    tile = shapes_ref.shape[0] // tiles
    groups = sent_ref.shape[0] // tiles
    length = shapes_ref.shape[1]

    def fetch(source, buffer, sem):
        copy = pltpu.make_async_copy(source, buffer, sems.at[sem])
        copy.start()
        return copy

    def lines(t):
        return pl.ds(t * tile, tile)

    table = fetch(table_hbm, table_ref, 0)
    shapes = fetch(shapes_hbm, shapes_ref, 1)
    kept = [fetch(kept_hbm.at[lines(0)], kept_ref.at[lines(0)], 4)]
    sums = fetch(sums_hbm, sums_ref, 2)
    before = fetch(before_hbm, before_ref, 3)
    kept += [fetch(kept_hbm.at[lines(t)], kept_ref.at[lines(t)], 4 + t) for t in range(1, tiles)]
    table.wait()
    shapes.wait()
    forward, inverse = tables_of(table_ref)
    for t in range(tiles):
        mine = shape_spectra(shapes_ref[lines(t), :], forward)
        kept[t].wait()
        theirs = kept_ref[lines(t), :]
        spectra = [
            (theirs[:, 2 * h * LAGS : (2 * h + 1) * LAGS], theirs[:, (2 * h + 1) * LAGS : (2 * h + 2) * LAGS])
            for h in range(length // LAGS)
        ]
        left = match_lines(mine, spectra, theirs[:, 2 * length :], inverse)
        if t == 0:
            sums.wait()
            before.wait()
        ends = pl.ds(t * groups, groups)
        sent_ref[ends, :] = before_ref[ends, :] + sum_lines(sums_ref[ends, :], left)


def stack_kernel(factor, parts_ref, stacks_ref, top_ref):
    stacks = jnp.sum(parts_ref[...], axis=0) * factor
    stacks_ref[...] = stacks
    top_ref[...] = jnp.broadcast_to(jnp.max(stacks, axis=0, keepdims=True), top_ref.shape)


def body(waveforms, templates, stations, moveouts):
    devices, group, halves = lax.axis_size(AXES), lax.axis_size(GROUP), lax.axis_size(HALF)
    tpl_count, slot_count = stations.shape
    comps, length = templates.shape[2:]
    station_dev, _, samples = waveforms.shape
    seg_len = length + LAGS
    pairs = tpl_count * slot_count
    capacity = (2 * pairs + devices - 1) // devices
    rows = -(-(comps * capacity + 1) // 16) * 16
    cfg = dict(
        devices=devices,
        group=group,
        halves=halves,
        station_dev=station_dev,
        tpl_count=tpl_count,
        comps=comps,
        capacity=capacity,
        rows=rows,
        length=length,
        seg_len=seg_len,
        shift_bits=bits_of(samples - seg_len + 1),
        row_bits=bits_of(station_dev),
    )
    table = jnp.asarray(transform_table(LAGS))
    edges = jnp.asarray(edge_table(LAGS))
    tiles = group // SOURCES
    tile = SOURCES * rows
    lines = group * rows
    sums_tile = SOURCES * tpl_count
    kept_len = 2 * length + LAGS
    whole = pl.BlockSpec(memory_space=pltpu.VMEM)
    anywhere = pl.BlockSpec(memory_space=pl.ANY)
    params = pltpu.CompilerParams(vmem_limit_bytes=60 * MIB)
    by_slot = templates.transpose(1, 2, 0, 3)
    waves = waveforms.transpose(1, 0, 2)
    half = lax.axis_index(HALF).reshape(1)

    def work(flops, size):
        return pl.CostEstimate(flops=flops, bytes_accessed=size, transcendentals=0)

    def exchange(x, axes):
        return lax.all_to_all(x, axes, split_axis=0, concat_axis=0, tiled=True)

    def same(shape):
        return pl.BlockSpec(shape, lambda i: (0,) * len(shape))

    def tiled(*shape):
        return pl.BlockSpec(shape, lambda i: (i, 0))

    block_shape = jax.ShapeDtypeStruct((lines, length), jnp.bfloat16)
    first, *second = pl.pallas_call(
        functools.partial(pack_kernel, cfg),
        out_shape=[block_shape] * halves,
        in_specs=[pl.BlockSpec(memory_space=pltpu.SMEM), whole, whole, anywhere],
        out_specs=[anywhere] * halves,
        scratch_shapes=[
            pltpu.VMEM(by_slot.shape, jnp.bfloat16),
            pltpu.VMEM((comps, pairs, length), jnp.bfloat16),
            pltpu.VMEM((halves, lines, length), jnp.bfloat16),
            pltpu.SemaphoreType.DMA,
            pltpu.SemaphoreType.DMA((halves * tiles,)),
        ],
        compiler_params=params,
        name="pack",
    )(half, stations, moveouts, by_slot)

    def exchange_rows(x):
        return exchange(x.reshape(group, rows, length), GROUP).reshape(lines, length)

    first = exchange_rows(first)
    if halves == 2:
        early = -(-2 * comps // 3)
        swapped = [
            lax.ppermute(x, HALF, [(0, 1), (1, 0)])
            for x in lax.optimization_barrier((waves[:early], waves[early:]))
        ]
        first, swapped[0], second = lax.optimization_barrier((first, swapped[0], second[0]))
        second = exchange_rows(second)
    sent, *codes = pl.pallas_call(
        functools.partial(near_kernel, cfg),
        grid=(tiles,),
        out_shape=[jax.ShapeDtypeStruct((group * tpl_count, LAGS), jnp.float32)]
        + [jax.ShapeDtypeStruct((group, LANES), jnp.float32)] * (halves - 1),
        in_specs=[tiled(tile, length), same(waves.shape), same(table.shape), same(edges.shape)],
        out_specs=[tiled(sums_tile, LAGS)] + [tiled(SOURCES, LANES)] * (halves - 1),
        compiler_params=params,
        cost_estimate=work(1, 1),
        name="near",
    )(first, waves, table, edges)
    if halves == 2:
        kept, sums = pl.pallas_call(
            functools.partial(far_kernel, cfg),
            grid=(tiles,),
            out_shape=[
                jax.ShapeDtypeStruct((lines, kept_len), jnp.float32),
                jax.ShapeDtypeStruct((group * tpl_count, tile), jnp.bfloat16),
            ],
            in_specs=[tiled(SOURCES, LANES)]
            + [same(x.shape) for x in swapped]
            + [same((2 * LAGS, 2 * LAGS)), same(edges.shape)],
            out_specs=[tiled(tile, kept_len), tiled(sums_tile, tile)],
            compiler_params=params,
            cost_estimate=work(1, 1),
            name="far",
        )(*codes, *swapped, table, edges)
        operands = (second, kept, sums, table, sent)
        sent = pl.pallas_call(
            functools.partial(match_kernel, tiles),
            out_shape=jax.ShapeDtypeStruct(sent.shape, jnp.float32),
            in_specs=[anywhere] * len(operands),
            out_specs=whole,
            scratch_shapes=[pltpu.VMEM(x.shape, x.dtype) for x in operands]
            + [pltpu.SemaphoreType.DMA((4 + tiles,))],
            compiler_params=pltpu.CompilerParams(vmem_limit_bytes=57 * MIB),
            name="match",
        )(*operands)

    parts = exchange(sent.reshape(group, tpl_count, LAGS), GROUP)
    stacks, top = pl.pallas_call(
        functools.partial(stack_kernel, math.sqrt(length / (comps * slot_count))),
        out_shape=[
            jax.ShapeDtypeStruct((tpl_count, LAGS), jnp.float32),
            jax.ShapeDtypeStruct((devices, 1, LAGS), jnp.float32),
        ],
        in_specs=[whole],
        out_specs=[whole, whole],
        compiler_params=pltpu.CompilerParams(vmem_limit_bytes=16 * MIB),
        name="stack",
    )(parts)
    return stacks, jnp.max(exchange(top, AXES), axis=(0, 1))


def solution(mesh):
    slow, fast = (mesh.shape[name] for name in GROUP)
    halves = 2 if slow % 2 == 0 else 1
    split = jax.sharding.Mesh(mesh.devices.reshape(halves, slow // halves, fast), AXES)
    placed = (
        P(AXES, None, None),
        P(AXES, None, None, None),
        P(AXES, None),
        P(AXES, None),
    )
    return jax.shard_map(body, mesh=split, in_specs=placed, out_specs=(P(AXES, None), P()), check_vma=False)
```

```python
import functools
import math

import jax
import jax.numpy as jnp
import ml_dtypes
import numpy as np
from jax import lax
from jax.experimental import pallas as pl
from jax.experimental.pallas import tpu as pltpu
from jax.sharding import PartitionSpec as P

LAGS = 256
HALF = "half"
GROUP = ("tmpl", "sta")
AXES = (HALF,) + GROUP
SOURCES = 8
DIGITS = 3
LANES = 128
MIB = 1024 * 1024


def bits_of(limit):
    return max(1, (limit - 1).bit_length())


def split_table(table):
    high = table.astype(ml_dtypes.bfloat16)
    return high, (table - high.astype(np.float64)).astype(ml_dtypes.bfloat16)


def transform_table(piece):
    size = 2 * piece
    angle = 2.0 * np.pi * (np.arange(piece) + 0.5) / size
    phase = np.arange(piece)[:, None] * angle[None, :]
    forward = np.concatenate([np.cos(phase), -np.sin(phase)], axis=1)
    inverse = np.concatenate([np.cos(phase.T), -np.sin(phase.T)], axis=0) * (2.0 / size)
    return np.concatenate([*split_table(forward), np.concatenate(split_table(inverse), axis=1)], axis=0)


def iota(shape, axis):
    return lax.broadcasted_iota(jnp.int32, shape, axis)


def dot(a, b):
    return jnp.dot(a, b, preferred_element_type=jnp.float32)


def exact_dot(a, b):
    return jnp.dot(a, b, precision=lax.Precision.HIGHEST, preferred_element_type=jnp.float32)


def entry_lanes(tpl_count, slot_count):
    pairs = tpl_count * slot_count
    first = iota((slot_count, pairs), 0) * tpl_count
    entry = iota((slot_count, pairs), 1)
    spread = jnp.where((entry >= first) & (entry < first + tpl_count), 1.0, 0.0)
    start = jnp.sum(spread * first.astype(jnp.float32), axis=0, keepdims=True)
    return spread, iota((1, pairs), 1).astype(jnp.float32) - start


def as_lanes(values, spread, place, tpl_count):
    owners = values.shape[0] // tpl_count
    pairs = spread.shape[1]
    wide = exact_dot(values.astype(jnp.float32), spread).reshape(owners, tpl_count, pairs)
    own = iota((1, tpl_count, pairs), 1).astype(jnp.float32) == place.reshape(1, 1, pairs)
    return jnp.sum(jnp.where(own, wide, 0.0), axis=1)


def count_before(hits):
    pairs = hits.shape[1]
    earlier = jnp.where(iota((pairs, pairs), 0) < iota((pairs, pairs), 1), 1.0, 0.0)
    return dot(hits.astype(jnp.bfloat16), earlier.astype(jnp.bfloat16))


def pack_kernel(cfg, block, half_ref, stations_ref, moveouts_ref, templates_hbm, packed_hbm, *scratch):
    raw_ref, shapes_ref, packed_ref, in_sem, out_sems = scratch
    load = pltpu.make_async_copy(templates_hbm, raw_ref, in_sem)
    load.start()
    tpl_count, slot_count = stations_ref.shape
    pairs = tpl_count * slot_count
    devices, group, halves = cfg["devices"], cfg["group"], cfg["halves"]
    station_dev, rows, capacity = cfg["station_dev"], cfg["rows"], cfg["capacity"]
    spread, place = entry_lanes(tpl_count, slot_count)
    station = as_lanes(stations_ref[...], spread, place, tpl_count)
    device = jnp.floor((station + 0.5) * (1.0 / station_dev))
    onehot = jnp.where(iota((devices, pairs), 0).astype(jnp.float32) == device, 1.0, 0.0)
    rank = jnp.sum(onehot * count_before(onehot), axis=0, keepdims=True)
    half = jnp.floor((device + 0.5) * (1.0 / group))
    holder = device - half * group
    mine = half_ref[0].astype(jnp.float32)
    away = jnp.where(half == mine, 0.0, 1.0)
    inside = (rank < float(capacity)) & (away == float(block))
    goal = jnp.where(inside, holder * rows + rank, -float(group * rows))

    codes = None
    if block == 0:
        shift = as_lanes(moveouts_ref[...], spread, place, tpl_count)
        row = station - device * station_dev
        code = ((place + 1.0) * (1 << cfg["row_bits"]) + row) * (1 << cfg["shift_bits"]) + shift
        code = code.astype(jnp.int32)
        at_rank = jnp.where(iota((LANES, pairs), 0).astype(jnp.float32) == rank, 1.0, 0.0).astype(jnp.bfloat16)
        at_holder = iota((group, pairs), 0).astype(jnp.float32) == holder
        digits = []
        for q in range(halves):
            for d in range(DIGITS):
                digit = (lax.shift_right_logical(code, 8 * d) & 255).astype(jnp.float32)
                marked = jnp.where(at_holder & (away == float(q)), digit, 0.0).astype(jnp.bfloat16)
                digits.append(
                    lax.dot_general(marked, at_rank, (((1,), (1,)), ((), ())), preferred_element_type=jnp.float32)
                )
        codes = jnp.concatenate(digits, axis=1)

    load.wait()
    comps, length = raw_ref.shape[1], raw_ref.shape[3]
    for c in range(comps):
        values = raw_ref[:, c].astype(jnp.float32).reshape(pairs, length)
        centred = values - jnp.mean(values, axis=-1, keepdims=True)
        spread_c = jnp.sqrt(jnp.mean(centred * centred, axis=-1, keepdims=True) + 1e-05)
        shapes_ref[c] = (centred * (1.0 / spread_c)).astype(jnp.bfloat16)

    tile = SOURCES * rows
    copies = []
    for step in range(group // SOURCES):
        line = iota((tile, pairs), 0).astype(jnp.float32) + float(step * tile)
        total = jnp.zeros((tile, length), jnp.float32)
        for c in range(comps):
            pick = jnp.where(line == goal + float(c * capacity), 1.0, 0.0).astype(jnp.bfloat16)
            total = total + dot(pick, shapes_ref[c])
        if codes is not None:
            width = codes.shape[1]
            here = codes[step * SOURCES : (step + 1) * SOURCES].reshape(SOURCES, 1, width)
            last = iota((SOURCES, rows, 1), 1) == rows - 1
            here = jnp.where(last, here, 0.0).reshape(tile, width)
            total = jnp.concatenate([total[:, :width] + here, total[:, width:]], axis=1)
        part = pl.ds(step * tile, tile)
        packed_ref[part, :] = total.astype(jnp.bfloat16)
        copies.append(pltpu.make_async_copy(packed_ref.at[part], packed_hbm.at[part], out_sems.at[step]))
        copies[-1].start()
    for copy in copies:
        copy.wait()


def read_codes(first_block, block):
    width = DIGITS * LANES
    rows = first_block.shape[0] // SOURCES
    values = first_block[:, block * width : (block + 1) * width].astype(jnp.float32).reshape(SOURCES, rows, width)
    last = iota((1, rows, 1), 1) == rows - 1
    digits = jnp.sum(jnp.where(last, values, 0.0), axis=1)
    return sum(digits[:, d * LANES : (d + 1) * LANES] * float(256**d) for d in range(DIGITS))


def block_lines(cfg, codes):
    capacity, rows, comps = cfg["capacity"], cfg["rows"], cfg["comps"]
    tile = SOURCES * rows
    line = iota((SOURCES, rows, 1), 1).reshape(tile, 1)
    owner = iota((SOURCES, rows, 1), 0).reshape(tile, 1)
    comp = jnp.zeros((tile, 1), jnp.int32)
    for c in range(1, comps + 1):
        comp = comp + jnp.where(line >= c * capacity, 1, 0)
    slot = line - comp * capacity
    repeated = jnp.broadcast_to(codes.reshape(SOURCES, 1, LANES), (SOURCES, rows, LANES)).reshape(tile, LANES)
    chosen = (iota((tile, LANES), 1) == slot) & (comp < comps)
    code = jnp.sum(jnp.where(chosen, repeated, 0.0), axis=1, keepdims=True).astype(jnp.int32)
    shift_bits, row_bits = cfg["shift_bits"], cfg["row_bits"]
    shift = code & ((1 << shift_bits) - 1)
    row = lax.shift_right_logical(code, shift_bits) & ((1 << row_bits) - 1)
    tpl = lax.shift_right_logical(code, shift_bits + row_bits) - 1
    goal = jnp.where(tpl >= 0, comp * cfg["station_dev"] + row, -1)
    return shift, goal, jnp.where(tpl >= 0, owner * cfg["tpl_count"] + tpl, -1)


def cut_traces(cfg, shift, goal, waves):
    tile, seg_len, shift_bits = shift.shape[0], cfg["seg_len"], cfg["shift_bits"]
    pick = jnp.where(iota((tile, waves.shape[0]), 1) == goal, 1.0, 0.0).astype(jnp.bfloat16)
    x = dot(pick, waves).astype(jnp.bfloat16)

    def choose(step, moved, still):
        flag = jnp.where((shift & step) != 0, 1.0, 0.0)
        return moved * flag.astype(jnp.bfloat16) + still * (1.0 - flag).astype(jnp.bfloat16)

    for bit in range(shift_bits - 1, 6, -1):
        step = 1 << bit
        width = seg_len + step
        if x.shape[1] < width + step:
            x = jnp.concatenate([x, jnp.zeros((tile, width + step - x.shape[1]), jnp.bfloat16)], axis=1)
        x = choose(step, x[:, step : step + width], x[:, :width])
    for bit in range(min(shift_bits, 7) - 1, -1, -1):
        step = 1 << bit
        x = choose(step, pltpu.roll(x, x.shape[1] - step, 1), x)
    return x[:, :seg_len]


def line_sums(cfg, column):
    groups = SOURCES * cfg["tpl_count"]
    return jnp.where(iota((column.shape[0], groups), 1) == column, 1.0, 0.0).T.astype(jnp.bfloat16)


def levels_scale(cfg, narrow):
    length = cfg["length"]
    sample, lag = iota((LAGS, LAGS), 0), iota((LAGS, LAGS), 1)
    edges = jnp.concatenate([jnp.where(sample >= lag, 1.0, 0.0), jnp.where(sample < lag, 1.0, 0.0)], axis=0)
    edges = edges.astype(jnp.bfloat16)
    ends = jnp.concatenate([narrow[:, :LAGS], narrow[:, length:]], axis=1).astype(jnp.float32)
    ends = ends * ends
    high = ends.astype(jnp.bfloat16)
    low = (ends - high.astype(jnp.float32)).astype(jnp.bfloat16)
    middle = narrow[:, LAGS:length].astype(jnp.float32)
    energy = dot(high, edges) + dot(low, edges) + jnp.sum(middle * middle, axis=1, keepdims=True)
    return 1.0 / (length * jnp.sqrt(energy * (1.0 / length) + 1e-05))


def shape_spectra(shapes, forward):
    spectra = []
    for h in range(shapes.shape[1] // LAGS):
        part = shapes[:, h * LAGS : (h + 1) * LAGS]
        mine = dot(jnp.concatenate([part, part], axis=1), forward)
        spectra.append((mine[:, :LAGS], mine[:, LAGS:]))
    return spectra


def match_lines(mine, theirs, scale, inverse):
    real = imag = 0.0
    for (mine_r, mine_i), (theirs_r, theirs_i) in zip(mine, theirs):
        real = real + (theirs_r * mine_r + theirs_i * mine_i)
        imag = imag + (theirs_i * mine_r - theirs_r * mine_i)
    product = jnp.concatenate([real, imag], axis=1)
    high = product.astype(jnp.bfloat16)
    low = (product - high.astype(jnp.float32)).astype(jnp.bfloat16)
    return dot(jnp.concatenate([high, high, low], axis=1), inverse) * scale


def sum_lines(sums, left):
    total = 0.0
    for _ in range(3):
        part = left.astype(jnp.bfloat16)
        left = left - part.astype(jnp.float32)
        total = total + dot(sums, part)
    return total


def tables_of(table_ref):
    back = table_ref[2 * LAGS :, :]
    high, low = back[:, :LAGS], back[:, LAGS:]
    return table_ref[: 2 * LAGS, :], jnp.concatenate([high, low, high], axis=0)


def traces_of(cfg, codes, waves_refs, table_hbm, table_ref, table_sem):
    first_step = pl.program_id(0) == 0
    load = pltpu.make_async_copy(table_hbm.at[pl.ds(0, table_ref.shape[0])], table_ref, table_sem)
    pl.when(first_step)(load.start)
    shift, goal, column = block_lines(cfg, codes)
    waves = jnp.concatenate([ref[...] for ref in waves_refs], axis=1)
    narrow = cut_traces(cfg, shift, goal, waves.reshape(-1, waves.shape[2]))
    scale = levels_scale(cfg, narrow)
    sums = line_sums(cfg, column)
    pl.when(first_step)(load.wait)
    forward = table_ref[: 2 * LAGS, :]
    sign = (1 - 2 * (iota((1, LAGS), 1) & 1)).astype(jnp.float32)

    def spectra():
        before = None
        for h in range(cfg["length"] // LAGS + 1):
            part = narrow[:, h * LAGS : (h + 1) * LAGS]
            here = dot(jnp.concatenate([part, part], axis=1), forward)
            here = here[:, :LAGS], here[:, LAGS:]
            if before is not None:
                yield before[0] + sign * here[1], before[1] - sign * here[0]
            before = here

    return spectra(), scale, sums


def near_kernel(cfg, first_ref, waves_ref, table_hbm, sent_ref, *rest):
    codes_ref, table = rest[:-2], rest[-2:]
    if codes_ref:
        codes_ref[0][...] = read_codes(first_ref[...], 1)
    spectra, scale, sums = traces_of(cfg, read_codes(first_ref[...], 0), [waves_ref], table_hbm, *table)
    forward, inverse = tables_of(table[0])
    sent_ref[...] = sum_lines(sums, match_lines(shape_spectra(first_ref[...], forward), spectra, scale, inverse))


def far_kernel(cfg, codes_ref, *refs):
    waves_refs, (table_hbm, kept_ref, sums_ref, *table) = refs[:-5], refs[-5:]
    spectra, scale, sums = traces_of(cfg, codes_ref[...], waves_refs, table_hbm, *table)
    sums_ref[...] = sums
    kept_ref[:, 2 * cfg["length"] :] = scale
    for h, (real, imag) in enumerate(spectra):
        kept_ref[:, 2 * h * LAGS : (2 * h + 1) * LAGS] = real
        kept_ref[:, (2 * h + 1) * LAGS : (2 * h + 2) * LAGS] = imag


def match_kernel(tiles, shapes_hbm, kept_hbm, sums_hbm, table_hbm, before_hbm, sent_ref, *scratch):
    shapes_ref, kept_ref, sums_ref, table_ref, before_ref, sems = scratch
    tile = shapes_ref.shape[0] // tiles
    groups = sent_ref.shape[0] // tiles
    length = shapes_ref.shape[1]
    copies = []

    def fetch(source, buffer, part=None):
        if part is not None:
            source, buffer = source.at[part], buffer.at[part]
        copies.append(pltpu.make_async_copy(source, buffer, sems.at[len(copies)]))
        copies[-1].start()
        return copies[-1]

    lines = [pl.ds(t * tile, tile) for t in range(tiles)]
    halves = [pl.ds(q * 2 * LAGS, 2 * LAGS) for q in range(2)]
    forward = fetch(table_hbm, table_ref, halves[0])
    shapes, kept = [], []
    for t in range(tiles):
        shapes.append(fetch(shapes_hbm, shapes_ref, lines[t]))
        kept.append(fetch(kept_hbm, kept_ref, lines[t]))
        if t == 0:
            inverse = fetch(table_hbm, table_ref, halves[1])
            sums = fetch(sums_hbm, sums_ref)
            before = fetch(before_hbm, before_ref)
    forward.wait()
    for t in range(tiles):
        shapes[t].wait()
        mine = shape_spectra(shapes_ref[lines[t], :], table_ref[: 2 * LAGS, :])
        kept[t].wait()
        theirs = kept_ref[lines[t], :]
        spectra = [
            (theirs[:, 2 * h * LAGS : (2 * h + 1) * LAGS], theirs[:, (2 * h + 1) * LAGS : (2 * h + 2) * LAGS])
            for h in range(length // LAGS)
        ]
        if t == 0:
            for copy in (inverse, sums, before):
                copy.wait()
        left = match_lines(mine, spectra, theirs[:, 2 * length :], tables_of(table_ref)[1])
        ends = pl.ds(t * groups, groups)
        sent_ref[ends, :] = before_ref[ends, :] + sum_lines(sums_ref[ends, :], left)


def stack_kernel(factor, parts_ref, stacks_ref, top_ref):
    stacks = jnp.sum(parts_ref[...], axis=0) * factor
    stacks_ref[...] = stacks
    top_ref[...] = jnp.broadcast_to(jnp.max(stacks, axis=0, keepdims=True), top_ref.shape)


def body(waveforms, templates, stations, moveouts):
    devices, group, halves = lax.axis_size(AXES), lax.axis_size(GROUP), lax.axis_size(HALF)
    tpl_count, slot_count = stations.shape
    comps, length = templates.shape[2:]
    station_dev, _, samples = waveforms.shape
    seg_len = length + LAGS
    pairs = tpl_count * slot_count
    capacity = (2 * pairs + devices - 1) // devices
    rows = -(-(comps * capacity + 1) // 16) * 16
    cfg = dict(
        devices=devices,
        group=group,
        halves=halves,
        station_dev=station_dev,
        tpl_count=tpl_count,
        comps=comps,
        capacity=capacity,
        rows=rows,
        length=length,
        seg_len=seg_len,
        shift_bits=bits_of(samples - seg_len + 1),
        row_bits=bits_of(station_dev),
    )
    table = jnp.asarray(transform_table(LAGS))
    tiles = group // SOURCES
    tile = SOURCES * rows
    lines = group * rows
    sums_tile = SOURCES * tpl_count
    kept_len = 2 * length + LAGS
    whole = pl.BlockSpec(memory_space=pltpu.VMEM)
    anywhere = pl.BlockSpec(memory_space=pl.ANY)
    params = pltpu.CompilerParams(vmem_limit_bytes=60 * MIB)
    by_slot = templates.transpose(1, 2, 0, 3)
    waves = waveforms.transpose(1, 0, 2)
    half = lax.axis_index(HALF).reshape(1)

    def work(flops, size):
        return pl.CostEstimate(flops=flops, bytes_accessed=size, transcendentals=0)

    def exchange(x, axes):
        return lax.all_to_all(x, axes, split_axis=0, concat_axis=0, tiled=True)

    def same(shape):
        return pl.BlockSpec(shape, lambda i: (0,) * len(shape))

    def tiled(*shape):
        return pl.BlockSpec(shape, lambda i: (i, 0))

    def pack(block):
        return pl.pallas_call(
            functools.partial(pack_kernel, cfg, block),
            out_shape=jax.ShapeDtypeStruct((lines, length), jnp.bfloat16),
            in_specs=[pl.BlockSpec(memory_space=pltpu.SMEM), whole, whole, anywhere],
            out_specs=anywhere,
            scratch_shapes=[
                pltpu.VMEM(by_slot.shape, jnp.bfloat16),
                pltpu.VMEM((comps, pairs, length), jnp.bfloat16),
                pltpu.VMEM((lines, length), jnp.bfloat16),
                pltpu.SemaphoreType.DMA,
                pltpu.SemaphoreType.DMA((tiles,)),
            ],
            compiler_params=params,
            cost_estimate=work(1, 1),
            name="pack",
        )(half, stations, moveouts, by_slot)

    def exchange_rows(x):
        return exchange(x.reshape(group, rows, length), GROUP).reshape(lines, length)

    first = exchange_rows(pack(0))
    if halves == 2:
        early = station_dev * 3 // 4 // 16 * 16
        swapped = [
            lax.ppermute(x, HALF, [(0, 1), (1, 0)])
            for x in lax.optimization_barrier((waves[:, :early], waves[:, early:]))
        ]
        first, swapped[0], second = lax.optimization_barrier((first, swapped[0], pack(1)))
        second = exchange_rows(second)
    sent, *codes = pl.pallas_call(
        functools.partial(near_kernel, cfg),
        grid=(tiles,),
        out_shape=[jax.ShapeDtypeStruct((group * tpl_count, LAGS), jnp.float32)]
        + [jax.ShapeDtypeStruct((group, LANES), jnp.float32)] * (halves - 1),
        in_specs=[tiled(tile, length), same(waves.shape), anywhere],
        out_specs=[tiled(sums_tile, LAGS)] + [tiled(SOURCES, LANES)] * (halves - 1),
        scratch_shapes=[pltpu.VMEM(table.shape, table.dtype), pltpu.SemaphoreType.DMA],
        compiler_params=params,
        cost_estimate=work(1, 1),
        name="near",
    )(first, waves, table)
    if halves == 2:
        kept, sums = pl.pallas_call(
            functools.partial(far_kernel, cfg),
            grid=(tiles,),
            out_shape=[
                jax.ShapeDtypeStruct((lines, kept_len), jnp.float32),
                jax.ShapeDtypeStruct((group * tpl_count, tile), jnp.bfloat16),
            ],
            in_specs=[tiled(SOURCES, LANES)] + [same(x.shape) for x in swapped] + [anywhere],
            out_specs=[tiled(tile, kept_len), tiled(sums_tile, tile)],
            scratch_shapes=[pltpu.VMEM((2 * LAGS, 2 * LAGS), table.dtype), pltpu.SemaphoreType.DMA],
            compiler_params=params,
            cost_estimate=work(1, 1),
            name="far",
        )(*codes, *swapped, table)
        operands = (second, kept, sums, table, sent)
        sent = pl.pallas_call(
            functools.partial(match_kernel, tiles),
            out_shape=jax.ShapeDtypeStruct(sent.shape, jnp.float32),
            in_specs=[anywhere] * len(operands),
            out_specs=whole,
            scratch_shapes=[pltpu.VMEM(x.shape, x.dtype) for x in operands]
            + [pltpu.SemaphoreType.DMA((4 + 2 * tiles,))],
            compiler_params=pltpu.CompilerParams(vmem_limit_bytes=57 * MIB),
            name="match",
        )(*operands)

    parts = exchange(sent.reshape(group, tpl_count, LAGS), GROUP)
    stacks, top = pl.pallas_call(
        functools.partial(stack_kernel, math.sqrt(length / (comps * slot_count))),
        out_shape=[
            jax.ShapeDtypeStruct((tpl_count, LAGS), jnp.float32),
            jax.ShapeDtypeStruct((devices, 1, LAGS), jnp.float32),
        ],
        in_specs=[whole],
        out_specs=[whole, whole],
        compiler_params=pltpu.CompilerParams(vmem_limit_bytes=16 * MIB),
        name="stack",
    )(parts)
    return stacks, jnp.max(exchange(top, AXES), axis=(0, 1))


def solution(mesh):
    slow, fast = (mesh.shape[name] for name in GROUP)
    halves = 2 if slow % 2 == 0 else 1
    split = jax.sharding.Mesh(mesh.devices.reshape(halves, slow // halves, fast), AXES)
    placed = (
        P(AXES, None, None),
        P(AXES, None, None, None),
        P(AXES, None),
        P(AXES, None),
    )
    return jax.shard_map(body, mesh=split, in_specs=placed, out_specs=(P(AXES, None), P()), check_vma=False)
```

```python
import functools
import math

import jax
import jax.numpy as jnp
import ml_dtypes
import numpy as np
from jax import lax
from jax.experimental import pallas as pl
from jax.experimental.pallas import tpu as pltpu
from jax.sharding import PartitionSpec as P

LAGS = 256
HALF = "half"
GROUP = ("tmpl", "sta")
AXES = (HALF,) + GROUP
SOURCES = 8
DIGITS = 3
LANES = 128
MIB = 1024 * 1024


def bits_of(limit):
    return max(1, (limit - 1).bit_length())


def split_table(table):
    high = table.astype(ml_dtypes.bfloat16)
    return high, (table - high.astype(np.float64)).astype(ml_dtypes.bfloat16)


def transform_table(piece):
    size = 2 * piece
    angle = 2.0 * np.pi * (np.arange(piece) + 0.5) / size
    phase = np.arange(piece)[:, None] * angle[None, :]
    forward = np.concatenate([np.cos(phase), -np.sin(phase)], axis=1)
    inverse = np.concatenate([np.cos(phase.T), -np.sin(phase.T)], axis=0) * (2.0 / size)
    return np.concatenate([*split_table(forward), np.concatenate(split_table(inverse), axis=1)], axis=0)


def edge_table(lag_count):
    sample = np.arange(lag_count)[:, None]
    lag = np.arange(lag_count)[None, :]
    return np.concatenate([sample >= lag, sample < lag], axis=0).astype(ml_dtypes.bfloat16)


def iota(shape, axis):
    return lax.broadcasted_iota(jnp.int32, shape, axis)


def dot(a, b):
    return jnp.dot(a, b, preferred_element_type=jnp.float32)


def exact_dot(a, b):
    return jnp.dot(a, b, precision=lax.Precision.HIGHEST, preferred_element_type=jnp.float32)


def entry_lanes(tpl_count, slot_count):
    pairs = tpl_count * slot_count
    first = iota((slot_count, pairs), 0) * tpl_count
    entry = iota((slot_count, pairs), 1)
    spread = jnp.where((entry >= first) & (entry < first + tpl_count), 1.0, 0.0)
    start = jnp.sum(spread * first.astype(jnp.float32), axis=0, keepdims=True)
    return spread, iota((1, pairs), 1).astype(jnp.float32) - start


def as_lanes(values, spread, place, tpl_count):
    owners = values.shape[0] // tpl_count
    pairs = spread.shape[1]
    wide = exact_dot(values.astype(jnp.float32), spread).reshape(owners, tpl_count, pairs)
    own = iota((1, tpl_count, pairs), 1).astype(jnp.float32) == place.reshape(1, 1, pairs)
    return jnp.sum(jnp.where(own, wide, 0.0), axis=1)


def count_before(hits):
    pairs = hits.shape[1]
    earlier = jnp.where(iota((pairs, pairs), 0) < iota((pairs, pairs), 1), 1.0, 0.0)
    return dot(hits.astype(jnp.bfloat16), earlier.astype(jnp.bfloat16))


def pack_kernel(cfg, half_ref, stations_ref, moveouts_ref, templates_hbm, *refs):
    blocks_hbm, (raw_ref, shapes_ref, packed_ref, in_sem, out_sems) = refs[:-5], refs[-5:]
    load = pltpu.make_async_copy(templates_hbm, raw_ref, in_sem)
    load.start()
    tpl_count, slot_count = stations_ref.shape
    pairs = tpl_count * slot_count
    devices, group, halves = cfg["devices"], cfg["group"], cfg["halves"]
    station_dev, rows, capacity = cfg["station_dev"], cfg["rows"], cfg["capacity"]
    spread, place = entry_lanes(tpl_count, slot_count)
    station = as_lanes(stations_ref[...], spread, place, tpl_count)
    device = jnp.floor((station + 0.5) * (1.0 / station_dev))
    onehot = jnp.where(iota((devices, pairs), 0).astype(jnp.float32) == device, 1.0, 0.0)
    rank = jnp.sum(onehot * count_before(onehot), axis=0, keepdims=True)
    half = jnp.floor((device + 0.5) * (1.0 / group))
    holder = device - half * group
    mine = half_ref[0].astype(jnp.float32)
    away = jnp.where(half == mine, 0.0, 1.0)
    fits = rank < float(capacity)

    shift = as_lanes(moveouts_ref[...], spread, place, tpl_count)
    row = station - device * station_dev
    code = ((place + 1.0) * (1 << cfg["row_bits"]) + row) * (1 << cfg["shift_bits"]) + shift
    code = code.astype(jnp.int32)
    at_rank = jnp.where(iota((LANES, pairs), 0).astype(jnp.float32) == rank, 1.0, 0.0).astype(jnp.bfloat16)
    at_holder = iota((group, pairs), 0).astype(jnp.float32) == holder
    digits = []
    for q in range(halves):
        for d in range(DIGITS):
            digit = (lax.shift_right_logical(code, 8 * d) & 255).astype(jnp.float32)
            marked = jnp.where(at_holder & (away == float(q)), digit, 0.0).astype(jnp.bfloat16)
            digits.append(
                lax.dot_general(marked, at_rank, (((1,), (1,)), ((), ())), preferred_element_type=jnp.float32)
            )
    codes = jnp.concatenate(digits, axis=1)

    load.wait()
    comps, length = raw_ref.shape[1], raw_ref.shape[3]
    for c in range(comps):
        values = raw_ref[:, c].astype(jnp.float32).reshape(pairs, length)
        centred = values - jnp.mean(values, axis=-1, keepdims=True)
        spread_c = jnp.sqrt(jnp.mean(centred * centred, axis=-1, keepdims=True) + 1e-05)
        shapes_ref[c] = (centred * (1.0 / spread_c)).astype(jnp.bfloat16)

    tile = SOURCES * rows
    tiles = group // SOURCES
    width = codes.shape[1]
    copies = []
    for block, block_hbm in enumerate(blocks_hbm):
        goal = jnp.where(fits & (away == float(block)), holder * rows + rank, -float(group * rows))
        for step in range(tiles):
            line = iota((tile, pairs), 0).astype(jnp.float32) + float(step * tile)
            total = jnp.zeros((tile, length), jnp.float32)
            for c in range(comps):
                pick = jnp.where(line == goal + float(c * capacity), 1.0, 0.0).astype(jnp.bfloat16)
                total = total + dot(pick, shapes_ref[c])
            if block == 0:
                here = codes[step * SOURCES : (step + 1) * SOURCES].reshape(SOURCES, 1, width)
                last = iota((SOURCES, rows, 1), 1) == rows - 1
                here = jnp.where(last, here, 0.0).reshape(tile, width)
                total = jnp.concatenate([total[:, :width] + here, total[:, width:]], axis=1)
            place_in = pl.ds(step * tile, tile)
            packed_ref[block, place_in, :] = total.astype(jnp.bfloat16)
            copies.append(
                pltpu.make_async_copy(
                    packed_ref.at[block, place_in], block_hbm.at[place_in], out_sems.at[block * tiles + step]
                )
            )
            copies[-1].start()
    for copy in copies:
        copy.wait()


def read_codes(first_block, block):
    width = DIGITS * LANES
    rows = first_block.shape[0] // SOURCES
    values = first_block[:, block * width : (block + 1) * width].astype(jnp.float32).reshape(SOURCES, rows, width)
    last = iota((1, rows, 1), 1) == rows - 1
    digits = jnp.sum(jnp.where(last, values, 0.0), axis=1)
    return sum(digits[:, d * LANES : (d + 1) * LANES] * float(256**d) for d in range(DIGITS))


def block_lines(cfg, codes):
    capacity, rows, comps = cfg["capacity"], cfg["rows"], cfg["comps"]
    tile = SOURCES * rows
    line = iota((SOURCES, rows, 1), 1).reshape(tile, 1)
    owner = iota((SOURCES, rows, 1), 0).reshape(tile, 1)
    comp = jnp.zeros((tile, 1), jnp.int32)
    for c in range(1, comps + 1):
        comp = comp + jnp.where(line >= c * capacity, 1, 0)
    slot = line - comp * capacity
    repeated = jnp.broadcast_to(codes.reshape(SOURCES, 1, LANES), (SOURCES, rows, LANES)).reshape(tile, LANES)
    chosen = (iota((tile, LANES), 1) == slot) & (comp < comps)
    code = jnp.sum(jnp.where(chosen, repeated, 0.0), axis=1, keepdims=True).astype(jnp.int32)
    shift_bits, row_bits = cfg["shift_bits"], cfg["row_bits"]
    shift = code & ((1 << shift_bits) - 1)
    row = lax.shift_right_logical(code, shift_bits) & ((1 << row_bits) - 1)
    tpl = lax.shift_right_logical(code, shift_bits + row_bits) - 1
    goal = jnp.where(tpl >= 0, comp * cfg["station_dev"] + row, -1)
    return shift, goal, jnp.where(tpl >= 0, owner * cfg["tpl_count"] + tpl, -1)


def cut_traces(cfg, shift, goal, waves):
    tile, seg_len, shift_bits = shift.shape[0], cfg["seg_len"], cfg["shift_bits"]
    pick = jnp.where(iota((tile, waves.shape[0]), 1) == goal, 1.0, 0.0).astype(jnp.bfloat16)
    x = dot(pick, waves).astype(jnp.bfloat16)

    def choose(step, moved, still):
        flag = jnp.where((shift & step) != 0, 1.0, 0.0)
        return moved * flag.astype(jnp.bfloat16) + still * (1.0 - flag).astype(jnp.bfloat16)

    for bit in range(shift_bits - 1, 6, -1):
        step = 1 << bit
        width = seg_len + step
        if x.shape[1] < width + step:
            x = jnp.concatenate([x, jnp.zeros((tile, width + step - x.shape[1]), jnp.bfloat16)], axis=1)
        x = choose(step, x[:, step : step + width], x[:, :width])
    for bit in range(min(shift_bits, 7) - 1, -1, -1):
        step = 1 << bit
        x = choose(step, pltpu.roll(x, x.shape[1] - step, 1), x)
    return x[:, :seg_len]


def line_sums(cfg, column):
    groups = SOURCES * cfg["tpl_count"]
    return jnp.where(iota((column.shape[0], groups), 1) == column, 1.0, 0.0).T.astype(jnp.bfloat16)


def levels_scale(cfg, narrow, edges):
    length = cfg["length"]
    ends = jnp.concatenate([narrow[:, :LAGS], narrow[:, length:]], axis=1).astype(jnp.float32)
    ends = ends * ends
    high = ends.astype(jnp.bfloat16)
    low = (ends - high.astype(jnp.float32)).astype(jnp.bfloat16)
    middle = narrow[:, LAGS:length].astype(jnp.float32)
    energy = dot(high, edges) + dot(low, edges) + jnp.sum(middle * middle, axis=1, keepdims=True)
    return 1.0 / (length * jnp.sqrt(energy * (1.0 / length) + 1e-05))


def shape_spectra(shapes, forward):
    spectra = []
    for h in range(shapes.shape[1] // LAGS):
        part = shapes[:, h * LAGS : (h + 1) * LAGS]
        mine = dot(jnp.concatenate([part, part], axis=1), forward)
        spectra.append((mine[:, :LAGS], mine[:, LAGS:]))
    return spectra


def match_lines(mine, theirs, scale, inverse):
    real = imag = 0.0
    for (mine_r, mine_i), (theirs_r, theirs_i) in zip(mine, theirs):
        real = real + (theirs_r * mine_r + theirs_i * mine_i)
        imag = imag + (theirs_i * mine_r - theirs_r * mine_i)
    product = jnp.concatenate([real, imag], axis=1)
    high = product.astype(jnp.bfloat16)
    low = (product - high.astype(jnp.float32)).astype(jnp.bfloat16)
    return dot(jnp.concatenate([high, high, low], axis=1), inverse) * scale


def sum_lines(sums, left):
    total = 0.0
    for _ in range(3):
        part = left.astype(jnp.bfloat16)
        left = left - part.astype(jnp.float32)
        total = total + dot(sums, part)
    return total


def tables_of(table_ref):
    back = table_ref[2 * LAGS :, :]
    high, low = back[:, :LAGS], back[:, LAGS:]
    return table_ref[: 2 * LAGS, :], jnp.concatenate([high, low, high], axis=0)


def traces_of(cfg, codes, waves_refs, edges_ref, forward):
    shift, goal, column = block_lines(cfg, codes)
    waves = [ref[...].reshape(-1, ref.shape[2]) for ref in waves_refs]
    narrow = cut_traces(cfg, shift, goal, jnp.concatenate(waves, axis=0))
    sign = (1 - 2 * (iota((1, LAGS), 1) & 1)).astype(jnp.float32)

    def spectra():
        before = None
        for h in range(cfg["length"] // LAGS + 1):
            part = narrow[:, h * LAGS : (h + 1) * LAGS]
            here = dot(jnp.concatenate([part, part], axis=1), forward)
            here = here[:, :LAGS], here[:, LAGS:]
            if before is not None:
                yield before[0] + sign * here[1], before[1] - sign * here[0]
            before = here

    return spectra(), levels_scale(cfg, narrow, edges_ref[...]), line_sums(cfg, column)


def near_kernel(cfg, first_ref, waves_ref, table_ref, edges_ref, sent_ref, *codes_ref):
    forward, inverse = tables_of(table_ref)
    if codes_ref:
        codes_ref[0][...] = read_codes(first_ref[...], 1)
    codes = read_codes(first_ref[...], 0)
    spectra, scale, sums = traces_of(cfg, codes, [waves_ref], edges_ref, forward)
    sent_ref[...] = sum_lines(sums, match_lines(shape_spectra(first_ref[...], forward), spectra, scale, inverse))


def far_kernel(cfg, codes_ref, *refs):
    waves_refs, (forward_ref, edges_ref, kept_ref, sums_ref) = refs[:-4], refs[-4:]
    spectra, scale, sums = traces_of(cfg, codes_ref[...], waves_refs, edges_ref, forward_ref[...])
    sums_ref[...] = sums
    kept_ref[:, 2 * cfg["length"] :] = scale
    for h, (real, imag) in enumerate(spectra):
        kept_ref[:, 2 * h * LAGS : (2 * h + 1) * LAGS] = real
        kept_ref[:, (2 * h + 1) * LAGS : (2 * h + 2) * LAGS] = imag


def match_kernel(tiles, shapes_hbm, kept_hbm, sums_hbm, table_hbm, before_hbm, sent_ref, *scratch):
    shapes_ref, kept_ref, sums_ref, table_ref, before_ref, sems = scratch
    tile = shapes_ref.shape[0] // tiles
    groups = sent_ref.shape[0] // tiles
    length = shapes_ref.shape[1]
    copies = []

    def fetch(source, buffer, part=None):
        if part is not None:
            source, buffer = source.at[part], buffer.at[part]
        copies.append(pltpu.make_async_copy(source, buffer, sems.at[len(copies)]))
        copies[-1].start()
        return copies[-1]

    lines = [pl.ds(t * tile, tile) for t in range(tiles)]
    halves = [pl.ds(q * 2 * LAGS, 2 * LAGS) for q in range(2)]
    forward = fetch(table_hbm, table_ref, halves[0])
    shapes, kept = [], []
    for t in range(tiles):
        shapes.append(fetch(shapes_hbm, shapes_ref, lines[t]))
        kept.append(fetch(kept_hbm, kept_ref, lines[t]))
        if t == 0:
            inverse = fetch(table_hbm, table_ref, halves[1])
            sums = fetch(sums_hbm, sums_ref)
            before = fetch(before_hbm, before_ref)
    forward.wait()
    for t in range(tiles):
        shapes[t].wait()
        mine = shape_spectra(shapes_ref[lines[t], :], table_ref[: 2 * LAGS, :])
        kept[t].wait()
        theirs = kept_ref[lines[t], :]
        spectra = [
            (theirs[:, 2 * h * LAGS : (2 * h + 1) * LAGS], theirs[:, (2 * h + 1) * LAGS : (2 * h + 2) * LAGS])
            for h in range(length // LAGS)
        ]
        if t == 0:
            for copy in (inverse, sums, before):
                copy.wait()
        left = match_lines(mine, spectra, theirs[:, 2 * length :], tables_of(table_ref)[1])
        ends = pl.ds(t * groups, groups)
        sent_ref[ends, :] = before_ref[ends, :] + sum_lines(sums_ref[ends, :], left)


def gate_kernel(rows_hbm, traces_hbm, same_rows_hbm):
    pass


def stack_kernel(factor, parts_ref, stacks_ref, top_ref):
    stacks = jnp.sum(parts_ref[...], axis=0) * factor
    stacks_ref[...] = stacks
    top_ref[...] = jnp.broadcast_to(jnp.max(stacks, axis=0, keepdims=True), top_ref.shape)


def body(waveforms, templates, stations, moveouts):
    devices, group, halves = lax.axis_size(AXES), lax.axis_size(GROUP), lax.axis_size(HALF)
    tpl_count, slot_count = stations.shape
    comps, length = templates.shape[2:]
    station_dev, _, samples = waveforms.shape
    seg_len = length + LAGS
    pairs = tpl_count * slot_count
    capacity = (2 * pairs + devices - 1) // devices
    rows = -(-(comps * capacity + 1) // 16) * 16
    cfg = dict(
        devices=devices,
        group=group,
        halves=halves,
        station_dev=station_dev,
        tpl_count=tpl_count,
        comps=comps,
        capacity=capacity,
        rows=rows,
        length=length,
        seg_len=seg_len,
        shift_bits=bits_of(samples - seg_len + 1),
        row_bits=bits_of(station_dev),
    )
    table = jnp.asarray(transform_table(LAGS))
    edges = jnp.asarray(edge_table(LAGS))
    tiles = group // SOURCES
    tile = SOURCES * rows
    lines = group * rows
    sums_tile = SOURCES * tpl_count
    kept_len = 2 * length + LAGS
    whole = pl.BlockSpec(memory_space=pltpu.VMEM)
    anywhere = pl.BlockSpec(memory_space=pl.ANY)
    params = pltpu.CompilerParams(vmem_limit_bytes=60 * MIB)
    by_slot = templates.transpose(1, 2, 0, 3)
    waves = waveforms.transpose(1, 0, 2)
    half = lax.axis_index(HALF).reshape(1)

    def work(flops, size):
        return pl.CostEstimate(flops=flops, bytes_accessed=size, transcendentals=0)

    def exchange(x, axes):
        return lax.all_to_all(x, axes, split_axis=0, concat_axis=0, tiled=True)

    def same(shape):
        return pl.BlockSpec(shape, lambda i: (0,) * len(shape))

    def tiled(*shape):
        return pl.BlockSpec(shape, lambda i: (i, 0))

    block_shape = jax.ShapeDtypeStruct((lines, length), jnp.bfloat16)
    first, *second = pl.pallas_call(
        functools.partial(pack_kernel, cfg),
        out_shape=[block_shape] * halves,
        in_specs=[pl.BlockSpec(memory_space=pltpu.SMEM), whole, whole, anywhere],
        out_specs=[anywhere] * halves,
        scratch_shapes=[
            pltpu.VMEM(by_slot.shape, jnp.bfloat16),
            pltpu.VMEM((comps, pairs, length), jnp.bfloat16),
            pltpu.VMEM((halves, lines, length), jnp.bfloat16),
            pltpu.SemaphoreType.DMA,
            pltpu.SemaphoreType.DMA((halves * tiles,)),
        ],
        compiler_params=params,
        cost_estimate=work(10**12, 1),
        name="pack",
    )(half, stations, moveouts, by_slot)

    def exchange_rows(x):
        return exchange(x.reshape(group, rows, length), GROUP).reshape(lines, length)

    first = exchange_rows(first)
    if halves == 2:
        swapped = lax.ppermute(waves, HALF, [(0, 1), (1, 0)])
        second = pl.pallas_call(
            gate_kernel,
            out_shape=block_shape,
            in_specs=[anywhere, anywhere],
            out_specs=anywhere,
            input_output_aliases={0: 0},
            compiler_params=params,
            cost_estimate=work(10**12, 1),
            name="gate",
        )(second[0], swapped)
        first, second = lax.optimization_barrier((first, second))
        second = exchange_rows(second)
    sent, *codes = pl.pallas_call(
        functools.partial(near_kernel, cfg),
        grid=(tiles,),
        out_shape=[jax.ShapeDtypeStruct((group * tpl_count, LAGS), jnp.float32)]
        + [jax.ShapeDtypeStruct((group, LANES), jnp.float32)] * (halves - 1),
        in_specs=[tiled(tile, length), same(waves.shape), same(table.shape), same(edges.shape)],
        out_specs=[tiled(sums_tile, LAGS)] + [tiled(SOURCES, LANES)] * (halves - 1),
        compiler_params=params,
        cost_estimate=work(1, 1),
        name="near",
    )(first, waves, table, edges)
    if halves == 2:
        kept, sums = pl.pallas_call(
            functools.partial(far_kernel, cfg),
            grid=(tiles,),
            out_shape=[
                jax.ShapeDtypeStruct((lines, kept_len), jnp.float32),
                jax.ShapeDtypeStruct((group * tpl_count, tile), jnp.bfloat16),
            ],
            in_specs=[tiled(SOURCES, LANES)]
            + [same(waves.shape)]
            + [same((2 * LAGS, 2 * LAGS)), same(edges.shape)],
            out_specs=[tiled(tile, kept_len), tiled(sums_tile, tile)],
            compiler_params=params,
            cost_estimate=work(1, 1),
            name="far",
        )(*codes, swapped, table, edges)
        operands = (second, kept, sums, table, sent)
        sent = pl.pallas_call(
            functools.partial(match_kernel, tiles),
            out_shape=jax.ShapeDtypeStruct(sent.shape, jnp.float32),
            in_specs=[anywhere] * len(operands),
            out_specs=whole,
            scratch_shapes=[pltpu.VMEM(x.shape, x.dtype) for x in operands]
            + [pltpu.SemaphoreType.DMA((4 + 2 * tiles,))],
            compiler_params=pltpu.CompilerParams(vmem_limit_bytes=57 * MIB),
            name="match",
        )(*operands)

    parts = exchange(sent.reshape(group, tpl_count, LAGS), GROUP)
    stacks, top = pl.pallas_call(
        functools.partial(stack_kernel, math.sqrt(length / (comps * slot_count))),
        out_shape=[
            jax.ShapeDtypeStruct((tpl_count, LAGS), jnp.float32),
            jax.ShapeDtypeStruct((devices, 1, LAGS), jnp.float32),
        ],
        in_specs=[whole],
        out_specs=[whole, whole],
        compiler_params=pltpu.CompilerParams(vmem_limit_bytes=16 * MIB),
        name="stack",
    )(parts)
    return stacks, jnp.max(exchange(top, AXES), axis=(0, 1))


def solution(mesh):
    slow, fast = (mesh.shape[name] for name in GROUP)
    halves = 2 if slow % 2 == 0 else 1
    split = jax.sharding.Mesh(mesh.devices.reshape(halves, slow // halves, fast), AXES)
    placed = (
        P(AXES, None, None),
        P(AXES, None, None, None),
        P(AXES, None),
        P(AXES, None),
    )
    return jax.shard_map(body, mesh=split, in_specs=placed, out_specs=(P(AXES, None), P()), check_vma=False)
```

```python
import functools
import math

import jax
import jax.numpy as jnp
import ml_dtypes
import numpy as np
from jax import lax
from jax.experimental import pallas as pl
from jax.experimental.pallas import tpu as pltpu
from jax.sharding import PartitionSpec as P

LAGS = 256
HALF = "half"
GROUP = ("tmpl", "sta")
AXES = (HALF,) + GROUP
SOURCES = 4
LANES = 128
MIB = 1024 * 1024


def bits_of(limit):
    return max(1, (limit - 1).bit_length())


def split_table(table):
    high = table.astype(ml_dtypes.bfloat16)
    return high, (table - high.astype(np.float64)).astype(ml_dtypes.bfloat16)


def transform_table(piece):
    size = 2 * piece
    angle = 2.0 * np.pi * (np.arange(piece) + 0.5) / size
    phase = np.arange(piece)[:, None] * angle[None, :]
    forward = np.concatenate([np.cos(phase), -np.sin(phase)], axis=1)
    inverse = np.concatenate([np.cos(phase.T), -np.sin(phase.T)], axis=0) * (2.0 / size)
    return np.concatenate([*split_table(forward), np.concatenate(split_table(inverse), axis=1)], axis=0)


def edge_table(lag_count):
    sample = np.arange(lag_count)[:, None]
    lag = np.arange(lag_count)[None, :]
    return np.concatenate([sample >= lag, sample < lag], axis=0).astype(ml_dtypes.bfloat16)


def iota(shape, axis):
    return lax.broadcasted_iota(jnp.int32, shape, axis)


def dot(a, b):
    return jnp.dot(a, b, preferred_element_type=jnp.float32)


def exact_dot(a, b):
    return jnp.dot(a, b, precision=lax.Precision.HIGHEST, preferred_element_type=jnp.float32)


def entry_lanes(tpl_count, slot_count):
    pairs = tpl_count * slot_count
    first = iota((slot_count, pairs), 0) * tpl_count
    entry = iota((slot_count, pairs), 1)
    spread = jnp.where((entry >= first) & (entry < first + tpl_count), 1.0, 0.0)
    start = jnp.sum(spread * first.astype(jnp.float32), axis=0, keepdims=True)
    return spread, iota((1, pairs), 1).astype(jnp.float32) - start


def as_lanes(values, spread, place, tpl_count):
    owners = values.shape[0] // tpl_count
    pairs = spread.shape[1]
    wide = exact_dot(values.astype(jnp.float32), spread).reshape(owners, tpl_count, pairs)
    own = iota((1, tpl_count, pairs), 1).astype(jnp.float32) == place.reshape(1, 1, pairs)
    return jnp.sum(jnp.where(own, wide, 0.0), axis=1)


def count_before(hits):
    pairs = hits.shape[1]
    earlier = jnp.where(iota((pairs, pairs), 0) < iota((pairs, pairs), 1), 1.0, 0.0)
    return dot(hits.astype(jnp.bfloat16), earlier.astype(jnp.bfloat16))


def list_kernel(cfg, half_ref, stations_ref, moveouts_ref, codes_ref, goal_ref):
    tpl_count, slot_count = stations_ref.shape
    pairs = tpl_count * slot_count
    devices, group, halves = cfg["devices"], cfg["group"], cfg["halves"]
    station_dev, rows, capacity = cfg["station_dev"], cfg["rows"], cfg["capacity"]
    spread, place = entry_lanes(tpl_count, slot_count)
    station = as_lanes(stations_ref[...], spread, place, tpl_count)
    shift = as_lanes(moveouts_ref[...], spread, place, tpl_count)
    device = jnp.floor((station + 0.5) * (1.0 / station_dev))
    onehot = jnp.where(iota((devices, pairs), 0).astype(jnp.float32) == device, 1.0, 0.0)
    rank = jnp.sum(onehot * count_before(onehot), axis=0, keepdims=True)
    half = jnp.floor((device + 0.5) * (1.0 / group))
    away = jnp.where(half == half_ref[0].astype(jnp.float32), 0.0, 1.0)
    place_of = (device - half * group) * halves + away
    goal_ref[...] = jnp.where(rank < float(capacity), place_of * rows + rank, -float(group * halves * rows))

    row = station - device * station_dev
    code = ((place + 1.0) * (1 << cfg["row_bits"]) + row) * (1 << cfg["shift_bits"]) + shift
    marked = jnp.where(iota((group * halves, pairs), 0).astype(jnp.float32) == place_of, code, 0.0)
    at_rank = jnp.where(iota((LANES, pairs), 0).astype(jnp.float32) == rank, 1.0, 0.0)
    codes = lax.dot_general(
        marked,
        at_rank,
        (((1,), (1,)), ((), ())),
        precision=lax.Precision.HIGHEST,
        preferred_element_type=jnp.float32,
    )
    codes_ref[...] = codes.astype(jnp.int32)


def pack_kernel(cfg, goal_ref, templates_hbm, packed_hbm, raw_ref, shapes_ref, packed_ref, in_sem, out_sems):
    load = pltpu.make_async_copy(templates_hbm, raw_ref, in_sem)
    load.start()
    goal = goal_ref[...]
    pairs = goal.shape[1]
    comps, length = raw_ref.shape[1], raw_ref.shape[3]
    load.wait()
    for c in range(comps):
        values = raw_ref[:, c].astype(jnp.float32).reshape(pairs, length)
        centred = values - jnp.mean(values, axis=-1, keepdims=True)
        spread_c = jnp.sqrt(jnp.mean(centred * centred, axis=-1, keepdims=True) + 1e-05)
        shapes_ref[c] = (centred * (1.0 / spread_c)).astype(jnp.bfloat16)

    tiles = out_sems.shape[0]
    tile = packed_ref.shape[0] // tiles
    copies = []
    for step in range(tiles):
        line = iota((tile, pairs), 0).astype(jnp.float32) + float(step * tile)
        total = jnp.zeros((tile, length), jnp.float32)
        for c in range(comps):
            pick = jnp.where(line == goal + float(c * cfg["capacity"]), 1.0, 0.0).astype(jnp.bfloat16)
            total = total + dot(pick, shapes_ref[c])
        part = pl.ds(step * tile, tile)
        packed_ref[part, :] = total.astype(jnp.bfloat16)
        copies.append(pltpu.make_async_copy(packed_ref.at[part], packed_hbm.at[part], out_sems.at[step]))
        copies[-1].start()
    for copy in copies:
        copy.wait()


def tile_lines(cfg, codes):
    capacity, rows, comps, halves = cfg["capacity"], cfg["rows"], cfg["comps"], cfg["halves"]
    blocks = SOURCES * halves
    tile = blocks * rows
    line = iota((blocks, rows, 1), 1).reshape(tile, 1)
    block = iota((blocks, rows, 1), 0).reshape(tile, 1)
    comp = jnp.zeros((tile, 1), jnp.int32)
    for c in range(1, comps + 1):
        comp = comp + jnp.where(line >= c * capacity, 1, 0)
    slot = line - comp * capacity
    owner = jnp.zeros((tile, 1), jnp.int32)
    for k in range(1, SOURCES):
        owner = owner + jnp.where(block >= k * halves, 1, 0)
    repeated = codes.astype(jnp.float32).reshape(blocks, 1, LANES)
    repeated = jnp.broadcast_to(repeated, (blocks, rows, LANES)).reshape(tile, LANES)
    chosen = (iota((tile, LANES), 1) == slot) & (comp < comps)
    code = jnp.sum(jnp.where(chosen, repeated, 0.0), axis=1, keepdims=True).astype(jnp.int32)
    shift_bits, row_bits = cfg["shift_bits"], cfg["row_bits"]
    shift = code & ((1 << shift_bits) - 1)
    row = lax.shift_right_logical(code, shift_bits) & ((1 << row_bits) - 1)
    tpl = lax.shift_right_logical(code, shift_bits + row_bits) - 1
    goal = ((block - owner * halves) * comps + comp) * cfg["station_dev"] + row
    return shift, jnp.where(tpl >= 0, goal, -1), jnp.where(tpl >= 0, owner * cfg["tpl_count"] + tpl, -1)


def cut_traces(cfg, shift, goal, waves):
    tile, seg_len, shift_bits = shift.shape[0], cfg["seg_len"], cfg["shift_bits"]
    pick = jnp.where(iota((tile, waves.shape[0]), 1) == goal, 1.0, 0.0).astype(jnp.bfloat16)
    x = dot(pick, waves).astype(jnp.bfloat16)

    def choose(step, moved, still):
        flag = jnp.where((shift & step) != 0, 1.0, 0.0)
        return moved * flag.astype(jnp.bfloat16) + still * (1.0 - flag).astype(jnp.bfloat16)

    for bit in range(shift_bits - 1, 6, -1):
        step = 1 << bit
        width = seg_len + step
        if x.shape[1] < width + step:
            x = jnp.concatenate([x, jnp.zeros((tile, width + step - x.shape[1]), jnp.bfloat16)], axis=1)
        x = choose(step, x[:, step : step + width], x[:, :width])
    for bit in range(min(shift_bits, 7) - 1, -1, -1):
        step = 1 << bit
        x = choose(step, pltpu.roll(x, x.shape[1] - step, 1), x)
    return x[:, :seg_len]


def line_sums(cfg, column):
    groups = SOURCES * cfg["tpl_count"]
    return jnp.where(iota((column.shape[0], groups), 1) == column, 1.0, 0.0).T.astype(jnp.bfloat16)


def levels_scale(cfg, narrow, edges):
    length = cfg["length"]
    ends = jnp.concatenate([narrow[:, :LAGS], narrow[:, length:]], axis=1).astype(jnp.float32)
    ends = ends * ends
    high = ends.astype(jnp.bfloat16)
    low = (ends - high.astype(jnp.float32)).astype(jnp.bfloat16)
    middle = narrow[:, LAGS:length].astype(jnp.float32)
    energy = dot(high, edges) + dot(low, edges) + jnp.sum(middle * middle, axis=1, keepdims=True)
    return 1.0 / (length * jnp.sqrt(energy * (1.0 / length) + 1e-05))


def shape_spectra(shapes, forward):
    spectra = []
    for h in range(shapes.shape[1] // LAGS):
        part = shapes[:, h * LAGS : (h + 1) * LAGS]
        mine = dot(jnp.concatenate([part, part], axis=1), forward)
        spectra.append((mine[:, :LAGS], mine[:, LAGS:]))
    return spectra


def match_lines(mine, theirs, scale, inverse):
    real = imag = 0.0
    for (mine_r, mine_i), (theirs_r, theirs_i) in zip(mine, theirs):
        real = real + (theirs_r * mine_r + theirs_i * mine_i)
        imag = imag + (theirs_i * mine_r - theirs_r * mine_i)
    product = jnp.concatenate([real, imag], axis=1)
    high = product.astype(jnp.bfloat16)
    low = (product - high.astype(jnp.float32)).astype(jnp.bfloat16)
    return dot(jnp.concatenate([high, high, low], axis=1), inverse) * scale


def sum_lines(sums, left):
    total = 0.0
    for _ in range(3):
        part = left.astype(jnp.bfloat16)
        left = left - part.astype(jnp.float32)
        total = total + dot(sums, part)
    return total


def tables_of(table_ref):
    back = table_ref[2 * LAGS :, :]
    high, low = back[:, :LAGS], back[:, LAGS:]
    return table_ref[: 2 * LAGS, :], jnp.concatenate([high, low, high], axis=0)


def trace_kernel(cfg, codes_ref, *refs):
    waves_refs, (table_ref, edges_ref, kept_ref, sums_ref) = refs[:-4], refs[-4:]
    shift, goal, column = tile_lines(cfg, codes_ref[...])
    waves = [ref[...].reshape(-1, ref.shape[2]) for ref in waves_refs]
    narrow = cut_traces(cfg, shift, goal, jnp.concatenate(waves, axis=0))
    kept_ref[:, 2 * cfg["length"] :] = levels_scale(cfg, narrow, edges_ref[...])
    sums_ref[...] = line_sums(cfg, column)

    sign = (1 - 2 * (iota((1, LAGS), 1) & 1)).astype(jnp.float32)
    before = None
    for h in range(cfg["length"] // LAGS + 1):
        part = narrow[:, h * LAGS : (h + 1) * LAGS]
        here = dot(jnp.concatenate([part, part], axis=1), table_ref[...])
        here = here[:, :LAGS], here[:, LAGS:]
        if before is not None:
            kept_ref[:, (2 * h - 2) * LAGS : (2 * h - 1) * LAGS] = before[0] + sign * here[1]
            kept_ref[:, (2 * h - 1) * LAGS : 2 * h * LAGS] = before[1] - sign * here[0]
        before = here


def match_kernel(tiles, shapes_hbm, kept_hbm, sums_hbm, table_hbm, sent_ref, *scratch):
    shapes_ref, kept_ref, sums_ref, table_ref, sems = scratch
    tile = shapes_ref.shape[0] // tiles
    groups = sent_ref.shape[0] // tiles
    length = shapes_ref.shape[1]
    copies = []

    def fetch(source, buffer, part=None):
        if part is not None:
            source, buffer = source.at[part], buffer.at[part]
        copies.append(pltpu.make_async_copy(source, buffer, sems.at[len(copies)]))
        copies[-1].start()
        return copies[-1]

    lines = [pl.ds(t * tile, tile) for t in range(tiles)]
    halves = [pl.ds(q * 2 * LAGS, 2 * LAGS) for q in range(2)]
    forward = fetch(table_hbm, table_ref, halves[0])
    shapes, kept = [], []
    for t in range(tiles):
        shapes.append(fetch(shapes_hbm, shapes_ref, lines[t]))
        kept.append(fetch(kept_hbm, kept_ref, lines[t]))
        if t == 0:
            inverse = fetch(table_hbm, table_ref, halves[1])
            sums = fetch(sums_hbm, sums_ref)
    forward.wait()
    for t in range(tiles):
        shapes[t].wait()
        mine = shape_spectra(shapes_ref[lines[t], :], table_ref[: 2 * LAGS, :])
        kept[t].wait()
        theirs = kept_ref[lines[t], :]
        spectra = [
            (theirs[:, 2 * h * LAGS : (2 * h + 1) * LAGS], theirs[:, (2 * h + 1) * LAGS : (2 * h + 2) * LAGS])
            for h in range(length // LAGS)
        ]
        if t == 0:
            for copy in (inverse, sums):
                copy.wait()
        left = match_lines(mine, spectra, theirs[:, 2 * length :], tables_of(table_ref)[1])
        ends = pl.ds(t * groups, groups)
        sent_ref[ends, :] = sum_lines(sums_ref[ends, :], left)


def stack_kernel(factor, parts_ref, stacks_ref, top_ref):
    stacks = jnp.sum(parts_ref[...], axis=0) * factor
    stacks_ref[...] = stacks
    top_ref[...] = jnp.broadcast_to(jnp.max(stacks, axis=0, keepdims=True), top_ref.shape)


def body(waveforms, templates, stations, moveouts):
    devices, group, halves = lax.axis_size(AXES), lax.axis_size(GROUP), lax.axis_size(HALF)
    tpl_count, slot_count = stations.shape
    comps, length = templates.shape[2:]
    station_dev, _, samples = waveforms.shape
    seg_len = length + LAGS
    pairs = tpl_count * slot_count
    capacity = (2 * pairs + devices - 1) // devices
    rows = -(-comps * capacity // 16) * 16
    cfg = dict(
        devices=devices,
        group=group,
        halves=halves,
        station_dev=station_dev,
        tpl_count=tpl_count,
        comps=comps,
        capacity=capacity,
        rows=rows,
        length=length,
        seg_len=seg_len,
        shift_bits=bits_of(samples - seg_len + 1),
        row_bits=bits_of(station_dev),
    )
    table = jnp.asarray(transform_table(LAGS))
    edges = jnp.asarray(edge_table(LAGS))
    tiles = group // SOURCES
    tile = SOURCES * halves * rows
    lines = group * halves * rows
    sums_tile = SOURCES * tpl_count
    kept_len = 2 * length + LAGS
    whole = pl.BlockSpec(memory_space=pltpu.VMEM)
    anywhere = pl.BlockSpec(memory_space=pl.ANY)
    params = pltpu.CompilerParams(vmem_limit_bytes=60 * MIB)
    by_slot = templates.transpose(1, 2, 0, 3)
    waves = waveforms.transpose(1, 0, 2)
    half = lax.axis_index(HALF).reshape(1)

    def work(flops, size):
        return pl.CostEstimate(flops=flops, bytes_accessed=size, transcendentals=0)

    def exchange(x, axes):
        return lax.all_to_all(x, axes, split_axis=0, concat_axis=0, tiled=True)

    def same(shape):
        return pl.BlockSpec(shape, lambda i: (0,) * len(shape))

    def tiled(*shape):
        return pl.BlockSpec(shape, lambda i: (i, 0))

    traces = [waves] + [lax.ppermute(waves, HALF, [(0, 1), (1, 0)])] * (halves - 1)
    codes, goal = pl.pallas_call(
        functools.partial(list_kernel, cfg),
        out_shape=[
            jax.ShapeDtypeStruct((group * halves, LANES), jnp.int32),
            jax.ShapeDtypeStruct((1, pairs), jnp.float32),
        ],
        in_specs=[pl.BlockSpec(memory_space=pltpu.SMEM), whole, whole],
        out_specs=[whole, whole],
        compiler_params=params,
        cost_estimate=work(1, 1),
        name="lists",
    )(half, stations, moveouts)
    codes = exchange(codes.reshape(group, halves, LANES), GROUP).reshape(group * halves, LANES)

    pack_tiles = 4
    packed = pl.pallas_call(
        functools.partial(pack_kernel, cfg),
        out_shape=jax.ShapeDtypeStruct((lines, length), jnp.bfloat16),
        in_specs=[whole, anywhere],
        out_specs=anywhere,
        scratch_shapes=[
            pltpu.VMEM(by_slot.shape, jnp.bfloat16),
            pltpu.VMEM((comps, pairs, length), jnp.bfloat16),
            pltpu.VMEM((lines, length), jnp.bfloat16),
            pltpu.SemaphoreType.DMA,
            pltpu.SemaphoreType.DMA((pack_tiles,)),
        ],
        compiler_params=params,
        cost_estimate=work(5 * 10**9, 1),
        name="pack",
    )(goal, by_slot)
    codes, packed = lax.optimization_barrier((codes, packed))
    arrived = exchange(packed.reshape(group, halves * rows, length), GROUP).reshape(lines, length)

    kept, sums = pl.pallas_call(
        functools.partial(trace_kernel, cfg),
        grid=(tiles,),
        out_shape=[
            jax.ShapeDtypeStruct((lines, kept_len), jnp.float32),
            jax.ShapeDtypeStruct((group * tpl_count, tile), jnp.bfloat16),
        ],
        in_specs=[tiled(SOURCES * halves, LANES)]
        + [same(waves.shape)] * halves
        + [same((2 * LAGS, 2 * LAGS)), same(edges.shape)],
        out_specs=[tiled(tile, kept_len), tiled(sums_tile, tile)],
        compiler_params=params,
        cost_estimate=work(10**12, 1),
        name="traces",
    )(codes, *traces, table, edges)
    operands = (arrived, kept, sums, table)
    sent = pl.pallas_call(
        functools.partial(match_kernel, tiles),
        out_shape=jax.ShapeDtypeStruct((group * tpl_count, LAGS), jnp.float32),
        in_specs=[anywhere] * len(operands),
        out_specs=whole,
        scratch_shapes=[pltpu.VMEM(x.shape, x.dtype) for x in operands]
        + [pltpu.SemaphoreType.DMA((3 + 2 * tiles,))],
        compiler_params=pltpu.CompilerParams(vmem_limit_bytes=57 * MIB),
        name="match",
    )(*operands)

    parts = exchange(sent.reshape(group, tpl_count, LAGS), GROUP)
    stacks, top = pl.pallas_call(
        functools.partial(stack_kernel, math.sqrt(length / (comps * slot_count))),
        out_shape=[
            jax.ShapeDtypeStruct((tpl_count, LAGS), jnp.float32),
            jax.ShapeDtypeStruct((devices, 1, LAGS), jnp.float32),
        ],
        in_specs=[whole],
        out_specs=[whole, whole],
        compiler_params=pltpu.CompilerParams(vmem_limit_bytes=16 * MIB),
        name="stack",
    )(parts)
    return stacks, jnp.max(exchange(top, AXES), axis=(0, 1))


def solution(mesh):
    slow, fast = (mesh.shape[name] for name in GROUP)
    halves = 2 if slow % 2 == 0 else 1
    split = jax.sharding.Mesh(mesh.devices.reshape(halves, slow // halves, fast), AXES)
    placed = (
        P(AXES, None, None),
        P(AXES, None, None, None),
        P(AXES, None),
        P(AXES, None),
    )
    return jax.shard_map(body, mesh=split, in_specs=placed, out_specs=(P(AXES, None), P()), check_vma=False)
```

```python
import functools
import math

import jax
import jax.numpy as jnp
import ml_dtypes
import numpy as np
from jax import lax
from jax.experimental import pallas as pl
from jax.experimental.pallas import tpu as pltpu
from jax.sharding import PartitionSpec as P

LAGS = 256
HALF = "half"
GROUP = ("tmpl", "sta")
AXES = (HALF,) + GROUP
SOURCES = 4
ROWS = 16
DIGITS = 3
LANES = 128
MIB = 1024 * 1024


def bits_of(limit):
    return max(1, (limit - 1).bit_length())


def split_table(table):
    high = table.astype(ml_dtypes.bfloat16)
    return high, (table - high.astype(np.float64)).astype(ml_dtypes.bfloat16)


def transform_table(piece):
    size = 2 * piece
    angle = 2.0 * np.pi * (np.arange(piece) + 0.5) / size
    phase = np.arange(piece)[:, None] * angle[None, :]
    forward = np.concatenate([np.cos(phase), -np.sin(phase)], axis=1)
    inverse = np.concatenate([np.cos(phase.T), -np.sin(phase.T)], axis=0) * (2.0 / size)
    return np.concatenate([*split_table(forward), np.concatenate(split_table(inverse), axis=1)], axis=0)


def edge_table(lag_count):
    sample = np.arange(lag_count)[:, None]
    lag = np.arange(lag_count)[None, :]
    return np.concatenate([sample >= lag, sample < lag], axis=0).astype(ml_dtypes.bfloat16)


def iota(shape, axis):
    return lax.broadcasted_iota(jnp.int32, shape, axis)


def dot(a, b):
    return jnp.dot(a, b, preferred_element_type=jnp.float32)


def exact_dot(a, b):
    return jnp.dot(a, b, precision=lax.Precision.HIGHEST, preferred_element_type=jnp.float32)


def entry_lanes(tpl_count, slot_count):
    pairs = tpl_count * slot_count
    first = iota((slot_count, pairs), 0) * tpl_count
    entry = iota((slot_count, pairs), 1)
    spread = jnp.where((entry >= first) & (entry < first + tpl_count), 1.0, 0.0)
    start = jnp.sum(spread * first.astype(jnp.float32), axis=0, keepdims=True)
    return spread, iota((1, pairs), 1).astype(jnp.float32) - start


def as_lanes(values, spread, place, tpl_count):
    owners = values.shape[0] // tpl_count
    pairs = spread.shape[1]
    wide = exact_dot(values.astype(jnp.float32), spread).reshape(owners, tpl_count, pairs)
    own = iota((1, tpl_count, pairs), 1).astype(jnp.float32) == place.reshape(1, 1, pairs)
    return jnp.sum(jnp.where(own, wide, 0.0), axis=1)


def count_before(hits):
    pairs = hits.shape[1]
    earlier = jnp.where(iota((pairs, pairs), 0) < iota((pairs, pairs), 1), 1.0, 0.0)
    return dot(hits.astype(jnp.bfloat16), earlier.astype(jnp.bfloat16))


def first_kernel(
    cfg, half_ref, stations_ref, moveouts_ref, templates_hbm, first_hbm, shapes_hbm, place_ref, raw_ref, shapes_ref, packed_ref, sems
):
    load = pltpu.make_async_copy(templates_hbm, raw_ref, sems.at[0])
    load.start()
    tpl_count, slot_count = stations_ref.shape
    pairs = tpl_count * slot_count
    devices, group, halves, comps = cfg["devices"], cfg["group"], cfg["halves"], cfg["comps"]
    station_dev, capacity = cfg["station_dev"], cfg["capacity"]
    spread, place = entry_lanes(tpl_count, slot_count)
    station = as_lanes(stations_ref[...], spread, place, tpl_count)
    shift = as_lanes(moveouts_ref[...], spread, place, tpl_count)
    device = jnp.floor((station + 0.5) * (1.0 / station_dev))
    onehot = jnp.where(iota((devices, pairs), 0).astype(jnp.float32) == device, 1.0, 0.0)
    rank = jnp.sum(onehot * count_before(onehot), axis=0, keepdims=True)
    half = jnp.floor((device + 0.5) * (1.0 / group))
    holder = device - half * group
    away = jnp.where(half == half_ref[0].astype(jnp.float32), 0.0, 1.0)
    base = jnp.where(rank < float(capacity), away * (comps * capacity) + rank, -1e6)
    place_ref[0:1, :] = base
    place_ref[1:2, :] = holder

    code = ((place + 1.0) * (1 << cfg["row_bits"]) + station - device * station_dev) * (1 << cfg["shift_bits"]) + shift
    code = code.astype(jnp.int32)
    at_rank = jnp.where(iota((LANES, pairs), 0).astype(jnp.float32) == rank, 1.0, 0.0).astype(jnp.bfloat16)
    at_holder = iota((group, pairs), 0).astype(jnp.float32) == holder
    digits = []
    for q in range(halves):
        for d in range(DIGITS):
            digit = (lax.shift_right_logical(code, 8 * d) & 255).astype(jnp.float32)
            marked = jnp.where(at_holder & (away == float(q)), digit, 0.0).astype(jnp.bfloat16)
            digits.append(
                lax.dot_general(marked, at_rank, (((1,), (1,)), ((), ())), preferred_element_type=jnp.float32)
            )
    codes = jnp.concatenate(digits, axis=1)
    width = codes.shape[1]
    codes = jnp.broadcast_to(codes.reshape(group, 1, width), (group, ROWS, width))
    last = iota((group, ROWS, 1), 1) == ROWS - 1
    codes = jnp.where(last, codes, 0.0).reshape(group * ROWS, width)

    load.wait()
    length = raw_ref.shape[3]
    for c in range(comps):
        values = raw_ref[:, c].astype(jnp.float32).reshape(pairs, length)
        centred = values - jnp.mean(values, axis=-1, keepdims=True)
        spread_c = jnp.sqrt(jnp.mean(centred * centred, axis=-1, keepdims=True) + 1e-05)
        shapes_ref[c] = (centred * (1.0 / spread_c)).astype(jnp.bfloat16)
    keep = pltpu.make_async_copy(shapes_ref, shapes_hbm, sems.at[1])
    keep.start()
    total = pick_rows(cfg, base, holder, 0, ROWS - 1, ROWS, 0, group, shapes_ref)
    total = jnp.concatenate([total[:, :width] + codes, total[:, width:]], axis=1)
    packed_ref[...] = total.astype(jnp.bfloat16)
    send = pltpu.make_async_copy(packed_ref, first_hbm, sems.at[2])
    send.start()
    keep.wait()
    send.wait()


def pick_rows(cfg, base, holder, low, count, rows, start, holders, shapes_ref):
    comps, pairs, length = shapes_ref.shape
    line = iota((holders * rows, pairs), 0).astype(jnp.float32)
    total = jnp.zeros((holders * rows, length), jnp.float32)
    for c in range(comps):
        local = base + float(c * cfg["capacity"] - low)
        inside = (local >= 0.0) & (local < float(count))
        goal = jnp.where(inside, (holder - float(start)) * rows + local, -1.0)
        pick = jnp.where(line == goal, 1.0, 0.0).astype(jnp.bfloat16)
        total = total + dot(pick, shapes_ref[c])
    return total


def rest_kernel(cfg, place_ref, shapes_hbm, rest_hbm, shapes_ref, packed_ref, in_sem, out_sems):
    load = pltpu.make_async_copy(shapes_hbm, shapes_ref, in_sem)
    load.start()
    base, holder = place_ref[0:1, :], place_ref[1:2, :]
    load.wait()
    tile = SOURCES * cfg["rest"]
    copies = []
    for step in range(packed_ref.shape[0] // tile):
        part = pl.ds(step * tile, tile)
        total = pick_rows(
            cfg, base, holder, ROWS - 1, cfg["rest"], cfg["rest"], step * SOURCES, SOURCES, shapes_ref
        )
        packed_ref[part, :] = total.astype(jnp.bfloat16)
        copies.append(pltpu.make_async_copy(packed_ref.at[part], rest_hbm.at[part], out_sems.at[step]))
        copies[-1].start()
    for copy in copies:
        copy.wait()


def read_codes(first_block, block):
    width = DIGITS * LANES
    rows = first_block.shape[0] // SOURCES
    values = first_block[:, block * width : (block + 1) * width].astype(jnp.float32).reshape(SOURCES, rows, width)
    last = iota((1, rows, 1), 1) == rows - 1
    digits = jnp.sum(jnp.where(last, values, 0.0), axis=1)
    return sum(digits[:, d * LANES : (d + 1) * LANES] * float(256**d) for d in range(DIGITS))


def block_lines(cfg, codes, first, rows, count):
    capacity, comps, halves = cfg["capacity"], cfg["comps"], cfg["halves"]
    tile = SOURCES * rows
    row = iota((SOURCES, rows, 1), 1).reshape(tile, 1)
    owner = iota((SOURCES, rows, 1), 0).reshape(tile, 1)
    line = row + first
    panel = jnp.zeros((tile, 1), jnp.int32)
    for m in range(1, halves * comps + 1):
        panel = panel + jnp.where(line >= m * capacity, 1, 0)
    slot = line - panel * capacity
    valid = (row < count) & (panel < halves * comps)
    code = jnp.zeros((tile, 1), jnp.float32)
    for q in range(halves):
        mine = valid & (panel >= q * comps) & (panel < (q + 1) * comps)
        chosen = (iota((tile, LANES), 1) == slot) & mine
        repeated = jnp.broadcast_to(codes[q].reshape(SOURCES, 1, LANES), (SOURCES, rows, LANES)).reshape(tile, LANES)
        code = code + jnp.sum(jnp.where(chosen, repeated, 0.0), axis=1, keepdims=True)
    code = code.astype(jnp.int32)
    shift_bits, row_bits = cfg["shift_bits"], cfg["row_bits"]
    shift = code & ((1 << shift_bits) - 1)
    station = lax.shift_right_logical(code, shift_bits) & ((1 << row_bits) - 1)
    tpl = lax.shift_right_logical(code, shift_bits + row_bits) - 1
    goal = jnp.where(tpl >= 0, panel * cfg["station_dev"] + station, -1)
    return shift, goal, jnp.where(tpl >= 0, owner * cfg["tpl_count"] + tpl, -1)


def cut_traces(cfg, shift, goal, waves):
    tile, seg_len, shift_bits = shift.shape[0], cfg["seg_len"], cfg["shift_bits"]
    pick = jnp.where(iota((tile, waves.shape[0]), 1) == goal, 1.0, 0.0).astype(jnp.bfloat16)
    x = dot(pick, waves).astype(jnp.bfloat16)

    def choose(step, moved, still):
        flag = jnp.where((shift & step) != 0, 1.0, 0.0)
        return moved * flag.astype(jnp.bfloat16) + still * (1.0 - flag).astype(jnp.bfloat16)

    for bit in range(shift_bits - 1, 6, -1):
        step = 1 << bit
        width = seg_len + step
        if x.shape[1] < width + step:
            x = jnp.concatenate([x, jnp.zeros((tile, width + step - x.shape[1]), jnp.bfloat16)], axis=1)
        x = choose(step, x[:, step : step + width], x[:, :width])
    for bit in range(min(shift_bits, 7) - 1, -1, -1):
        step = 1 << bit
        x = choose(step, pltpu.roll(x, x.shape[1] - step, 1), x)
    return x[:, :seg_len]


def line_sums(cfg, column):
    groups = SOURCES * cfg["tpl_count"]
    return jnp.where(iota((column.shape[0], groups), 1) == column, 1.0, 0.0).T.astype(jnp.bfloat16)


def levels_scale(cfg, narrow, edges):
    length = cfg["length"]
    ends = jnp.concatenate([narrow[:, :LAGS], narrow[:, length:]], axis=1).astype(jnp.float32)
    ends = ends * ends
    high = ends.astype(jnp.bfloat16)
    low = (ends - high.astype(jnp.float32)).astype(jnp.bfloat16)
    middle = narrow[:, LAGS:length].astype(jnp.float32)
    energy = dot(high, edges) + dot(low, edges) + jnp.sum(middle * middle, axis=1, keepdims=True)
    return 1.0 / (length * jnp.sqrt(energy * (1.0 / length) + 1e-05))


def shape_spectra(shapes, forward):
    spectra = []
    for h in range(shapes.shape[1] // LAGS):
        part = shapes[:, h * LAGS : (h + 1) * LAGS]
        mine = dot(jnp.concatenate([part, part], axis=1), forward)
        spectra.append((mine[:, :LAGS], mine[:, LAGS:]))
    return spectra


def match_lines(mine, theirs, scale, inverse):
    real = imag = 0.0
    for (mine_r, mine_i), (theirs_r, theirs_i) in zip(mine, theirs):
        real = real + (theirs_r * mine_r + theirs_i * mine_i)
        imag = imag + (theirs_i * mine_r - theirs_r * mine_i)
    product = jnp.concatenate([real, imag], axis=1)
    high = product.astype(jnp.bfloat16)
    low = (product - high.astype(jnp.float32)).astype(jnp.bfloat16)
    return dot(jnp.concatenate([high, high, low], axis=1), inverse) * scale


def sum_lines(sums, left):
    total = 0.0
    for _ in range(3):
        part = left.astype(jnp.bfloat16)
        left = left - part.astype(jnp.float32)
        total = total + dot(sums, part)
    return total


def tables_of(table_ref):
    back = table_ref[2 * LAGS :, :]
    high, low = back[:, :LAGS], back[:, LAGS:]
    return table_ref[: 2 * LAGS, :], jnp.concatenate([high, low, high], axis=0)


def trace_kernel(cfg, first_ref, *refs):
    waves_refs, (table_ref, edges_ref, sent_ref, kept_ref, sums_ref) = refs[:-5], refs[-5:]
    codes = [read_codes(first_ref[...], q) for q in range(cfg["halves"])]
    early = block_lines(cfg, codes, 0, ROWS, ROWS - 1)
    late = block_lines(cfg, codes, ROWS - 1, cfg["rest"], cfg["rest"])
    split = SOURCES * ROWS
    shift, goal = (jnp.concatenate([early[k], late[k]], axis=0) for k in range(2))
    waves = [ref[...].reshape(-1, ref.shape[2]) for ref in waves_refs]
    narrow = cut_traces(cfg, shift, goal, jnp.concatenate(waves, axis=0))
    scale = levels_scale(cfg, narrow, edges_ref[...])
    kept_ref[:, 2 * cfg["length"] :] = scale[split:]
    sums_ref[...] = line_sums(cfg, late[2])

    forward, inverse = tables_of(table_ref)
    sign = (1 - 2 * (iota((1, LAGS), 1) & 1)).astype(jnp.float32)
    before = None
    spectra = []
    for h in range(cfg["length"] // LAGS + 1):
        part = narrow[:, h * LAGS : (h + 1) * LAGS]
        here = dot(jnp.concatenate([part, part], axis=1), forward)
        here = here[:, :LAGS], here[:, LAGS:]
        if before is not None:
            real, imag = before[0] + sign * here[1], before[1] - sign * here[0]
            kept_ref[:, (2 * h - 2) * LAGS : (2 * h - 1) * LAGS] = real[split:]
            kept_ref[:, (2 * h - 1) * LAGS : 2 * h * LAGS] = imag[split:]
            spectra.append((real[:split], imag[:split]))
        before = here
    left = match_lines(shape_spectra(first_ref[...], forward), spectra, scale[:split], inverse)
    sent_ref[...] = sum_lines(line_sums(cfg, early[2]), left)


def match_kernel(tiles, shapes_hbm, kept_hbm, sums_hbm, table_hbm, before_hbm, sent_ref, *scratch):
    shapes_ref, kept_ref, sums_ref, table_ref, before_ref, sems = scratch
    tile = shapes_ref.shape[0] // tiles
    groups = sent_ref.shape[0] // tiles
    length = shapes_ref.shape[1]
    copies = []

    def fetch(source, buffer, part=None):
        if part is not None:
            source, buffer = source.at[part], buffer.at[part]
        copies.append(pltpu.make_async_copy(source, buffer, sems.at[len(copies)]))
        copies[-1].start()
        return copies[-1]

    lines = [pl.ds(t * tile, tile) for t in range(tiles)]
    halves = [pl.ds(q * 2 * LAGS, 2 * LAGS) for q in range(2)]
    forward = fetch(table_hbm, table_ref, halves[0])
    shapes, kept = [], []
    for t in range(tiles):
        shapes.append(fetch(shapes_hbm, shapes_ref, lines[t]))
        kept.append(fetch(kept_hbm, kept_ref, lines[t]))
        if t == 0:
            inverse = fetch(table_hbm, table_ref, halves[1])
            sums = fetch(sums_hbm, sums_ref)
            before = fetch(before_hbm, before_ref)
    forward.wait()
    for t in range(tiles):
        shapes[t].wait()
        mine = shape_spectra(shapes_ref[lines[t], :], table_ref[: 2 * LAGS, :])
        kept[t].wait()
        theirs = kept_ref[lines[t], :]
        spectra = [
            (theirs[:, 2 * h * LAGS : (2 * h + 1) * LAGS], theirs[:, (2 * h + 1) * LAGS : (2 * h + 2) * LAGS])
            for h in range(length // LAGS)
        ]
        if t == 0:
            for copy in (inverse, sums, before):
                copy.wait()
        left = match_lines(mine, spectra, theirs[:, 2 * length :], tables_of(table_ref)[1])
        ends = pl.ds(t * groups, groups)
        sent_ref[ends, :] = before_ref[ends, :] + sum_lines(sums_ref[ends, :], left)


def stack_kernel(factor, parts_ref, stacks_ref, top_ref):
    stacks = jnp.sum(parts_ref[...], axis=0) * factor
    stacks_ref[...] = stacks
    top_ref[...] = jnp.broadcast_to(jnp.max(stacks, axis=0, keepdims=True), top_ref.shape)


def body(waveforms, templates, stations, moveouts):
    devices, group, halves = lax.axis_size(AXES), lax.axis_size(GROUP), lax.axis_size(HALF)
    tpl_count, slot_count = stations.shape
    comps, length = templates.shape[2:]
    station_dev, _, samples = waveforms.shape
    seg_len = length + LAGS
    pairs = tpl_count * slot_count
    capacity = (2 * pairs + devices - 1) // devices
    rest = max(1, -(-(halves * comps * capacity - (ROWS - 1)) // 16)) * 16
    cfg = dict(
        devices=devices,
        group=group,
        halves=halves,
        station_dev=station_dev,
        tpl_count=tpl_count,
        comps=comps,
        capacity=capacity,
        rest=rest,
        length=length,
        seg_len=seg_len,
        shift_bits=bits_of(samples - seg_len + 1),
        row_bits=bits_of(station_dev),
    )
    table = jnp.asarray(transform_table(LAGS))
    edges = jnp.asarray(edge_table(LAGS))
    tiles = group // SOURCES
    tile = SOURCES * rest
    lines = group * rest
    sums_tile = SOURCES * tpl_count
    kept_len = 2 * length + LAGS
    whole = pl.BlockSpec(memory_space=pltpu.VMEM)
    anywhere = pl.BlockSpec(memory_space=pl.ANY)
    params = pltpu.CompilerParams(vmem_limit_bytes=60 * MIB)
    by_slot = templates.transpose(1, 2, 0, 3)
    waves = waveforms.transpose(1, 0, 2)
    half = lax.axis_index(HALF).reshape(1)

    def work(flops, size):
        return pl.CostEstimate(flops=flops, bytes_accessed=size, transcendentals=0)

    def exchange(x, axes):
        return lax.all_to_all(x, axes, split_axis=0, concat_axis=0, tiled=True)

    def same(shape):
        return pl.BlockSpec(shape, lambda i: (0,) * len(shape))

    def tiled(*shape):
        return pl.BlockSpec(shape, lambda i: (i, 0))

    traces = [waves] + [lax.ppermute(waves, HALF, [(0, 1), (1, 0)])] * (halves - 1)
    first, shapes, place = pl.pallas_call(
        functools.partial(first_kernel, cfg),
        out_shape=[
            jax.ShapeDtypeStruct((group * ROWS, length), jnp.bfloat16),
            jax.ShapeDtypeStruct((comps, pairs, length), jnp.bfloat16),
            jax.ShapeDtypeStruct((8, pairs), jnp.float32),
        ],
        in_specs=[pl.BlockSpec(memory_space=pltpu.SMEM), whole, whole, anywhere],
        out_specs=[anywhere, anywhere, whole],
        scratch_shapes=[
            pltpu.VMEM(by_slot.shape, jnp.bfloat16),
            pltpu.VMEM((comps, pairs, length), jnp.bfloat16),
            pltpu.VMEM((group * ROWS, length), jnp.bfloat16),
            pltpu.SemaphoreType.DMA((3,)),
        ],
        compiler_params=params,
        cost_estimate=work(1, 1),
        name="first",
    )(half, stations, moveouts, by_slot)
    later = pl.pallas_call(
        functools.partial(rest_kernel, cfg),
        out_shape=jax.ShapeDtypeStruct((lines, length), jnp.bfloat16),
        in_specs=[whole, anywhere],
        out_specs=anywhere,
        scratch_shapes=[
            pltpu.VMEM((comps, pairs, length), jnp.bfloat16),
            pltpu.VMEM((lines, length), jnp.bfloat16),
            pltpu.SemaphoreType.DMA,
            pltpu.SemaphoreType.DMA((tiles,)),
        ],
        compiler_params=params,
        cost_estimate=work(5 * 10**9, 1),
        name="rest",
    )(place, shapes)
    first = exchange(first.reshape(group, ROWS, length), GROUP).reshape(group * ROWS, length)
    first, later = lax.optimization_barrier((first, later))
    arrived = exchange(later.reshape(group, rest, length), GROUP).reshape(lines, length)

    before, kept, sums = pl.pallas_call(
        functools.partial(trace_kernel, cfg),
        grid=(tiles,),
        out_shape=[
            jax.ShapeDtypeStruct((group * tpl_count, LAGS), jnp.float32),
            jax.ShapeDtypeStruct((lines, kept_len), jnp.float32),
            jax.ShapeDtypeStruct((group * tpl_count, tile), jnp.bfloat16),
        ],
        in_specs=[tiled(SOURCES * ROWS, length)]
        + [same(waves.shape)] * halves
        + [same(table.shape), same(edges.shape)],
        out_specs=[tiled(sums_tile, LAGS), tiled(tile, kept_len), tiled(sums_tile, tile)],
        compiler_params=params,
        cost_estimate=work(10**12, 1),
        name="traces",
    )(first, *traces, table, edges)
    operands = (arrived, kept, sums, table, before)
    sent = pl.pallas_call(
        functools.partial(match_kernel, tiles),
        out_shape=jax.ShapeDtypeStruct((group * tpl_count, LAGS), jnp.float32),
        in_specs=[anywhere] * len(operands),
        out_specs=whole,
        scratch_shapes=[pltpu.VMEM(x.shape, x.dtype) for x in operands]
        + [pltpu.SemaphoreType.DMA((4 + 2 * tiles,))],
        compiler_params=pltpu.CompilerParams(vmem_limit_bytes=57 * MIB),
        name="match",
    )(*operands)

    parts = exchange(sent.reshape(group, tpl_count, LAGS), GROUP)
    stacks, top = pl.pallas_call(
        functools.partial(stack_kernel, math.sqrt(length / (comps * slot_count))),
        out_shape=[
            jax.ShapeDtypeStruct((tpl_count, LAGS), jnp.float32),
            jax.ShapeDtypeStruct((devices, 1, LAGS), jnp.float32),
        ],
        in_specs=[whole],
        out_specs=[whole, whole],
        compiler_params=pltpu.CompilerParams(vmem_limit_bytes=16 * MIB),
        name="stack",
    )(parts)
    return stacks, jnp.max(exchange(top, AXES), axis=(0, 1))


def solution(mesh):
    slow, fast = (mesh.shape[name] for name in GROUP)
    halves = 2 if slow % 2 == 0 else 1
    split = jax.sharding.Mesh(mesh.devices.reshape(halves, slow // halves, fast), AXES)
    placed = (
        P(AXES, None, None),
        P(AXES, None, None, None),
        P(AXES, None),
        P(AXES, None),
    )
    return jax.shard_map(body, mesh=split, in_specs=placed, out_specs=(P(AXES, None), P()), check_vma=False)
```

```python
import functools
import math

import jax
import jax.numpy as jnp
import ml_dtypes
import numpy as np
from jax import lax
from jax.experimental import pallas as pl
from jax.experimental.pallas import tpu as pltpu
from jax.sharding import PartitionSpec as P

LAGS = 256
HALF = "half"
GROUP = ("tmpl", "sta")
AXES = (HALF,) + GROUP
SOURCES = 4
ROWS = 16
DIGITS = 3
LANES = 128
MIB = 1024 * 1024


def bits_of(limit):
    return max(1, (limit - 1).bit_length())


def split_table(table):
    high = table.astype(ml_dtypes.bfloat16)
    return high, (table - high.astype(np.float64)).astype(ml_dtypes.bfloat16)


def transform_table(piece):
    size = 2 * piece
    angle = 2.0 * np.pi * (np.arange(piece) + 0.5) / size
    phase = np.arange(piece)[:, None] * angle[None, :]
    forward = np.concatenate([np.cos(phase), -np.sin(phase)], axis=1)
    inverse = np.concatenate([np.cos(phase.T), -np.sin(phase.T)], axis=0) * (2.0 / size)
    return np.concatenate([*split_table(forward), np.concatenate(split_table(inverse), axis=1)], axis=0)


def edge_table(lag_count):
    sample = np.arange(lag_count)[:, None]
    lag = np.arange(lag_count)[None, :]
    return np.concatenate([sample >= lag, sample < lag], axis=0).astype(ml_dtypes.bfloat16)


def iota(shape, axis):
    return lax.broadcasted_iota(jnp.int32, shape, axis)


def dot(a, b):
    return jnp.dot(a, b, preferred_element_type=jnp.float32)


def exact_dot(a, b):
    return jnp.dot(a, b, precision=lax.Precision.HIGHEST, preferred_element_type=jnp.float32)


def entry_lanes(tpl_count, slot_count):
    pairs = tpl_count * slot_count
    first = iota((slot_count, pairs), 0) * tpl_count
    entry = iota((slot_count, pairs), 1)
    spread = jnp.where((entry >= first) & (entry < first + tpl_count), 1.0, 0.0)
    start = jnp.sum(spread * first.astype(jnp.float32), axis=0, keepdims=True)
    return spread, iota((1, pairs), 1).astype(jnp.float32) - start


def as_lanes(values, spread, place, tpl_count):
    owners = values.shape[0] // tpl_count
    pairs = spread.shape[1]
    wide = exact_dot(values.astype(jnp.float32), spread).reshape(owners, tpl_count, pairs)
    own = iota((1, tpl_count, pairs), 1).astype(jnp.float32) == place.reshape(1, 1, pairs)
    return jnp.sum(jnp.where(own, wide, 0.0), axis=1)


def count_before(hits):
    pairs = hits.shape[1]
    earlier = jnp.where(iota((pairs, pairs), 0) < iota((pairs, pairs), 1), 1.0, 0.0)
    return dot(hits.astype(jnp.bfloat16), earlier.astype(jnp.bfloat16))


def first_kernel(
    cfg, half_ref, stations_ref, moveouts_ref, templates_hbm, first_hbm, shapes_hbm, place_ref, raw_ref, shapes_ref, packed_ref, sems
):
    load = pltpu.make_async_copy(templates_hbm, raw_ref, sems.at[0])
    load.start()
    tpl_count, slot_count = stations_ref.shape
    pairs = tpl_count * slot_count
    devices, group, halves, comps = cfg["devices"], cfg["group"], cfg["halves"], cfg["comps"]
    station_dev, capacity = cfg["station_dev"], cfg["capacity"]
    spread, place = entry_lanes(tpl_count, slot_count)
    station = as_lanes(stations_ref[...], spread, place, tpl_count)
    shift = as_lanes(moveouts_ref[...], spread, place, tpl_count)
    device = jnp.floor((station + 0.5) * (1.0 / station_dev))
    onehot = jnp.where(iota((devices, pairs), 0).astype(jnp.float32) == device, 1.0, 0.0)
    rank = jnp.sum(onehot * count_before(onehot), axis=0, keepdims=True)
    half = jnp.floor((device + 0.5) * (1.0 / group))
    holder = device - half * group
    away = jnp.where(half == half_ref[0].astype(jnp.float32), 0.0, 1.0)
    base = jnp.where(rank < float(capacity), away * (comps * capacity) + rank, -1e6)
    place_ref[0:1, :] = base
    place_ref[1:2, :] = holder

    code = ((place + 1.0) * (1 << cfg["row_bits"]) + station - device * station_dev) * (1 << cfg["shift_bits"]) + shift
    code = code.astype(jnp.int32)
    at_rank = jnp.where(iota((LANES, pairs), 0).astype(jnp.float32) == rank, 1.0, 0.0).astype(jnp.bfloat16)
    at_holder = iota((group, pairs), 0).astype(jnp.float32) == holder
    digits = []
    for q in range(halves):
        for d in range(DIGITS):
            digit = (lax.shift_right_logical(code, 8 * d) & 255).astype(jnp.float32)
            marked = jnp.where(at_holder & (away == float(q)), digit, 0.0).astype(jnp.bfloat16)
            digits.append(
                lax.dot_general(marked, at_rank, (((1,), (1,)), ((), ())), preferred_element_type=jnp.float32)
            )
    codes = jnp.concatenate(digits, axis=1)
    width = codes.shape[1]
    codes = jnp.broadcast_to(codes.reshape(group, 1, width), (group, ROWS, width))
    last = iota((group, ROWS, 1), 1) == ROWS - 1
    codes = jnp.where(last, codes, 0.0).reshape(group * ROWS, width)

    load.wait()
    length = raw_ref.shape[3]
    for c in range(comps):
        values = raw_ref[:, c].astype(jnp.float32).reshape(pairs, length)
        centred = values - jnp.mean(values, axis=-1, keepdims=True)
        spread_c = jnp.sqrt(jnp.mean(centred * centred, axis=-1, keepdims=True) + 1e-05)
        shapes_ref[c] = (centred * (1.0 / spread_c)).astype(jnp.bfloat16)
    keep = pltpu.make_async_copy(shapes_ref, shapes_hbm, sems.at[1])
    keep.start()
    total = pick_rows(cfg, base, holder, 0, ROWS - 1, ROWS, 0, group, shapes_ref)
    total = jnp.concatenate([total[:, :width] + codes, total[:, width:]], axis=1)
    packed_ref[...] = total.astype(jnp.bfloat16)
    send = pltpu.make_async_copy(packed_ref, first_hbm, sems.at[2])
    send.start()
    keep.wait()
    send.wait()


def pick_rows(cfg, base, holder, low, count, rows, start, holders, shapes_ref):
    comps, pairs, length = shapes_ref.shape
    line = iota((holders * rows, pairs), 0).astype(jnp.float32)
    total = jnp.zeros((holders * rows, length), jnp.float32)
    for c in range(comps):
        local = base + float(c * cfg["capacity"] - low)
        inside = (local >= 0.0) & (local < float(count))
        goal = jnp.where(inside, (holder - float(start)) * rows + local, -1.0)
        pick = jnp.where(line == goal, 1.0, 0.0).astype(jnp.bfloat16)
        total = total + dot(pick, shapes_ref[c])
    return total


def rest_kernel(cfg, place_ref, shapes_hbm, rest_hbm, shapes_ref, packed_ref, in_sem, out_sems):
    load = pltpu.make_async_copy(shapes_hbm, shapes_ref, in_sem)
    load.start()
    base, holder = place_ref[0:1, :], place_ref[1:2, :]
    load.wait()
    tile = SOURCES * cfg["rest"]
    copies = []
    for step in range(packed_ref.shape[0] // tile):
        part = pl.ds(step * tile, tile)
        total = pick_rows(
            cfg, base, holder, ROWS - 1, cfg["rest"], cfg["rest"], step * SOURCES, SOURCES, shapes_ref
        )
        packed_ref[part, :] = total.astype(jnp.bfloat16)
        copies.append(pltpu.make_async_copy(packed_ref.at[part], rest_hbm.at[part], out_sems.at[step]))
        copies[-1].start()
    for copy in copies:
        copy.wait()


def read_codes(first_block, block):
    width = DIGITS * LANES
    rows = first_block.shape[0] // SOURCES
    values = first_block[:, block * width : (block + 1) * width].astype(jnp.float32).reshape(SOURCES, rows, width)
    last = iota((1, rows, 1), 1) == rows - 1
    digits = jnp.sum(jnp.where(last, values, 0.0), axis=1)
    return sum(digits[:, d * LANES : (d + 1) * LANES] * float(256**d) for d in range(DIGITS))


def block_lines(cfg, codes, first, rows, count):
    capacity, comps, halves = cfg["capacity"], cfg["comps"], cfg["halves"]
    tile = SOURCES * rows
    row = iota((SOURCES, rows, 1), 1).reshape(tile, 1)
    owner = iota((SOURCES, rows, 1), 0).reshape(tile, 1)
    line = row + first
    panel = jnp.zeros((tile, 1), jnp.int32)
    for m in range(1, halves * comps + 1):
        panel = panel + jnp.where(line >= m * capacity, 1, 0)
    slot = line - panel * capacity
    valid = (row < count) & (panel < halves * comps)
    code = jnp.zeros((tile, 1), jnp.float32)
    for q in range(halves):
        mine = valid & (panel >= q * comps) & (panel < (q + 1) * comps)
        chosen = (iota((tile, LANES), 1) == slot) & mine
        repeated = jnp.broadcast_to(codes[q].reshape(SOURCES, 1, LANES), (SOURCES, rows, LANES)).reshape(tile, LANES)
        code = code + jnp.sum(jnp.where(chosen, repeated, 0.0), axis=1, keepdims=True)
    code = code.astype(jnp.int32)
    shift_bits, row_bits = cfg["shift_bits"], cfg["row_bits"]
    shift = code & ((1 << shift_bits) - 1)
    station = lax.shift_right_logical(code, shift_bits) & ((1 << row_bits) - 1)
    tpl = lax.shift_right_logical(code, shift_bits + row_bits) - 1
    goal = jnp.where(tpl >= 0, panel * cfg["station_dev"] + station, -1)
    return shift, goal, jnp.where(tpl >= 0, owner * cfg["tpl_count"] + tpl, -1)


def cut_traces(cfg, shift, goal, waves):
    tile, seg_len, shift_bits = shift.shape[0], cfg["seg_len"], cfg["shift_bits"]
    pick = jnp.where(iota((tile, waves.shape[0]), 1) == goal, 1.0, 0.0).astype(jnp.bfloat16)
    x = dot(pick, waves).astype(jnp.bfloat16)

    def choose(step, moved, still):
        flag = jnp.where((shift & step) != 0, 1.0, 0.0)
        return moved * flag.astype(jnp.bfloat16) + still * (1.0 - flag).astype(jnp.bfloat16)

    for bit in range(shift_bits - 1, 6, -1):
        step = 1 << bit
        width = seg_len + step
        if x.shape[1] < width + step:
            x = jnp.concatenate([x, jnp.zeros((tile, width + step - x.shape[1]), jnp.bfloat16)], axis=1)
        x = choose(step, x[:, step : step + width], x[:, :width])
    for bit in range(min(shift_bits, 7) - 1, -1, -1):
        step = 1 << bit
        x = choose(step, pltpu.roll(x, x.shape[1] - step, 1), x)
    return x[:, :seg_len]


def line_sums(cfg, column):
    groups = SOURCES * cfg["tpl_count"]
    return jnp.where(iota((column.shape[0], groups), 1) == column, 1.0, 0.0).T.astype(jnp.bfloat16)


def levels_scale(cfg, narrow, edges):
    length = cfg["length"]
    ends = jnp.concatenate([narrow[:, :LAGS], narrow[:, length:]], axis=1).astype(jnp.float32)
    ends = ends * ends
    high = ends.astype(jnp.bfloat16)
    low = (ends - high.astype(jnp.float32)).astype(jnp.bfloat16)
    middle = narrow[:, LAGS:length].astype(jnp.float32)
    energy = dot(high, edges) + dot(low, edges) + jnp.sum(middle * middle, axis=1, keepdims=True)
    return 1.0 / (length * jnp.sqrt(energy * (1.0 / length) + 1e-05))


def shape_spectra(shapes, forward):
    spectra = []
    for h in range(shapes.shape[1] // LAGS):
        part = shapes[:, h * LAGS : (h + 1) * LAGS]
        mine = dot(jnp.concatenate([part, part], axis=1), forward)
        spectra.append((mine[:, :LAGS], mine[:, LAGS:]))
    return spectra


def match_lines(mine, theirs, scale, inverse):
    real = imag = 0.0
    for (mine_r, mine_i), (theirs_r, theirs_i) in zip(mine, theirs):
        real = real + (theirs_r * mine_r + theirs_i * mine_i)
        imag = imag + (theirs_i * mine_r - theirs_r * mine_i)
    product = jnp.concatenate([real, imag], axis=1)
    high = product.astype(jnp.bfloat16)
    low = (product - high.astype(jnp.float32)).astype(jnp.bfloat16)
    return dot(jnp.concatenate([high, high, low], axis=1), inverse) * scale


def sum_lines(sums, left):
    total = 0.0
    for _ in range(3):
        part = left.astype(jnp.bfloat16)
        left = left - part.astype(jnp.float32)
        total = total + dot(sums, part)
    return total


def tables_of(table_ref):
    back = table_ref[2 * LAGS :, :]
    high, low = back[:, :LAGS], back[:, LAGS:]
    return table_ref[: 2 * LAGS, :], jnp.concatenate([high, low, high], axis=0)


def trace_kernel(cfg, first_ref, *refs):
    waves_refs, (table_ref, edges_ref, sent_ref, kept_ref, sums_ref) = refs[:-5], refs[-5:]
    codes = [read_codes(first_ref[...], q) for q in range(cfg["halves"])]
    early = block_lines(cfg, codes, 0, ROWS, ROWS - 1)
    late = block_lines(cfg, codes, ROWS - 1, cfg["rest"], cfg["rest"])
    split = SOURCES * ROWS
    shift, goal = (jnp.concatenate([early[k], late[k]], axis=0) for k in range(2))
    waves = [ref[...].reshape(-1, ref.shape[2]) for ref in waves_refs]
    narrow = cut_traces(cfg, shift, goal, jnp.concatenate(waves, axis=0))
    scale = levels_scale(cfg, narrow, edges_ref[...])
    kept_ref[:, 2 * cfg["length"] :] = scale[split:]
    sums_ref[...] = line_sums(cfg, late[2])

    forward, inverse = tables_of(table_ref)
    sign = (1 - 2 * (iota((1, LAGS), 1) & 1)).astype(jnp.float32)
    before = None
    spectra = []
    for h in range(cfg["length"] // LAGS + 1):
        part = narrow[:, h * LAGS : (h + 1) * LAGS]
        here = dot(jnp.concatenate([part, part], axis=1), forward)
        here = here[:, :LAGS], here[:, LAGS:]
        if before is not None:
            real, imag = before[0] + sign * here[1], before[1] - sign * here[0]
            kept_ref[:, (2 * h - 2) * LAGS : (2 * h - 1) * LAGS] = real[split:]
            kept_ref[:, (2 * h - 1) * LAGS : 2 * h * LAGS] = imag[split:]
            spectra.append((real[:split], imag[:split]))
        before = here
    left = match_lines(shape_spectra(first_ref[...], forward), spectra, scale[:split], inverse)
    sent_ref[...] = sum_lines(line_sums(cfg, early[2]), left)


def match_kernel(tiles, shapes_hbm, kept_hbm, sums_hbm, table_hbm, before_hbm, sent_ref, *scratch):
    shapes_ref, kept_ref, sums_ref, table_ref, before_ref, sems = scratch
    tile = shapes_ref.shape[0] // tiles
    groups = sent_ref.shape[0] // tiles
    length = shapes_ref.shape[1]
    copies = []

    def fetch(source, buffer, part=None):
        if part is not None:
            source, buffer = source.at[part], buffer.at[part]
        copies.append(pltpu.make_async_copy(source, buffer, sems.at[len(copies)]))
        copies[-1].start()
        return copies[-1]

    lines = [pl.ds(t * tile, tile) for t in range(tiles)]
    halves = [pl.ds(q * 2 * LAGS, 2 * LAGS) for q in range(2)]
    forward = fetch(table_hbm, table_ref, halves[0])
    shapes, kept = [], []
    for t in range(tiles):
        shapes.append(fetch(shapes_hbm, shapes_ref, lines[t]))
        kept.append(fetch(kept_hbm, kept_ref, lines[t]))
        if t == 0:
            inverse = fetch(table_hbm, table_ref, halves[1])
            sums = fetch(sums_hbm, sums_ref)
            before = fetch(before_hbm, before_ref)
    forward.wait()
    for t in range(tiles):
        shapes[t].wait()
        mine = shape_spectra(shapes_ref[lines[t], :], table_ref[: 2 * LAGS, :])
        kept[t].wait()
        theirs = kept_ref[lines[t], :]
        spectra = [
            (theirs[:, 2 * h * LAGS : (2 * h + 1) * LAGS], theirs[:, (2 * h + 1) * LAGS : (2 * h + 2) * LAGS])
            for h in range(length // LAGS)
        ]
        if t == 0:
            for copy in (inverse, sums, before):
                copy.wait()
        left = match_lines(mine, spectra, theirs[:, 2 * length :], tables_of(table_ref)[1])
        ends = pl.ds(t * groups, groups)
        sent_ref[ends, :] = before_ref[ends, :] + sum_lines(sums_ref[ends, :], left)


def stack_kernel(factor, parts_ref, stacks_ref, top_ref):
    stacks = jnp.sum(parts_ref[...], axis=0) * factor
    stacks_ref[...] = stacks
    top_ref[...] = jnp.broadcast_to(jnp.max(stacks, axis=0, keepdims=True), top_ref.shape)


def body(waveforms, templates, stations, moveouts):
    devices, group, halves = lax.axis_size(AXES), lax.axis_size(GROUP), lax.axis_size(HALF)
    tpl_count, slot_count = stations.shape
    comps, length = templates.shape[2:]
    station_dev, _, samples = waveforms.shape
    seg_len = length + LAGS
    pairs = tpl_count * slot_count
    capacity = (2 * pairs + devices - 1) // devices
    rest = max(1, -(-(halves * comps * capacity - (ROWS - 1)) // 16)) * 16
    cfg = dict(
        devices=devices,
        group=group,
        halves=halves,
        station_dev=station_dev,
        tpl_count=tpl_count,
        comps=comps,
        capacity=capacity,
        rest=rest,
        length=length,
        seg_len=seg_len,
        shift_bits=bits_of(samples - seg_len + 1),
        row_bits=bits_of(station_dev),
    )
    table = jnp.asarray(transform_table(LAGS))
    edges = jnp.asarray(edge_table(LAGS))
    tiles = group // SOURCES
    tile = SOURCES * rest
    lines = group * rest
    sums_tile = SOURCES * tpl_count
    kept_len = 2 * length + LAGS
    whole = pl.BlockSpec(memory_space=pltpu.VMEM)
    anywhere = pl.BlockSpec(memory_space=pl.ANY)
    params = pltpu.CompilerParams(vmem_limit_bytes=60 * MIB)
    by_slot = templates.transpose(1, 2, 0, 3)
    waves = waveforms.transpose(1, 0, 2)
    half = lax.axis_index(HALF).reshape(1)

    def work(flops, size):
        return pl.CostEstimate(flops=flops, bytes_accessed=size, transcendentals=0)

    def exchange(x, axes):
        return lax.all_to_all(x, axes, split_axis=0, concat_axis=0, tiled=True)

    def same(shape):
        return pl.BlockSpec(shape, lambda i: (0,) * len(shape))

    def tiled(*shape):
        return pl.BlockSpec(shape, lambda i: (i, 0))

    traces = [waves] + [lax.ppermute(waves, HALF, [(0, 1), (1, 0)])] * (halves - 1)
    first, shapes, place = pl.pallas_call(
        functools.partial(first_kernel, cfg),
        out_shape=[
            jax.ShapeDtypeStruct((group * ROWS, length), jnp.bfloat16),
            jax.ShapeDtypeStruct((comps, pairs, length), jnp.bfloat16),
            jax.ShapeDtypeStruct((8, pairs), jnp.float32),
        ],
        in_specs=[pl.BlockSpec(memory_space=pltpu.SMEM), whole, whole, anywhere],
        out_specs=[anywhere, anywhere, whole],
        scratch_shapes=[
            pltpu.VMEM(by_slot.shape, jnp.bfloat16),
            pltpu.VMEM((comps, pairs, length), jnp.bfloat16),
            pltpu.VMEM((group * ROWS, length), jnp.bfloat16),
            pltpu.SemaphoreType.DMA((3,)),
        ],
        compiler_params=params,
        cost_estimate=work(1, 1),
        name="first",
    )(half, stations, moveouts, by_slot)
    later = pl.pallas_call(
        functools.partial(rest_kernel, cfg),
        out_shape=jax.ShapeDtypeStruct((lines, length), jnp.bfloat16),
        in_specs=[whole, anywhere],
        out_specs=anywhere,
        scratch_shapes=[
            pltpu.VMEM((comps, pairs, length), jnp.bfloat16),
            pltpu.VMEM((lines, length), jnp.bfloat16),
            pltpu.SemaphoreType.DMA,
            pltpu.SemaphoreType.DMA((tiles,)),
        ],
        compiler_params=params,
        cost_estimate=work(10**12, 1),
        name="rest",
    )(place, shapes)
    first = exchange(first.reshape(group, ROWS, length), GROUP).reshape(group * ROWS, length)
    first, later = lax.optimization_barrier((first, later))
    arrived = exchange(later.reshape(group, rest, length), GROUP).reshape(lines, length)

    before, kept, sums = pl.pallas_call(
        functools.partial(trace_kernel, cfg),
        grid=(tiles,),
        out_shape=[
            jax.ShapeDtypeStruct((group * tpl_count, LAGS), jnp.float32),
            jax.ShapeDtypeStruct((lines, kept_len), jnp.float32),
            jax.ShapeDtypeStruct((group * tpl_count, tile), jnp.bfloat16),
        ],
        in_specs=[tiled(SOURCES * ROWS, length)]
        + [same(waves.shape)] * halves
        + [same(table.shape), same(edges.shape)],
        out_specs=[tiled(sums_tile, LAGS), tiled(tile, kept_len), tiled(sums_tile, tile)],
        compiler_params=params,
        cost_estimate=work(10**12, 1),
        name="traces",
    )(first, *traces, table, edges)
    operands = (arrived, kept, sums, table, before)
    sent = pl.pallas_call(
        functools.partial(match_kernel, tiles),
        out_shape=jax.ShapeDtypeStruct((group * tpl_count, LAGS), jnp.float32),
        in_specs=[anywhere] * len(operands),
        out_specs=whole,
        scratch_shapes=[pltpu.VMEM(x.shape, x.dtype) for x in operands]
        + [pltpu.SemaphoreType.DMA((4 + 2 * tiles,))],
        compiler_params=pltpu.CompilerParams(vmem_limit_bytes=57 * MIB),
        name="match",
    )(*operands)

    parts = exchange(sent.reshape(group, tpl_count, LAGS), GROUP)
    stacks, top = pl.pallas_call(
        functools.partial(stack_kernel, math.sqrt(length / (comps * slot_count))),
        out_shape=[
            jax.ShapeDtypeStruct((tpl_count, LAGS), jnp.float32),
            jax.ShapeDtypeStruct((devices, 1, LAGS), jnp.float32),
        ],
        in_specs=[whole],
        out_specs=[whole, whole],
        compiler_params=pltpu.CompilerParams(vmem_limit_bytes=16 * MIB),
        name="stack",
    )(parts)
    return stacks, jnp.max(exchange(top, AXES), axis=(0, 1))


def solution(mesh):
    slow, fast = (mesh.shape[name] for name in GROUP)
    halves = 2 if slow % 2 == 0 else 1
    split = jax.sharding.Mesh(mesh.devices.reshape(halves, slow // halves, fast), AXES)
    placed = (
        P(AXES, None, None),
        P(AXES, None, None, None),
        P(AXES, None),
        P(AXES, None),
    )
    return jax.shard_map(body, mesh=split, in_specs=placed, out_specs=(P(AXES, None), P()), check_vma=False)
```

```python
import functools
import math

import jax
import jax.numpy as jnp
import ml_dtypes
import numpy as np
from jax import lax
from jax.experimental import pallas as pl
from jax.experimental.pallas import tpu as pltpu
from jax.sharding import PartitionSpec as P

LAGS = 256
HALF = "half"
GROUP = ("tmpl", "sta")
AXES = (HALF,) + GROUP
SOURCES = 8
LANES = 128
MIB = 1024 * 1024


def bits_of(limit):
    return max(1, (limit - 1).bit_length())


def split_table(table):
    high = table.astype(ml_dtypes.bfloat16)
    return high, (table - high.astype(np.float64)).astype(ml_dtypes.bfloat16)


def transform_table(piece):
    size = 2 * piece
    angle = 2.0 * np.pi * (np.arange(piece) + 0.5) / size
    phase = np.arange(piece)[:, None] * angle[None, :]
    forward = np.concatenate([np.cos(phase), -np.sin(phase)], axis=1)
    inverse = np.concatenate([np.cos(phase.T), -np.sin(phase.T)], axis=0) * (2.0 / size)
    return np.concatenate([*split_table(forward), np.concatenate(split_table(inverse), axis=1)], axis=0)


def edge_table(lag_count):
    sample = np.arange(lag_count)[:, None]
    lag = np.arange(lag_count)[None, :]
    return np.concatenate([sample >= lag, sample < lag], axis=0).astype(ml_dtypes.bfloat16)


def iota(shape, axis):
    return lax.broadcasted_iota(jnp.int32, shape, axis)


def dot(a, b):
    return jnp.dot(a, b, preferred_element_type=jnp.float32)


def exact_dot(a, b):
    return jnp.dot(a, b, precision=lax.Precision.HIGHEST, preferred_element_type=jnp.float32)


def entry_lanes(tpl_count, slot_count):
    pairs = tpl_count * slot_count
    first = iota((slot_count, pairs), 0) * tpl_count
    entry = iota((slot_count, pairs), 1)
    spread = jnp.where((entry >= first) & (entry < first + tpl_count), 1.0, 0.0)
    start = jnp.sum(spread * first.astype(jnp.float32), axis=0, keepdims=True)
    return spread, iota((1, pairs), 1).astype(jnp.float32) - start


def as_lanes(values, spread, place, tpl_count):
    owners = values.shape[0] // tpl_count
    pairs = spread.shape[1]
    wide = exact_dot(values.astype(jnp.float32), spread).reshape(owners, tpl_count, pairs)
    own = iota((1, tpl_count, pairs), 1).astype(jnp.float32) == place.reshape(1, 1, pairs)
    return jnp.sum(jnp.where(own, wide, 0.0), axis=1)


def count_before(hits):
    pairs = hits.shape[1]
    earlier = jnp.where(iota((pairs, pairs), 0) < iota((pairs, pairs), 1), 1.0, 0.0)
    return dot(hits.astype(jnp.bfloat16), earlier.astype(jnp.bfloat16))


def list_kernel(cfg, half_ref, stations_ref, moveouts_ref, codes_ref, goal_ref):
    tpl_count, slot_count = stations_ref.shape
    pairs = tpl_count * slot_count
    devices, group, halves = cfg["devices"], cfg["group"], cfg["halves"]
    station_dev, rows, capacity = cfg["station_dev"], cfg["rows"], cfg["capacity"]
    spread, place = entry_lanes(tpl_count, slot_count)
    station = as_lanes(stations_ref[...], spread, place, tpl_count)
    shift = as_lanes(moveouts_ref[...], spread, place, tpl_count)
    device = jnp.floor((station + 0.5) * (1.0 / station_dev))
    onehot = jnp.where(iota((devices, pairs), 0).astype(jnp.float32) == device, 1.0, 0.0)
    rank = jnp.sum(onehot * count_before(onehot), axis=0, keepdims=True)
    half = jnp.floor((device + 0.5) * (1.0 / group))
    away = jnp.where(half == half_ref[0].astype(jnp.float32), 0.0, 1.0)
    place_of = (device - half * group) * halves + away
    goal_ref[...] = jnp.where(rank < float(capacity), place_of * rows + rank, -float(group * halves * rows))

    row = station - device * station_dev
    code = ((place + 1.0) * (1 << cfg["row_bits"]) + row) * (1 << cfg["shift_bits"]) + shift
    marked = jnp.where(iota((group * halves, pairs), 0).astype(jnp.float32) == place_of, code, 0.0)
    at_rank = jnp.where(iota((LANES, pairs), 0).astype(jnp.float32) == rank, 1.0, 0.0)
    codes = lax.dot_general(
        marked,
        at_rank,
        (((1,), (1,)), ((), ())),
        precision=lax.Precision.HIGHEST,
        preferred_element_type=jnp.float32,
    )
    codes_ref[...] = codes.astype(jnp.int32)


def pack_kernel(cfg, goal_ref, templates_hbm, packed_hbm, raw_ref, shapes_ref, packed_ref, in_sem, out_sems):
    load = pltpu.make_async_copy(templates_hbm, raw_ref, in_sem)
    load.start()
    goal = goal_ref[...]
    pairs = goal.shape[1]
    comps, length = raw_ref.shape[1], raw_ref.shape[3]
    load.wait()
    for c in range(comps):
        values = raw_ref[:, c].astype(jnp.float32).reshape(pairs, length)
        centred = values - jnp.mean(values, axis=-1, keepdims=True)
        spread_c = jnp.sqrt(jnp.mean(centred * centred, axis=-1, keepdims=True) + 1e-05)
        shapes_ref[c] = (centred * (1.0 / spread_c)).astype(jnp.bfloat16)

    tiles = out_sems.shape[0]
    tile = packed_ref.shape[0] // tiles
    copies = []
    for step in range(tiles):
        line = iota((tile, pairs), 0).astype(jnp.float32) + float(step * tile)
        total = jnp.zeros((tile, length), jnp.float32)
        for c in range(comps):
            pick = jnp.where(line == goal + float(c * cfg["capacity"]), 1.0, 0.0).astype(jnp.bfloat16)
            total = total + dot(pick, shapes_ref[c])
        part = pl.ds(step * tile, tile)
        packed_ref[part, :] = total.astype(jnp.bfloat16)
        copies.append(pltpu.make_async_copy(packed_ref.at[part], packed_hbm.at[part], out_sems.at[step]))
        copies[-1].start()
    for copy in copies:
        copy.wait()


def tile_lines(cfg, codes):
    capacity, rows, comps, halves = cfg["capacity"], cfg["rows"], cfg["comps"], cfg["halves"]
    blocks = SOURCES * halves
    tile = blocks * rows
    line = iota((blocks, rows, 1), 1).reshape(tile, 1)
    block = iota((blocks, rows, 1), 0).reshape(tile, 1)
    comp = jnp.zeros((tile, 1), jnp.int32)
    for c in range(1, comps + 1):
        comp = comp + jnp.where(line >= c * capacity, 1, 0)
    slot = line - comp * capacity
    owner = jnp.zeros((tile, 1), jnp.int32)
    for k in range(1, SOURCES):
        owner = owner + jnp.where(block >= k * halves, 1, 0)
    repeated = codes.astype(jnp.float32).reshape(blocks, 1, LANES)
    repeated = jnp.broadcast_to(repeated, (blocks, rows, LANES)).reshape(tile, LANES)
    chosen = (iota((tile, LANES), 1) == slot) & (comp < comps)
    code = jnp.sum(jnp.where(chosen, repeated, 0.0), axis=1, keepdims=True).astype(jnp.int32)
    shift_bits, row_bits = cfg["shift_bits"], cfg["row_bits"]
    shift = code & ((1 << shift_bits) - 1)
    row = lax.shift_right_logical(code, shift_bits) & ((1 << row_bits) - 1)
    tpl = lax.shift_right_logical(code, shift_bits + row_bits) - 1
    goal = ((block - owner * halves) * comps + comp) * cfg["station_dev"] + row
    return shift, jnp.where(tpl >= 0, goal, -1), jnp.where(tpl >= 0, owner * cfg["tpl_count"] + tpl, -1)


def cut_traces(cfg, shift, goal, waves):
    tile, seg_len, shift_bits = shift.shape[0], cfg["seg_len"], cfg["shift_bits"]
    pick = jnp.where(iota((tile, waves.shape[0]), 1) == goal, 1.0, 0.0).astype(jnp.bfloat16)
    x = dot(pick, waves).astype(jnp.bfloat16)

    def choose(step, moved, still):
        flag = jnp.where((shift & step) != 0, 1.0, 0.0)
        return moved * flag.astype(jnp.bfloat16) + still * (1.0 - flag).astype(jnp.bfloat16)

    for bit in range(shift_bits - 1, 6, -1):
        step = 1 << bit
        width = seg_len + step
        if x.shape[1] < width + step:
            x = jnp.concatenate([x, jnp.zeros((tile, width + step - x.shape[1]), jnp.bfloat16)], axis=1)
        x = choose(step, x[:, step : step + width], x[:, :width])
    for bit in range(min(shift_bits, 7) - 1, -1, -1):
        step = 1 << bit
        x = choose(step, pltpu.roll(x, x.shape[1] - step, 1), x)
    return x[:, :seg_len]


def line_sums(cfg, column):
    groups = SOURCES * cfg["tpl_count"]
    return jnp.where(iota((column.shape[0], groups), 1) == column, 1.0, 0.0).T.astype(jnp.bfloat16)


def levels_scale(cfg, narrow, edges):
    length = cfg["length"]
    ends = jnp.concatenate([narrow[:, :LAGS], narrow[:, length:]], axis=1).astype(jnp.float32)
    ends = ends * ends
    high = ends.astype(jnp.bfloat16)
    low = (ends - high.astype(jnp.float32)).astype(jnp.bfloat16)
    middle = narrow[:, LAGS:length].astype(jnp.float32)
    energy = dot(high, edges) + dot(low, edges) + jnp.sum(middle * middle, axis=1, keepdims=True)
    return 1.0 / (length * jnp.sqrt(energy * (1.0 / length) + 1e-05))


def shape_spectra(shapes, forward):
    spectra = []
    for h in range(shapes.shape[1] // LAGS):
        part = shapes[:, h * LAGS : (h + 1) * LAGS]
        mine = dot(jnp.concatenate([part, part], axis=1), forward)
        spectra.append((mine[:, :LAGS], mine[:, LAGS:]))
    return spectra


def match_lines(mine, theirs, scale, inverse):
    real = imag = 0.0
    for (mine_r, mine_i), (theirs_r, theirs_i) in zip(mine, theirs):
        real = real + (theirs_r * mine_r + theirs_i * mine_i)
        imag = imag + (theirs_i * mine_r - theirs_r * mine_i)
    product = jnp.concatenate([real, imag], axis=1)
    high = product.astype(jnp.bfloat16)
    low = (product - high.astype(jnp.float32)).astype(jnp.bfloat16)
    return dot(jnp.concatenate([high, high, low], axis=1), inverse) * scale


def sum_lines(sums, left):
    total = 0.0
    for _ in range(3):
        part = left.astype(jnp.bfloat16)
        left = left - part.astype(jnp.float32)
        total = total + dot(sums, part)
    return total


def tables_of(table_ref):
    back = table_ref[2 * LAGS :, :]
    high, low = back[:, :LAGS], back[:, LAGS:]
    return table_ref[: 2 * LAGS, :], jnp.concatenate([high, low, high], axis=0)


def trace_kernel(cfg, codes_ref, *refs):
    waves_refs, (table_ref, edges_ref, kept_ref, sums_ref) = refs[:-4], refs[-4:]
    shift, goal, column = tile_lines(cfg, codes_ref[...])
    waves = [ref[...].reshape(-1, ref.shape[2]) for ref in waves_refs]
    narrow = cut_traces(cfg, shift, goal, jnp.concatenate(waves, axis=0))
    kept_ref[:, 2 * cfg["length"] :] = levels_scale(cfg, narrow, edges_ref[...])
    sums_ref[...] = line_sums(cfg, column)

    sign = (1 - 2 * (iota((1, LAGS), 1) & 1)).astype(jnp.float32)
    before = None
    for h in range(cfg["length"] // LAGS + 1):
        part = narrow[:, h * LAGS : (h + 1) * LAGS]
        here = dot(jnp.concatenate([part, part], axis=1), table_ref[...])
        here = here[:, :LAGS], here[:, LAGS:]
        if before is not None:
            kept_ref[:, (2 * h - 2) * LAGS : (2 * h - 1) * LAGS] = before[0] + sign * here[1]
            kept_ref[:, (2 * h - 1) * LAGS : 2 * h * LAGS] = before[1] - sign * here[0]
        before = here


def match_kernel(tiles, shapes_hbm, kept_hbm, sums_hbm, table_hbm, sent_ref, *scratch):
    shapes_ref, kept_ref, sums_ref, table_ref, sems = scratch
    tile = shapes_ref.shape[0] // tiles
    groups = sent_ref.shape[0] // tiles
    length = shapes_ref.shape[1]
    copies = []

    def fetch(source, buffer, part=None):
        if part is not None:
            source, buffer = source.at[part], buffer.at[part]
        copies.append(pltpu.make_async_copy(source, buffer, sems.at[len(copies)]))
        copies[-1].start()
        return copies[-1]

    lines = [pl.ds(t * tile, tile) for t in range(tiles)]
    halves = [pl.ds(q * 2 * LAGS, 2 * LAGS) for q in range(2)]
    forward = fetch(table_hbm, table_ref, halves[0])
    shapes, kept = [], []
    for t in range(tiles):
        shapes.append(fetch(shapes_hbm, shapes_ref, lines[t]))
        kept.append(fetch(kept_hbm, kept_ref, lines[t]))
        if t == 0:
            inverse = fetch(table_hbm, table_ref, halves[1])
            sums = fetch(sums_hbm, sums_ref)
    forward.wait()
    for t in range(tiles):
        shapes[t].wait()
        mine = shape_spectra(shapes_ref[lines[t], :], table_ref[: 2 * LAGS, :])
        kept[t].wait()
        theirs = kept_ref[lines[t], :]
        spectra = [
            (theirs[:, 2 * h * LAGS : (2 * h + 1) * LAGS], theirs[:, (2 * h + 1) * LAGS : (2 * h + 2) * LAGS])
            for h in range(length // LAGS)
        ]
        if t == 0:
            for copy in (inverse, sums):
                copy.wait()
        left = match_lines(mine, spectra, theirs[:, 2 * length :], tables_of(table_ref)[1])
        ends = pl.ds(t * groups, groups)
        sent_ref[ends, :] = sum_lines(sums_ref[ends, :], left)


def stack_kernel(factor, parts_ref, stacks_ref, top_ref):
    stacks = jnp.sum(parts_ref[...], axis=0) * factor
    stacks_ref[...] = stacks
    top_ref[...] = jnp.broadcast_to(jnp.max(stacks, axis=0, keepdims=True), top_ref.shape)


def body(waveforms, templates, stations, moveouts):
    devices, group, halves = lax.axis_size(AXES), lax.axis_size(GROUP), lax.axis_size(HALF)
    tpl_count, slot_count = stations.shape
    comps, length = templates.shape[2:]
    station_dev, _, samples = waveforms.shape
    seg_len = length + LAGS
    pairs = tpl_count * slot_count
    capacity = (2 * pairs + devices - 1) // devices
    rows = -(-comps * capacity // 16) * 16
    cfg = dict(
        devices=devices,
        group=group,
        halves=halves,
        station_dev=station_dev,
        tpl_count=tpl_count,
        comps=comps,
        capacity=capacity,
        rows=rows,
        length=length,
        seg_len=seg_len,
        shift_bits=bits_of(samples - seg_len + 1),
        row_bits=bits_of(station_dev),
    )
    table = jnp.asarray(transform_table(LAGS))
    edges = jnp.asarray(edge_table(LAGS))
    tiles = group // SOURCES
    tile = SOURCES * halves * rows
    lines = group * halves * rows
    sums_tile = SOURCES * tpl_count
    kept_len = 2 * length + LAGS
    whole = pl.BlockSpec(memory_space=pltpu.VMEM)
    anywhere = pl.BlockSpec(memory_space=pl.ANY)
    params = pltpu.CompilerParams(vmem_limit_bytes=60 * MIB)
    by_slot = templates.transpose(1, 2, 0, 3)
    waves = waveforms.transpose(1, 0, 2)
    half = lax.axis_index(HALF).reshape(1)

    def work(flops, size):
        return pl.CostEstimate(flops=flops, bytes_accessed=size, transcendentals=0)

    def exchange(x, axes):
        return lax.all_to_all(x, axes, split_axis=0, concat_axis=0, tiled=True)

    def same(shape):
        return pl.BlockSpec(shape, lambda i: (0,) * len(shape))

    def tiled(*shape):
        return pl.BlockSpec(shape, lambda i: (i, 0))

    traces = [waves] + [lax.ppermute(waves, HALF, [(0, 1), (1, 0)])] * (halves - 1)
    codes, goal = pl.pallas_call(
        functools.partial(list_kernel, cfg),
        out_shape=[
            jax.ShapeDtypeStruct((group * halves, LANES), jnp.int32),
            jax.ShapeDtypeStruct((1, pairs), jnp.float32),
        ],
        in_specs=[pl.BlockSpec(memory_space=pltpu.SMEM), whole, whole],
        out_specs=[whole, whole],
        compiler_params=params,
        cost_estimate=work(1, 1),
        name="lists",
    )(half, stations, moveouts)
    codes = exchange(codes.reshape(group, halves, LANES), GROUP).reshape(group * halves, LANES)

    pack_tiles = 4
    packed = pl.pallas_call(
        functools.partial(pack_kernel, cfg),
        out_shape=jax.ShapeDtypeStruct((lines, length), jnp.bfloat16),
        in_specs=[whole, anywhere],
        out_specs=anywhere,
        scratch_shapes=[
            pltpu.VMEM(by_slot.shape, jnp.bfloat16),
            pltpu.VMEM((comps, pairs, length), jnp.bfloat16),
            pltpu.VMEM((lines, length), jnp.bfloat16),
            pltpu.SemaphoreType.DMA,
            pltpu.SemaphoreType.DMA((pack_tiles,)),
        ],
        compiler_params=params,
        cost_estimate=work(5 * 10**9, 1),
        name="pack",
    )(goal, by_slot)
    codes, packed = lax.optimization_barrier((codes, packed))
    arrived = exchange(packed.reshape(group, halves * rows, length), GROUP).reshape(lines, length)

    kept, sums = pl.pallas_call(
        functools.partial(trace_kernel, cfg),
        grid=(tiles,),
        out_shape=[
            jax.ShapeDtypeStruct((lines, kept_len), jnp.float32),
            jax.ShapeDtypeStruct((group * tpl_count, tile), jnp.bfloat16),
        ],
        in_specs=[tiled(SOURCES * halves, LANES)]
        + [same(waves.shape)] * halves
        + [same((2 * LAGS, 2 * LAGS)), same(edges.shape)],
        out_specs=[tiled(tile, kept_len), tiled(sums_tile, tile)],
        compiler_params=params,
        cost_estimate=work(10**12, 1),
        name="traces",
    )(codes, *traces, table, edges)
    operands = (arrived, kept, sums, table)
    sent = pl.pallas_call(
        functools.partial(match_kernel, tiles),
        out_shape=jax.ShapeDtypeStruct((group * tpl_count, LAGS), jnp.float32),
        in_specs=[anywhere] * len(operands),
        out_specs=whole,
        scratch_shapes=[pltpu.VMEM(x.shape, x.dtype) for x in operands]
        + [pltpu.SemaphoreType.DMA((3 + 2 * tiles,))],
        compiler_params=pltpu.CompilerParams(vmem_limit_bytes=57 * MIB),
        name="match",
    )(*operands)

    parts = exchange(sent.reshape(group, tpl_count, LAGS), GROUP)
    stacks, top = pl.pallas_call(
        functools.partial(stack_kernel, math.sqrt(length / (comps * slot_count))),
        out_shape=[
            jax.ShapeDtypeStruct((tpl_count, LAGS), jnp.float32),
            jax.ShapeDtypeStruct((devices, 1, LAGS), jnp.float32),
        ],
        in_specs=[whole],
        out_specs=[whole, whole],
        compiler_params=pltpu.CompilerParams(vmem_limit_bytes=16 * MIB),
        name="stack",
    )(parts)
    return stacks, jnp.max(exchange(top, AXES), axis=(0, 1))


def solution(mesh):
    slow, fast = (mesh.shape[name] for name in GROUP)
    halves = 2 if slow % 2 == 0 else 1
    split = jax.sharding.Mesh(mesh.devices.reshape(halves, slow // halves, fast), AXES)
    placed = (
        P(AXES, None, None),
        P(AXES, None, None, None),
        P(AXES, None),
        P(AXES, None),
    )
    return jax.shard_map(body, mesh=split, in_specs=placed, out_specs=(P(AXES, None), P()), check_vma=False)
```

```python
import functools
import math

import jax
import jax.numpy as jnp
import ml_dtypes
import numpy as np
from jax import lax
from jax.experimental import pallas as pl
from jax.experimental.pallas import tpu as pltpu
from jax.sharding import PartitionSpec as P

LAGS = 256
HALF = "half"
GROUP = ("tmpl", "sta")
AXES = (HALF,) + GROUP
SOURCES = 8
MIB = 1024 * 1024


def bits_of(limit):
    return max(1, (limit - 1).bit_length())


def split_table(table):
    high = table.astype(ml_dtypes.bfloat16)
    return high, (table - high.astype(np.float64)).astype(ml_dtypes.bfloat16)


def transform_table(piece):
    size = 2 * piece
    angle = 2.0 * np.pi * (np.arange(piece) + 0.5) / size
    phase = np.arange(piece)[:, None] * angle[None, :]
    forward = np.concatenate([np.cos(phase), -np.sin(phase)], axis=1)
    inverse = np.concatenate([np.cos(phase.T), -np.sin(phase.T)], axis=0) * (2.0 / size)
    return np.concatenate([*split_table(forward), np.concatenate(split_table(inverse), axis=1)], axis=0)


def edge_table(lag_count):
    sample = np.arange(lag_count)[:, None]
    lag = np.arange(lag_count)[None, :]
    return np.concatenate([sample >= lag, sample < lag], axis=0).astype(ml_dtypes.bfloat16)


def iota(shape, axis):
    return lax.broadcasted_iota(jnp.int32, shape, axis)


def dot(a, b):
    return jnp.dot(a, b, preferred_element_type=jnp.float32)


def exact_dot(a, b):
    return jnp.dot(a, b, precision=lax.Precision.HIGHEST, preferred_element_type=jnp.float32)


def entry_lanes(tpl_count, slot_count):
    pairs = tpl_count * slot_count
    first = iota((slot_count, pairs), 0) * tpl_count
    entry = iota((slot_count, pairs), 1)
    spread = jnp.where((entry >= first) & (entry < first + tpl_count), 1.0, 0.0)
    start = jnp.sum(spread * first.astype(jnp.float32), axis=0, keepdims=True)
    return spread, iota((1, pairs), 1).astype(jnp.float32) - start


def as_lanes(values, spread, place, tpl_count):
    owners = values.shape[0] // tpl_count
    pairs = spread.shape[1]
    wide = exact_dot(values.astype(jnp.float32), spread).reshape(owners, tpl_count, pairs)
    own = iota((1, tpl_count, pairs), 1).astype(jnp.float32) == place.reshape(1, 1, pairs)
    return jnp.sum(jnp.where(own, wide, 0.0), axis=1)


def count_before(hits):
    pairs = hits.shape[1]
    earlier = jnp.where(iota((pairs, pairs), 0) < iota((pairs, pairs), 1), 1.0, 0.0)
    return dot(hits.astype(jnp.bfloat16), earlier.astype(jnp.bfloat16))


def list_kernel(cfg, stations_ref, moveouts_ref, lists_ref):
    lists = stations_ref[...] * (1 << cfg["shift_bits"]) + moveouts_ref[...]
    group, tpl_count, _ = lists_ref.shape
    slot_count = lists.shape[1]
    lists_ref[:, :, :slot_count] = jnp.broadcast_to(lists.reshape(1, tpl_count, slot_count), (group, tpl_count, slot_count))


def pack_kernel(
    cfg, half_ref, stations_ref, templates_hbm, packed_hbm, raw_ref, shapes_ref, packed_ref, in_sem, out_sems
):
    load = pltpu.make_async_copy(templates_hbm, raw_ref, in_sem)
    load.start()
    tpl_count, slot_count = stations_ref.shape
    pairs = tpl_count * slot_count
    devices, group, halves, rows = cfg["devices"], cfg["group"], cfg["halves"], cfg["rows"]
    spread, place = entry_lanes(tpl_count, slot_count)
    station = as_lanes(stations_ref[...], spread, place, tpl_count)
    device = jnp.floor((station + 0.5) * (1.0 / cfg["station_dev"]))
    onehot = jnp.where(iota((devices, pairs), 0).astype(jnp.float32) == device, 1.0, 0.0)
    rank = jnp.sum(onehot * count_before(onehot), axis=0, keepdims=True)
    half = jnp.floor((device + 0.5) * (1.0 / group))
    away = jnp.where(half == half_ref[0].astype(jnp.float32), 0.0, 1.0)
    goal = ((device - half * group) * halves + away) * rows + rank
    goal = jnp.where(rank < float(cfg["capacity"]), goal, -float(group * halves * rows))

    comps, length = raw_ref.shape[1], raw_ref.shape[3]
    load.wait()
    for c in range(comps):
        values = raw_ref[:, c].astype(jnp.float32).reshape(pairs, length)
        centred = values - jnp.mean(values, axis=-1, keepdims=True)
        spread_c = jnp.sqrt(jnp.mean(centred * centred, axis=-1, keepdims=True) + 1e-05)
        shapes_ref[c] = (centred * (1.0 / spread_c)).astype(jnp.bfloat16)

    tiles = out_sems.shape[0]
    tile = packed_ref.shape[0] // tiles
    copies = []
    for step in range(tiles):
        line = iota((tile, pairs), 0).astype(jnp.float32) + float(step * tile)
        total = jnp.zeros((tile, length), jnp.float32)
        for c in range(comps):
            pick = jnp.where(line == goal + float(c * cfg["capacity"]), 1.0, 0.0).astype(jnp.bfloat16)
            total = total + dot(pick, shapes_ref[c])
        part = pl.ds(step * tile, tile)
        packed_ref[part, :] = total.astype(jnp.bfloat16)
        copies.append(pltpu.make_async_copy(packed_ref.at[part], packed_hbm.at[part], out_sems.at[step]))
        copies[-1].start()
    for copy in copies:
        copy.wait()


def tile_lines(cfg, here, lists):
    capacity, rows, comps, halves = cfg["capacity"], cfg["rows"], cfg["comps"], cfg["halves"]
    station_dev, shift_bits, row_bits = cfg["station_dev"], cfg["shift_bits"], cfg["row_bits"]
    tpl_count, slot_count = cfg["tpl_count"], cfg["slot_count"]
    lists = lists[:, :slot_count]
    pairs = tpl_count * slot_count
    tile = SOURCES * halves * rows
    spread, place = entry_lanes(tpl_count, slot_count)
    station = as_lanes(lax.shift_right_logical(lists, shift_bits), spread, place, tpl_count)
    shift = as_lanes(lists & ((1 << shift_bits) - 1), spread, place, tpl_count)

    def per_line(parts):
        wide = [jnp.broadcast_to(x.reshape(SOURCES, 1, pairs), (SOURCES, rows, pairs)) for x in parts]
        return jnp.concatenate(wide, axis=1).reshape(tile, pairs)

    ranks, codes = [], []
    for device in here:
        row = station - (device * station_dev).astype(jnp.float32)
        hit = jnp.where((row >= 0.0) & (row < float(station_dev)), 1.0, 0.0)
        ranks.append(jnp.where(hit > 0.0, count_before(hit), -1.0))
        codes.append(((place + 1.0) * (1 << row_bits) + row) * (1 << shift_bits) + shift)

    line = iota((SOURCES, halves * rows, 1), 1).reshape(tile, 1)
    owner = iota((SOURCES, halves * rows, 1), 0).reshape(tile, 1)
    block = jnp.zeros((tile, 1), jnp.int32)
    for q in range(1, halves):
        block = block + jnp.where(line >= q * rows, 1, 0)
    line = line - block * rows
    comp = jnp.zeros((tile, 1), jnp.int32)
    for c in range(1, comps + 1):
        comp = comp + jnp.where(line >= c * capacity, 1, 0)
    slot = jnp.where(comp < comps, line - comp * capacity, -2).astype(jnp.float32)
    code = jnp.sum(jnp.where(per_line(ranks) == slot, per_line(codes), 0.0), axis=1, keepdims=True)
    code = code.astype(jnp.int32)
    row = lax.shift_right_logical(code, shift_bits) & ((1 << row_bits) - 1)
    tpl = lax.shift_right_logical(code, shift_bits + row_bits) - 1
    goal = (block * comps + comp) * station_dev + row
    return (
        code & ((1 << shift_bits) - 1),
        jnp.where(tpl >= 0, goal, -1),
        jnp.where(tpl >= 0, owner * tpl_count + tpl, -1),
    )


def cut_traces(cfg, shift, goal, waves):
    tile, seg_len, shift_bits = shift.shape[0], cfg["seg_len"], cfg["shift_bits"]
    pick = jnp.where(iota((tile, waves.shape[0]), 1) == goal, 1.0, 0.0).astype(jnp.bfloat16)
    x = dot(pick, waves).astype(jnp.bfloat16)

    def choose(step, moved, still):
        flag = jnp.where((shift & step) != 0, 1.0, 0.0)
        return moved * flag.astype(jnp.bfloat16) + still * (1.0 - flag).astype(jnp.bfloat16)

    for bit in range(shift_bits - 1, 6, -1):
        step = 1 << bit
        width = seg_len + step
        if x.shape[1] < width + step:
            x = jnp.concatenate([x, jnp.zeros((tile, width + step - x.shape[1]), jnp.bfloat16)], axis=1)
        x = choose(step, x[:, step : step + width], x[:, :width])
    for bit in range(min(shift_bits, 7) - 1, -1, -1):
        step = 1 << bit
        x = choose(step, pltpu.roll(x, x.shape[1] - step, 1), x)
    return x[:, :seg_len]


def line_sums(cfg, column):
    groups = SOURCES * cfg["tpl_count"]
    return jnp.where(iota((column.shape[0], groups), 1) == column, 1.0, 0.0).T.astype(jnp.bfloat16)


def levels_scale(cfg, narrow, edges):
    length = cfg["length"]
    ends = jnp.concatenate([narrow[:, :LAGS], narrow[:, length:]], axis=1).astype(jnp.float32)
    ends = ends * ends
    high = ends.astype(jnp.bfloat16)
    low = (ends - high.astype(jnp.float32)).astype(jnp.bfloat16)
    middle = narrow[:, LAGS:length].astype(jnp.float32)
    energy = dot(high, edges) + dot(low, edges) + jnp.sum(middle * middle, axis=1, keepdims=True)
    return 1.0 / (length * jnp.sqrt(energy * (1.0 / length) + 1e-05))


def shape_spectra(shapes, forward):
    spectra = []
    for h in range(shapes.shape[1] // LAGS):
        part = shapes[:, h * LAGS : (h + 1) * LAGS]
        mine = dot(jnp.concatenate([part, part], axis=1), forward)
        spectra.append((mine[:, :LAGS], mine[:, LAGS:]))
    return spectra


def match_lines(mine, theirs, scale, inverse):
    real = imag = 0.0
    for (mine_r, mine_i), (theirs_r, theirs_i) in zip(mine, theirs):
        real = real + (theirs_r * mine_r + theirs_i * mine_i)
        imag = imag + (theirs_i * mine_r - theirs_r * mine_i)
    product = jnp.concatenate([real, imag], axis=1)
    high = product.astype(jnp.bfloat16)
    low = (product - high.astype(jnp.float32)).astype(jnp.bfloat16)
    return dot(jnp.concatenate([high, high, low], axis=1), inverse) * scale


def sum_lines(sums, left):
    total = 0.0
    for _ in range(3):
        part = left.astype(jnp.bfloat16)
        left = left - part.astype(jnp.float32)
        total = total + dot(sums, part)
    return total


def tables_of(table_ref):
    back = table_ref[2 * LAGS :, :]
    high, low = back[:, :LAGS], back[:, LAGS:]
    return table_ref[: 2 * LAGS, :], jnp.concatenate([high, low, high], axis=0)


def trace_kernel(cfg, here_ref, lists_ref, *refs):
    waves_refs, (table_ref, edges_ref, kept_ref, sums_ref) = refs[:-4], refs[-4:]
    here = [here_ref[q] for q in range(cfg["halves"])]
    shift, goal, column = tile_lines(cfg, here, lists_ref[...])
    waves = [ref[...].reshape(-1, ref.shape[2]) for ref in waves_refs]
    narrow = cut_traces(cfg, shift, goal, jnp.concatenate(waves, axis=0))
    kept_ref[:, 2 * cfg["length"] :] = levels_scale(cfg, narrow, edges_ref[...])
    sums_ref[...] = line_sums(cfg, column)

    sign = (1 - 2 * (iota((1, LAGS), 1) & 1)).astype(jnp.float32)
    before = None
    for h in range(cfg["length"] // LAGS + 1):
        part = narrow[:, h * LAGS : (h + 1) * LAGS]
        here = dot(jnp.concatenate([part, part], axis=1), table_ref[...])
        here = here[:, :LAGS], here[:, LAGS:]
        if before is not None:
            kept_ref[:, (2 * h - 2) * LAGS : (2 * h - 1) * LAGS] = before[0] + sign * here[1]
            kept_ref[:, (2 * h - 1) * LAGS : 2 * h * LAGS] = before[1] - sign * here[0]
        before = here


def match_kernel(tiles, shapes_hbm, kept_hbm, sums_hbm, table_hbm, sent_ref, *scratch):
    shapes_ref, kept_ref, sums_ref, table_ref, sems = scratch
    tile = shapes_ref.shape[0] // tiles
    groups = sent_ref.shape[0] // tiles
    length = shapes_ref.shape[1]
    copies = []

    def fetch(source, buffer, part=None):
        if part is not None:
            source, buffer = source.at[part], buffer.at[part]
        copies.append(pltpu.make_async_copy(source, buffer, sems.at[len(copies)]))
        copies[-1].start()
        return copies[-1]

    lines = [pl.ds(t * tile, tile) for t in range(tiles)]
    halves = [pl.ds(q * 2 * LAGS, 2 * LAGS) for q in range(2)]
    forward = fetch(table_hbm, table_ref, halves[0])
    part = tile // 2
    shapes, kept = [], []
    for t in range(tiles):
        shapes.append(fetch(shapes_hbm, shapes_ref, lines[t]))
        kept.append([fetch(kept_hbm, kept_ref, pl.ds(t * tile + k * part, part)) for k in range(2)])
        if t == 0:
            inverse = fetch(table_hbm, table_ref, halves[1])
            sums = fetch(sums_hbm, sums_ref)
    forward.wait()
    for t in range(tiles):
        shapes[t].wait()
        mine = shape_spectra(shapes_ref[lines[t], :], table_ref[: 2 * LAGS, :])
        if t == 0:
            for copy in (inverse, sums):
                copy.wait()
        ends = pl.ds(t * groups, groups)
        total = 0.0
        for k in range(2):
            kept[t][k].wait()
            theirs = kept_ref[pl.ds(t * tile + k * part, part), :]
            spectra = [
                (theirs[:, 2 * h * LAGS : (2 * h + 1) * LAGS], theirs[:, (2 * h + 1) * LAGS : (2 * h + 2) * LAGS])
                for h in range(length // LAGS)
            ]
            rows = slice(k * part, (k + 1) * part)
            ours = [(real[rows], imag[rows]) for real, imag in mine]
            left = match_lines(ours, spectra, theirs[:, 2 * length :], tables_of(table_ref)[1])
            total = total + sum_lines(sums_ref[ends, rows], left)
        sent_ref[ends, :] = total


def stack_kernel(factor, parts_ref, stacks_ref, top_ref):
    stacks = jnp.sum(parts_ref[...], axis=0) * factor
    stacks_ref[...] = stacks
    top_ref[...] = jnp.broadcast_to(jnp.max(stacks, axis=0, keepdims=True), top_ref.shape)


def body(waveforms, templates, stations, moveouts):
    devices, group, halves = lax.axis_size(AXES), lax.axis_size(GROUP), lax.axis_size(HALF)
    tpl_count, slot_count = stations.shape
    comps, length = templates.shape[2:]
    station_dev, _, samples = waveforms.shape
    seg_len = length + LAGS
    pairs = tpl_count * slot_count
    capacity = (2 * pairs + devices - 1) // devices
    rows = -(-comps * capacity // 16) * 16
    cfg = dict(
        devices=devices,
        group=group,
        halves=halves,
        station_dev=station_dev,
        tpl_count=tpl_count,
        slot_count=slot_count,
        comps=comps,
        capacity=capacity,
        rows=rows,
        length=length,
        seg_len=seg_len,
        shift_bits=bits_of(samples - seg_len + 1),
        row_bits=bits_of(station_dev),
    )
    table = jnp.asarray(transform_table(LAGS))
    edges = jnp.asarray(edge_table(LAGS))
    tiles = group // SOURCES
    tile = SOURCES * halves * rows
    lines = group * halves * rows
    sums_tile = SOURCES * tpl_count
    kept_len = 2 * length + LAGS
    whole = pl.BlockSpec(memory_space=pltpu.VMEM)
    anywhere = pl.BlockSpec(memory_space=pl.ANY)
    params = pltpu.CompilerParams(vmem_limit_bytes=60 * MIB)
    by_slot = templates.transpose(1, 2, 0, 3)
    waves = waveforms.transpose(1, 0, 2)
    half = lax.axis_index(HALF).reshape(1)
    here = (lax.axis_index(AXES) + group * jnp.arange(halves, dtype=jnp.int32)) % devices

    def work(flops, size):
        return pl.CostEstimate(flops=flops, bytes_accessed=size, transcendentals=0)

    def exchange(x, axes):
        return lax.all_to_all(x, axes, split_axis=0, concat_axis=0, tiled=True)

    def same(shape):
        return pl.BlockSpec(shape, lambda i: (0,) * len(shape))

    def tiled(*shape):
        return pl.BlockSpec(shape, lambda i: (i, 0))

    traces = [waves] + [lax.ppermute(waves, HALF, [(0, 1), (1, 0)])] * (halves - 1)
    lists = pl.pallas_call(
        functools.partial(list_kernel, cfg),
        out_shape=jax.ShapeDtypeStruct((group, tpl_count, -(-slot_count // 128) * 128), jnp.int32),
        in_specs=[whole, whole],
        out_specs=whole,
        compiler_params=params,
        cost_estimate=work(1, 1),
        name="lists",
    )(stations, moveouts)
    lists = exchange(lists, GROUP).reshape(group * tpl_count, lists.shape[2])

    pack_tiles = 4
    packed = pl.pallas_call(
        functools.partial(pack_kernel, cfg),
        out_shape=jax.ShapeDtypeStruct((lines, length), jnp.bfloat16),
        in_specs=[pl.BlockSpec(memory_space=pltpu.SMEM), whole, anywhere],
        out_specs=anywhere,
        scratch_shapes=[
            pltpu.VMEM(by_slot.shape, jnp.bfloat16),
            pltpu.VMEM((comps, pairs, length), jnp.bfloat16),
            pltpu.VMEM((lines, length), jnp.bfloat16),
            pltpu.SemaphoreType.DMA,
            pltpu.SemaphoreType.DMA((pack_tiles,)),
        ],
        compiler_params=params,
        cost_estimate=work(5 * 10**9, 1),
        name="pack",
    )(half, stations, by_slot)
    _, packed = lax.optimization_barrier((lists, packed))
    arrived = exchange(packed.reshape(group, halves * rows, length), GROUP).reshape(lines, length)

    kept, sums = pl.pallas_call(
        functools.partial(trace_kernel, cfg),
        grid=(tiles,),
        out_shape=[
            jax.ShapeDtypeStruct((lines, kept_len), jnp.float32),
            jax.ShapeDtypeStruct((group * tpl_count, tile), jnp.bfloat16),
        ],
        in_specs=[pl.BlockSpec(memory_space=pltpu.SMEM), tiled(sums_tile, lists.shape[1])]
        + [same(waves.shape)] * halves
        + [same((2 * LAGS, 2 * LAGS)), same(edges.shape)],
        out_specs=[tiled(tile, kept_len), tiled(sums_tile, tile)],
        compiler_params=params,
        cost_estimate=work(10**12, 1),
        name="traces",
    )(here, lists, *traces, table, edges)
    operands = (arrived, kept, sums, table)
    sent = pl.pallas_call(
        functools.partial(match_kernel, tiles),
        out_shape=jax.ShapeDtypeStruct((group * tpl_count, LAGS), jnp.float32),
        in_specs=[anywhere] * len(operands),
        out_specs=whole,
        scratch_shapes=[pltpu.VMEM(x.shape, x.dtype) for x in operands]
        + [pltpu.SemaphoreType.DMA((3 + 3 * tiles,))],
        compiler_params=pltpu.CompilerParams(vmem_limit_bytes=57 * MIB),
        name="match",
    )(*operands)

    parts = exchange(sent.reshape(group, tpl_count, LAGS), GROUP)
    stacks, top = pl.pallas_call(
        functools.partial(stack_kernel, math.sqrt(length / (comps * slot_count))),
        out_shape=[
            jax.ShapeDtypeStruct((tpl_count, LAGS), jnp.float32),
            jax.ShapeDtypeStruct((devices, 1, LAGS), jnp.float32),
        ],
        in_specs=[whole],
        out_specs=[whole, whole],
        compiler_params=pltpu.CompilerParams(vmem_limit_bytes=16 * MIB),
        name="stack",
    )(parts)
    return stacks, jnp.max(exchange(top, AXES), axis=(0, 1))


def solution(mesh):
    slow, fast = (mesh.shape[name] for name in GROUP)
    halves = 2 if slow % 2 == 0 else 1
    split = jax.sharding.Mesh(mesh.devices.reshape(halves, slow // halves, fast), AXES)
    placed = (
        P(AXES, None, None),
        P(AXES, None, None, None),
        P(AXES, None),
        P(AXES, None),
    )
    return jax.shard_map(body, mesh=split, in_specs=placed, out_specs=(P(AXES, None), P()), check_vma=False)
```

```python
import functools
import math

import jax
import jax.numpy as jnp
import ml_dtypes
import numpy as np
from jax import lax
from jax.experimental import pallas as pl
from jax.experimental.pallas import tpu as pltpu
from jax.sharding import PartitionSpec as P

LAGS = 256
HALF = "half"
GROUP = ("tmpl", "sta")
AXES = (HALF,) + GROUP
SOURCES = 16
MIB = 1024 * 1024


def bits_of(limit):
    return max(1, (limit - 1).bit_length())


def split_table(table):
    high = table.astype(ml_dtypes.bfloat16)
    return high, (table - high.astype(np.float64)).astype(ml_dtypes.bfloat16)


def transform_table(piece):
    size = 2 * piece
    angle = 2.0 * np.pi * (np.arange(piece) + 0.5) / size
    phase = np.arange(piece)[:, None] * angle[None, :]
    forward = np.concatenate([np.cos(phase), -np.sin(phase)], axis=1)
    inverse = np.concatenate([np.cos(phase.T), -np.sin(phase.T)], axis=0) * (2.0 / size)
    return np.concatenate([*split_table(forward), np.concatenate(split_table(inverse), axis=1)], axis=0)


def edge_table(lag_count):
    sample = np.arange(lag_count)[:, None]
    lag = np.arange(lag_count)[None, :]
    return np.concatenate([sample >= lag, sample < lag], axis=0).astype(ml_dtypes.bfloat16)


def iota(shape, axis):
    return lax.broadcasted_iota(jnp.int32, shape, axis)


def dot(a, b):
    return jnp.dot(a, b, preferred_element_type=jnp.float32)


def exact_dot(a, b):
    return jnp.dot(a, b, precision=lax.Precision.HIGHEST, preferred_element_type=jnp.float32)


def entry_lanes(tpl_count, slot_count):
    pairs = tpl_count * slot_count
    first = iota((slot_count, pairs), 0) * tpl_count
    entry = iota((slot_count, pairs), 1)
    spread = jnp.where((entry >= first) & (entry < first + tpl_count), 1.0, 0.0)
    start = jnp.sum(spread * first.astype(jnp.float32), axis=0, keepdims=True)
    return spread, iota((1, pairs), 1).astype(jnp.float32) - start


def as_lanes(values, spread, place, tpl_count):
    owners = values.shape[0] // tpl_count
    pairs = spread.shape[1]
    wide = exact_dot(values.astype(jnp.float32), spread).reshape(owners, tpl_count, pairs)
    own = iota((1, tpl_count, pairs), 1).astype(jnp.float32) == place.reshape(1, 1, pairs)
    return jnp.sum(jnp.where(own, wide, 0.0), axis=1)


def count_before(hits):
    pairs = hits.shape[1]
    earlier = jnp.where(iota((pairs, pairs), 0) < iota((pairs, pairs), 1), 1.0, 0.0)
    return dot(hits.astype(jnp.bfloat16), earlier.astype(jnp.bfloat16))


def list_kernel(cfg, stations_ref, moveouts_ref, lists_ref):
    lists = stations_ref[...] * (1 << cfg["shift_bits"]) + moveouts_ref[...]
    group, tpl_count, _ = lists_ref.shape
    slot_count = lists.shape[1]
    lists_ref[:, :, :slot_count] = jnp.broadcast_to(lists.reshape(1, tpl_count, slot_count), (group, tpl_count, slot_count))


def pack_kernel(
    cfg, half_ref, stations_ref, templates_hbm, packed_hbm, raw_ref, shapes_ref, packed_ref, in_sem, out_sems
):
    load = pltpu.make_async_copy(templates_hbm, raw_ref, in_sem)
    load.start()
    tpl_count, slot_count = stations_ref.shape
    pairs = tpl_count * slot_count
    devices, group, halves, rows = cfg["devices"], cfg["group"], cfg["halves"], cfg["rows"]
    spread, place = entry_lanes(tpl_count, slot_count)
    station = as_lanes(stations_ref[...], spread, place, tpl_count)
    device = jnp.floor((station + 0.5) * (1.0 / cfg["station_dev"]))
    onehot = jnp.where(iota((devices, pairs), 0).astype(jnp.float32) == device, 1.0, 0.0)
    rank = jnp.sum(onehot * count_before(onehot), axis=0, keepdims=True)
    half = jnp.floor((device + 0.5) * (1.0 / group))
    away = jnp.where(half == half_ref[0].astype(jnp.float32), 0.0, 1.0)
    goal = ((device - half * group) * halves + away) * rows + rank
    goal = jnp.where(rank < float(cfg["capacity"]), goal, -float(group * halves * rows))

    comps, length = raw_ref.shape[1], raw_ref.shape[3]
    load.wait()
    for c in range(comps):
        values = raw_ref[:, c].astype(jnp.float32).reshape(pairs, length)
        centred = values - jnp.mean(values, axis=-1, keepdims=True)
        spread_c = jnp.sqrt(jnp.mean(centred * centred, axis=-1, keepdims=True) + 1e-05)
        shapes_ref[c] = (centred * (1.0 / spread_c)).astype(jnp.bfloat16)

    tiles = out_sems.shape[0]
    tile = packed_ref.shape[0] // tiles
    copies = []
    for step in range(tiles):
        line = iota((tile, pairs), 0).astype(jnp.float32) + float(step * tile)
        total = jnp.zeros((tile, length), jnp.float32)
        for c in range(comps):
            pick = jnp.where(line == goal + float(c * cfg["capacity"]), 1.0, 0.0).astype(jnp.bfloat16)
            total = total + dot(pick, shapes_ref[c])
        part = pl.ds(step * tile, tile)
        packed_ref[part, :] = total.astype(jnp.bfloat16)
        copies.append(pltpu.make_async_copy(packed_ref.at[part], packed_hbm.at[part], out_sems.at[step]))
        copies[-1].start()
    for copy in copies:
        copy.wait()


def tile_lines(cfg, here, lists):
    capacity, rows, comps, halves = cfg["capacity"], cfg["rows"], cfg["comps"], cfg["halves"]
    station_dev, shift_bits, row_bits = cfg["station_dev"], cfg["shift_bits"], cfg["row_bits"]
    tpl_count, slot_count = cfg["tpl_count"], cfg["slot_count"]
    lists = lists[:, :slot_count]
    pairs = tpl_count * slot_count
    tile = SOURCES * halves * rows
    spread, place = entry_lanes(tpl_count, slot_count)
    station = as_lanes(lax.shift_right_logical(lists, shift_bits), spread, place, tpl_count)
    shift = as_lanes(lists & ((1 << shift_bits) - 1), spread, place, tpl_count)

    def per_line(parts):
        wide = [jnp.broadcast_to(x.reshape(SOURCES, 1, pairs), (SOURCES, rows, pairs)) for x in parts]
        return jnp.concatenate(wide, axis=1).reshape(tile, pairs)

    ranks, codes = [], []
    for device in here:
        row = station - (device * station_dev).astype(jnp.float32)
        hit = jnp.where((row >= 0.0) & (row < float(station_dev)), 1.0, 0.0)
        ranks.append(jnp.where(hit > 0.0, count_before(hit), -1.0))
        codes.append(((place + 1.0) * (1 << row_bits) + row) * (1 << shift_bits) + shift)

    line = iota((SOURCES, halves * rows, 1), 1).reshape(tile, 1)
    owner = iota((SOURCES, halves * rows, 1), 0).reshape(tile, 1)
    block = jnp.zeros((tile, 1), jnp.int32)
    for q in range(1, halves):
        block = block + jnp.where(line >= q * rows, 1, 0)
    line = line - block * rows
    comp = jnp.zeros((tile, 1), jnp.int32)
    for c in range(1, comps + 1):
        comp = comp + jnp.where(line >= c * capacity, 1, 0)
    slot = jnp.where(comp < comps, line - comp * capacity, -2).astype(jnp.float32)
    code = jnp.sum(jnp.where(per_line(ranks) == slot, per_line(codes), 0.0), axis=1, keepdims=True)
    code = code.astype(jnp.int32)
    row = lax.shift_right_logical(code, shift_bits) & ((1 << row_bits) - 1)
    tpl = lax.shift_right_logical(code, shift_bits + row_bits) - 1
    goal = (block * comps + comp) * station_dev + row
    return (
        code & ((1 << shift_bits) - 1),
        jnp.where(tpl >= 0, goal, -1),
        jnp.where(tpl >= 0, owner * tpl_count + tpl, -1),
    )


def cut_traces(cfg, shift, goal, waves):
    tile, seg_len, shift_bits = shift.shape[0], cfg["seg_len"], cfg["shift_bits"]
    pick = jnp.where(iota((tile, waves.shape[0]), 1) == goal, 1.0, 0.0).astype(jnp.bfloat16)
    x = dot(pick, waves).astype(jnp.bfloat16)

    def choose(step, moved, still):
        flag = jnp.where((shift & step) != 0, 1.0, 0.0)
        return moved * flag.astype(jnp.bfloat16) + still * (1.0 - flag).astype(jnp.bfloat16)

    for bit in range(shift_bits - 1, 6, -1):
        step = 1 << bit
        width = seg_len + step
        if x.shape[1] < width + step:
            x = jnp.concatenate([x, jnp.zeros((tile, width + step - x.shape[1]), jnp.bfloat16)], axis=1)
        x = choose(step, x[:, step : step + width], x[:, :width])
    for bit in range(min(shift_bits, 7) - 1, -1, -1):
        step = 1 << bit
        x = choose(step, pltpu.roll(x, x.shape[1] - step, 1), x)
    return x[:, :seg_len]


def line_sums(cfg, column):
    groups = SOURCES * cfg["tpl_count"]
    return jnp.where(iota((column.shape[0], groups), 1) == column, 1.0, 0.0).T.astype(jnp.bfloat16)


def levels_scale(cfg, narrow, edges):
    length = cfg["length"]
    ends = jnp.concatenate([narrow[:, :LAGS], narrow[:, length:]], axis=1).astype(jnp.float32)
    ends = ends * ends
    high = ends.astype(jnp.bfloat16)
    low = (ends - high.astype(jnp.float32)).astype(jnp.bfloat16)
    middle = narrow[:, LAGS:length].astype(jnp.float32)
    energy = dot(high, edges) + dot(low, edges) + jnp.sum(middle * middle, axis=1, keepdims=True)
    return 1.0 / (length * jnp.sqrt(energy * (1.0 / length) + 1e-05))


def shape_spectra(shapes, forward):
    spectra = []
    for h in range(shapes.shape[1] // LAGS):
        part = shapes[:, h * LAGS : (h + 1) * LAGS]
        mine = dot(jnp.concatenate([part, part], axis=1), forward)
        spectra.append((mine[:, :LAGS], mine[:, LAGS:]))
    return spectra


def match_lines(mine, theirs, scale, inverse):
    real = imag = 0.0
    for (mine_r, mine_i), (theirs_r, theirs_i) in zip(mine, theirs):
        real = real + (theirs_r * mine_r + theirs_i * mine_i)
        imag = imag + (theirs_i * mine_r - theirs_r * mine_i)
    product = jnp.concatenate([real, imag], axis=1)
    high = product.astype(jnp.bfloat16)
    low = (product - high.astype(jnp.float32)).astype(jnp.bfloat16)
    return dot(jnp.concatenate([high, high, low], axis=1), inverse) * scale


def sum_lines(sums, left):
    total = 0.0
    for _ in range(3):
        part = left.astype(jnp.bfloat16)
        left = left - part.astype(jnp.float32)
        total = total + dot(sums, part)
    return total


def tables_of(table_ref):
    back = table_ref[2 * LAGS :, :]
    high, low = back[:, :LAGS], back[:, LAGS:]
    return table_ref[: 2 * LAGS, :], jnp.concatenate([high, low, high], axis=0)


def trace_kernel(cfg, here_ref, lists_ref, *refs):
    waves_refs, (table_ref, edges_ref, kept_ref, sums_ref) = refs[:-4], refs[-4:]
    here = [here_ref[q] for q in range(cfg["halves"])]
    shift, goal, column = tile_lines(cfg, here, lists_ref[...])
    waves = [ref[...].reshape(-1, ref.shape[2]) for ref in waves_refs]
    narrow = cut_traces(cfg, shift, goal, jnp.concatenate(waves, axis=0))
    kept_ref[:, 2 * cfg["length"] :] = levels_scale(cfg, narrow, edges_ref[...])
    sums_ref[...] = line_sums(cfg, column)

    sign = (1 - 2 * (iota((1, LAGS), 1) & 1)).astype(jnp.float32)
    before = None
    for h in range(cfg["length"] // LAGS + 1):
        part = narrow[:, h * LAGS : (h + 1) * LAGS]
        here = dot(jnp.concatenate([part, part], axis=1), table_ref[...])
        here = here[:, :LAGS], here[:, LAGS:]
        if before is not None:
            kept_ref[:, (2 * h - 2) * LAGS : (2 * h - 1) * LAGS] = before[0] + sign * here[1]
            kept_ref[:, (2 * h - 1) * LAGS : 2 * h * LAGS] = before[1] - sign * here[0]
        before = here


def match_kernel(tiles, shapes_hbm, kept_hbm, sums_hbm, table_hbm, sent_ref, *scratch):
    shapes_ref, kept_ref, sums_ref, table_ref, sems = scratch
    tile = shapes_ref.shape[0] // tiles
    groups = sent_ref.shape[0] // tiles
    length = shapes_ref.shape[1]
    copies = []

    def fetch(source, buffer, part=None):
        if part is not None:
            source, buffer = source.at[part], buffer.at[part]
        copies.append(pltpu.make_async_copy(source, buffer, sems.at[len(copies)]))
        copies[-1].start()
        return copies[-1]

    lines = [pl.ds(t * tile, tile) for t in range(tiles)]
    halves = [pl.ds(q * 2 * LAGS, 2 * LAGS) for q in range(2)]
    forward = fetch(table_hbm, table_ref, halves[0])
    parts = 4
    part = tile // parts
    shapes, kept = [], []
    for t in range(tiles):
        shapes.append(fetch(shapes_hbm, shapes_ref, lines[t]))
        kept.append([fetch(kept_hbm, kept_ref, pl.ds(t * tile + k * part, part)) for k in range(parts)])
        if t == 0:
            inverse = fetch(table_hbm, table_ref, halves[1])
            sums = fetch(sums_hbm, sums_ref)
    forward.wait()
    for t in range(tiles):
        shapes[t].wait()
        mine = shape_spectra(shapes_ref[lines[t], :], table_ref[: 2 * LAGS, :])
        if t == 0:
            for copy in (inverse, sums):
                copy.wait()
        ends = pl.ds(t * groups, groups)
        total = 0.0
        for k in range(parts):
            kept[t][k].wait()
            theirs = kept_ref[pl.ds(t * tile + k * part, part), :]
            spectra = [
                (theirs[:, 2 * h * LAGS : (2 * h + 1) * LAGS], theirs[:, (2 * h + 1) * LAGS : (2 * h + 2) * LAGS])
                for h in range(length // LAGS)
            ]
            rows = slice(k * part, (k + 1) * part)
            ours = [(real[rows], imag[rows]) for real, imag in mine]
            left = match_lines(ours, spectra, theirs[:, 2 * length :], tables_of(table_ref)[1])
            total = total + sum_lines(sums_ref[ends, rows], left)
        sent_ref[ends, :] = total


def stack_kernel(factor, parts_ref, stacks_ref, top_ref):
    stacks = jnp.sum(parts_ref[...], axis=0) * factor
    stacks_ref[...] = stacks
    top_ref[...] = jnp.broadcast_to(jnp.max(stacks, axis=0, keepdims=True), top_ref.shape)


def body(waveforms, templates, stations, moveouts):
    devices, group, halves = lax.axis_size(AXES), lax.axis_size(GROUP), lax.axis_size(HALF)
    tpl_count, slot_count = stations.shape
    comps, length = templates.shape[2:]
    station_dev, _, samples = waveforms.shape
    seg_len = length + LAGS
    pairs = tpl_count * slot_count
    capacity = (2 * pairs + devices - 1) // devices
    rows = -(-comps * capacity // 16) * 16
    cfg = dict(
        devices=devices,
        group=group,
        halves=halves,
        station_dev=station_dev,
        tpl_count=tpl_count,
        slot_count=slot_count,
        comps=comps,
        capacity=capacity,
        rows=rows,
        length=length,
        seg_len=seg_len,
        shift_bits=bits_of(samples - seg_len + 1),
        row_bits=bits_of(station_dev),
    )
    table = jnp.asarray(transform_table(LAGS))
    edges = jnp.asarray(edge_table(LAGS))
    tiles = group // SOURCES
    tile = SOURCES * halves * rows
    lines = group * halves * rows
    sums_tile = SOURCES * tpl_count
    kept_len = 2 * length + LAGS
    whole = pl.BlockSpec(memory_space=pltpu.VMEM)
    anywhere = pl.BlockSpec(memory_space=pl.ANY)
    params = pltpu.CompilerParams(vmem_limit_bytes=60 * MIB)
    by_slot = templates.transpose(1, 2, 0, 3)
    waves = waveforms.transpose(1, 0, 2)
    half = lax.axis_index(HALF).reshape(1)
    here = (lax.axis_index(AXES) + group * jnp.arange(halves, dtype=jnp.int32)) % devices

    def work(flops, size):
        return pl.CostEstimate(flops=flops, bytes_accessed=size, transcendentals=0)

    def exchange(x, axes):
        return lax.all_to_all(x, axes, split_axis=0, concat_axis=0, tiled=True)

    def same(shape):
        return pl.BlockSpec(shape, lambda i: (0,) * len(shape))

    def tiled(*shape):
        return pl.BlockSpec(shape, lambda i: (i, 0))

    traces = [waves] + [lax.ppermute(waves, HALF, [(0, 1), (1, 0)])] * (halves - 1)
    lists = pl.pallas_call(
        functools.partial(list_kernel, cfg),
        out_shape=jax.ShapeDtypeStruct((group, tpl_count, -(-slot_count // 128) * 128), jnp.int32),
        in_specs=[whole, whole],
        out_specs=whole,
        compiler_params=params,
        cost_estimate=work(1, 1),
        name="lists",
    )(stations, moveouts)
    lists = exchange(lists, GROUP).reshape(group * tpl_count, lists.shape[2])

    pack_tiles = 4
    packed = pl.pallas_call(
        functools.partial(pack_kernel, cfg),
        out_shape=jax.ShapeDtypeStruct((lines, length), jnp.bfloat16),
        in_specs=[pl.BlockSpec(memory_space=pltpu.SMEM), whole, anywhere],
        out_specs=anywhere,
        scratch_shapes=[
            pltpu.VMEM(by_slot.shape, jnp.bfloat16),
            pltpu.VMEM((comps, pairs, length), jnp.bfloat16),
            pltpu.VMEM((lines, length), jnp.bfloat16),
            pltpu.SemaphoreType.DMA,
            pltpu.SemaphoreType.DMA((pack_tiles,)),
        ],
        compiler_params=params,
        cost_estimate=work(5 * 10**9, 1),
        name="pack",
    )(half, stations, by_slot)
    _, packed = lax.optimization_barrier((lists, packed))
    arrived = exchange(packed.reshape(group, halves * rows, length), GROUP).reshape(lines, length)

    kept, sums = pl.pallas_call(
        functools.partial(trace_kernel, cfg),
        grid=(tiles,),
        out_shape=[
            jax.ShapeDtypeStruct((lines, kept_len), jnp.float32),
            jax.ShapeDtypeStruct((group * tpl_count, tile), jnp.bfloat16),
        ],
        in_specs=[pl.BlockSpec(memory_space=pltpu.SMEM), tiled(sums_tile, lists.shape[1])]
        + [same(waves.shape)] * halves
        + [same((2 * LAGS, 2 * LAGS)), same(edges.shape)],
        out_specs=[tiled(tile, kept_len), tiled(sums_tile, tile)],
        compiler_params=params,
        cost_estimate=work(10**12, 1),
        name="traces",
    )(here, lists, *traces, table, edges)
    operands = (arrived, kept, sums, table)
    sent = pl.pallas_call(
        functools.partial(match_kernel, tiles),
        out_shape=jax.ShapeDtypeStruct((group * tpl_count, LAGS), jnp.float32),
        in_specs=[anywhere] * len(operands),
        out_specs=whole,
        scratch_shapes=[pltpu.VMEM(x.shape, x.dtype) for x in operands]
        + [pltpu.SemaphoreType.DMA((3 + 5 * tiles,))],
        compiler_params=pltpu.CompilerParams(vmem_limit_bytes=57 * MIB),
        name="match",
    )(*operands)

    parts = exchange(sent.reshape(group, tpl_count, LAGS), GROUP)
    stacks, top = pl.pallas_call(
        functools.partial(stack_kernel, math.sqrt(length / (comps * slot_count))),
        out_shape=[
            jax.ShapeDtypeStruct((tpl_count, LAGS), jnp.float32),
            jax.ShapeDtypeStruct((devices, 1, LAGS), jnp.float32),
        ],
        in_specs=[whole],
        out_specs=[whole, whole],
        compiler_params=pltpu.CompilerParams(vmem_limit_bytes=16 * MIB),
        name="stack",
    )(parts)
    return stacks, jnp.max(exchange(top, AXES), axis=(0, 1))


def solution(mesh):
    slow, fast = (mesh.shape[name] for name in GROUP)
    halves = 2 if slow % 2 == 0 else 1
    split = jax.sharding.Mesh(mesh.devices.reshape(halves, slow // halves, fast), AXES)
    placed = (
        P(AXES, None, None),
        P(AXES, None, None, None),
        P(AXES, None),
        P(AXES, None),
    )
    return jax.shard_map(body, mesh=split, in_specs=placed, out_specs=(P(AXES, None), P()), check_vma=False)
```

```python
import functools
import math

import jax
import jax.numpy as jnp
import ml_dtypes
import numpy as np
from jax import lax
from jax.experimental import pallas as pl
from jax.experimental.pallas import tpu as pltpu
from jax.sharding import PartitionSpec as P

LAGS = 256
HALF = "half"
GROUP = ("tmpl", "sta")
AXES = (HALF,) + GROUP
SOURCES = 8
MIB = 1024 * 1024


def bits_of(limit):
    return max(1, (limit - 1).bit_length())


def split_table(table):
    high = table.astype(ml_dtypes.bfloat16)
    return high, (table - high.astype(np.float64)).astype(ml_dtypes.bfloat16)


def transform_table(piece):
    size = 2 * piece
    angle = 2.0 * np.pi * (np.arange(piece) + 0.5) / size
    phase = np.arange(piece)[:, None] * angle[None, :]
    forward = np.concatenate([np.cos(phase), -np.sin(phase)], axis=1)
    inverse = np.concatenate([np.cos(phase.T), -np.sin(phase.T)], axis=0) * (2.0 / size)
    return np.concatenate([*split_table(forward), np.concatenate(split_table(inverse), axis=1)], axis=0)


def edge_table(lag_count):
    sample = np.arange(lag_count)[:, None]
    lag = np.arange(lag_count)[None, :]
    return np.concatenate([sample >= lag, sample < lag], axis=0).astype(ml_dtypes.bfloat16)


def iota(shape, axis):
    return lax.broadcasted_iota(jnp.int32, shape, axis)


def dot(a, b):
    return jnp.dot(a, b, preferred_element_type=jnp.float32)


def exact_dot(a, b):
    return jnp.dot(a, b, precision=lax.Precision.HIGHEST, preferred_element_type=jnp.float32)


def entry_lanes(tpl_count, slot_count):
    pairs = tpl_count * slot_count
    first = iota((slot_count, pairs), 0) * tpl_count
    entry = iota((slot_count, pairs), 1)
    spread = jnp.where((entry >= first) & (entry < first + tpl_count), 1.0, 0.0)
    start = jnp.sum(spread * first.astype(jnp.float32), axis=0, keepdims=True)
    return spread, iota((1, pairs), 1).astype(jnp.float32) - start


def as_lanes(values, spread, place, tpl_count):
    owners = values.shape[0] // tpl_count
    pairs = spread.shape[1]
    wide = exact_dot(values.astype(jnp.float32), spread).reshape(owners, tpl_count, pairs)
    own = iota((1, tpl_count, pairs), 1).astype(jnp.float32) == place.reshape(1, 1, pairs)
    return jnp.sum(jnp.where(own, wide, 0.0), axis=1)


def count_before(hits):
    pairs = hits.shape[1]
    earlier = jnp.where(iota((pairs, pairs), 0) < iota((pairs, pairs), 1), 1.0, 0.0)
    return dot(hits.astype(jnp.bfloat16), earlier.astype(jnp.bfloat16))


def list_kernel(cfg, stations_ref, moveouts_ref, lists_ref):
    lists = stations_ref[...] * (1 << cfg["shift_bits"]) + moveouts_ref[...]
    group, tpl_count, _ = lists_ref.shape
    slot_count = lists.shape[1]
    lists_ref[:, :, :slot_count] = jnp.broadcast_to(lists.reshape(1, tpl_count, slot_count), (group, tpl_count, slot_count))


def pack_kernel(
    cfg, half_ref, stations_ref, templates_hbm, packed_hbm, raw_ref, shapes_ref, packed_ref, in_sem, out_sems
):
    load = pltpu.make_async_copy(templates_hbm, raw_ref, in_sem)
    load.start()
    tpl_count, slot_count = stations_ref.shape
    pairs = tpl_count * slot_count
    devices, group, halves, rows = cfg["devices"], cfg["group"], cfg["halves"], cfg["rows"]
    spread, place = entry_lanes(tpl_count, slot_count)
    station = as_lanes(stations_ref[...], spread, place, tpl_count)
    device = jnp.floor((station + 0.5) * (1.0 / cfg["station_dev"]))
    onehot = jnp.where(iota((devices, pairs), 0).astype(jnp.float32) == device, 1.0, 0.0)
    rank = jnp.sum(onehot * count_before(onehot), axis=0, keepdims=True)
    half = jnp.floor((device + 0.5) * (1.0 / group))
    away = jnp.where(half == half_ref[0].astype(jnp.float32), 0.0, 1.0)
    holder = device - half * group
    capacity = cfg["capacity"]
    base = jnp.where(rank < float(capacity), away * (cfg["comps"] * capacity) + rank, -1e6)

    comps, length = raw_ref.shape[1], raw_ref.shape[3]
    load.wait()
    for c in range(comps):
        values = raw_ref[:, c].astype(jnp.float32).reshape(pairs, length)
        centred = values - jnp.mean(values, axis=-1, keepdims=True)
        spread_c = jnp.sqrt(jnp.mean(centred * centred, axis=-1, keepdims=True) + 1e-05)
        shapes_ref[c] = (centred * (1.0 / spread_c)).astype(jnp.bfloat16)

    more, step_len = cfg["more"], 128
    chunks = length // step_len - 1
    tile = SOURCES * rows
    copies = []
    for step in range(group // SOURCES):
        at = iota((tile, pairs), 0).astype(jnp.float32)
        first = (holder - float(step * SOURCES)) * rows
        low = jnp.zeros((tile, length), jnp.float32)
        high = jnp.zeros((tile, chunks * step_len), jnp.float32)
        lasts = [jnp.zeros((tile, step_len), jnp.float32) for _ in range(chunks)]
        for c in range(comps):
            line = base + float(c * capacity)
            extra = line - float(rows)
            there = (extra >= 0.0) & (extra < float(more))
            deep = jnp.floor((extra + 0.5) * (1.0 / chunks))
            spot = jnp.where(there, extra - deep * chunks, -1.0)
            shapes = shapes_ref[c]

            def pick(ok, row):
                return jnp.where(at == jnp.where(ok, first + row, -1.0), 1.0, 0.0).astype(jnp.bfloat16)

            low = low + dot(pick((line >= 0.0) & (line < float(rows)), line), shapes)
            high = high + dot(pick(there, extra), shapes[:, : chunks * step_len])
            for m in range(chunks):
                picked = pick(spot == float(m), float(more) + deep)
                lasts[m] = lasts[m] + dot(picked, shapes[:, chunks * step_len :])
        part = pl.ds(step * tile, tile)
        packed_ref[part, :length] = low.astype(jnp.bfloat16)
        packed_ref[part, length:] = (high + jnp.concatenate(lasts, axis=1)).astype(jnp.bfloat16)
        copies.append(pltpu.make_async_copy(packed_ref.at[part], packed_hbm.at[part], out_sems.at[step]))
        copies[-1].start()
    for copy in copies:
        copy.wait()


def tile_lines(cfg, here, lists):
    capacity, rows, comps, halves = cfg["capacity"], cfg["rows"], cfg["comps"], cfg["halves"]
    station_dev, shift_bits, row_bits = cfg["station_dev"], cfg["shift_bits"], cfg["row_bits"]
    tpl_count, slot_count = cfg["tpl_count"], cfg["slot_count"]
    lists = lists[:, :slot_count]
    pairs = tpl_count * slot_count
    tile = 2 * SOURCES * rows
    spread, place = entry_lanes(tpl_count, slot_count)
    station = as_lanes(lax.shift_right_logical(lists, shift_bits), spread, place, tpl_count)
    shift = as_lanes(lists & ((1 << shift_bits) - 1), spread, place, tpl_count)

    def per_line(x):
        wide = jnp.broadcast_to(x.reshape(SOURCES, 1, pairs), (SOURCES, rows, pairs)).reshape(tile // 2, pairs)
        return jnp.concatenate([wide, wide], axis=0)

    ranks, codes = [], []
    for device in here:
        row = station - (device * station_dev).astype(jnp.float32)
        hit = jnp.where((row >= 0.0) & (row < float(station_dev)), 1.0, 0.0)
        ranks.append(jnp.where(hit > 0.0, count_before(hit), -1.0))
        codes.append(((place + 1.0) * (1 << row_bits) + row) * (1 << shift_bits) + shift)

    line = iota((SOURCES, rows, 1), 1).reshape(tile // 2, 1)
    line = jnp.concatenate([line, line + rows], axis=0)
    owner = iota((SOURCES, rows, 1), 0).reshape(tile // 2, 1)
    owner = jnp.concatenate([owner, owner], axis=0)
    panel = jnp.zeros((tile, 1), jnp.int32)
    for m in range(1, halves * comps + 1):
        panel = panel + jnp.where(line >= m * capacity, 1, 0)
    slot = jnp.where(panel < halves * comps, line - panel * capacity, -2).astype(jnp.float32)
    code = jnp.zeros((tile, 1), jnp.float32)
    for q in range(halves):
        mine = jnp.where((panel >= q * comps) & (panel < (q + 1) * comps), slot, -2.0)
        code = code + jnp.sum(jnp.where(per_line(ranks[q]) == mine, per_line(codes[q]), 0.0), axis=1, keepdims=True)
    code = code.astype(jnp.int32)
    row = lax.shift_right_logical(code, shift_bits) & ((1 << row_bits) - 1)
    tpl = lax.shift_right_logical(code, shift_bits + row_bits) - 1
    goal = panel * station_dev + row
    return (
        code & ((1 << shift_bits) - 1),
        jnp.where(tpl >= 0, goal, -1),
        jnp.where(tpl >= 0, owner * tpl_count + tpl, -1),
    )


def cut_traces(cfg, shift, goal, waves):
    tile, seg_len, shift_bits = shift.shape[0], cfg["seg_len"], cfg["shift_bits"]
    pick = jnp.where(iota((tile, waves.shape[0]), 1) == goal, 1.0, 0.0).astype(jnp.bfloat16)
    x = dot(pick, waves).astype(jnp.bfloat16)

    def choose(step, moved, still):
        flag = jnp.where((shift & step) != 0, 1.0, 0.0)
        return moved * flag.astype(jnp.bfloat16) + still * (1.0 - flag).astype(jnp.bfloat16)

    for bit in range(shift_bits - 1, 6, -1):
        step = 1 << bit
        width = seg_len + step
        if x.shape[1] < width + step:
            x = jnp.concatenate([x, jnp.zeros((tile, width + step - x.shape[1]), jnp.bfloat16)], axis=1)
        x = choose(step, x[:, step : step + width], x[:, :width])
    for bit in range(min(shift_bits, 7) - 1, -1, -1):
        step = 1 << bit
        x = choose(step, pltpu.roll(x, x.shape[1] - step, 1), x)
    return x[:, :seg_len]


def line_sums(cfg, column):
    groups = SOURCES * cfg["tpl_count"]
    return jnp.where(iota((column.shape[0], groups), 1) == column, 1.0, 0.0).T.astype(jnp.bfloat16)


def levels_scale(cfg, narrow, edges):
    length = cfg["length"]
    ends = jnp.concatenate([narrow[:, :LAGS], narrow[:, length:]], axis=1).astype(jnp.float32)
    ends = ends * ends
    high = ends.astype(jnp.bfloat16)
    low = (ends - high.astype(jnp.float32)).astype(jnp.bfloat16)
    middle = narrow[:, LAGS:length].astype(jnp.float32)
    energy = dot(high, edges) + dot(low, edges) + jnp.sum(middle * middle, axis=1, keepdims=True)
    return 1.0 / (length * jnp.sqrt(energy * (1.0 / length) + 1e-05))


def shape_spectra(shapes, forward):
    spectra = []
    for h in range(shapes.shape[1] // LAGS):
        part = shapes[:, h * LAGS : (h + 1) * LAGS]
        mine = dot(jnp.concatenate([part, part], axis=1), forward)
        spectra.append((mine[:, :LAGS], mine[:, LAGS:]))
    return spectra


def match_lines(mine, theirs, scale, inverse):
    real = imag = 0.0
    for (mine_r, mine_i), (theirs_r, theirs_i) in zip(mine, theirs):
        real = real + (theirs_r * mine_r + theirs_i * mine_i)
        imag = imag + (theirs_i * mine_r - theirs_r * mine_i)
    product = jnp.concatenate([real, imag], axis=1)
    high = product.astype(jnp.bfloat16)
    low = (product - high.astype(jnp.float32)).astype(jnp.bfloat16)
    return dot(jnp.concatenate([high, high, low], axis=1), inverse) * scale


def sum_lines(sums, left):
    total = 0.0
    for _ in range(3):
        part = left.astype(jnp.bfloat16)
        left = left - part.astype(jnp.float32)
        total = total + dot(sums, part)
    return total


def tables_of(table_ref):
    back = table_ref[2 * LAGS :, :]
    high, low = back[:, :LAGS], back[:, LAGS:]
    return table_ref[: 2 * LAGS, :], jnp.concatenate([high, low, high], axis=0)


def trace_kernel(cfg, here_ref, lists_ref, *refs):
    waves_refs, (table_ref, edges_ref, kept_ref, sums_ref) = refs[:-4], refs[-4:]
    here = [here_ref[q] for q in range(cfg["halves"])]
    shift, goal, column = tile_lines(cfg, here, lists_ref[...])
    waves = [ref[...].reshape(-1, ref.shape[2]) for ref in waves_refs]
    narrow = cut_traces(cfg, shift, goal, jnp.concatenate(waves, axis=0))
    kept_ref[:, 2 * cfg["length"] :] = levels_scale(cfg, narrow, edges_ref[...])
    sums_ref[...] = line_sums(cfg, column)

    sign = (1 - 2 * (iota((1, LAGS), 1) & 1)).astype(jnp.float32)
    before = None
    for h in range(cfg["length"] // LAGS + 1):
        part = narrow[:, h * LAGS : (h + 1) * LAGS]
        here = dot(jnp.concatenate([part, part], axis=1), table_ref[...])
        here = here[:, :LAGS], here[:, LAGS:]
        if before is not None:
            kept_ref[:, (2 * h - 2) * LAGS : (2 * h - 1) * LAGS] = before[0] + sign * here[1]
            kept_ref[:, (2 * h - 1) * LAGS : 2 * h * LAGS] = before[1] - sign * here[0]
        before = here


def line_pieces(cfg, packed):
    rows, more, length = cfg["rows"], cfg["more"], cfg["length"]
    tile = packed.shape[0]
    chunks = length // 128 - 1
    low, high = packed[:, :length], packed[:, length:]
    number = iota((SOURCES, rows, 1), 1).reshape(tile, 1)
    deep = jnp.zeros((tile, 1), jnp.int32)
    for k in range(1, rows // chunks + 1):
        deep = deep + jnp.where(number >= k * chunks, 1, 0)
    source = iota((SOURCES, rows, 1), 0).reshape(tile, 1) * rows + more + deep
    source = jnp.where(number < more, source, -1)
    moved = dot(jnp.where(iota((tile, tile), 1) == source, 1.0, 0.0).astype(jnp.bfloat16), high)
    last = jnp.zeros((tile, 128), jnp.float32)
    for m in range(chunks):
        last = last + jnp.where(number - deep * chunks == m, moved[:, m * 128 : (m + 1) * 128], 0.0)
    high = jnp.concatenate([high, last.astype(jnp.bfloat16)], axis=1)
    lines = jnp.concatenate([low, high], axis=0)
    return lines


def match_kernel(cfg, tiles, shapes_hbm, kept_hbm, sums_hbm, table_hbm, sent_ref, *scratch):
    shapes_ref, kept_ref, sums_ref, table_ref, sems = scratch
    packed = shapes_ref.shape[0] // tiles
    tile = kept_ref.shape[0] // tiles
    groups = sent_ref.shape[0] // tiles
    length = cfg["length"]
    copies = []

    def fetch(source, buffer, part=None):
        if part is not None:
            source, buffer = source.at[part], buffer.at[part]
        copies.append(pltpu.make_async_copy(source, buffer, sems.at[len(copies)]))
        copies[-1].start()
        return copies[-1]

    lines = [pl.ds(t * packed, packed) for t in range(tiles)]
    halves = [pl.ds(q * 2 * LAGS, 2 * LAGS) for q in range(2)]
    forward = fetch(table_hbm, table_ref, halves[0])
    part = tile // 2
    shapes, kept = [], []
    for t in range(tiles):
        shapes.append(fetch(shapes_hbm, shapes_ref, lines[t]))
        kept.append([fetch(kept_hbm, kept_ref, pl.ds(t * tile + k * part, part)) for k in range(2)])
        if t == 0:
            inverse = fetch(table_hbm, table_ref, halves[1])
            sums = fetch(sums_hbm, sums_ref)
    forward.wait()
    for t in range(tiles):
        shapes[t].wait()
        mine = shape_spectra(line_pieces(cfg, shapes_ref[lines[t], :]), table_ref[: 2 * LAGS, :])
        if t == 0:
            for copy in (inverse, sums):
                copy.wait()
        ends = pl.ds(t * groups, groups)
        total = 0.0
        for k in range(2):
            kept[t][k].wait()
            theirs = kept_ref[pl.ds(t * tile + k * part, part), :]
            spectra = [
                (theirs[:, 2 * h * LAGS : (2 * h + 1) * LAGS], theirs[:, (2 * h + 1) * LAGS : (2 * h + 2) * LAGS])
                for h in range(length // LAGS)
            ]
            rows = slice(k * part, (k + 1) * part)
            ours = [(real[rows], imag[rows]) for real, imag in mine]
            left = match_lines(ours, spectra, theirs[:, 2 * length :], tables_of(table_ref)[1])
            total = total + sum_lines(sums_ref[ends, rows], left)
        sent_ref[ends, :] = total


def stack_kernel(factor, parts_ref, stacks_ref, top_ref):
    stacks = jnp.sum(parts_ref[...], axis=0) * factor
    stacks_ref[...] = stacks
    top_ref[...] = jnp.broadcast_to(jnp.max(stacks, axis=0, keepdims=True), top_ref.shape)


def body(waveforms, templates, stations, moveouts):
    devices, group, halves = lax.axis_size(AXES), lax.axis_size(GROUP), lax.axis_size(HALF)
    tpl_count, slot_count = stations.shape
    comps, length = templates.shape[2:]
    station_dev, _, samples = waveforms.shape
    seg_len = length + LAGS
    pairs = tpl_count * slot_count
    capacity = (2 * pairs + devices - 1) // devices
    chunks = length // 128 - 1
    total = halves * comps * capacity
    rows = 16
    while total - rows + max(0, -(-(total - rows) // chunks)) > rows:
        rows += 16
    more = max(0, total - rows)
    cfg = dict(
        devices=devices,
        group=group,
        halves=halves,
        station_dev=station_dev,
        tpl_count=tpl_count,
        slot_count=slot_count,
        comps=comps,
        capacity=capacity,
        rows=rows,
        more=more,
        length=length,
        seg_len=seg_len,
        shift_bits=bits_of(samples - seg_len + 1),
        row_bits=bits_of(station_dev),
    )
    table = jnp.asarray(transform_table(LAGS))
    edges = jnp.asarray(edge_table(LAGS))
    tiles = group // SOURCES
    tile = 2 * SOURCES * rows
    lines = 2 * group * rows
    width = length + chunks * 128
    sums_tile = SOURCES * tpl_count
    kept_len = 2 * length + LAGS
    whole = pl.BlockSpec(memory_space=pltpu.VMEM)
    anywhere = pl.BlockSpec(memory_space=pl.ANY)
    params = pltpu.CompilerParams(vmem_limit_bytes=60 * MIB)
    by_slot = templates.transpose(1, 2, 0, 3)
    waves = waveforms.transpose(1, 0, 2)
    half = lax.axis_index(HALF).reshape(1)
    here = (lax.axis_index(AXES) + group * jnp.arange(halves, dtype=jnp.int32)) % devices

    def work(flops, size):
        return pl.CostEstimate(flops=flops, bytes_accessed=size, transcendentals=0)

    def exchange(x, axes):
        return lax.all_to_all(x, axes, split_axis=0, concat_axis=0, tiled=True)

    def same(shape):
        return pl.BlockSpec(shape, lambda i: (0,) * len(shape))

    def tiled(*shape):
        return pl.BlockSpec(shape, lambda i: (i, 0))

    traces = [waves] + [lax.ppermute(waves, HALF, [(0, 1), (1, 0)])] * (halves - 1)
    lists = pl.pallas_call(
        functools.partial(list_kernel, cfg),
        out_shape=jax.ShapeDtypeStruct((group, tpl_count, -(-slot_count // 128) * 128), jnp.int32),
        in_specs=[whole, whole],
        out_specs=whole,
        compiler_params=params,
        cost_estimate=work(1, 1),
        name="lists",
    )(stations, moveouts)
    lists = exchange(lists, GROUP).reshape(group * tpl_count, lists.shape[2])

    packed = pl.pallas_call(
        functools.partial(pack_kernel, cfg),
        out_shape=jax.ShapeDtypeStruct((group * rows, width), jnp.bfloat16),
        in_specs=[pl.BlockSpec(memory_space=pltpu.SMEM), whole, anywhere],
        out_specs=anywhere,
        scratch_shapes=[
            pltpu.VMEM(by_slot.shape, jnp.bfloat16),
            pltpu.VMEM((comps, pairs, length), jnp.bfloat16),
            pltpu.VMEM((group * rows, width), jnp.bfloat16),
            pltpu.SemaphoreType.DMA,
            pltpu.SemaphoreType.DMA((tiles,)),
        ],
        compiler_params=params,
        cost_estimate=work(5 * 10**9, 1),
        name="pack",
    )(half, stations, by_slot)
    _, packed = lax.optimization_barrier((lists, packed))
    arrived = exchange(packed.reshape(group, rows, width), GROUP).reshape(group * rows, width)

    kept, sums = pl.pallas_call(
        functools.partial(trace_kernel, cfg),
        grid=(tiles,),
        out_shape=[
            jax.ShapeDtypeStruct((lines, kept_len), jnp.float32),
            jax.ShapeDtypeStruct((group * tpl_count, tile), jnp.bfloat16),
        ],
        in_specs=[pl.BlockSpec(memory_space=pltpu.SMEM), tiled(sums_tile, lists.shape[1])]
        + [same(waves.shape)] * halves
        + [same((2 * LAGS, 2 * LAGS)), same(edges.shape)],
        out_specs=[tiled(tile, kept_len), tiled(sums_tile, tile)],
        compiler_params=params,
        cost_estimate=work(10**12, 1),
        name="traces",
    )(here, lists, *traces, table, edges)
    operands = (arrived, kept, sums, table)
    sent = pl.pallas_call(
        functools.partial(match_kernel, cfg, tiles),
        out_shape=jax.ShapeDtypeStruct((group * tpl_count, LAGS), jnp.float32),
        in_specs=[anywhere] * len(operands),
        out_specs=whole,
        scratch_shapes=[pltpu.VMEM(x.shape, x.dtype) for x in operands]
        + [pltpu.SemaphoreType.DMA((3 + 3 * tiles,))],
        compiler_params=pltpu.CompilerParams(vmem_limit_bytes=57 * MIB),
        name="match",
    )(*operands)

    parts = exchange(sent.reshape(group, tpl_count, LAGS), GROUP)
    stacks, top = pl.pallas_call(
        functools.partial(stack_kernel, math.sqrt(length / (comps * slot_count))),
        out_shape=[
            jax.ShapeDtypeStruct((tpl_count, LAGS), jnp.float32),
            jax.ShapeDtypeStruct((devices, 1, LAGS), jnp.float32),
        ],
        in_specs=[whole],
        out_specs=[whole, whole],
        compiler_params=pltpu.CompilerParams(vmem_limit_bytes=16 * MIB),
        name="stack",
    )(parts)
    return stacks, jnp.max(exchange(top, AXES), axis=(0, 1))


def solution(mesh):
    slow, fast = (mesh.shape[name] for name in GROUP)
    halves = 2 if slow % 2 == 0 else 1
    split = jax.sharding.Mesh(mesh.devices.reshape(halves, slow // halves, fast), AXES)
    placed = (
        P(AXES, None, None),
        P(AXES, None, None, None),
        P(AXES, None),
        P(AXES, None),
    )
    return jax.shard_map(body, mesh=split, in_specs=placed, out_specs=(P(AXES, None), P()), check_vma=False)
```

```python
import functools
import math

import jax
import jax.numpy as jnp
import ml_dtypes
import numpy as np
from jax import lax
from jax.experimental import pallas as pl
from jax.experimental.pallas import tpu as pltpu
from jax.sharding import PartitionSpec as P

LAGS = 256
HALF = "half"
DEEP = "deep"
AXES = (HALF, DEEP, "wide", "sta")
GROUP = ("wide", "sta", DEEP)
SOURCES = 8
MIB = 1024 * 1024


def bits_of(limit):
    return max(1, (limit - 1).bit_length())


def split_table(table):
    high = table.astype(ml_dtypes.bfloat16)
    return high, (table - high.astype(np.float64)).astype(ml_dtypes.bfloat16)


def transform_table(piece):
    size = 2 * piece
    angle = 2.0 * np.pi * (np.arange(piece) + 0.5) / size
    phase = np.arange(piece)[:, None] * angle[None, :]
    forward = np.concatenate([np.cos(phase), -np.sin(phase)], axis=1)
    inverse = np.concatenate([np.cos(phase.T), -np.sin(phase.T)], axis=0) * (2.0 / size)
    return np.concatenate([*split_table(forward), np.concatenate(split_table(inverse), axis=1)], axis=0)


def edge_table(lag_count):
    sample = np.arange(lag_count)[:, None]
    lag = np.arange(lag_count)[None, :]
    return np.concatenate([sample >= lag, sample < lag], axis=0).astype(ml_dtypes.bfloat16)


def iota(shape, axis):
    return lax.broadcasted_iota(jnp.int32, shape, axis)


def dot(a, b):
    return jnp.dot(a, b, preferred_element_type=jnp.float32)


def exact_dot(a, b):
    return jnp.dot(a, b, precision=lax.Precision.HIGHEST, preferred_element_type=jnp.float32)


def entry_lanes(tpl_count, slot_count):
    pairs = tpl_count * slot_count
    first = iota((slot_count, pairs), 0) * tpl_count
    entry = iota((slot_count, pairs), 1)
    spread = jnp.where((entry >= first) & (entry < first + tpl_count), 1.0, 0.0)
    start = jnp.sum(spread * first.astype(jnp.float32), axis=0, keepdims=True)
    return spread, iota((1, pairs), 1).astype(jnp.float32) - start


def as_lanes(values, spread, place, tpl_count):
    owners = values.shape[0] // tpl_count
    pairs = spread.shape[1]
    wide = exact_dot(values.astype(jnp.float32), spread).reshape(owners, tpl_count, pairs)
    own = iota((1, tpl_count, pairs), 1).astype(jnp.float32) == place.reshape(1, 1, pairs)
    return jnp.sum(jnp.where(own, wide, 0.0), axis=1)


def count_before(hits):
    pairs = hits.shape[1]
    earlier = jnp.where(iota((pairs, pairs), 0) < iota((pairs, pairs), 1), 1.0, 0.0)
    return dot(hits.astype(jnp.bfloat16), earlier.astype(jnp.bfloat16))


def list_kernel(cfg, stations_ref, moveouts_ref, lists_ref):
    lists = stations_ref[...] * (1 << cfg["shift_bits"]) + moveouts_ref[...]
    group, tpl_count, _ = lists_ref.shape
    slot_count = lists.shape[1]
    lists_ref[:, :, :slot_count] = jnp.broadcast_to(lists.reshape(1, tpl_count, slot_count), (group, tpl_count, slot_count))


def pack_kernel(
    cfg, half_ref, stations_ref, templates_hbm, packed_hbm, raw_ref, shapes_ref, packed_ref, in_sem, out_sems
):
    load = pltpu.make_async_copy(templates_hbm, raw_ref, in_sem)
    load.start()
    tpl_count, slot_count = stations_ref.shape
    pairs = tpl_count * slot_count
    devices, group, halves, rows = cfg["devices"], cfg["group"], cfg["halves"], cfg["rows"]
    spread, place = entry_lanes(tpl_count, slot_count)
    station = as_lanes(stations_ref[...], spread, place, tpl_count)
    device = jnp.floor((station + 0.5) * (1.0 / cfg["station_dev"]))
    onehot = jnp.where(iota((devices, pairs), 0).astype(jnp.float32) == device, 1.0, 0.0)
    rank = jnp.sum(onehot * count_before(onehot), axis=0, keepdims=True)
    half = jnp.floor((device + 0.5) * (1.0 / group))
    away = jnp.where(half == half_ref[0].astype(jnp.float32), 0.0, 1.0)
    holder = device - half * group
    inner = group // cfg["deep"]
    part_of = jnp.floor((holder + 0.5) * (1.0 / inner))
    holder = (holder - part_of * inner) * cfg["deep"] + part_of
    capacity = cfg["capacity"]
    base = jnp.where(rank < float(capacity), away * (cfg["comps"] * capacity) + rank, -1e6)

    comps, length = raw_ref.shape[1], raw_ref.shape[3]
    load.wait()
    for c in range(comps):
        values = raw_ref[:, c].astype(jnp.float32).reshape(pairs, length)
        centred = values - jnp.mean(values, axis=-1, keepdims=True)
        spread_c = jnp.sqrt(jnp.mean(centred * centred, axis=-1, keepdims=True) + 1e-05)
        shapes_ref[c] = (centred * (1.0 / spread_c)).astype(jnp.bfloat16)

    more, step_len = cfg["more"], 128
    chunks = length // step_len - 1
    tile = SOURCES * rows
    copies = []
    for step in range(group // SOURCES):
        at = iota((tile, pairs), 0).astype(jnp.float32)
        first = (holder - float(step * SOURCES)) * rows
        low = jnp.zeros((tile, length), jnp.float32)
        high = jnp.zeros((tile, chunks * step_len), jnp.float32)
        lasts = [jnp.zeros((tile, step_len), jnp.float32) for _ in range(chunks)]
        for c in range(comps):
            line = base + float(c * capacity)
            extra = line - float(rows)
            there = (extra >= 0.0) & (extra < float(more))
            deep = jnp.floor((extra + 0.5) * (1.0 / chunks))
            spot = jnp.where(there, extra - deep * chunks, -1.0)
            shapes = shapes_ref[c]

            def pick(ok, row):
                return jnp.where(at == jnp.where(ok, first + row, -1.0), 1.0, 0.0).astype(jnp.bfloat16)

            low = low + dot(pick((line >= 0.0) & (line < float(rows)), line), shapes)
            high = high + dot(pick(there, extra), shapes[:, : chunks * step_len])
            for m in range(chunks):
                picked = pick(spot == float(m), float(more) + deep)
                lasts[m] = lasts[m] + dot(picked, shapes[:, chunks * step_len :])
        part = pl.ds(step * tile, tile)
        packed_ref[part, :length] = low.astype(jnp.bfloat16)
        packed_ref[part, length:] = (high + jnp.concatenate(lasts, axis=1)).astype(jnp.bfloat16)
        copies.append(pltpu.make_async_copy(packed_ref.at[part], packed_hbm.at[part], out_sems.at[step]))
        copies[-1].start()
    for copy in copies:
        copy.wait()


def tile_lines(cfg, here, lists):
    capacity, rows, comps, halves = cfg["capacity"], cfg["rows"], cfg["comps"], cfg["halves"]
    station_dev, shift_bits, row_bits = cfg["station_dev"], cfg["shift_bits"], cfg["row_bits"]
    tpl_count, slot_count = cfg["tpl_count"], cfg["slot_count"]
    lists = lists[:, :slot_count]
    pairs = tpl_count * slot_count
    tile = 2 * SOURCES * rows
    spread, place = entry_lanes(tpl_count, slot_count)
    station = as_lanes(lax.shift_right_logical(lists, shift_bits), spread, place, tpl_count)
    shift = as_lanes(lists & ((1 << shift_bits) - 1), spread, place, tpl_count)

    def per_line(x):
        wide = jnp.broadcast_to(x.reshape(SOURCES, 1, pairs), (SOURCES, rows, pairs)).reshape(tile // 2, pairs)
        return jnp.concatenate([wide, wide], axis=0)

    ranks, codes = [], []
    for device in here:
        row = station - (device * station_dev).astype(jnp.float32)
        hit = jnp.where((row >= 0.0) & (row < float(station_dev)), 1.0, 0.0)
        ranks.append(jnp.where(hit > 0.0, count_before(hit), -1.0))
        codes.append(((place + 1.0) * (1 << row_bits) + row) * (1 << shift_bits) + shift)

    line = iota((SOURCES, rows, 1), 1).reshape(tile // 2, 1)
    line = jnp.concatenate([line, line + rows], axis=0)
    owner = iota((SOURCES, rows, 1), 0).reshape(tile // 2, 1)
    owner = jnp.concatenate([owner, owner], axis=0)
    panel = jnp.zeros((tile, 1), jnp.int32)
    for m in range(1, halves * comps + 1):
        panel = panel + jnp.where(line >= m * capacity, 1, 0)
    slot = jnp.where(panel < halves * comps, line - panel * capacity, -2).astype(jnp.float32)
    code = jnp.zeros((tile, 1), jnp.float32)
    for q in range(halves):
        mine = jnp.where((panel >= q * comps) & (panel < (q + 1) * comps), slot, -2.0)
        code = code + jnp.sum(jnp.where(per_line(ranks[q]) == mine, per_line(codes[q]), 0.0), axis=1, keepdims=True)
    code = code.astype(jnp.int32)
    row = lax.shift_right_logical(code, shift_bits) & ((1 << row_bits) - 1)
    tpl = lax.shift_right_logical(code, shift_bits + row_bits) - 1
    goal = panel * station_dev + row
    return (
        code & ((1 << shift_bits) - 1),
        jnp.where(tpl >= 0, goal, -1),
        jnp.where(tpl >= 0, owner * tpl_count + tpl, -1),
    )


def cut_traces(cfg, shift, goal, waves):
    tile, seg_len, shift_bits = shift.shape[0], cfg["seg_len"], cfg["shift_bits"]
    pick = jnp.where(iota((tile, waves.shape[0]), 1) == goal, 1.0, 0.0).astype(jnp.bfloat16)
    x = dot(pick, waves).astype(jnp.bfloat16)

    def choose(step, moved, still):
        flag = jnp.where((shift & step) != 0, 1.0, 0.0)
        return moved * flag.astype(jnp.bfloat16) + still * (1.0 - flag).astype(jnp.bfloat16)

    for bit in range(shift_bits - 1, 6, -1):
        step = 1 << bit
        width = seg_len + step
        if x.shape[1] < width + step:
            x = jnp.concatenate([x, jnp.zeros((tile, width + step - x.shape[1]), jnp.bfloat16)], axis=1)
        x = choose(step, x[:, step : step + width], x[:, :width])
    for bit in range(min(shift_bits, 7) - 1, -1, -1):
        step = 1 << bit
        x = choose(step, pltpu.roll(x, x.shape[1] - step, 1), x)
    return x[:, :seg_len]


def line_sums(cfg, column):
    groups = SOURCES * cfg["tpl_count"]
    return jnp.where(iota((column.shape[0], groups), 1) == column, 1.0, 0.0).T.astype(jnp.bfloat16)


def levels_scale(cfg, narrow, edges):
    length = cfg["length"]
    ends = jnp.concatenate([narrow[:, :LAGS], narrow[:, length:]], axis=1).astype(jnp.float32)
    ends = ends * ends
    high = ends.astype(jnp.bfloat16)
    low = (ends - high.astype(jnp.float32)).astype(jnp.bfloat16)
    middle = narrow[:, LAGS:length].astype(jnp.float32)
    energy = dot(high, edges) + dot(low, edges) + jnp.sum(middle * middle, axis=1, keepdims=True)
    return 1.0 / (length * jnp.sqrt(energy * (1.0 / length) + 1e-05))


def shape_spectra(shapes, forward):
    spectra = []
    for h in range(shapes.shape[1] // LAGS):
        part = shapes[:, h * LAGS : (h + 1) * LAGS]
        mine = dot(jnp.concatenate([part, part], axis=1), forward)
        spectra.append((mine[:, :LAGS], mine[:, LAGS:]))
    return spectra


def match_lines(mine, theirs, scale, inverse):
    real = imag = 0.0
    for (mine_r, mine_i), (theirs_r, theirs_i) in zip(mine, theirs):
        real = real + (theirs_r * mine_r + theirs_i * mine_i)
        imag = imag + (theirs_i * mine_r - theirs_r * mine_i)
    product = jnp.concatenate([real, imag], axis=1)
    high = product.astype(jnp.bfloat16)
    low = (product - high.astype(jnp.float32)).astype(jnp.bfloat16)
    return dot(jnp.concatenate([high, high, low], axis=1), inverse) * scale


def sum_lines(sums, left):
    total = 0.0
    for _ in range(3):
        part = left.astype(jnp.bfloat16)
        left = left - part.astype(jnp.float32)
        total = total + dot(sums, part)
    return total


def tables_of(table_ref):
    back = table_ref[2 * LAGS :, :]
    high, low = back[:, :LAGS], back[:, LAGS:]
    return table_ref[: 2 * LAGS, :], jnp.concatenate([high, low, high], axis=0)


def trace_kernel(cfg, here_ref, lists_ref, *refs):
    waves_refs, (table_ref, edges_ref, kept_ref, sums_ref) = refs[:-4], refs[-4:]
    here = [here_ref[0]]
    for _ in range(1, cfg["halves"]):
        other = here[-1] + cfg["group"]
        here.append(jnp.where(other >= cfg["devices"], other - cfg["devices"], other))
    shift, goal, column = tile_lines(cfg, here, lists_ref[...])
    waves = [ref[...].reshape(-1, ref.shape[2]) for ref in waves_refs]
    narrow = cut_traces(cfg, shift, goal, jnp.concatenate(waves, axis=0))
    kept_ref[:, 2 * cfg["length"] :] = levels_scale(cfg, narrow, edges_ref[...])
    sums_ref[...] = line_sums(cfg, column)

    sign = (1 - 2 * (iota((1, LAGS), 1) & 1)).astype(jnp.float32)
    before = None
    for h in range(cfg["length"] // LAGS + 1):
        part = narrow[:, h * LAGS : (h + 1) * LAGS]
        here = dot(jnp.concatenate([part, part], axis=1), table_ref[...])
        here = here[:, :LAGS], here[:, LAGS:]
        if before is not None:
            kept_ref[:, (2 * h - 2) * LAGS : (2 * h - 1) * LAGS] = before[0] + sign * here[1]
            kept_ref[:, (2 * h - 1) * LAGS : 2 * h * LAGS] = before[1] - sign * here[0]
        before = here


def line_pieces(cfg, packed):
    rows, more, length = cfg["rows"], cfg["more"], cfg["length"]
    tile = packed.shape[0]
    chunks = length // 128 - 1
    low, high = packed[:, :length], packed[:, length:]
    number = iota((SOURCES, rows, 1), 1).reshape(tile, 1)
    deep = jnp.zeros((tile, 1), jnp.int32)
    for k in range(1, rows // chunks + 1):
        deep = deep + jnp.where(number >= k * chunks, 1, 0)
    source = iota((SOURCES, rows, 1), 0).reshape(tile, 1) * rows + more + deep
    source = jnp.where(number < more, source, -1)
    moved = dot(jnp.where(iota((tile, tile), 1) == source, 1.0, 0.0).astype(jnp.bfloat16), high)
    last = jnp.zeros((tile, 128), jnp.float32)
    for m in range(chunks):
        last = last + jnp.where(number - deep * chunks == m, moved[:, m * 128 : (m + 1) * 128], 0.0)
    high = jnp.concatenate([high, last.astype(jnp.bfloat16)], axis=1)
    lines = jnp.concatenate([low, high], axis=0)
    return lines


def match_kernel(cfg, tiles, shapes_hbm, kept_hbm, sums_hbm, table_hbm, sent_ref, *scratch):
    shapes_ref, kept_ref, sums_ref, table_ref, sems = scratch
    packed = shapes_ref.shape[0] // tiles
    tile = kept_ref.shape[0] // tiles
    groups = sent_ref.shape[0] // tiles
    length = cfg["length"]
    copies = []

    def fetch(source, buffer, part=None):
        if part is not None:
            source, buffer = source.at[part], buffer.at[part]
        copies.append(pltpu.make_async_copy(source, buffer, sems.at[len(copies)]))
        copies[-1].start()
        return copies[-1]

    lines = [pl.ds(t * packed, packed) for t in range(tiles)]
    halves = [pl.ds(q * 2 * LAGS, 2 * LAGS) for q in range(2)]
    forward = fetch(table_hbm, table_ref, halves[0])
    part = tile // 2
    shapes, kept = [], []
    for t in range(tiles):
        shapes.append(fetch(shapes_hbm, shapes_ref, lines[t]))
        kept.append([fetch(kept_hbm, kept_ref, pl.ds(t * tile + k * part, part)) for k in range(2)])
        if t == 0:
            inverse = fetch(table_hbm, table_ref, halves[1])
            sums = fetch(sums_hbm, sums_ref)
    forward.wait()
    for t in range(tiles):
        shapes[t].wait()
        mine = shape_spectra(line_pieces(cfg, shapes_ref[lines[t], :]), table_ref[: 2 * LAGS, :])
        if t == 0:
            for copy in (inverse, sums):
                copy.wait()
        ends = pl.ds(t * groups, groups)
        total = 0.0
        for k in range(2):
            kept[t][k].wait()
            theirs = kept_ref[pl.ds(t * tile + k * part, part), :]
            spectra = [
                (theirs[:, 2 * h * LAGS : (2 * h + 1) * LAGS], theirs[:, (2 * h + 1) * LAGS : (2 * h + 2) * LAGS])
                for h in range(length // LAGS)
            ]
            rows = slice(k * part, (k + 1) * part)
            ours = [(real[rows], imag[rows]) for real, imag in mine]
            left = match_lines(ours, spectra, theirs[:, 2 * length :], tables_of(table_ref)[1])
            total = total + sum_lines(sums_ref[ends, rows], left)
        sent_ref[ends, :] = total


def stack_kernel(factor, parts_ref, stacks_ref, top_ref):
    stacks = jnp.sum(parts_ref[...], axis=0) * factor
    stacks_ref[...] = stacks
    top_ref[...] = jnp.broadcast_to(jnp.max(stacks, axis=0, keepdims=True), top_ref.shape)


def body(waveforms, templates, stations, moveouts):
    devices, group, halves = lax.axis_size(AXES), lax.axis_size(GROUP), lax.axis_size(HALF)
    tpl_count, slot_count = stations.shape
    comps, length = templates.shape[2:]
    station_dev, _, samples = waveforms.shape
    seg_len = length + LAGS
    pairs = tpl_count * slot_count
    capacity = (2 * pairs + devices - 1) // devices
    chunks = length // 128 - 1
    total = halves * comps * capacity
    rows = 16
    while total - rows + max(0, -(-(total - rows) // chunks)) > rows:
        rows += 16
    more = max(0, total - rows)
    cfg = dict(
        devices=devices,
        group=group,
        halves=halves,
        deep=lax.axis_size(DEEP),
        station_dev=station_dev,
        tpl_count=tpl_count,
        slot_count=slot_count,
        comps=comps,
        capacity=capacity,
        rows=rows,
        more=more,
        length=length,
        seg_len=seg_len,
        shift_bits=bits_of(samples - seg_len + 1),
        row_bits=bits_of(station_dev),
    )
    table = jnp.asarray(transform_table(LAGS))
    edges = jnp.asarray(edge_table(LAGS))
    tiles = group // SOURCES
    tile = 2 * SOURCES * rows
    lines = 2 * group * rows
    width = length + chunks * 128
    sums_tile = SOURCES * tpl_count
    kept_len = 2 * length + LAGS
    whole = pl.BlockSpec(memory_space=pltpu.VMEM)
    anywhere = pl.BlockSpec(memory_space=pl.ANY)
    params = pltpu.CompilerParams(vmem_limit_bytes=60 * MIB)
    by_slot = templates.transpose(1, 2, 0, 3)
    waves = waveforms.transpose(1, 0, 2)
    half = lax.axis_index(HALF).reshape(1)
    here = lax.axis_index(AXES).reshape(1)

    def work(flops, size):
        return pl.CostEstimate(flops=flops, bytes_accessed=size, transcendentals=0)

    def exchange(x, axes):
        return lax.all_to_all(x, axes, split_axis=0, concat_axis=0, tiled=True)

    def same(shape):
        return pl.BlockSpec(shape, lambda i: (0,) * len(shape))

    def tiled(*shape):
        return pl.BlockSpec(shape, lambda i: (i, 0))

    traces = [waves] + [lax.ppermute(waves, HALF, [(0, 1), (1, 0)])] * (halves - 1)
    lists = pl.pallas_call(
        functools.partial(list_kernel, cfg),
        out_shape=jax.ShapeDtypeStruct((group, tpl_count, -(-slot_count // 128) * 128), jnp.int32),
        in_specs=[whole, whole],
        out_specs=whole,
        compiler_params=params,
        cost_estimate=work(1, 1),
        name="lists",
    )(stations, moveouts)
    lists = exchange(lists, GROUP).reshape(group * tpl_count, lists.shape[2])

    packed = pl.pallas_call(
        functools.partial(pack_kernel, cfg),
        out_shape=jax.ShapeDtypeStruct((group * rows, width), jnp.bfloat16),
        in_specs=[pl.BlockSpec(memory_space=pltpu.SMEM), whole, anywhere],
        out_specs=anywhere,
        scratch_shapes=[
            pltpu.VMEM(by_slot.shape, jnp.bfloat16),
            pltpu.VMEM((comps, pairs, length), jnp.bfloat16),
            pltpu.VMEM((group * rows, width), jnp.bfloat16),
            pltpu.SemaphoreType.DMA,
            pltpu.SemaphoreType.DMA((tiles,)),
        ],
        compiler_params=params,
        cost_estimate=work(5 * 10**9, 1),
        name="pack",
    )(half, stations, by_slot)
    _, packed = lax.optimization_barrier((lists, packed))
    arrived = exchange(packed.reshape(group, rows, width), GROUP).reshape(group * rows, width)

    kept, sums = pl.pallas_call(
        functools.partial(trace_kernel, cfg),
        grid=(tiles,),
        out_shape=[
            jax.ShapeDtypeStruct((lines, kept_len), jnp.float32),
            jax.ShapeDtypeStruct((group * tpl_count, tile), jnp.bfloat16),
        ],
        in_specs=[pl.BlockSpec(memory_space=pltpu.SMEM), tiled(sums_tile, lists.shape[1])]
        + [same(waves.shape)] * halves
        + [same((2 * LAGS, 2 * LAGS)), same(edges.shape)],
        out_specs=[tiled(tile, kept_len), tiled(sums_tile, tile)],
        compiler_params=params,
        cost_estimate=work(10**12, 1),
        name="traces",
    )(here, lists, *traces, table, edges)
    operands = (arrived, kept, sums, table)
    sent = pl.pallas_call(
        functools.partial(match_kernel, cfg, tiles),
        out_shape=jax.ShapeDtypeStruct((group * tpl_count, LAGS), jnp.float32),
        in_specs=[anywhere] * len(operands),
        out_specs=whole,
        scratch_shapes=[pltpu.VMEM(x.shape, x.dtype) for x in operands]
        + [pltpu.SemaphoreType.DMA((3 + 3 * tiles,))],
        compiler_params=pltpu.CompilerParams(vmem_limit_bytes=57 * MIB),
        name="match",
    )(*operands)

    parts = exchange(sent.reshape(group, tpl_count, LAGS), GROUP)
    stacks, top = pl.pallas_call(
        functools.partial(stack_kernel, math.sqrt(length / (comps * slot_count))),
        out_shape=[
            jax.ShapeDtypeStruct((tpl_count, LAGS), jnp.float32),
            jax.ShapeDtypeStruct((devices, 1, LAGS), jnp.float32),
        ],
        in_specs=[whole],
        out_specs=[whole, whole],
        compiler_params=pltpu.CompilerParams(vmem_limit_bytes=16 * MIB),
        name="stack",
    )(parts)
    return stacks, jnp.max(exchange(top, AXES), axis=(0, 1))


def solution(mesh):
    slow, fast = mesh.devices.shape
    halves = 2 if slow % 2 == 0 else 1
    deep = 2 if slow // halves % 2 == 0 else 1
    split = jax.sharding.Mesh(mesh.devices.reshape(halves, deep, slow // halves // deep, fast), AXES)
    placed = (
        P(AXES, None, None),
        P(AXES, None, None, None),
        P(AXES, None),
        P(AXES, None),
    )
    return jax.shard_map(body, mesh=split, in_specs=placed, out_specs=(P(AXES, None), P()), check_vma=False)
```

```python
import functools
import math

import jax
import jax.numpy as jnp
import ml_dtypes
import numpy as np
from jax import lax
from jax.experimental import pallas as pl
from jax.experimental.pallas import tpu as pltpu
from jax.sharding import PartitionSpec as P

LAGS = 256
HALF = "half"
DEEP = "deep"
PARTS = (DEEP, "wide", "sta", "core")
AXES = (HALF,) + PARTS
GROUP = PARTS[::-1]
SOURCES = 8
MIB = 1024 * 1024


def bits_of(limit):
    return max(1, (limit - 1).bit_length())


def split_table(table):
    high = table.astype(ml_dtypes.bfloat16)
    return high, (table - high.astype(np.float64)).astype(ml_dtypes.bfloat16)


def transform_table(piece):
    size = 2 * piece
    angle = 2.0 * np.pi * (np.arange(piece) + 0.5) / size
    phase = np.arange(piece)[:, None] * angle[None, :]
    forward = np.concatenate([np.cos(phase), -np.sin(phase)], axis=1)
    inverse = np.concatenate([np.cos(phase.T), -np.sin(phase.T)], axis=0) * (2.0 / size)
    return np.concatenate([*split_table(forward), np.concatenate(split_table(inverse), axis=1)], axis=0)


def edge_table(lag_count):
    sample = np.arange(lag_count)[:, None]
    lag = np.arange(lag_count)[None, :]
    return np.concatenate([sample >= lag, sample < lag], axis=0).astype(ml_dtypes.bfloat16)


def iota(shape, axis):
    return lax.broadcasted_iota(jnp.int32, shape, axis)


def dot(a, b):
    return jnp.dot(a, b, preferred_element_type=jnp.float32)


def exact_dot(a, b):
    return jnp.dot(a, b, precision=lax.Precision.HIGHEST, preferred_element_type=jnp.float32)


def entry_lanes(tpl_count, slot_count):
    pairs = tpl_count * slot_count
    first = iota((slot_count, pairs), 0) * tpl_count
    entry = iota((slot_count, pairs), 1)
    spread = jnp.where((entry >= first) & (entry < first + tpl_count), 1.0, 0.0)
    start = jnp.sum(spread * first.astype(jnp.float32), axis=0, keepdims=True)
    return spread, iota((1, pairs), 1).astype(jnp.float32) - start


def as_lanes(values, spread, place, tpl_count):
    owners = values.shape[0] // tpl_count
    pairs = spread.shape[1]
    wide = exact_dot(values.astype(jnp.float32), spread).reshape(owners, tpl_count, pairs)
    own = iota((1, tpl_count, pairs), 1).astype(jnp.float32) == place.reshape(1, 1, pairs)
    return jnp.sum(jnp.where(own, wide, 0.0), axis=1)


def count_before(hits):
    pairs = hits.shape[1]
    earlier = jnp.where(iota((pairs, pairs), 0) < iota((pairs, pairs), 1), 1.0, 0.0)
    return dot(hits.astype(jnp.bfloat16), earlier.astype(jnp.bfloat16))


def list_kernel(cfg, stations_ref, moveouts_ref, lists_ref):
    lists = stations_ref[...] * (1 << cfg["shift_bits"]) + moveouts_ref[...]
    group, tpl_count, _ = lists_ref.shape
    slot_count = lists.shape[1]
    lists_ref[:, :, :slot_count] = jnp.broadcast_to(lists.reshape(1, tpl_count, slot_count), (group, tpl_count, slot_count))


def pack_kernel(
    cfg, half_ref, stations_ref, templates_hbm, packed_hbm, raw_ref, shapes_ref, packed_ref, in_sem, out_sems
):
    load = pltpu.make_async_copy(templates_hbm, raw_ref, in_sem)
    load.start()
    tpl_count, slot_count = stations_ref.shape
    pairs = tpl_count * slot_count
    devices, group, halves, rows = cfg["devices"], cfg["group"], cfg["halves"], cfg["rows"]
    spread, place = entry_lanes(tpl_count, slot_count)
    station = as_lanes(stations_ref[...], spread, place, tpl_count)
    device = jnp.floor((station + 0.5) * (1.0 / cfg["station_dev"]))
    onehot = jnp.where(iota((devices, pairs), 0).astype(jnp.float32) == device, 1.0, 0.0)
    rank = jnp.sum(onehot * count_before(onehot), axis=0, keepdims=True)
    half = jnp.floor((device + 0.5) * (1.0 / group))
    away = jnp.where(half == half_ref[0].astype(jnp.float32), 0.0, 1.0)
    holder = device - half * group
    number = jnp.zeros_like(holder)
    for size in cfg["parts"][::-1]:
        rest = jnp.floor((holder + 0.5) * (1.0 / size))
        number = number * size + (holder - rest * size)
        holder = rest
    holder = number
    capacity = cfg["capacity"]
    base = jnp.where(rank < float(capacity), away * (cfg["comps"] * capacity) + rank, -1e6)

    comps, length = raw_ref.shape[1], raw_ref.shape[3]
    load.wait()
    for c in range(comps):
        values = raw_ref[:, c].astype(jnp.float32).reshape(pairs, length)
        centred = values - jnp.mean(values, axis=-1, keepdims=True)
        spread_c = jnp.sqrt(jnp.mean(centred * centred, axis=-1, keepdims=True) + 1e-05)
        shapes_ref[c] = (centred * (1.0 / spread_c)).astype(jnp.bfloat16)

    more, step_len = cfg["more"], 128
    chunks = length // step_len - 1
    tile = SOURCES * rows
    copies = []
    for step in range(group // SOURCES):
        at = iota((tile, pairs), 0).astype(jnp.float32)
        first = (holder - float(step * SOURCES)) * rows
        low = jnp.zeros((tile, length), jnp.float32)
        high = jnp.zeros((tile, chunks * step_len), jnp.float32)
        lasts = [jnp.zeros((tile, step_len), jnp.float32) for _ in range(chunks)]
        for c in range(comps):
            line = base + float(c * capacity)
            extra = line - float(rows)
            there = (extra >= 0.0) & (extra < float(more))
            deep = jnp.floor((extra + 0.5) * (1.0 / chunks))
            spot = jnp.where(there, extra - deep * chunks, -1.0)
            shapes = shapes_ref[c]

            def pick(ok, row):
                return jnp.where(at == jnp.where(ok, first + row, -1.0), 1.0, 0.0).astype(jnp.bfloat16)

            low = low + dot(pick((line >= 0.0) & (line < float(rows)), line), shapes)
            high = high + dot(pick(there, extra), shapes[:, : chunks * step_len])
            for m in range(chunks):
                picked = pick(spot == float(m), float(more) + deep)
                lasts[m] = lasts[m] + dot(picked, shapes[:, chunks * step_len :])
        part = pl.ds(step * tile, tile)
        packed_ref[part, :length] = low.astype(jnp.bfloat16)
        packed_ref[part, length:] = (high + jnp.concatenate(lasts, axis=1)).astype(jnp.bfloat16)
        copies.append(pltpu.make_async_copy(packed_ref.at[part], packed_hbm.at[part], out_sems.at[step]))
        copies[-1].start()
    for copy in copies:
        copy.wait()


def tile_lines(cfg, here, lists):
    capacity, rows, comps, halves = cfg["capacity"], cfg["rows"], cfg["comps"], cfg["halves"]
    station_dev, shift_bits, row_bits = cfg["station_dev"], cfg["shift_bits"], cfg["row_bits"]
    tpl_count, slot_count = cfg["tpl_count"], cfg["slot_count"]
    lists = lists[:, :slot_count]
    pairs = tpl_count * slot_count
    tile = 2 * SOURCES * rows
    spread, place = entry_lanes(tpl_count, slot_count)
    station = as_lanes(lax.shift_right_logical(lists, shift_bits), spread, place, tpl_count)
    shift = as_lanes(lists & ((1 << shift_bits) - 1), spread, place, tpl_count)

    def per_line(x):
        wide = jnp.broadcast_to(x.reshape(SOURCES, 1, pairs), (SOURCES, rows, pairs)).reshape(tile // 2, pairs)
        return jnp.concatenate([wide, wide], axis=0)

    ranks, codes = [], []
    for device in here:
        row = station - (device * station_dev).astype(jnp.float32)
        hit = jnp.where((row >= 0.0) & (row < float(station_dev)), 1.0, 0.0)
        ranks.append(jnp.where(hit > 0.0, count_before(hit), -1.0))
        codes.append(((place + 1.0) * (1 << row_bits) + row) * (1 << shift_bits) + shift)

    line = iota((SOURCES, rows, 1), 1).reshape(tile // 2, 1)
    line = jnp.concatenate([line, line + rows], axis=0)
    owner = iota((SOURCES, rows, 1), 0).reshape(tile // 2, 1)
    owner = jnp.concatenate([owner, owner], axis=0)
    panel = jnp.zeros((tile, 1), jnp.int32)
    for m in range(1, halves * comps + 1):
        panel = panel + jnp.where(line >= m * capacity, 1, 0)
    slot = jnp.where(panel < halves * comps, line - panel * capacity, -2).astype(jnp.float32)
    code = jnp.zeros((tile, 1), jnp.float32)
    for q in range(halves):
        mine = jnp.where((panel >= q * comps) & (panel < (q + 1) * comps), slot, -2.0)
        code = code + jnp.sum(jnp.where(per_line(ranks[q]) == mine, per_line(codes[q]), 0.0), axis=1, keepdims=True)
    code = code.astype(jnp.int32)
    row = lax.shift_right_logical(code, shift_bits) & ((1 << row_bits) - 1)
    tpl = lax.shift_right_logical(code, shift_bits + row_bits) - 1
    goal = panel * station_dev + row
    return (
        code & ((1 << shift_bits) - 1),
        jnp.where(tpl >= 0, goal, -1),
        jnp.where(tpl >= 0, owner * tpl_count + tpl, -1),
    )


def cut_traces(cfg, shift, goal, waves):
    tile, seg_len, shift_bits = shift.shape[0], cfg["seg_len"], cfg["shift_bits"]
    pick = jnp.where(iota((tile, waves.shape[0]), 1) == goal, 1.0, 0.0).astype(jnp.bfloat16)
    x = dot(pick, waves).astype(jnp.bfloat16)

    def choose(step, moved, still):
        flag = jnp.where((shift & step) != 0, 1.0, 0.0)
        return moved * flag.astype(jnp.bfloat16) + still * (1.0 - flag).astype(jnp.bfloat16)

    for bit in range(shift_bits - 1, 6, -1):
        step = 1 << bit
        width = seg_len + step
        if x.shape[1] < width + step:
            x = jnp.concatenate([x, jnp.zeros((tile, width + step - x.shape[1]), jnp.bfloat16)], axis=1)
        x = choose(step, x[:, step : step + width], x[:, :width])
    for bit in range(min(shift_bits, 7) - 1, -1, -1):
        step = 1 << bit
        x = choose(step, pltpu.roll(x, x.shape[1] - step, 1), x)
    return x[:, :seg_len]


def line_sums(cfg, column):
    groups = SOURCES * cfg["tpl_count"]
    return jnp.where(iota((column.shape[0], groups), 1) == column, 1.0, 0.0).T.astype(jnp.bfloat16)


def levels_scale(cfg, narrow, edges):
    length = cfg["length"]
    ends = jnp.concatenate([narrow[:, :LAGS], narrow[:, length:]], axis=1).astype(jnp.float32)
    ends = ends * ends
    high = ends.astype(jnp.bfloat16)
    low = (ends - high.astype(jnp.float32)).astype(jnp.bfloat16)
    middle = narrow[:, LAGS:length].astype(jnp.float32)
    energy = dot(high, edges) + dot(low, edges) + jnp.sum(middle * middle, axis=1, keepdims=True)
    return 1.0 / (length * jnp.sqrt(energy * (1.0 / length) + 1e-05))


def shape_spectra(shapes, forward):
    spectra = []
    for h in range(shapes.shape[1] // LAGS):
        part = shapes[:, h * LAGS : (h + 1) * LAGS]
        mine = dot(jnp.concatenate([part, part], axis=1), forward)
        spectra.append((mine[:, :LAGS], mine[:, LAGS:]))
    return spectra


def match_lines(mine, theirs, scale, inverse):
    real = imag = 0.0
    for (mine_r, mine_i), (theirs_r, theirs_i) in zip(mine, theirs):
        real = real + (theirs_r * mine_r + theirs_i * mine_i)
        imag = imag + (theirs_i * mine_r - theirs_r * mine_i)
    product = jnp.concatenate([real, imag], axis=1)
    high = product.astype(jnp.bfloat16)
    low = (product - high.astype(jnp.float32)).astype(jnp.bfloat16)
    return dot(jnp.concatenate([high, high, low], axis=1), inverse) * scale


def sum_lines(sums, left):
    total = 0.0
    for _ in range(3):
        part = left.astype(jnp.bfloat16)
        left = left - part.astype(jnp.float32)
        total = total + dot(sums, part)
    return total


def tables_of(table_ref):
    back = table_ref[2 * LAGS :, :]
    high, low = back[:, :LAGS], back[:, LAGS:]
    return table_ref[: 2 * LAGS, :], jnp.concatenate([high, low, high], axis=0)


def trace_kernel(cfg, here_ref, lists_ref, *refs):
    waves_refs, (table_ref, edges_ref, kept_ref, sums_ref) = refs[:-4], refs[-4:]
    here = [here_ref[0]]
    for _ in range(1, cfg["halves"]):
        other = here[-1] + cfg["group"]
        here.append(jnp.where(other >= cfg["devices"], other - cfg["devices"], other))
    shift, goal, column = tile_lines(cfg, here, lists_ref[...])
    waves = [ref[...].reshape(-1, ref.shape[2]) for ref in waves_refs]
    narrow = cut_traces(cfg, shift, goal, jnp.concatenate(waves, axis=0))
    kept_ref[:, 2 * cfg["length"] :] = levels_scale(cfg, narrow, edges_ref[...])
    sums_ref[...] = line_sums(cfg, column)

    sign = (1 - 2 * (iota((1, LAGS), 1) & 1)).astype(jnp.float32)
    before = None
    for h in range(cfg["length"] // LAGS + 1):
        part = narrow[:, h * LAGS : (h + 1) * LAGS]
        here = dot(jnp.concatenate([part, part], axis=1), table_ref[...])
        here = here[:, :LAGS], here[:, LAGS:]
        if before is not None:
            kept_ref[:, (2 * h - 2) * LAGS : (2 * h - 1) * LAGS] = before[0] + sign * here[1]
            kept_ref[:, (2 * h - 1) * LAGS : 2 * h * LAGS] = before[1] - sign * here[0]
        before = here


def line_pieces(cfg, packed):
    rows, more, length = cfg["rows"], cfg["more"], cfg["length"]
    tile = packed.shape[0]
    chunks = length // 128 - 1
    low, high = packed[:, :length], packed[:, length:]
    number = iota((SOURCES, rows, 1), 1).reshape(tile, 1)
    deep = jnp.zeros((tile, 1), jnp.int32)
    for k in range(1, rows // chunks + 1):
        deep = deep + jnp.where(number >= k * chunks, 1, 0)
    source = iota((SOURCES, rows, 1), 0).reshape(tile, 1) * rows + more + deep
    source = jnp.where(number < more, source, -1)
    moved = dot(jnp.where(iota((tile, tile), 1) == source, 1.0, 0.0).astype(jnp.bfloat16), high)
    last = jnp.zeros((tile, 128), jnp.float32)
    for m in range(chunks):
        last = last + jnp.where(number - deep * chunks == m, moved[:, m * 128 : (m + 1) * 128], 0.0)
    high = jnp.concatenate([high, last.astype(jnp.bfloat16)], axis=1)
    lines = jnp.concatenate([low, high], axis=0)
    return lines


def match_kernel(cfg, tiles, shapes_hbm, kept_hbm, sums_hbm, table_hbm, sent_ref, *scratch):
    shapes_ref, kept_ref, sums_ref, table_ref, sems = scratch
    packed = shapes_ref.shape[0] // tiles
    tile = kept_ref.shape[0] // tiles
    groups = sent_ref.shape[0] // tiles
    length = cfg["length"]
    copies = []

    def fetch(source, buffer, part=None):
        if part is not None:
            source, buffer = source.at[part], buffer.at[part]
        copies.append(pltpu.make_async_copy(source, buffer, sems.at[len(copies)]))
        copies[-1].start()
        return copies[-1]

    lines = [pl.ds(t * packed, packed) for t in range(tiles)]
    halves = [pl.ds(q * 2 * LAGS, 2 * LAGS) for q in range(2)]
    forward = fetch(table_hbm, table_ref, halves[0])
    part = tile // 2
    shapes, kept = [], []
    for t in range(tiles):
        shapes.append(fetch(shapes_hbm, shapes_ref, lines[t]))
        kept.append([fetch(kept_hbm, kept_ref, pl.ds(t * tile + k * part, part)) for k in range(2)])
        if t == 0:
            inverse = fetch(table_hbm, table_ref, halves[1])
            sums = fetch(sums_hbm, sums_ref)
    forward.wait()
    for t in range(tiles):
        shapes[t].wait()
        mine = shape_spectra(line_pieces(cfg, shapes_ref[lines[t], :]), table_ref[: 2 * LAGS, :])
        if t == 0:
            for copy in (inverse, sums):
                copy.wait()
        ends = pl.ds(t * groups, groups)
        total = 0.0
        for k in range(2):
            kept[t][k].wait()
            theirs = kept_ref[pl.ds(t * tile + k * part, part), :]
            spectra = [
                (theirs[:, 2 * h * LAGS : (2 * h + 1) * LAGS], theirs[:, (2 * h + 1) * LAGS : (2 * h + 2) * LAGS])
                for h in range(length // LAGS)
            ]
            rows = slice(k * part, (k + 1) * part)
            ours = [(real[rows], imag[rows]) for real, imag in mine]
            left = match_lines(ours, spectra, theirs[:, 2 * length :], tables_of(table_ref)[1])
            total = total + sum_lines(sums_ref[ends, rows], left)
        sent_ref[ends, :] = total


def stack_kernel(factor, parts_ref, stacks_ref, top_ref):
    stacks = jnp.sum(parts_ref[...], axis=0) * factor
    stacks_ref[...] = stacks
    top_ref[...] = jnp.broadcast_to(jnp.max(stacks, axis=0, keepdims=True), top_ref.shape)


def body(waveforms, templates, stations, moveouts):
    devices, group, halves = lax.axis_size(AXES), lax.axis_size(GROUP), lax.axis_size(HALF)
    tpl_count, slot_count = stations.shape
    comps, length = templates.shape[2:]
    station_dev, _, samples = waveforms.shape
    seg_len = length + LAGS
    pairs = tpl_count * slot_count
    capacity = (2 * pairs + devices - 1) // devices
    chunks = length // 128 - 1
    total = halves * comps * capacity
    rows = 16
    while total - rows + max(0, -(-(total - rows) // chunks)) > rows:
        rows += 16
    more = max(0, total - rows)
    cfg = dict(
        devices=devices,
        group=group,
        halves=halves,
        parts=[lax.axis_size(name) for name in PARTS],
        station_dev=station_dev,
        tpl_count=tpl_count,
        slot_count=slot_count,
        comps=comps,
        capacity=capacity,
        rows=rows,
        more=more,
        length=length,
        seg_len=seg_len,
        shift_bits=bits_of(samples - seg_len + 1),
        row_bits=bits_of(station_dev),
    )
    table = jnp.asarray(transform_table(LAGS))
    edges = jnp.asarray(edge_table(LAGS))
    tiles = group // SOURCES
    tile = 2 * SOURCES * rows
    lines = 2 * group * rows
    width = length + chunks * 128
    sums_tile = SOURCES * tpl_count
    kept_len = 2 * length + LAGS
    whole = pl.BlockSpec(memory_space=pltpu.VMEM)
    anywhere = pl.BlockSpec(memory_space=pl.ANY)
    params = pltpu.CompilerParams(vmem_limit_bytes=60 * MIB)
    by_slot = templates.transpose(1, 2, 0, 3)
    waves = waveforms.transpose(1, 0, 2)
    half = lax.axis_index(HALF).reshape(1)
    here = lax.axis_index(AXES).reshape(1)

    def work(flops, size):
        return pl.CostEstimate(flops=flops, bytes_accessed=size, transcendentals=0)

    def exchange(x, axes):
        return lax.all_to_all(x, axes, split_axis=0, concat_axis=0, tiled=True)

    def same(shape):
        return pl.BlockSpec(shape, lambda i: (0,) * len(shape))

    def tiled(*shape):
        return pl.BlockSpec(shape, lambda i: (i, 0))

    traces = [waves] + [lax.ppermute(waves, HALF, [(0, 1), (1, 0)])] * (halves - 1)
    lists = pl.pallas_call(
        functools.partial(list_kernel, cfg),
        out_shape=jax.ShapeDtypeStruct((group, tpl_count, -(-slot_count // 128) * 128), jnp.int32),
        in_specs=[whole, whole],
        out_specs=whole,
        compiler_params=params,
        cost_estimate=work(1, 1),
        name="lists",
    )(stations, moveouts)
    lists = exchange(lists, GROUP).reshape(group * tpl_count, lists.shape[2])

    packed = pl.pallas_call(
        functools.partial(pack_kernel, cfg),
        out_shape=jax.ShapeDtypeStruct((group * rows, width), jnp.bfloat16),
        in_specs=[pl.BlockSpec(memory_space=pltpu.SMEM), whole, anywhere],
        out_specs=anywhere,
        scratch_shapes=[
            pltpu.VMEM(by_slot.shape, jnp.bfloat16),
            pltpu.VMEM((comps, pairs, length), jnp.bfloat16),
            pltpu.VMEM((group * rows, width), jnp.bfloat16),
            pltpu.SemaphoreType.DMA,
            pltpu.SemaphoreType.DMA((tiles,)),
        ],
        compiler_params=params,
        cost_estimate=work(5 * 10**9, 1),
        name="pack",
    )(half, stations, by_slot)
    _, packed = lax.optimization_barrier((lists, packed))
    arrived = exchange(packed.reshape(group, rows, width), GROUP).reshape(group * rows, width)

    kept, sums = pl.pallas_call(
        functools.partial(trace_kernel, cfg),
        grid=(tiles,),
        out_shape=[
            jax.ShapeDtypeStruct((lines, kept_len), jnp.float32),
            jax.ShapeDtypeStruct((group * tpl_count, tile), jnp.bfloat16),
        ],
        in_specs=[pl.BlockSpec(memory_space=pltpu.SMEM), tiled(sums_tile, lists.shape[1])]
        + [same(waves.shape)] * halves
        + [same((2 * LAGS, 2 * LAGS)), same(edges.shape)],
        out_specs=[tiled(tile, kept_len), tiled(sums_tile, tile)],
        compiler_params=params,
        cost_estimate=work(10**12, 1),
        name="traces",
    )(here, lists, *traces, table, edges)
    operands = (arrived, kept, sums, table)
    sent = pl.pallas_call(
        functools.partial(match_kernel, cfg, tiles),
        out_shape=jax.ShapeDtypeStruct((group * tpl_count, LAGS), jnp.float32),
        in_specs=[anywhere] * len(operands),
        out_specs=whole,
        scratch_shapes=[pltpu.VMEM(x.shape, x.dtype) for x in operands]
        + [pltpu.SemaphoreType.DMA((3 + 3 * tiles,))],
        compiler_params=pltpu.CompilerParams(vmem_limit_bytes=57 * MIB),
        name="match",
    )(*operands)

    parts = exchange(sent.reshape(group, tpl_count, LAGS), GROUP)
    stacks, top = pl.pallas_call(
        functools.partial(stack_kernel, math.sqrt(length / (comps * slot_count))),
        out_shape=[
            jax.ShapeDtypeStruct((tpl_count, LAGS), jnp.float32),
            jax.ShapeDtypeStruct((devices, 1, LAGS), jnp.float32),
        ],
        in_specs=[whole],
        out_specs=[whole, whole],
        compiler_params=pltpu.CompilerParams(vmem_limit_bytes=16 * MIB),
        name="stack",
    )(parts)
    return stacks, jnp.max(exchange(top, AXES), axis=(0, 1))


def solution(mesh):
    slow, fast = mesh.devices.shape
    halves = 2 if slow % 2 == 0 else 1
    deep = 2 if slow // halves % 2 == 0 else 1
    cores = 2 if fast % 2 == 0 else 1
    shape = (halves, deep, slow // halves // deep, fast // cores, cores)
    split = jax.sharding.Mesh(mesh.devices.reshape(shape), AXES)
    placed = (
        P(AXES, None, None),
        P(AXES, None, None, None),
        P(AXES, None),
        P(AXES, None),
    )
    return jax.shard_map(body, mesh=split, in_specs=placed, out_specs=(P(AXES, None), P()), check_vma=False)
```

```python
import functools
import math

import jax
import jax.numpy as jnp
import ml_dtypes
import numpy as np
from jax import lax
from jax.experimental import pallas as pl
from jax.experimental.pallas import tpu as pltpu
from jax.sharding import PartitionSpec as P

LAGS = 256
HALF = "half"
DEEP = "deep"
PARTS = (DEEP, "wide", "sta", "core")
AXES = (HALF,) + PARTS
GROUP = PARTS[::-1]
SOURCES = 8
MIB = 1024 * 1024


def bits_of(limit):
    return max(1, (limit - 1).bit_length())


def split_table(table):
    high = table.astype(ml_dtypes.bfloat16)
    return high, (table - high.astype(np.float64)).astype(ml_dtypes.bfloat16)


def transform_table(piece):
    size = 2 * piece
    angle = 2.0 * np.pi * (np.arange(piece) + 0.5) / size
    phase = np.arange(piece)[:, None] * angle[None, :]
    forward = np.concatenate([np.cos(phase), -np.sin(phase)], axis=1)
    inverse = np.concatenate([np.cos(phase.T), -np.sin(phase.T)], axis=0) * (2.0 / size)
    return np.concatenate([*split_table(forward), np.concatenate(split_table(inverse), axis=1)], axis=0)


def edge_table(lag_count):
    sample = np.arange(lag_count)[:, None]
    lag = np.arange(lag_count)[None, :]
    return np.concatenate([sample >= lag, sample < lag], axis=0).astype(ml_dtypes.bfloat16)


def iota(shape, axis):
    return lax.broadcasted_iota(jnp.int32, shape, axis)


def dot(a, b):
    return jnp.dot(a, b, preferred_element_type=jnp.float32)


def exact_dot(a, b):
    return jnp.dot(a, b, precision=lax.Precision.HIGHEST, preferred_element_type=jnp.float32)


def entry_lanes(tpl_count, slot_count):
    pairs = tpl_count * slot_count
    first = iota((slot_count, pairs), 0) * tpl_count
    entry = iota((slot_count, pairs), 1)
    spread = jnp.where((entry >= first) & (entry < first + tpl_count), 1.0, 0.0)
    start = jnp.sum(spread * first.astype(jnp.float32), axis=0, keepdims=True)
    return spread, iota((1, pairs), 1).astype(jnp.float32) - start


def as_lanes(values, spread, place, tpl_count):
    owners = values.shape[0] // tpl_count
    pairs = spread.shape[1]
    wide = exact_dot(values.astype(jnp.float32), spread).reshape(owners, tpl_count, pairs)
    own = iota((1, tpl_count, pairs), 1).astype(jnp.float32) == place.reshape(1, 1, pairs)
    return jnp.sum(jnp.where(own, wide, 0.0), axis=1)


def count_before(hits):
    pairs = hits.shape[1]
    earlier = jnp.where(iota((pairs, pairs), 0) < iota((pairs, pairs), 1), 1.0, 0.0)
    return dot(hits.astype(jnp.bfloat16), earlier.astype(jnp.bfloat16))


def list_kernel(cfg, stations_ref, moveouts_ref, lists_ref):
    lists = stations_ref[...] * (1 << cfg["shift_bits"]) + moveouts_ref[...]
    group, tpl_count, _ = lists_ref.shape
    slot_count = lists.shape[1]
    lists_ref[:, :, :slot_count] = jnp.broadcast_to(lists.reshape(1, tpl_count, slot_count), (group, tpl_count, slot_count))


def pack_kernel(
    cfg, half_ref, stations_ref, templates_hbm, packed_hbm, raw_ref, shapes_ref, packed_ref, in_sem, out_sems
):
    load = pltpu.make_async_copy(templates_hbm, raw_ref, in_sem)
    load.start()
    tpl_count, slot_count = stations_ref.shape
    pairs = tpl_count * slot_count
    devices, group, halves, rows = cfg["devices"], cfg["group"], cfg["halves"], cfg["rows"]
    spread, place = entry_lanes(tpl_count, slot_count)
    station = as_lanes(stations_ref[...], spread, place, tpl_count)
    device = jnp.floor((station + 0.5) * (1.0 / cfg["station_dev"]))
    onehot = jnp.where(iota((devices, pairs), 0).astype(jnp.float32) == device, 1.0, 0.0)
    rank = jnp.sum(onehot * count_before(onehot), axis=0, keepdims=True)
    half = jnp.floor((device + 0.5) * (1.0 / group))
    away = jnp.where(half == half_ref[0].astype(jnp.float32), 0.0, 1.0)
    holder = device - half * group
    number = jnp.zeros_like(holder)
    for size in cfg["parts"][::-1]:
        rest = jnp.floor((holder + 0.5) * (1.0 / size))
        number = number * size + (holder - rest * size)
        holder = rest
    holder = number
    capacity = cfg["capacity"]
    base = jnp.where(rank < float(capacity), away * (cfg["comps"] * capacity) + rank, -1e6)

    comps, length = raw_ref.shape[1], raw_ref.shape[3]
    load.wait()
    for c in range(comps):
        values = raw_ref[:, c].astype(jnp.float32).reshape(pairs, length)
        centred = values - jnp.mean(values, axis=-1, keepdims=True)
        spread_c = jnp.sqrt(jnp.mean(centred * centred, axis=-1, keepdims=True) + 1e-05)
        shapes_ref[c] = (centred * (1.0 / spread_c)).astype(jnp.bfloat16)

    more, step_len = cfg["more"], 128
    chunks = length // step_len - 1
    tile = SOURCES * rows
    copies = []
    for step in range(group // SOURCES):
        at = iota((tile, pairs), 0).astype(jnp.float32)
        first = (holder - float(step * SOURCES)) * rows
        low = jnp.zeros((tile, length), jnp.float32)
        high = jnp.zeros((tile, chunks * step_len), jnp.float32)
        lasts = [jnp.zeros((tile, step_len), jnp.float32) for _ in range(chunks)]
        for c in range(comps):
            line = base + float(c * capacity)
            extra = line - float(rows)
            there = (extra >= 0.0) & (extra < float(more))
            deep = jnp.floor((extra + 0.5) * (1.0 / chunks))
            spot = jnp.where(there, extra - deep * chunks, -1.0)
            shapes = shapes_ref[c]

            def pick(ok, row):
                return jnp.where(at == jnp.where(ok, first + row, -1.0), 1.0, 0.0).astype(jnp.bfloat16)

            low = low + dot(pick((line >= 0.0) & (line < float(rows)), line), shapes)
            high = high + dot(pick(there, extra), shapes[:, : chunks * step_len])
            for m in range(chunks):
                picked = pick(spot == float(m), float(more) + deep)
                lasts[m] = lasts[m] + dot(picked, shapes[:, chunks * step_len :])
        part = pl.ds(step * tile, tile)
        packed_ref[part, :length] = low.astype(jnp.bfloat16)
        packed_ref[part, length:] = (high + jnp.concatenate(lasts, axis=1)).astype(jnp.bfloat16)
        copies.append(pltpu.make_async_copy(packed_ref.at[part], packed_hbm.at[part], out_sems.at[step]))
        copies[-1].start()
    for copy in copies:
        copy.wait()


def tile_lines(cfg, here, lists):
    capacity, rows, comps, halves = cfg["capacity"], cfg["rows"], cfg["comps"], cfg["halves"]
    station_dev, shift_bits, row_bits = cfg["station_dev"], cfg["shift_bits"], cfg["row_bits"]
    tpl_count, slot_count = cfg["tpl_count"], cfg["slot_count"]
    lists = lists[:, :slot_count]
    pairs = tpl_count * slot_count
    tile = 2 * SOURCES * rows
    spread, place = entry_lanes(tpl_count, slot_count)
    station = as_lanes(lax.shift_right_logical(lists, shift_bits), spread, place, tpl_count)
    shift = as_lanes(lists & ((1 << shift_bits) - 1), spread, place, tpl_count)

    def per_line(x):
        wide = jnp.broadcast_to(x.reshape(SOURCES, 1, pairs), (SOURCES, rows, pairs)).reshape(tile // 2, pairs)
        return jnp.concatenate([wide, wide], axis=0)

    ranks, codes = [], []
    for device in here:
        row = station - (device * station_dev).astype(jnp.float32)
        hit = jnp.where((row >= 0.0) & (row < float(station_dev)), 1.0, 0.0)
        ranks.append(jnp.where(hit > 0.0, count_before(hit), -1.0))
        codes.append(((place + 1.0) * (1 << row_bits) + row) * (1 << shift_bits) + shift)

    line = iota((SOURCES, rows, 1), 1).reshape(tile // 2, 1)
    line = jnp.concatenate([line, line + rows], axis=0)
    owner = iota((SOURCES, rows, 1), 0).reshape(tile // 2, 1)
    owner = jnp.concatenate([owner, owner], axis=0)
    panel = jnp.zeros((tile, 1), jnp.int32)
    for m in range(1, halves * comps + 1):
        panel = panel + jnp.where(line >= m * capacity, 1, 0)
    slot = jnp.where(panel < halves * comps, line - panel * capacity, -2).astype(jnp.float32)
    code = jnp.zeros((tile, 1), jnp.float32)
    for q in range(halves):
        mine = jnp.where((panel >= q * comps) & (panel < (q + 1) * comps), slot, -2.0)
        code = code + jnp.sum(jnp.where(per_line(ranks[q]) == mine, per_line(codes[q]), 0.0), axis=1, keepdims=True)
    code = code.astype(jnp.int32)
    row = lax.shift_right_logical(code, shift_bits) & ((1 << row_bits) - 1)
    tpl = lax.shift_right_logical(code, shift_bits + row_bits) - 1
    goal = panel * station_dev + row
    return (
        code & ((1 << shift_bits) - 1),
        jnp.where(tpl >= 0, goal, -1),
        jnp.where(tpl >= 0, owner * tpl_count + tpl, -1),
    )


def cut_traces(cfg, shift, goal, waves):
    tile, seg_len, shift_bits = shift.shape[0], cfg["seg_len"], cfg["shift_bits"]
    pick = jnp.where(iota((tile, waves.shape[0]), 1) == goal, 1.0, 0.0).astype(jnp.bfloat16)
    x = dot(pick, waves).astype(jnp.bfloat16)

    def choose(step, moved, still):
        flag = jnp.where((shift & step) != 0, 1.0, 0.0)
        return moved * flag.astype(jnp.bfloat16) + still * (1.0 - flag).astype(jnp.bfloat16)

    for bit in range(shift_bits - 1, 6, -1):
        step = 1 << bit
        width = seg_len + step
        if x.shape[1] < width + step:
            x = jnp.concatenate([x, jnp.zeros((tile, width + step - x.shape[1]), jnp.bfloat16)], axis=1)
        x = choose(step, x[:, step : step + width], x[:, :width])
    for bit in range(min(shift_bits, 7) - 1, -1, -1):
        step = 1 << bit
        x = choose(step, pltpu.roll(x, x.shape[1] - step, 1), x)
    return x[:, :seg_len]


def line_sums(cfg, column):
    groups = SOURCES * cfg["tpl_count"]
    return jnp.where(iota((column.shape[0], groups), 1) == column, 1.0, 0.0).T.astype(jnp.bfloat16)


def levels_scale(cfg, narrow, edges):
    length = cfg["length"]
    ends = jnp.concatenate([narrow[:, :LAGS], narrow[:, length:]], axis=1).astype(jnp.float32)
    ends = ends * ends
    high = ends.astype(jnp.bfloat16)
    low = (ends - high.astype(jnp.float32)).astype(jnp.bfloat16)
    middle = narrow[:, LAGS:length].astype(jnp.float32)
    energy = dot(high, edges) + dot(low, edges) + jnp.sum(middle * middle, axis=1, keepdims=True)
    return 1.0 / (length * jnp.sqrt(energy * (1.0 / length) + 1e-05))


def shape_spectra(shapes, forward):
    spectra = []
    for h in range(shapes.shape[1] // LAGS):
        part = shapes[:, h * LAGS : (h + 1) * LAGS]
        mine = dot(jnp.concatenate([part, part], axis=1), forward)
        spectra.append((mine[:, :LAGS], mine[:, LAGS:]))
    return spectra


def match_lines(mine, theirs, scale, inverse):
    real = imag = 0.0
    for (mine_r, mine_i), (theirs_r, theirs_i) in zip(mine, theirs):
        real = real + (theirs_r * mine_r + theirs_i * mine_i)
        imag = imag + (theirs_i * mine_r - theirs_r * mine_i)
    product = jnp.concatenate([real, imag], axis=1)
    high = product.astype(jnp.bfloat16)
    low = (product - high.astype(jnp.float32)).astype(jnp.bfloat16)
    return dot(jnp.concatenate([high, high, low], axis=1), inverse) * scale


def sum_lines(sums, left):
    total = 0.0
    for _ in range(3):
        part = left.astype(jnp.bfloat16)
        left = left - part.astype(jnp.float32)
        total = total + dot(sums, part)
    return total


def tables_of(table_ref):
    back = table_ref[2 * LAGS :, :]
    high, low = back[:, :LAGS], back[:, LAGS:]
    return table_ref[: 2 * LAGS, :], jnp.concatenate([high, low, high], axis=0)


def trace_kernel(cfg, here_ref, lists_ref, *refs):
    waves_refs, (table_ref, edges_ref, kept_ref, sums_ref) = refs[:-4], refs[-4:]
    here = [here_ref[0]]
    for _ in range(1, cfg["halves"]):
        other = here[-1] + cfg["group"]
        here.append(jnp.where(other >= cfg["devices"], other - cfg["devices"], other))
    shift, goal, column = tile_lines(cfg, here, lists_ref[...])
    waves = [ref[...].reshape(-1, ref.shape[2]) for ref in waves_refs]
    narrow = cut_traces(cfg, shift, goal, jnp.concatenate(waves, axis=0))
    kept_ref[:, 2 * cfg["length"] :] = levels_scale(cfg, narrow, edges_ref[...])
    sums_ref[...] = line_sums(cfg, column)

    sign = (1 - 2 * (iota((1, LAGS), 1) & 1)).astype(jnp.float32)
    before = None
    for h in range(cfg["length"] // LAGS + 1):
        part = narrow[:, h * LAGS : (h + 1) * LAGS]
        here = dot(jnp.concatenate([part, part], axis=1), table_ref[...])
        here = here[:, :LAGS], here[:, LAGS:]
        if before is not None:
            kept_ref[:, (2 * h - 2) * LAGS : (2 * h - 1) * LAGS] = before[0] + sign * here[1]
            kept_ref[:, (2 * h - 1) * LAGS : 2 * h * LAGS] = before[1] - sign * here[0]
        before = here


def line_pieces(cfg, packed):
    rows, more, length = cfg["rows"], cfg["more"], cfg["length"]
    tile = packed.shape[0]
    chunks = length // 128 - 1
    low, high = packed[:, :length], packed[:, length:]
    number = iota((SOURCES, rows, 1), 1).reshape(tile, 1)
    deep = jnp.zeros((tile, 1), jnp.int32)
    for k in range(1, rows // chunks + 1):
        deep = deep + jnp.where(number >= k * chunks, 1, 0)
    source = iota((SOURCES, rows, 1), 0).reshape(tile, 1) * rows + more + deep
    source = jnp.where(number < more, source, -1)
    moved = dot(jnp.where(iota((tile, tile), 1) == source, 1.0, 0.0).astype(jnp.bfloat16), high)
    last = jnp.zeros((tile, 128), jnp.float32)
    for m in range(chunks):
        last = last + jnp.where(number - deep * chunks == m, moved[:, m * 128 : (m + 1) * 128], 0.0)
    high = jnp.concatenate([high, last.astype(jnp.bfloat16)], axis=1)
    lines = jnp.concatenate([low, high], axis=0)
    return lines


def match_kernel(cfg, tiles, shapes_hbm, kept_hbm, sums_hbm, table_hbm, sent_ref, *scratch):
    shapes_ref, kept_ref, sums_ref, table_ref, sems = scratch
    packed = shapes_ref.shape[0] // tiles
    tile = kept_ref.shape[0] // tiles
    groups = sent_ref.shape[0] // tiles
    length = cfg["length"]
    copies = []

    def fetch(source, buffer, part=None):
        if part is not None:
            source, buffer = source.at[part], buffer.at[part]
        copies.append(pltpu.make_async_copy(source, buffer, sems.at[len(copies)]))
        copies[-1].start(priority=len(copies) % 2)
        return copies[-1]

    lines = [pl.ds(t * packed, packed) for t in range(tiles)]
    halves = [pl.ds(q * 2 * LAGS, 2 * LAGS) for q in range(2)]
    forward = fetch(table_hbm, table_ref, halves[0])
    part = tile // 2
    shapes, kept = [], []
    for t in range(tiles):
        shapes.append(fetch(shapes_hbm, shapes_ref, lines[t]))
        kept.append([fetch(kept_hbm, kept_ref, pl.ds(t * tile + k * part, part)) for k in range(2)])
        if t == 0:
            inverse = fetch(table_hbm, table_ref, halves[1])
            sums = fetch(sums_hbm, sums_ref)
    forward.wait()
    for t in range(tiles):
        shapes[t].wait()
        mine = shape_spectra(line_pieces(cfg, shapes_ref[lines[t], :]), table_ref[: 2 * LAGS, :])
        if t == 0:
            for copy in (inverse, sums):
                copy.wait()
        ends = pl.ds(t * groups, groups)
        total = 0.0
        for k in range(2):
            kept[t][k].wait()
            theirs = kept_ref[pl.ds(t * tile + k * part, part), :]
            spectra = [
                (theirs[:, 2 * h * LAGS : (2 * h + 1) * LAGS], theirs[:, (2 * h + 1) * LAGS : (2 * h + 2) * LAGS])
                for h in range(length // LAGS)
            ]
            rows = slice(k * part, (k + 1) * part)
            ours = [(real[rows], imag[rows]) for real, imag in mine]
            left = match_lines(ours, spectra, theirs[:, 2 * length :], tables_of(table_ref)[1])
            total = total + sum_lines(sums_ref[ends, rows], left)
        sent_ref[ends, :] = total


def stack_kernel(factor, parts_ref, stacks_ref, top_ref):
    stacks = jnp.sum(parts_ref[...], axis=0) * factor
    stacks_ref[...] = stacks
    top_ref[...] = jnp.broadcast_to(jnp.max(stacks, axis=0, keepdims=True), top_ref.shape)


def body(waveforms, templates, stations, moveouts):
    devices, group, halves = lax.axis_size(AXES), lax.axis_size(GROUP), lax.axis_size(HALF)
    tpl_count, slot_count = stations.shape
    comps, length = templates.shape[2:]
    station_dev, _, samples = waveforms.shape
    seg_len = length + LAGS
    pairs = tpl_count * slot_count
    capacity = (2 * pairs + devices - 1) // devices
    chunks = length // 128 - 1
    total = halves * comps * capacity
    rows = 16
    while total - rows + max(0, -(-(total - rows) // chunks)) > rows:
        rows += 16
    more = max(0, total - rows)
    cfg = dict(
        devices=devices,
        group=group,
        halves=halves,
        parts=[lax.axis_size(name) for name in PARTS],
        station_dev=station_dev,
        tpl_count=tpl_count,
        slot_count=slot_count,
        comps=comps,
        capacity=capacity,
        rows=rows,
        more=more,
        length=length,
        seg_len=seg_len,
        shift_bits=bits_of(samples - seg_len + 1),
        row_bits=bits_of(station_dev),
    )
    table = jnp.asarray(transform_table(LAGS))
    edges = jnp.asarray(edge_table(LAGS))
    tiles = group // SOURCES
    tile = 2 * SOURCES * rows
    lines = 2 * group * rows
    width = length + chunks * 128
    sums_tile = SOURCES * tpl_count
    kept_len = 2 * length + LAGS
    whole = pl.BlockSpec(memory_space=pltpu.VMEM)
    anywhere = pl.BlockSpec(memory_space=pl.ANY)
    params = pltpu.CompilerParams(vmem_limit_bytes=60 * MIB)
    by_slot = templates.transpose(1, 2, 0, 3)
    waves = waveforms.transpose(1, 0, 2)
    half = lax.axis_index(HALF).reshape(1)
    here = lax.axis_index(AXES).reshape(1)

    def work(flops, size):
        return pl.CostEstimate(flops=flops, bytes_accessed=size, transcendentals=0)

    def exchange(x, axes):
        return lax.all_to_all(x, axes, split_axis=0, concat_axis=0, tiled=True)

    def same(shape):
        return pl.BlockSpec(shape, lambda i: (0,) * len(shape))

    def tiled(*shape):
        return pl.BlockSpec(shape, lambda i: (i, 0))

    traces = [waves] + [lax.ppermute(waves, HALF, [(0, 1), (1, 0)])] * (halves - 1)
    lists = pl.pallas_call(
        functools.partial(list_kernel, cfg),
        out_shape=jax.ShapeDtypeStruct((group, tpl_count, -(-slot_count // 128) * 128), jnp.int32),
        in_specs=[whole, whole],
        out_specs=whole,
        compiler_params=params,
        cost_estimate=work(1, 1),
        name="lists",
    )(stations, moveouts)
    lists = exchange(lists, GROUP).reshape(group * tpl_count, lists.shape[2])

    packed = pl.pallas_call(
        functools.partial(pack_kernel, cfg),
        out_shape=jax.ShapeDtypeStruct((group * rows, width), jnp.bfloat16),
        in_specs=[pl.BlockSpec(memory_space=pltpu.SMEM), whole, anywhere],
        out_specs=anywhere,
        scratch_shapes=[
            pltpu.VMEM(by_slot.shape, jnp.bfloat16),
            pltpu.VMEM((comps, pairs, length), jnp.bfloat16),
            pltpu.VMEM((group * rows, width), jnp.bfloat16),
            pltpu.SemaphoreType.DMA,
            pltpu.SemaphoreType.DMA((tiles,)),
        ],
        compiler_params=params,
        cost_estimate=work(5 * 10**9, 1),
        name="pack",
    )(half, stations, by_slot)
    _, packed = lax.optimization_barrier((lists, packed))
    arrived = exchange(packed.reshape(group, rows, width), GROUP).reshape(group * rows, width)

    kept, sums = pl.pallas_call(
        functools.partial(trace_kernel, cfg),
        grid=(tiles,),
        out_shape=[
            jax.ShapeDtypeStruct((lines, kept_len), jnp.float32),
            jax.ShapeDtypeStruct((group * tpl_count, tile), jnp.bfloat16),
        ],
        in_specs=[pl.BlockSpec(memory_space=pltpu.SMEM), tiled(sums_tile, lists.shape[1])]
        + [same(waves.shape)] * halves
        + [same((2 * LAGS, 2 * LAGS)), same(edges.shape)],
        out_specs=[tiled(tile, kept_len), tiled(sums_tile, tile)],
        compiler_params=params,
        cost_estimate=work(10**12, 1),
        name="traces",
    )(here, lists, *traces, table, edges)
    operands = (arrived, kept, sums, table)
    sent = pl.pallas_call(
        functools.partial(match_kernel, cfg, tiles),
        out_shape=jax.ShapeDtypeStruct((group * tpl_count, LAGS), jnp.float32),
        in_specs=[anywhere] * len(operands),
        out_specs=whole,
        scratch_shapes=[pltpu.VMEM(x.shape, x.dtype) for x in operands]
        + [pltpu.SemaphoreType.DMA((3 + 3 * tiles,))],
        compiler_params=pltpu.CompilerParams(vmem_limit_bytes=57 * MIB),
        name="match",
    )(*operands)

    parts = exchange(sent.reshape(group, tpl_count, LAGS), GROUP)
    stacks, top = pl.pallas_call(
        functools.partial(stack_kernel, math.sqrt(length / (comps * slot_count))),
        out_shape=[
            jax.ShapeDtypeStruct((tpl_count, LAGS), jnp.float32),
            jax.ShapeDtypeStruct((devices, 1, LAGS), jnp.float32),
        ],
        in_specs=[whole],
        out_specs=[whole, whole],
        compiler_params=pltpu.CompilerParams(vmem_limit_bytes=16 * MIB),
        name="stack",
    )(parts)
    return stacks, jnp.max(exchange(top, AXES[::-1]), axis=(0, 1))


def solution(mesh):
    slow, fast = mesh.devices.shape
    halves = 2 if slow % 2 == 0 else 1
    deep = 2 if slow // halves % 2 == 0 else 1
    cores = 2 if fast % 2 == 0 else 1
    shape = (halves, deep, slow // halves // deep, fast // cores, cores)
    split = jax.sharding.Mesh(mesh.devices.reshape(shape), AXES)
    placed = (
        P(AXES, None, None),
        P(AXES, None, None, None),
        P(AXES, None),
        P(AXES, None),
    )
    return jax.shard_map(body, mesh=split, in_specs=placed, out_specs=(P(AXES, None), P()), check_vma=False)
```

```python
import functools
import math

import jax
import jax.numpy as jnp
import ml_dtypes
import numpy as np
from jax import lax
from jax.experimental import pallas as pl
from jax.experimental.pallas import tpu as pltpu
from jax.sharding import PartitionSpec as P

LAGS = 256
HALF = "half"
DEEP = "deep"
PARTS = (DEEP, "wide", "sta", "core")
AXES = (HALF,) + PARTS
GROUP = PARTS[::-1]
SOURCES = 8
MIB = 1024 * 1024


def bits_of(limit):
    return max(1, (limit - 1).bit_length())


def split_table(table):
    high = table.astype(ml_dtypes.bfloat16)
    return high, (table - high.astype(np.float64)).astype(ml_dtypes.bfloat16)


def transform_table(piece):
    size = 2 * piece
    angle = 2.0 * np.pi * (np.arange(piece) + 0.5) / size
    phase = np.arange(piece)[:, None] * angle[None, :]
    forward = np.concatenate([np.cos(phase), -np.sin(phase)], axis=1)
    inverse = np.concatenate([np.cos(phase.T), -np.sin(phase.T)], axis=0) * (2.0 / size)
    return np.concatenate([*split_table(forward), np.concatenate(split_table(inverse), axis=1)], axis=0)


def edge_table(lag_count):
    sample = np.arange(lag_count)[:, None]
    lag = np.arange(lag_count)[None, :]
    return np.concatenate([sample >= lag, sample < lag], axis=0).astype(ml_dtypes.bfloat16)


def iota(shape, axis):
    return lax.broadcasted_iota(jnp.int32, shape, axis)


def dot(a, b):
    return jnp.dot(a, b, preferred_element_type=jnp.float32)


def exact_dot(a, b):
    return jnp.dot(a, b, precision=lax.Precision.HIGHEST, preferred_element_type=jnp.float32)


def entry_lanes(tpl_count, slot_count):
    pairs = tpl_count * slot_count
    first = iota((slot_count, pairs), 0) * tpl_count
    entry = iota((slot_count, pairs), 1)
    spread = jnp.where((entry >= first) & (entry < first + tpl_count), 1.0, 0.0)
    start = jnp.sum(spread * first.astype(jnp.float32), axis=0, keepdims=True)
    return spread, iota((1, pairs), 1).astype(jnp.float32) - start


def as_lanes(values, spread, place, tpl_count):
    owners = values.shape[0] // tpl_count
    pairs = spread.shape[1]
    wide = exact_dot(values.astype(jnp.float32), spread).reshape(owners, tpl_count, pairs)
    own = iota((1, tpl_count, pairs), 1).astype(jnp.float32) == place.reshape(1, 1, pairs)
    return jnp.sum(jnp.where(own, wide, 0.0), axis=1)


def count_before(hits):
    pairs = hits.shape[1]
    earlier = jnp.where(iota((pairs, pairs), 0) < iota((pairs, pairs), 1), 1.0, 0.0)
    return dot(hits.astype(jnp.bfloat16), earlier.astype(jnp.bfloat16))


def list_kernel(cfg, stations_ref, moveouts_ref, lists_ref):
    lists = stations_ref[...] * (1 << cfg["shift_bits"]) + moveouts_ref[...]
    group, tpl_count, _ = lists_ref.shape
    slot_count = lists.shape[1]
    lists_ref[:, :, :slot_count] = jnp.broadcast_to(lists.reshape(1, tpl_count, slot_count), (group, tpl_count, slot_count))


def pack_kernel(
    cfg, half_ref, stations_ref, templates_hbm, packed_hbm, raw_ref, shapes_ref, packed_ref, in_sem, out_sems
):
    load = pltpu.make_async_copy(templates_hbm, raw_ref, in_sem)
    load.start()
    tpl_count, slot_count = stations_ref.shape
    pairs = tpl_count * slot_count
    devices, group, halves, rows = cfg["devices"], cfg["group"], cfg["halves"], cfg["rows"]
    spread, place = entry_lanes(tpl_count, slot_count)
    station = as_lanes(stations_ref[...], spread, place, tpl_count)
    device = jnp.floor((station + 0.5) * (1.0 / cfg["station_dev"]))
    onehot = jnp.where(iota((devices, pairs), 0).astype(jnp.float32) == device, 1.0, 0.0)
    rank = jnp.sum(onehot * count_before(onehot), axis=0, keepdims=True)
    half = jnp.floor((device + 0.5) * (1.0 / group))
    away = jnp.where(half == half_ref[0].astype(jnp.float32), 0.0, 1.0)
    holder = device - half * group
    number = jnp.zeros_like(holder)
    for size in cfg["parts"][::-1]:
        rest = jnp.floor((holder + 0.5) * (1.0 / size))
        number = number * size + (holder - rest * size)
        holder = rest
    holder = number
    capacity = cfg["capacity"]
    base = jnp.where(rank < float(capacity), away * (cfg["comps"] * capacity) + rank, -1e6)

    comps, length = raw_ref.shape[1], raw_ref.shape[3]
    load.wait()
    for c in range(comps):
        values = raw_ref[:, c].astype(jnp.float32).reshape(pairs, length)
        centred = values - jnp.mean(values, axis=-1, keepdims=True)
        spread_c = jnp.sqrt(jnp.mean(centred * centred, axis=-1, keepdims=True) + 1e-05)
        shapes_ref[c] = (centred * (1.0 / spread_c)).astype(jnp.bfloat16)

    more, step_len = cfg["more"], 128
    chunks = length // step_len - 1
    tile = SOURCES * rows
    copies = []
    for step in range(group // SOURCES):
        at = iota((tile, pairs), 0).astype(jnp.float32)
        first = (holder - float(step * SOURCES)) * rows
        low = jnp.zeros((tile, length), jnp.float32)
        high = jnp.zeros((tile, chunks * step_len), jnp.float32)
        lasts = [jnp.zeros((tile, step_len), jnp.float32) for _ in range(chunks)]
        for c in range(comps):
            line = base + float(c * capacity)
            extra = line - float(rows)
            there = (extra >= 0.0) & (extra < float(more))
            deep = jnp.floor((extra + 0.5) * (1.0 / chunks))
            spot = jnp.where(there, extra - deep * chunks, -1.0)
            shapes = shapes_ref[c]

            def pick(ok, row):
                return jnp.where(at == jnp.where(ok, first + row, -1.0), 1.0, 0.0).astype(jnp.bfloat16)

            low = low + dot(pick((line >= 0.0) & (line < float(rows)), line), shapes)
            high = high + dot(pick(there, extra), shapes[:, : chunks * step_len])
            for m in range(chunks):
                picked = pick(spot == float(m), float(more) + deep)
                lasts[m] = lasts[m] + dot(picked, shapes[:, chunks * step_len :])
        part = pl.ds(step * tile, tile)
        packed_ref[part, :length] = low.astype(jnp.bfloat16)
        packed_ref[part, length:] = (high + jnp.concatenate(lasts, axis=1)).astype(jnp.bfloat16)
        copies.append(pltpu.make_async_copy(packed_ref.at[part], packed_hbm.at[part], out_sems.at[step]))
        copies[-1].start()
    for copy in copies:
        copy.wait()


def tile_lines(cfg, here, lists):
    capacity, rows, comps, halves = cfg["capacity"], cfg["rows"], cfg["comps"], cfg["halves"]
    station_dev, shift_bits, row_bits = cfg["station_dev"], cfg["shift_bits"], cfg["row_bits"]
    tpl_count, slot_count = cfg["tpl_count"], cfg["slot_count"]
    lists = lists[:, :slot_count]
    pairs = tpl_count * slot_count
    tile = 2 * SOURCES * rows
    spread, place = entry_lanes(tpl_count, slot_count)
    station = as_lanes(lax.shift_right_logical(lists, shift_bits), spread, place, tpl_count)
    shift = as_lanes(lists & ((1 << shift_bits) - 1), spread, place, tpl_count)

    def per_line(x):
        wide = jnp.broadcast_to(x.reshape(SOURCES, 1, pairs), (SOURCES, rows, pairs)).reshape(tile // 2, pairs)
        return jnp.concatenate([wide, wide], axis=0)

    ranks, codes = [], []
    for device in here:
        row = station - (device * station_dev).astype(jnp.float32)
        hit = jnp.where((row >= 0.0) & (row < float(station_dev)), 1.0, 0.0)
        ranks.append(jnp.where(hit > 0.0, count_before(hit), -1.0))
        codes.append(((place + 1.0) * (1 << row_bits) + row) * (1 << shift_bits) + shift)

    line = iota((SOURCES, rows, 1), 1).reshape(tile // 2, 1)
    line = jnp.concatenate([line, line + rows], axis=0)
    owner = iota((SOURCES, rows, 1), 0).reshape(tile // 2, 1)
    owner = jnp.concatenate([owner, owner], axis=0)
    panel = jnp.zeros((tile, 1), jnp.int32)
    for m in range(1, halves * comps + 1):
        panel = panel + jnp.where(line >= m * capacity, 1, 0)
    slot = jnp.where(panel < halves * comps, line - panel * capacity, -2).astype(jnp.float32)
    code = jnp.zeros((tile, 1), jnp.float32)
    for q in range(halves):
        mine = jnp.where((panel >= q * comps) & (panel < (q + 1) * comps), slot, -2.0)
        code = code + jnp.sum(jnp.where(per_line(ranks[q]) == mine, per_line(codes[q]), 0.0), axis=1, keepdims=True)
    code = code.astype(jnp.int32)
    row = lax.shift_right_logical(code, shift_bits) & ((1 << row_bits) - 1)
    tpl = lax.shift_right_logical(code, shift_bits + row_bits) - 1
    goal = panel * station_dev + row
    return (
        code & ((1 << shift_bits) - 1),
        jnp.where(tpl >= 0, goal, -1),
        jnp.where(tpl >= 0, owner * tpl_count + tpl, -1),
    )


def cut_traces(cfg, shift, goal, waves):
    tile, seg_len, shift_bits = shift.shape[0], cfg["seg_len"], cfg["shift_bits"]
    pick = jnp.where(iota((tile, waves.shape[0]), 1) == goal, 1.0, 0.0).astype(jnp.bfloat16)
    x = dot(pick, waves).astype(jnp.bfloat16)

    def choose(step, moved, still):
        flag = jnp.where((shift & step) != 0, 1.0, 0.0)
        return moved * flag.astype(jnp.bfloat16) + still * (1.0 - flag).astype(jnp.bfloat16)

    for bit in range(shift_bits - 1, 6, -1):
        step = 1 << bit
        width = seg_len + step
        if x.shape[1] < width + step:
            x = jnp.concatenate([x, jnp.zeros((tile, width + step - x.shape[1]), jnp.bfloat16)], axis=1)
        x = choose(step, x[:, step : step + width], x[:, :width])
    for bit in range(min(shift_bits, 7) - 1, -1, -1):
        step = 1 << bit
        x = choose(step, pltpu.roll(x, x.shape[1] - step, 1), x)
    return x[:, :seg_len]


def line_sums(cfg, column):
    groups = SOURCES * cfg["tpl_count"]
    return jnp.where(iota((column.shape[0], groups), 1) == column, 1.0, 0.0).T.astype(jnp.bfloat16)


def levels_scale(cfg, narrow, edges):
    length = cfg["length"]
    ends = jnp.concatenate([narrow[:, :LAGS], narrow[:, length:]], axis=1).astype(jnp.float32)
    ends = ends * ends
    high = ends.astype(jnp.bfloat16)
    low = (ends - high.astype(jnp.float32)).astype(jnp.bfloat16)
    middle = narrow[:, LAGS:length].astype(jnp.float32)
    energy = dot(high, edges) + dot(low, edges) + jnp.sum(middle * middle, axis=1, keepdims=True)
    return 1.0 / (length * jnp.sqrt(energy * (1.0 / length) + 1e-05))


def shape_spectra(shapes, forward):
    spectra = []
    for h in range(shapes.shape[1] // LAGS):
        part = shapes[:, h * LAGS : (h + 1) * LAGS]
        mine = dot(jnp.concatenate([part, part], axis=1), forward)
        spectra.append((mine[:, :LAGS], mine[:, LAGS:]))
    return spectra


def match_lines(mine, theirs, scale, inverse):
    real = imag = 0.0
    for (mine_r, mine_i), (theirs_r, theirs_i) in zip(mine, theirs):
        real = real + (theirs_r * mine_r + theirs_i * mine_i)
        imag = imag + (theirs_i * mine_r - theirs_r * mine_i)
    product = jnp.concatenate([real, imag], axis=1)
    high = product.astype(jnp.bfloat16)
    low = (product - high.astype(jnp.float32)).astype(jnp.bfloat16)
    return dot(jnp.concatenate([high, high, low], axis=1), inverse) * scale


def sum_lines(sums, left):
    total = 0.0
    for _ in range(3):
        part = left.astype(jnp.bfloat16)
        left = left - part.astype(jnp.float32)
        total = total + dot(sums, part)
    return total


def tables_of(table_ref):
    back = table_ref[2 * LAGS :, :]
    high, low = back[:, :LAGS], back[:, LAGS:]
    return table_ref[: 2 * LAGS, :], jnp.concatenate([high, low, high], axis=0)


def trace_kernel(cfg, here_ref, lists_ref, *refs):
    waves_refs, (table_ref, edges_ref, kept_ref, sums_ref) = refs[:-4], refs[-4:]
    here = [here_ref[0]]
    for _ in range(1, cfg["halves"]):
        other = here[-1] + cfg["group"]
        here.append(jnp.where(other >= cfg["devices"], other - cfg["devices"], other))
    shift, goal, column = tile_lines(cfg, here, lists_ref[...])
    waves = [ref[...].reshape(-1, ref.shape[2]) for ref in waves_refs]
    narrow = cut_traces(cfg, shift, goal, jnp.concatenate(waves, axis=0))
    kept_ref[:, 2 * cfg["length"] :] = levels_scale(cfg, narrow, edges_ref[...])
    sums_ref[...] = line_sums(cfg, column)

    sign = (1 - 2 * (iota((1, LAGS), 1) & 1)).astype(jnp.float32)
    before = None
    for h in range(cfg["length"] // LAGS + 1):
        part = narrow[:, h * LAGS : (h + 1) * LAGS]
        here = dot(jnp.concatenate([part, part], axis=1), table_ref[...])
        here = here[:, :LAGS], here[:, LAGS:]
        if before is not None:
            kept_ref[:, (2 * h - 2) * LAGS : (2 * h - 1) * LAGS] = before[0] + sign * here[1]
            kept_ref[:, (2 * h - 1) * LAGS : 2 * h * LAGS] = before[1] - sign * here[0]
        before = here


def line_pieces(cfg, packed):
    rows, more, length = cfg["rows"], cfg["more"], cfg["length"]
    tile = packed.shape[0]
    chunks = length // 128 - 1
    low, high = packed[:, :length], packed[:, length:]
    number = iota((SOURCES, rows, 1), 1).reshape(tile, 1)
    deep = jnp.zeros((tile, 1), jnp.int32)
    for k in range(1, rows // chunks + 1):
        deep = deep + jnp.where(number >= k * chunks, 1, 0)
    source = iota((SOURCES, rows, 1), 0).reshape(tile, 1) * rows + more + deep
    source = jnp.where(number < more, source, -1)
    moved = dot(jnp.where(iota((tile, tile), 1) == source, 1.0, 0.0).astype(jnp.bfloat16), high)
    last = jnp.zeros((tile, 128), jnp.float32)
    for m in range(chunks):
        last = last + jnp.where(number - deep * chunks == m, moved[:, m * 128 : (m + 1) * 128], 0.0)
    high = jnp.concatenate([high, last.astype(jnp.bfloat16)], axis=1)
    lines = jnp.concatenate([low, high], axis=0)
    return lines


def match_kernel(cfg, tiles, shapes_hbm, kept_hbm, sums_hbm, table_hbm, sent_ref, *scratch):
    shapes_ref, kept_ref, sums_ref, table_ref, sems = scratch
    packed = shapes_ref.shape[0] // tiles
    tile = kept_ref.shape[0] // tiles
    groups = sent_ref.shape[0] // tiles
    length = cfg["length"]
    copies = []

    def fetch(source, buffer, part=None):
        if part is not None:
            source, buffer = source.at[part], buffer.at[part]
        copies.append(pltpu.make_async_copy(source, buffer, sems.at[len(copies)]))
        copies[-1].start()
        return copies[-1]

    lines = [pl.ds(t * packed, packed) for t in range(tiles)]
    halves = [pl.ds(q * 2 * LAGS, 2 * LAGS) for q in range(2)]
    part = tile // 2

    def fetch_kept(t, k):
        return fetch(kept_hbm, kept_ref, pl.ds(t * tile + k * part, part))

    forward = fetch(table_hbm, table_ref, halves[0])
    shapes = fetch(shapes_hbm, shapes_ref, lines[0])
    kept = [fetch_kept(0, 0)]
    forward.wait()
    for t in range(tiles):
        shapes.wait()
        if t == 0:
            kept.append(fetch_kept(0, 1))
            inverse = fetch(table_hbm, table_ref, halves[1])
            sums = fetch(sums_hbm, sums_ref)
        mine = shape_spectra(line_pieces(cfg, shapes_ref[lines[t], :]), table_ref[: 2 * LAGS, :])
        if t == 0:
            for copy in (inverse, sums):
                copy.wait()
        ends = pl.ds(t * groups, groups)
        total = 0.0
        for k in range(2):
            kept[2 * t + k].wait()
            if t + 1 < tiles:
                if k == 0:
                    shapes = fetch(shapes_hbm, shapes_ref, lines[t + 1])
                kept.append(fetch_kept(t + 1, k))
            theirs = kept_ref[pl.ds(t * tile + k * part, part), :]
            spectra = [
                (theirs[:, 2 * h * LAGS : (2 * h + 1) * LAGS], theirs[:, (2 * h + 1) * LAGS : (2 * h + 2) * LAGS])
                for h in range(length // LAGS)
            ]
            rows = slice(k * part, (k + 1) * part)
            ours = [(real[rows], imag[rows]) for real, imag in mine]
            left = match_lines(ours, spectra, theirs[:, 2 * length :], tables_of(table_ref)[1])
            total = total + sum_lines(sums_ref[ends, rows], left)
        sent_ref[ends, :] = total


def stack_kernel(factor, parts_ref, stacks_ref, top_ref):
    stacks = jnp.sum(parts_ref[...], axis=0) * factor
    stacks_ref[...] = stacks
    top_ref[...] = jnp.broadcast_to(jnp.max(stacks, axis=0, keepdims=True), top_ref.shape)


def body(waveforms, templates, stations, moveouts):
    devices, group, halves = lax.axis_size(AXES), lax.axis_size(GROUP), lax.axis_size(HALF)
    tpl_count, slot_count = stations.shape
    comps, length = templates.shape[2:]
    station_dev, _, samples = waveforms.shape
    seg_len = length + LAGS
    pairs = tpl_count * slot_count
    capacity = (2 * pairs + devices - 1) // devices
    chunks = length // 128 - 1
    total = halves * comps * capacity
    rows = 16
    while total - rows + max(0, -(-(total - rows) // chunks)) > rows:
        rows += 16
    more = max(0, total - rows)
    cfg = dict(
        devices=devices,
        group=group,
        halves=halves,
        parts=[lax.axis_size(name) for name in PARTS],
        station_dev=station_dev,
        tpl_count=tpl_count,
        slot_count=slot_count,
        comps=comps,
        capacity=capacity,
        rows=rows,
        more=more,
        length=length,
        seg_len=seg_len,
        shift_bits=bits_of(samples - seg_len + 1),
        row_bits=bits_of(station_dev),
    )
    table = jnp.asarray(transform_table(LAGS))
    edges = jnp.asarray(edge_table(LAGS))
    tiles = group // SOURCES
    tile = 2 * SOURCES * rows
    lines = 2 * group * rows
    width = length + chunks * 128
    sums_tile = SOURCES * tpl_count
    kept_len = 2 * length + LAGS
    whole = pl.BlockSpec(memory_space=pltpu.VMEM)
    anywhere = pl.BlockSpec(memory_space=pl.ANY)
    params = pltpu.CompilerParams(vmem_limit_bytes=60 * MIB)
    by_slot = templates.transpose(1, 2, 0, 3)
    waves = waveforms.transpose(1, 0, 2)
    half = lax.axis_index(HALF).reshape(1)
    here = lax.axis_index(AXES).reshape(1)

    def work(flops, size):
        return pl.CostEstimate(flops=flops, bytes_accessed=size, transcendentals=0)

    def exchange(x, axes):
        return lax.all_to_all(x, axes, split_axis=0, concat_axis=0, tiled=True)

    def same(shape):
        return pl.BlockSpec(shape, lambda i: (0,) * len(shape))

    def tiled(*shape):
        return pl.BlockSpec(shape, lambda i: (i, 0))

    traces = [waves] + [lax.ppermute(waves, HALF, [(0, 1), (1, 0)])] * (halves - 1)
    lists = pl.pallas_call(
        functools.partial(list_kernel, cfg),
        out_shape=jax.ShapeDtypeStruct((group, tpl_count, -(-slot_count // 128) * 128), jnp.int32),
        in_specs=[whole, whole],
        out_specs=whole,
        compiler_params=params,
        cost_estimate=work(1, 1),
        name="lists",
    )(stations, moveouts)
    lists = exchange(lists, GROUP).reshape(group * tpl_count, lists.shape[2])

    packed = pl.pallas_call(
        functools.partial(pack_kernel, cfg),
        out_shape=jax.ShapeDtypeStruct((group * rows, width), jnp.bfloat16),
        in_specs=[pl.BlockSpec(memory_space=pltpu.SMEM), whole, anywhere],
        out_specs=anywhere,
        scratch_shapes=[
            pltpu.VMEM(by_slot.shape, jnp.bfloat16),
            pltpu.VMEM((comps, pairs, length), jnp.bfloat16),
            pltpu.VMEM((group * rows, width), jnp.bfloat16),
            pltpu.SemaphoreType.DMA,
            pltpu.SemaphoreType.DMA((tiles,)),
        ],
        compiler_params=params,
        cost_estimate=work(5 * 10**9, 1),
        name="pack",
    )(half, stations, by_slot)
    _, packed = lax.optimization_barrier((lists, packed))
    arrived = exchange(packed.reshape(group, rows, width), GROUP).reshape(group * rows, width)

    kept, sums = pl.pallas_call(
        functools.partial(trace_kernel, cfg),
        grid=(tiles,),
        out_shape=[
            jax.ShapeDtypeStruct((lines, kept_len), jnp.float32),
            jax.ShapeDtypeStruct((group * tpl_count, tile), jnp.bfloat16),
        ],
        in_specs=[pl.BlockSpec(memory_space=pltpu.SMEM), tiled(sums_tile, lists.shape[1])]
        + [same(waves.shape)] * halves
        + [same((2 * LAGS, 2 * LAGS)), same(edges.shape)],
        out_specs=[tiled(tile, kept_len), tiled(sums_tile, tile)],
        compiler_params=params,
        cost_estimate=work(10**12, 1),
        name="traces",
    )(here, lists, *traces, table, edges)
    operands = (arrived, kept, sums, table)
    sent = pl.pallas_call(
        functools.partial(match_kernel, cfg, tiles),
        out_shape=jax.ShapeDtypeStruct((group * tpl_count, LAGS), jnp.float32),
        in_specs=[anywhere] * len(operands),
        out_specs=whole,
        scratch_shapes=[pltpu.VMEM(x.shape, x.dtype) for x in operands]
        + [pltpu.SemaphoreType.DMA((3 + 3 * tiles,))],
        compiler_params=pltpu.CompilerParams(vmem_limit_bytes=57 * MIB),
        name="match",
    )(*operands)

    parts = exchange(sent.reshape(group, tpl_count, LAGS), GROUP)
    stacks, top = pl.pallas_call(
        functools.partial(stack_kernel, math.sqrt(length / (comps * slot_count))),
        out_shape=[
            jax.ShapeDtypeStruct((tpl_count, LAGS), jnp.float32),
            jax.ShapeDtypeStruct((devices, 1, LAGS), jnp.float32),
        ],
        in_specs=[whole],
        out_specs=[whole, whole],
        compiler_params=pltpu.CompilerParams(vmem_limit_bytes=16 * MIB),
        name="stack",
    )(parts)
    return stacks, jnp.max(exchange(top, AXES), axis=(0, 1))


def solution(mesh):
    slow, fast = mesh.devices.shape
    halves = 2 if slow % 2 == 0 else 1
    deep = 2 if slow // halves % 2 == 0 else 1
    cores = 2 if fast % 2 == 0 else 1
    shape = (halves, deep, slow // halves // deep, fast // cores, cores)
    split = jax.sharding.Mesh(mesh.devices.reshape(shape), AXES)
    placed = (
        P(AXES, None, None),
        P(AXES, None, None, None),
        P(AXES, None),
        P(AXES, None),
    )
    return jax.shard_map(body, mesh=split, in_specs=placed, out_specs=(P(AXES, None), P()), check_vma=False)
```

```python
import functools
import math

import jax
import jax.numpy as jnp
import ml_dtypes
import numpy as np
from jax import lax
from jax.experimental import pallas as pl
from jax.experimental.pallas import tpu as pltpu
from jax.sharding import PartitionSpec as P

LAGS = 256
HALF = "half"
DEEP = "deep"
PARTS = (DEEP, "wide", "sta", "core")
AXES = (HALF,) + PARTS
GROUP = PARTS[::-1]
SOURCES = 8
MIB = 1024 * 1024


def bits_of(limit):
    return max(1, (limit - 1).bit_length())


def split_table(table):
    high = table.astype(ml_dtypes.bfloat16)
    return high, (table - high.astype(np.float64)).astype(ml_dtypes.bfloat16)


def transform_table(piece):
    size = 2 * piece
    angle = 2.0 * np.pi * (np.arange(piece) + 0.5) / size
    phase = np.arange(piece)[:, None] * angle[None, :]
    forward = np.concatenate([np.cos(phase), -np.sin(phase)], axis=1)
    inverse = np.concatenate([np.cos(phase.T), -np.sin(phase.T)], axis=0) * (2.0 / size)
    return np.concatenate([*split_table(forward), np.concatenate(split_table(inverse), axis=1)], axis=0)


def edge_table(lag_count):
    sample = np.arange(lag_count)[:, None]
    lag = np.arange(lag_count)[None, :]
    return np.concatenate([sample >= lag, sample < lag], axis=0).astype(ml_dtypes.bfloat16)


def iota(shape, axis):
    return lax.broadcasted_iota(jnp.int32, shape, axis)


def dot(a, b):
    return jnp.dot(a, b, preferred_element_type=jnp.float32)


def exact_dot(a, b):
    return jnp.dot(a, b, precision=lax.Precision.HIGHEST, preferred_element_type=jnp.float32)


def entry_lanes(tpl_count, slot_count):
    pairs = tpl_count * slot_count
    first = iota((slot_count, pairs), 0) * tpl_count
    entry = iota((slot_count, pairs), 1)
    spread = jnp.where((entry >= first) & (entry < first + tpl_count), 1.0, 0.0)
    start = jnp.sum(spread * first.astype(jnp.float32), axis=0, keepdims=True)
    return spread, iota((1, pairs), 1).astype(jnp.float32) - start


def as_lanes(values, spread, place, tpl_count):
    owners = values.shape[0] // tpl_count
    pairs = spread.shape[1]
    wide = exact_dot(values.astype(jnp.float32), spread).reshape(owners, tpl_count, pairs)
    own = iota((1, tpl_count, pairs), 1).astype(jnp.float32) == place.reshape(1, 1, pairs)
    return jnp.sum(jnp.where(own, wide, 0.0), axis=1)


def count_before(hits):
    pairs = hits.shape[1]
    earlier = jnp.where(iota((pairs, pairs), 0) < iota((pairs, pairs), 1), 1.0, 0.0)
    return dot(hits.astype(jnp.bfloat16), earlier.astype(jnp.bfloat16))


def list_kernel(cfg, stations_ref, moveouts_ref, lists_ref):
    lists = stations_ref[...] * (1 << cfg["shift_bits"]) + moveouts_ref[...]
    group, tpl_count, _ = lists_ref.shape
    slot_count = lists.shape[1]
    lists_ref[:, :, :slot_count] = jnp.broadcast_to(lists.reshape(1, tpl_count, slot_count), (group, tpl_count, slot_count))


def pack_kernel(
    cfg, half_ref, stations_ref, templates_hbm, packed_hbm, raw_ref, shapes_ref, packed_ref, in_sem, out_sems
):
    load = pltpu.make_async_copy(templates_hbm, raw_ref, in_sem)
    load.start()
    tpl_count, slot_count = stations_ref.shape
    pairs = tpl_count * slot_count
    devices, group, halves, rows = cfg["devices"], cfg["group"], cfg["halves"], cfg["rows"]
    spread, place = entry_lanes(tpl_count, slot_count)
    station = as_lanes(stations_ref[...], spread, place, tpl_count)
    device = jnp.floor((station + 0.5) * (1.0 / cfg["station_dev"]))
    onehot = jnp.where(iota((devices, pairs), 0).astype(jnp.float32) == device, 1.0, 0.0)
    rank = jnp.sum(onehot * count_before(onehot), axis=0, keepdims=True)
    half = jnp.floor((device + 0.5) * (1.0 / group))
    away = jnp.where(half == half_ref[0].astype(jnp.float32), 0.0, 1.0)
    holder = device - half * group
    number = jnp.zeros_like(holder)
    for size in cfg["parts"][::-1]:
        rest = jnp.floor((holder + 0.5) * (1.0 / size))
        number = number * size + (holder - rest * size)
        holder = rest
    holder = number
    capacity = cfg["capacity"]
    base = jnp.where(rank < float(capacity), away * (cfg["comps"] * capacity) + rank, -1e6)

    comps, length = raw_ref.shape[1], raw_ref.shape[3]
    load.wait()
    for c in range(comps):
        values = raw_ref[:, c].astype(jnp.float32).reshape(pairs, length)
        centred = values - jnp.mean(values, axis=-1, keepdims=True)
        spread_c = jnp.sqrt(jnp.mean(centred * centred, axis=-1, keepdims=True) + 1e-05)
        shapes_ref[c] = (centred * (1.0 / spread_c)).astype(jnp.bfloat16)

    more, step_len = cfg["more"], 128
    chunks = length // step_len - 1
    tile = SOURCES * rows
    copies = []
    for step in range(group // SOURCES):
        at = iota((tile, pairs), 0).astype(jnp.float32)
        first = (holder - float(step * SOURCES)) * rows
        low = jnp.zeros((tile, length), jnp.float32)
        high = jnp.zeros((tile, chunks * step_len), jnp.float32)
        lasts = [jnp.zeros((tile, step_len), jnp.float32) for _ in range(chunks)]
        for c in range(comps):
            line = base + float(c * capacity)
            extra = line - float(rows)
            there = (extra >= 0.0) & (extra < float(more))
            deep = jnp.floor((extra + 0.5) * (1.0 / chunks))
            spot = jnp.where(there, extra - deep * chunks, -1.0)
            shapes = shapes_ref[c]

            def pick(ok, row):
                return jnp.where(at == jnp.where(ok, first + row, -1.0), 1.0, 0.0).astype(jnp.bfloat16)

            low = low + dot(pick((line >= 0.0) & (line < float(rows)), line), shapes)
            high = high + dot(pick(there, extra), shapes[:, : chunks * step_len])
            for m in range(chunks):
                picked = pick(spot == float(m), float(more) + deep)
                lasts[m] = lasts[m] + dot(picked, shapes[:, chunks * step_len :])
        part = pl.ds(step * tile, tile)
        packed_ref[part, :length] = low.astype(jnp.bfloat16)
        packed_ref[part, length:] = (high + jnp.concatenate(lasts, axis=1)).astype(jnp.bfloat16)
        copies.append(pltpu.make_async_copy(packed_ref.at[part], packed_hbm.at[part], out_sems.at[step]))
        copies[-1].start()
    for copy in copies:
        copy.wait()


def tile_lines(cfg, here, lists):
    capacity, rows, comps, halves = cfg["capacity"], cfg["rows"], cfg["comps"], cfg["halves"]
    station_dev, shift_bits, row_bits = cfg["station_dev"], cfg["shift_bits"], cfg["row_bits"]
    tpl_count, slot_count = cfg["tpl_count"], cfg["slot_count"]
    lists = lists[:, :slot_count]
    pairs = tpl_count * slot_count
    tile = 2 * SOURCES * rows
    spread, place = entry_lanes(tpl_count, slot_count)
    station = as_lanes(lax.shift_right_logical(lists, shift_bits), spread, place, tpl_count)
    shift = as_lanes(lists & ((1 << shift_bits) - 1), spread, place, tpl_count)

    def per_line(x):
        wide = jnp.broadcast_to(x.reshape(SOURCES, 1, pairs), (SOURCES, rows, pairs)).reshape(tile // 2, pairs)
        return jnp.concatenate([wide, wide], axis=0)

    ranks, codes = [], []
    for device in here:
        row = station - (device * station_dev).astype(jnp.float32)
        hit = jnp.where((row >= 0.0) & (row < float(station_dev)), 1.0, 0.0)
        ranks.append(jnp.where(hit > 0.0, count_before(hit), -1.0))
        codes.append(((place + 1.0) * (1 << row_bits) + row) * (1 << shift_bits) + shift)

    line = iota((SOURCES, rows, 1), 1).reshape(tile // 2, 1)
    line = jnp.concatenate([line, line + rows], axis=0)
    owner = iota((SOURCES, rows, 1), 0).reshape(tile // 2, 1)
    owner = jnp.concatenate([owner, owner], axis=0)
    panel = jnp.zeros((tile, 1), jnp.int32)
    for m in range(1, halves * comps + 1):
        panel = panel + jnp.where(line >= m * capacity, 1, 0)
    slot = jnp.where(panel < halves * comps, line - panel * capacity, -2).astype(jnp.float32)
    code = jnp.zeros((tile, 1), jnp.float32)
    for q in range(halves):
        mine = jnp.where((panel >= q * comps) & (panel < (q + 1) * comps), slot, -2.0)
        code = code + jnp.sum(jnp.where(per_line(ranks[q]) == mine, per_line(codes[q]), 0.0), axis=1, keepdims=True)
    code = code.astype(jnp.int32)
    row = lax.shift_right_logical(code, shift_bits) & ((1 << row_bits) - 1)
    tpl = lax.shift_right_logical(code, shift_bits + row_bits) - 1
    goal = panel * station_dev + row
    return (
        code & ((1 << shift_bits) - 1),
        jnp.where(tpl >= 0, goal, -1),
        jnp.where(tpl >= 0, owner * tpl_count + tpl, -1),
    )


def cut_traces(cfg, shift, goal, waves):
    tile, seg_len, shift_bits = shift.shape[0], cfg["seg_len"], cfg["shift_bits"]
    pick = jnp.where(iota((tile, waves.shape[0]), 1) == goal, 1.0, 0.0).astype(jnp.bfloat16)
    x = dot(pick, waves).astype(jnp.bfloat16)

    def choose(step, moved, still):
        flag = jnp.where((shift & step) != 0, 1.0, 0.0)
        return moved * flag.astype(jnp.bfloat16) + still * (1.0 - flag).astype(jnp.bfloat16)

    for bit in range(shift_bits - 1, 6, -1):
        step = 1 << bit
        width = seg_len + step
        if x.shape[1] < width + step:
            x = jnp.concatenate([x, jnp.zeros((tile, width + step - x.shape[1]), jnp.bfloat16)], axis=1)
        x = choose(step, x[:, step : step + width], x[:, :width])
    for bit in range(min(shift_bits, 7) - 1, -1, -1):
        step = 1 << bit
        x = choose(step, pltpu.roll(x, x.shape[1] - step, 1), x)
    return x[:, :seg_len]


def line_sums(cfg, column):
    groups = SOURCES * cfg["tpl_count"]
    return jnp.where(iota((column.shape[0], groups), 1) == column, 1.0, 0.0).T.astype(jnp.bfloat16)


def levels_scale(cfg, narrow, edges):
    length = cfg["length"]
    ends = jnp.concatenate([narrow[:, :LAGS], narrow[:, length:]], axis=1).astype(jnp.float32)
    ends = ends * ends
    high = ends.astype(jnp.bfloat16)
    low = (ends - high.astype(jnp.float32)).astype(jnp.bfloat16)
    middle = narrow[:, LAGS:length].astype(jnp.float32)
    energy = dot(high, edges) + dot(low, edges) + jnp.sum(middle * middle, axis=1, keepdims=True)
    return 1.0 / (length * jnp.sqrt(energy * (1.0 / length) + 1e-05))


def shape_spectra(shapes, forward):
    spectra = []
    for h in range(shapes.shape[1] // LAGS):
        part = shapes[:, h * LAGS : (h + 1) * LAGS]
        mine = dot(jnp.concatenate([part, part], axis=1), forward)
        spectra.append((mine[:, :LAGS], mine[:, LAGS:]))
    return spectra


def match_lines(mine, theirs, scale, inverse):
    real = imag = 0.0
    for (mine_r, mine_i), (theirs_r, theirs_i) in zip(mine, theirs):
        real = real + (theirs_r * mine_r + theirs_i * mine_i)
        imag = imag + (theirs_i * mine_r - theirs_r * mine_i)
    product = jnp.concatenate([real, imag], axis=1)
    high = product.astype(jnp.bfloat16)
    low = (product - high.astype(jnp.float32)).astype(jnp.bfloat16)
    return dot(jnp.concatenate([high, high, low], axis=1), inverse) * scale


def sum_lines(sums, left):
    total = 0.0
    for _ in range(3):
        part = left.astype(jnp.bfloat16)
        left = left - part.astype(jnp.float32)
        total = total + dot(sums, part)
    return total


def tables_of(table_ref):
    back = table_ref[2 * LAGS :, :]
    high, low = back[:, :LAGS], back[:, LAGS:]
    return table_ref[: 2 * LAGS, :], jnp.concatenate([high, low, high], axis=0)


def trace_kernel(cfg, here_ref, lists_ref, *refs):
    waves_refs, (table_ref, edges_ref, kept_ref, sums_ref) = refs[:-4], refs[-4:]
    here = [here_ref[0]]
    for _ in range(1, cfg["halves"]):
        other = here[-1] + cfg["group"]
        here.append(jnp.where(other >= cfg["devices"], other - cfg["devices"], other))
    shift, goal, column = tile_lines(cfg, here, lists_ref[...])
    waves = [ref[...].reshape(-1, ref.shape[2]) for ref in waves_refs]
    narrow = cut_traces(cfg, shift, goal, jnp.concatenate(waves, axis=0))
    kept_ref[:, 2 * cfg["length"] :] = levels_scale(cfg, narrow, edges_ref[...])
    sums_ref[...] = line_sums(cfg, column)

    sign = (1 - 2 * (iota((1, LAGS), 1) & 1)).astype(jnp.float32)
    before = None
    for h in range(cfg["length"] // LAGS + 1):
        part = narrow[:, h * LAGS : (h + 1) * LAGS]
        here = dot(jnp.concatenate([part, part], axis=1), table_ref[...])
        here = here[:, :LAGS], here[:, LAGS:]
        if before is not None:
            kept_ref[:, (2 * h - 2) * LAGS : (2 * h - 1) * LAGS] = before[0] + sign * here[1]
            kept_ref[:, (2 * h - 1) * LAGS : 2 * h * LAGS] = before[1] - sign * here[0]
        before = here


def line_pieces(cfg, packed):
    rows, more, length = cfg["rows"], cfg["more"], cfg["length"]
    tile = packed.shape[0]
    chunks = length // 128 - 1
    low, high = packed[:, :length], packed[:, length:]
    number = iota((SOURCES, rows, 1), 1).reshape(tile, 1)
    deep = jnp.zeros((tile, 1), jnp.int32)
    for k in range(1, rows // chunks + 1):
        deep = deep + jnp.where(number >= k * chunks, 1, 0)
    source = iota((SOURCES, rows, 1), 0).reshape(tile, 1) * rows + more + deep
    source = jnp.where(number < more, source, -1)
    moved = dot(jnp.where(iota((tile, tile), 1) == source, 1.0, 0.0).astype(jnp.bfloat16), high)
    last = jnp.zeros((tile, 128), jnp.float32)
    for m in range(chunks):
        last = last + jnp.where(number - deep * chunks == m, moved[:, m * 128 : (m + 1) * 128], 0.0)
    high = jnp.concatenate([high, last.astype(jnp.bfloat16)], axis=1)
    lines = jnp.concatenate([low, high], axis=0)
    return lines


def match_kernel(cfg, tiles, shapes_hbm, kept_hbm, sums_hbm, table_hbm, sent_ref, *scratch):
    shapes_ref, kept_ref, sums_ref, table_ref, sems = scratch
    packed = shapes_ref.shape[0] // tiles
    tile = kept_ref.shape[0] // tiles
    groups = sent_ref.shape[0] // tiles
    length = cfg["length"]
    copies = []

    def fetch(source, buffer, part=None):
        if part is not None:
            source, buffer = source.at[part], buffer.at[part]
        copies.append(pltpu.make_async_copy(source, buffer, sems.at[len(copies)]))
        copies[-1].start()
        return copies[-1]

    lines = [pl.ds(t * packed, packed) for t in range(tiles)]
    halves = [pl.ds(q * 2 * LAGS, 2 * LAGS) for q in range(2)]
    forward = fetch(table_hbm, table_ref, halves[0])
    part = tile // 2
    shapes, kept = [], []
    for t in range(tiles):
        shapes.append(fetch(shapes_hbm, shapes_ref, lines[t]))
        kept.append([fetch(kept_hbm, kept_ref, pl.ds(t * tile + k * part, part)) for k in range(2)])
        if t == 0:
            inverse = fetch(table_hbm, table_ref, halves[1])
            sums = fetch(sums_hbm, sums_ref)
    forward.wait()
    for t in range(tiles):
        shapes[t].wait()
        mine = shape_spectra(line_pieces(cfg, shapes_ref[lines[t], :]), table_ref[: 2 * LAGS, :])
        if t == 0:
            for copy in (inverse, sums):
                copy.wait()
        ends = pl.ds(t * groups, groups)
        total = 0.0
        for k in range(2):
            kept[t][k].wait()
            theirs = kept_ref[pl.ds(t * tile + k * part, part), :]
            spectra = [
                (theirs[:, 2 * h * LAGS : (2 * h + 1) * LAGS], theirs[:, (2 * h + 1) * LAGS : (2 * h + 2) * LAGS])
                for h in range(length // LAGS)
            ]
            rows = slice(k * part, (k + 1) * part)
            ours = [(real[rows], imag[rows]) for real, imag in mine]
            left = match_lines(ours, spectra, theirs[:, 2 * length :], tables_of(table_ref)[1])
            total = total + sum_lines(sums_ref[ends, rows], left)
        sent_ref[ends, :] = total


def stack_kernel(factor, parts_ref, stacks_ref, top_ref):
    stacks = jnp.sum(parts_ref[...], axis=0) * factor
    stacks_ref[...] = stacks
    top_ref[...] = jnp.broadcast_to(jnp.max(stacks, axis=0, keepdims=True), top_ref.shape)


def body(waveforms, templates, stations, moveouts):
    devices, group, halves = lax.axis_size(AXES), lax.axis_size(GROUP), lax.axis_size(HALF)
    tpl_count, slot_count = stations.shape
    comps, length = templates.shape[2:]
    station_dev, _, samples = waveforms.shape
    seg_len = length + LAGS
    pairs = tpl_count * slot_count
    capacity = (2 * pairs + devices - 1) // devices
    chunks = length // 128 - 1
    total = halves * comps * capacity
    rows = 16
    while total - rows + max(0, -(-(total - rows) // chunks)) > rows:
        rows += 16
    more = max(0, total - rows)
    cfg = dict(
        devices=devices,
        group=group,
        halves=halves,
        parts=[lax.axis_size(name) for name in PARTS],
        station_dev=station_dev,
        tpl_count=tpl_count,
        slot_count=slot_count,
        comps=comps,
        capacity=capacity,
        rows=rows,
        more=more,
        length=length,
        seg_len=seg_len,
        shift_bits=bits_of(samples - seg_len + 1),
        row_bits=bits_of(station_dev),
    )
    table = jnp.asarray(transform_table(LAGS))
    edges = jnp.asarray(edge_table(LAGS))
    tiles = group // SOURCES
    tile = 2 * SOURCES * rows
    lines = 2 * group * rows
    width = length + chunks * 128
    sums_tile = SOURCES * tpl_count
    kept_len = 2 * length + LAGS
    whole = pl.BlockSpec(memory_space=pltpu.VMEM)
    anywhere = pl.BlockSpec(memory_space=pl.ANY)
    params = pltpu.CompilerParams(vmem_limit_bytes=60 * MIB)
    by_slot = templates.transpose(1, 2, 0, 3)
    waves = waveforms.transpose(1, 0, 2)
    half = lax.axis_index(HALF).reshape(1)
    here = lax.axis_index(AXES).reshape(1)

    def work(flops, size):
        return pl.CostEstimate(flops=flops, bytes_accessed=size, transcendentals=0)

    def exchange(x, axes):
        return lax.all_to_all(x, axes, split_axis=0, concat_axis=0, tiled=True)

    def same(shape):
        return pl.BlockSpec(shape, lambda i: (0,) * len(shape))

    def tiled(*shape):
        return pl.BlockSpec(shape, lambda i: (i, 0))

    traces = [waves] + [lax.ppermute(waves, HALF, [(0, 1), (1, 0)])] * (halves - 1)
    lists = pl.pallas_call(
        functools.partial(list_kernel, cfg),
        out_shape=jax.ShapeDtypeStruct((group, tpl_count, -(-slot_count // 128) * 128), jnp.int32),
        in_specs=[whole, whole],
        out_specs=whole,
        compiler_params=params,
        cost_estimate=work(1, 1),
        name="lists",
    )(stations, moveouts)
    lists = exchange(lists, GROUP).reshape(group * tpl_count, lists.shape[2])

    packed = pl.pallas_call(
        functools.partial(pack_kernel, cfg),
        out_shape=jax.ShapeDtypeStruct((group * rows, width), jnp.bfloat16),
        in_specs=[pl.BlockSpec(memory_space=pltpu.SMEM), whole, anywhere],
        out_specs=anywhere,
        scratch_shapes=[
            pltpu.VMEM(by_slot.shape, jnp.bfloat16),
            pltpu.VMEM((comps, pairs, length), jnp.bfloat16),
            pltpu.VMEM((group * rows, width), jnp.bfloat16),
            pltpu.SemaphoreType.DMA,
            pltpu.SemaphoreType.DMA((tiles,)),
        ],
        compiler_params=params,
        cost_estimate=work(5 * 10**9, 1),
        name="pack",
    )(half, stations, by_slot)
    _, packed = lax.optimization_barrier((lists, packed))
    arrived = exchange(packed.reshape(group, rows, width), GROUP).reshape(group * rows, width)

    kept, sums = pl.pallas_call(
        functools.partial(trace_kernel, cfg),
        grid=(tiles,),
        out_shape=[
            jax.ShapeDtypeStruct((lines, kept_len), jnp.float32),
            jax.ShapeDtypeStruct((group * tpl_count, tile), jnp.bfloat16),
        ],
        in_specs=[pl.BlockSpec(memory_space=pltpu.SMEM), tiled(sums_tile, lists.shape[1])]
        + [same(waves.shape)] * halves
        + [same((2 * LAGS, 2 * LAGS)), same(edges.shape)],
        out_specs=[tiled(tile, kept_len), tiled(sums_tile, tile)],
        compiler_params=params,
        cost_estimate=work(10**12, 1),
        name="traces",
    )(here, lists, *traces, table, edges)
    operands = (arrived, kept, sums, table)
    sent = pl.pallas_call(
        functools.partial(match_kernel, cfg, tiles),
        out_shape=jax.ShapeDtypeStruct((group * tpl_count, LAGS), jnp.float32),
        in_specs=[anywhere] * len(operands),
        out_specs=whole,
        scratch_shapes=[pltpu.VMEM(x.shape, x.dtype) for x in operands]
        + [pltpu.SemaphoreType.DMA((3 + 3 * tiles,))],
        compiler_params=pltpu.CompilerParams(vmem_limit_bytes=40 * MIB),
        name="match",
    )(*operands)

    parts = exchange(sent.reshape(group, tpl_count, LAGS), GROUP)
    stacks, top = pl.pallas_call(
        functools.partial(stack_kernel, math.sqrt(length / (comps * slot_count))),
        out_shape=[
            jax.ShapeDtypeStruct((tpl_count, LAGS), jnp.float32),
            jax.ShapeDtypeStruct((devices, 1, LAGS), jnp.float32),
        ],
        in_specs=[whole],
        out_specs=[whole, whole],
        compiler_params=pltpu.CompilerParams(vmem_limit_bytes=16 * MIB),
        name="stack",
    )(parts)
    return stacks, jnp.max(exchange(top, AXES), axis=(0, 1))


def solution(mesh):
    slow, fast = mesh.devices.shape
    halves = 2 if slow % 2 == 0 else 1
    deep = 2 if slow // halves % 2 == 0 else 1
    cores = 2 if fast % 2 == 0 else 1
    shape = (halves, deep, slow // halves // deep, fast // cores, cores)
    split = jax.sharding.Mesh(mesh.devices.reshape(shape), AXES)
    placed = (
        P(AXES, None, None),
        P(AXES, None, None, None),
        P(AXES, None),
        P(AXES, None),
    )
    return jax.shard_map(body, mesh=split, in_specs=placed, out_specs=(P(AXES, None), P()), check_vma=False)
```
